32 devices in a mesh: fsdp: 16 (over z, y, core), seq: 2 (over x).
Axes of the slice: x: 2, y: 2, z: 4, core: 2. Of those that a mesh axis runs over, the one named last changes fastest.
Arguments:
- tokens: bfloat16 [16, 1024, 1536], P('fsdp', 'seq'), may hold values from -6 to 6
- segments: int32 [16, 1024], P('fsdp', 'seq'), may hold values from 0 to 4, as said below
- norm_gain: bfloat16 [1536], P(('fsdp', 'seq')), may hold values from 0.5 to 1.5
- in_weight: bfloat16 [1536, 6448], P(('fsdp', 'seq')), may hold values from -0.15625 to 0.15625
- conv_weight: bfloat16 [3328, 4], P(('fsdp', 'seq')), may hold values from -3 to 3
- conv_bias: bfloat16 [3328], P(('fsdp', 'seq')), may hold values from -1.5 to 1.5
- dt_bias: float32 [48], replicated, may hold values from -7 to -2
- a_log: float32 [48], replicated, may hold values from -4 to 1
- d_skip: float32 [48], replicated, may hold values from 0.5 to 1.5
- gated_gain: bfloat16 [3072], P(('fsdp', 'seq')), may hold values from 0.5 to 1.5
- out_weight: bfloat16 [3072, 1536], P(('fsdp', 'seq')), may hold values from -0.109375 to 0.109375
- cotangent: bfloat16 [16, 1024, 1536], P('fsdp', 'seq'), may hold values from -6 to 6
Outputs:
- block_out: bfloat16 [16, 1024, 1536], P('fsdp', 'seq')
- input_grad: float32 [16, 1024, 1536], P('fsdp', 'seq')
- norm_gain_grad: float32 [1536], P(('fsdp', 'seq'))
- in_weight_grad: float32 [1536, 6448], P(('fsdp', 'seq'))
- conv_weight_grad: float32 [3328, 4], P(('fsdp', 'seq'))
- conv_bias_grad: float32 [3328], P(('fsdp', 'seq'))
- dt_bias_grad: float32 [48], replicated
- a_log_grad: float32 [48], replicated
- d_skip_grad: float32 [48], replicated
- gated_gain_grad: float32 [3072], P(('fsdp', 'seq'))
- out_weight_grad: float32 [3072, 1536], P(('fsdp', 'seq'))
The draws below stay inside these ranges and needn't reach their ends.
Inputs may be any that keep to these rules, and one draw needn't show every extreme that they name: `segments`: within a sequence the numbers start at 0 and never fall, each sequence holds five documents of 102 tokens or more, and in every sequence one document runs from its first piece of 512 tokens into its last.
All inputs are finite; a program needn't handle non-finite values.
Results may differ from the reference program's by a relative error of at most 0.011.
Values may be sent and summed in bfloat16 or wider, within the bound.
No kernel may reach another device: no remote copies, remote signals or barrier semaphores. Data moves between devices by JAX's collectives and lax.ppermute only.
A program may use at most 144 MiB of HBM per device.

```python
import math
import jax
import jax.numpy as jnp
from jax import lax

D = 1536
NH = 48
HD = 64
NS = 128
KW = 4
SPAN = 256
DI = 3072
CONV = 3328
PROJ = 6448
LEN = 1024
SEQS = 16
GAP = 102


def draw_segments(key, part):
    key = jax.random.fold_in(key, 11)
    keys = jax.random.split(key, 4)
    first = jax.random.randint(keys[0], (SEQS, 1), GAP, 2 * GAP + 1)
    start = jax.random.randint(keys[1], (SEQS, 1), first + GAP, first + 2 * GAP + 1)
    final = jax.random.randint(keys[2], (SEQS, 1), LEN - 2 * GAP, LEN - GAP + 1)
    stop = jax.random.randint(keys[3], (SEQS, 1), final - 2 * GAP, final - GAP + 1)
    places = jnp.arange(LEN)[None, :]
    total = (places >= first).astype(jnp.int32) + (places >= start).astype(jnp.int32)
    total = total + (places >= stop).astype(jnp.int32) + (places >= final).astype(jnp.int32)
    return total.astype(jnp.int32)


def block_scale(own_key, shape, cuts, low, largest):
    loudness = 1.0
    for axis_at, parts in cuts:
        draws = jax.random.uniform(jax.random.fold_in(jax.random.fold_in(own_key, 6), axis_at), (parts,), jnp.float32, low / len(cuts), largest / len(cuts))
        loudness = loudness * jnp.repeat(jnp.exp(draws), shape[axis_at] // parts).reshape((-1,) + (1,) * (len(shape) - 1 - axis_at))
    return loudness


def scatter_about(rng, shape, deviation, most, shards=(), held_as=jnp.bfloat16):
    values = deviation * jax.random.normal(rng, shape, jnp.float32)
    if shards:
        values = values * block_scale(rng, shape, shards, -0.22, 0.18)
    return jnp.clip(values, -most, most).astype(held_as)


def setup_inputs(seed: int = 0) -> dict:
    key_of = jax.random.split(jax.random.key(seed), 13)
    return {
        "tokens": scatter_about(key_of[0], (SEQS, LEN, D), 1.0, 6.0, ((0, 16), (1, 2))),
        "segments": draw_segments(jax.random.fold_in(key_of[12], 71), 0),
        "norm_gain": jnp.clip(1.0 + 0.1 * jax.random.normal(key_of[2], (D,), jnp.float32), 0.5, 1.5).astype(jnp.bfloat16),
        "in_weight": scatter_about(key_of[3], (D, PROJ), D ** -0.5, 0.15625, ((0, 32),)),
        "conv_weight": scatter_about(key_of[4], (CONV, KW), KW ** -0.5, 3.0, ((0, 32),)),
        "conv_bias": scatter_about(key_of[5], (CONV,), 0.3, 1.5, ((0, 32),)),
        "dt_bias": jnp.clip(jax.random.uniform(key_of[6], (NH,), jnp.float32, -7.0, -2.0), -7.0, -2.0),
        "a_log": jnp.clip(jax.random.uniform(key_of[7], (NH,), jnp.float32, -4.0, 1.0), -4.0, 1.0),
        "d_skip": jnp.clip(jax.random.uniform(key_of[8], (NH,), jnp.float32, 0.5, 1.5), 0.5, 1.5),
        "gated_gain": jnp.clip(1.0 + 0.1 * jax.random.normal(key_of[9], (DI,), jnp.float32), 0.5, 1.5).astype(jnp.bfloat16),
        "out_weight": scatter_about(key_of[10], (DI, D), DI ** -0.5, 0.109375, ((0, 32),)),
        "cotangent": scatter_about(key_of[11], (SEQS, LEN, D), 1.0, 6.0, ((0, 16), (1, 2))),
    }


@jax.custom_vjp
def low(v):
    return lax.optimization_barrier(v.astype(jnp.bfloat16)).astype(jnp.float32)

@jax.custom_vjp
def low_back(v):
    return v

def low_keep(v):
    return (low(v), None)

def low_pass(kept, grad):
    return (grad,)

def back_keep(v):
    return (v, None)

def back_low(kept, grad):
    return (low(grad),)
low.defvjp(low_keep, low_pass)
low_back.defvjp(back_keep, back_low)
EPS = 1e-05
HIGH = lax.Precision.HIGHEST

def rms_scale(values, gain):
    return values * lax.rsqrt(lax.optimization_barrier(jnp.mean(values * values, axis=-1, keepdims=True)) + EPS) * gain

def conv_act(xbc_in, seg_in, conv_w, conv_b):
    length = xbc_in.shape[1]
    padded = jnp.pad(xbc_in, ((0, 0), (KW - 1, 0), (0, 0)))
    seg_pad = jnp.pad(seg_in, ((0, 0), (KW - 1, 0)), constant_values=-1.0)
    total = conv_b + jnp.zeros_like(xbc_in)
    for offset in range(KW):
        same = (seg_pad[:, offset:offset + length] == seg_in).astype(jnp.float32)
        total = total + padded[:, offset:offset + length] * conv_w[:, offset] * same[:, :, None]
    return jax.nn.silu(total)

def span_step(carry, block):
    state, before = carry
    x_heads, b_proj, c_proj, step_dt, log_decay, seg_blk = block
    size = seg_blk.shape[1]
    cum_decay = jnp.cumsum(log_decay, axis=1)
    order = jnp.arange(size)
    lower = order[:, None] >= order[None, :]
    inside = ((seg_blk[:, :, None] == seg_blk[:, None, :]) & lower[None]).astype(jnp.float32)
    spread = cum_decay[:, :, None, :] - cum_decay[:, None, :, :]
    decay = jnp.exp(jnp.where(inside[..., None] > 0, spread, 0.0)) * inside[..., None]
    scores = jnp.einsum('gin,gjn->gij', c_proj, b_proj, precision=HIGH)
    mixing = decay * scores[..., None] * step_dt[:, None, :, :]
    result = jnp.einsum('gijh,gjhp->gihp', mixing, x_heads, precision=HIGH)
    keep = (seg_blk == before[:, None]).astype(jnp.float32)[:, :, None] * jnp.exp(cum_decay)
    result = result + jnp.einsum('gin,ghpn->gihp', c_proj, state, precision=HIGH) * keep[..., None]
    final = seg_blk[:, -1]
    tail = (seg_blk == final[:, None]).astype(jnp.float32)[:, :, None] * jnp.exp(cum_decay[:, -1:, :] - cum_decay) * step_dt
    fresh = jnp.einsum('gjh,gjhp,gjn->ghpn', tail, x_heads, b_proj, precision=HIGH)
    carry_on = (final == before).astype(jnp.float32)[:, None] * jnp.exp(cum_decay[:, -1, :])
    state = carry_on[:, :, None, None] * state + fresh
    return ((state, final), result)

def layer(x_in, seg_in, gain_one, in_w, conv_w, conv_b, dt_bias, a_log, d_skip, gain_two, out_w):
    groups = x_in.shape[0]
    length = x_in.shape[1]
    normed = low(rms_scale(x_in, gain_one))
    proj = low(low_back(jnp.einsum('gtd,de->gte', normed, in_w, precision=HIGH)))
    gate_z = proj[..., :DI]
    xbc = proj[..., DI:DI + CONV]
    raw_dt = proj[..., DI + CONV:]
    act = conv_act(xbc, seg_in, conv_w, conv_b)
    x_heads = act[..., :DI].reshape(groups, length, NH, HD)
    b_proj = act[..., DI:DI + NS]
    c_proj = act[..., DI + NS:]
    step_dt = jax.nn.softplus(raw_dt + dt_bias)
    log_decay = -jnp.exp(a_log) * step_dt
    count = length // SPAN

    def blocks(values):
        return jnp.moveaxis(values.reshape((groups, count, SPAN) + values.shape[2:]), 1, 0)
    start = (jnp.zeros((groups, NH, HD, NS), jnp.float32), jnp.full((groups,), -1.0, jnp.float32))
    _, pieces = lax.scan(jax.checkpoint(span_step), start, (blocks(x_heads), blocks(b_proj), blocks(c_proj), blocks(step_dt), blocks(log_decay), blocks(seg_in)))
    mixed = jnp.moveaxis(pieces, 0, 1).reshape(groups, length, NH, HD) + d_skip[:, None] * x_heads
    gated = mixed.reshape(groups, length, DI) * jax.nn.silu(gate_z)
    normed_two = low(rms_scale(gated, gain_two))
    return x_in + jnp.einsum('gtc,cd->gtd', normed_two, out_w, precision=HIGH)

def reference(tokens, segments, norm_gain, in_weight, conv_weight, conv_bias, dt_bias, a_log, d_skip, gated_gain, out_weight, cotangent):
    group = math.gcd(SEQS, max(1, 4096 // LEN))
    rounds = SEQS // group
    params = (norm_gain.astype(jnp.float32), in_weight.astype(jnp.float32), conv_weight.astype(jnp.float32), conv_bias.astype(jnp.float32), dt_bias.astype(jnp.float32), a_log.astype(jnp.float32), d_skip.astype(jnp.float32), gated_gain.astype(jnp.float32), out_weight.astype(jnp.float32))
    x_all = tokens.astype(jnp.float32).reshape(rounds, group, LEN, D)
    seg_all = segments.astype(jnp.float32).reshape(rounds, group, LEN)
    cot_all = cotangent.astype(jnp.float32).reshape(rounds, group, LEN, D)

    def visit(totals, item):
        x_grp, seg_grp, cot_grp = item

        def forward(x_val, *weights):
            return layer(x_val, seg_grp, *weights)
        result, pull = jax.vjp(forward, x_grp, *params)
        grads = pull(cot_grp)
        return (tuple((total + grad for total, grad in zip(totals, grads[1:]))), (result, grads[0]))
    zeros = tuple((jnp.zeros_like(entry) for entry in params))
    totals, outputs = lax.scan(visit, zeros, (x_all, seg_all, cot_all))
    results, input_grads = outputs
    return (results.reshape(SEQS, LEN, D).astype(jnp.bfloat16), input_grads.reshape(SEQS, LEN, D), totals[0], totals[1], totals[2], totals[3], totals[4], totals[5], totals[6], totals[7], totals[8])
```

```python
import jax
import jax.numpy as jnp
import numpy as np
from jax import lax
from jax.experimental import pallas as pl
from jax.experimental.pallas import tpu as pltpu
from jax.sharding import Mesh
from jax.sharding import PartitionSpec as P

D = 1536
NH = 48
HD = 64
NS = 128
KW = 4
DI = 3072
CONV = 3328
LEN = 1024

EPS = 1e-05
HIGH = lax.Precision.HIGHEST
F32 = jnp.float32
BF16 = jnp.bfloat16

PARTS = 4
MYH = NH // PARTS
MYC = MYH * HD
BCW = 2 * NS // PARTS
LANES = 128
W1 = MYC + LANES
Q = 128
FAR = -1e30

SWAP = [(0, 1), (1, 0)]


def swap(value, axis):
    return lax.ppermute(value, axis, SWAP)


def pick(value, at, dim=0):
    return lax.dynamic_index_in_dim(value, at, dim, False)


def in_order(mine, other, place):
    buf = jnp.zeros((2,) + mine.shape, mine.dtype)
    buf = lax.dynamic_update_index_in_dim(buf, mine, place, 0)
    return lax.dynamic_update_index_in_dim(buf, other, 1 - place, 0)


def group_gather(value, core, side):
    pair = in_order(value, swap(value, "seq"), side)
    return in_order(pair, swap(pair, "core"), core)


def group_sum(value):
    value = value + swap(value, "core")
    return value + swap(value, "seq")


def group_scatter(value, core, side):
    kept = pick(value, core).astype(F32) + swap(pick(value, 1 - core), "core").astype(F32)
    sent = swap(pick(kept, 1 - side).astype(BF16), "seq")
    return pick(kept, side) + sent.astype(F32)


def ring_order(count):
    return list(range(0, count, 2)) + list(range(count - 1, 0, -2))


def ring_pairs(count):
    order = ring_order(count)
    right = [(order[i], order[(i + 1) % count]) for i in range(count)]
    return right, [(b, a) for a, b in right]


def ring_place(count):
    order = np.array(ring_order(count), np.int32)
    return jnp.asarray(np.argsort(order).astype(np.int32))[lax.axis_index("zy")], jnp.asarray(order)


def ring_gather(block):
    count = lax.axis_size("zy")
    rows = block.shape[0]
    half = rows // 2
    right, left = ring_pairs(count)
    place, order = ring_place(count)

    def put(full, part, at, off=0):
        return lax.dynamic_update_slice(full, part[None], (order[at % count], off, 0))

    full = put(jnp.zeros((count,) + block.shape, block.dtype), block, place)
    ahead = back = block
    for step in range(1, count // 2):
        ahead = lax.ppermute(ahead, "zy", right)
        back = lax.ppermute(back, "zy", left)
        full = put(full, ahead, place - step + count)
        full = put(full, back, place + step)
    ahead = lax.ppermute(ahead[:half], "zy", right)
    back = lax.ppermute(back[half:], "zy", left)
    full = put(full, ahead, place + count // 2)
    return put(full, back, place + count // 2, half)


def ring_scatter(full):
    count, rows, cols = full.shape
    half = rows // 2
    right, left = ring_pairs(count)
    place, order = ring_place(count)

    def get(at, off=0, size=rows):
        return lax.dynamic_slice(full, (order[at % count], off, 0), (1, size, cols))[0].astype(F32)

    far = place + count // 2
    ahead = lax.ppermute(get(far, 0, half).astype(BF16), "zy", right)
    back = lax.ppermute(get(far, half, rows - half).astype(BF16), "zy", left)
    for step in range(count // 2 - 1, 0, -1):
        one, two = get(place + step), get(place + count - step)
        if step == count // 2 - 1:
            one = jnp.concatenate([one[:half] + ahead, one[half:]], axis=0)
            two = jnp.concatenate([two[:half], two[half:] + back], axis=0)
        else:
            one, two = one + ahead, two + back
        ahead = lax.ppermute(one.astype(BF16), "zy", right)
        back = lax.ppermute(two.astype(BF16), "zy", left)
    return get(place) + ahead.astype(F32) + back.astype(F32)


def zy_exchange(value, bit):
    count = lax.axis_size("zy")
    return lax.ppermute(value, "zy", [(i, i ^ bit) for i in range(count)])


def small_gather(value, core, side):
    count = lax.axis_size("zy")
    held = group_gather(value, core, side)[None]
    place = lax.axis_index("zy")
    bit = 1
    while bit < count:
        other = zy_exchange(held, bit)
        upper = (place // bit) % 2
        pair = in_order(held, other, upper)
        held = pair.reshape((2 * bit,) + value.shape[:0] + held.shape[1:])
        bit *= 2
    return held


def zy_sum(value):
    count = lax.axis_size("zy")
    bit = 1
    while bit < count:
        value = value + zy_exchange(value, bit)
        bit *= 2
    return value


def head_split(count):
    rows = DI // count
    if rows % (2 * HD) == 0 and count % 2 == 0:
        return count // 2, rows // (2 * HD)
    return 1, MYH


def split_heads(value, dim, split):
    q, i = split
    size = value.shape[dim]
    unit = size // NH
    shape = value.shape
    value = value.reshape(shape[:dim] + (2, q, 2, i * unit) + shape[dim + 1 :])
    value = jnp.swapaxes(value, dim + 1, dim + 2)
    return value.reshape(shape[:dim] + (2, 2, size // PARTS) + shape[dim + 1 :])


def join_heads(value, dim, split):
    q, i = split
    shape = value.shape
    mine = shape[dim + 2]
    value = value.reshape(shape[:dim] + (2, 2, q, mine // q) + shape[dim + 3 :])
    value = jnp.swapaxes(value, dim + 1, dim + 2)
    return value.reshape(shape[:dim] + (PARTS * mine,) + shape[dim + 3 :])


def split_columns(weight, split):
    rows = weight.shape[0]
    gate = split_heads(weight[:, :DI], 1, split)
    x_cols = split_heads(weight[:, DI : 2 * DI], 1, split)
    bc_cols = weight[:, 2 * DI : 2 * DI + 2 * NS].reshape(rows, 2, 2, BCW)
    dt_cols = split_heads(weight[:, DI + CONV :], 1, split)
    pad = jnp.zeros((rows, 2, 2, LANES - BCW - MYH), weight.dtype)
    first = jnp.concatenate([x_cols, dt_cols, pad, bc_cols], axis=3)
    return jnp.transpose(first, (1, 2, 0, 3)), jnp.transpose(gate, (1, 2, 0, 3))


def join_columns(first, gate, split):
    rows = first.shape[2]
    first = jnp.transpose(first, (2, 0, 1, 3))
    gate = jnp.transpose(gate, (2, 0, 1, 3))
    return jnp.concatenate(
        [
            join_heads(gate, 1, split),
            join_heads(first[..., :MYC], 1, split),
            first[..., W1 - BCW :].reshape(rows, 2 * NS),
            join_heads(first[..., MYC : MYC + MYH], 1, split),
        ],
        axis=1,
    )


def to_group(blocks, core, side):
    kept, got = pick(blocks, core), swap(pick(blocks, 1 - core), "core")
    pair = in_order(kept, got, core)
    kept, got = pick(pair, side, 1), swap(pick(pair, 1 - side, 1), "seq")
    return jnp.swapaxes(in_order(kept, got, side), 0, 1)


def from_group(blocks, core, side):
    kept, got = pick(blocks, side, 1), swap(pick(blocks, 1 - side, 1), "seq")
    pair = in_order(kept, got, side)
    kept, got = pick(pair, core, 1), swap(pick(pair, 1 - core, 1), "core")
    return in_order(kept, got, core)


DIAGONAL = [(0, 0), (1, 2), (2, 1), (3, 3)]


def nt(a, b):
    return lax.dot_general(a, b, (((1,), (1,)), ((), ())), preferred_element_type=F32)


def nn(a, b):
    return lax.dot_general(a, b, (((1,), (0,)), ((), ())), preferred_element_type=F32)


def exact(a, b):
    return lax.dot_general(
        a, b, (((1,), (0,)), ((), ())), preferred_element_type=F32, precision=HIGH
    )


def in_two(value, axis):
    top = value.astype(BF16)
    return jnp.concatenate([top, (value - top.astype(F32)).astype(BF16)], axis=axis)


def over_heads(value, heads_ref):
    return nn(in_two(value, 1), heads_ref[...])


def sum_heads(value, heads_ref):
    top = value.astype(BF16)
    low = (value - top.astype(F32)).astype(BF16)
    heads = heads_ref[:LANES, :]
    return nt(top, heads) + nt(low, heads)


def softplus(value):
    return jnp.maximum(value, 0.0) + jnp.log1p(jnp.exp(-jnp.abs(value)))


def conv_total(ext_ref, raw_ref, halo_ref, taps_ref, marks, width):
    ext_ref[0:8, :width] = halo_ref[8:16, :].astype(F32)
    ext_ref[8 : 8 + Q, :width] = raw_ref[...].astype(F32)
    total = taps_ref[4:5, :] + ext_ref[8 : 8 + Q, :width] * taps_ref[3:4, :]
    for k in range(KW - 1):
        total = total + ext_ref[5 + k : 5 + k + Q, :width] * taps_ref[k : k + 1, :] * marks[:, 1 + k : 2 + k]
    return total


def decays(dt_ref, head_ref, lower):
    raw = dt_ref[...].astype(F32)
    lane = lax.broadcasted_iota(jnp.int32, (Q, LANES), 1)
    live = (lane < MYH).astype(F32)
    shifted = raw * live + head_ref[0:1, :]
    step = softplus(shifted) * live
    rate = -jnp.exp(head_ref[1:2, :])
    log_decay = rate * step
    return shifted, step, rate, log_decay, exact(lower, log_decay)


def scan_forward(
    x_ref, x_halo, bc_ref, bc_halo, dt_ref, marks_ref, row_ref, x_taps, bc_taps, head_ref, heads_ref,
    y_ref, state_ref, bc_out, ext, held,
):
    chunk = pl.program_id(1)

    @pl.when(chunk == 0)
    def _():
        held[...] = jnp.zeros_like(held)

    marks = marks_ref[...]
    x_act = conv_total(ext, x_ref, x_halo, x_taps, marks, MYC)
    x_act = x_act * lax.logistic(x_act)
    bc_act = conv_total(ext, bc_ref, bc_halo, bc_taps, marks, 2 * NS)
    bc_act = (bc_act * lax.logistic(bc_act)).astype(BF16)
    bc_out[...] = bc_act
    b, c = bc_act[:, :NS], bc_act[:, NS:]
    at_row = lax.broadcasted_iota(jnp.int32, (Q, Q), 0)
    at_col = lax.broadcasted_iota(jnp.int32, (Q, Q), 1)
    lower = (at_row >= at_col).astype(F32)
    _, step, _, _, cum = decays(dt_ref, head_ref, lower)
    cum_t = cum.T
    shut = jnp.where((at_row >= at_col) & (marks[:, 0:1] == row_ref[0]), 0.0, FAR)
    scores = nt(c, b)
    state = held[...]
    state_low = state.astype(BF16)
    state_ref[0] = state_low
    last = cum[Q - 1 : Q, :]
    x_step = x_act * over_heads(step, heads_ref)
    keep = over_heads(jnp.exp(cum) * marks[:, 7:8], heads_ref)
    y = nn(c, state_low) * keep + x_act * x_taps[5:6, :]
    tail = over_heads(jnp.exp(last - cum) * marks[:, 8:9], heads_ref)
    carry = over_heads(jnp.broadcast_to(jnp.exp(last) * marks[Q - 1 : Q, 7:8], (8, LANES)), heads_ref)
    held[...] = state * carry[0:1, :] + nn(b.T, (x_step * tail).astype(BF16))
    lane = lax.broadcasted_iota(jnp.int32, (Q, LANES), 1)
    for pair in range(MYH // 2):
        cols = slice(pair * LANES, (pair + 1) * LANES)
        mixing = []
        for head in (2 * pair, 2 * pair + 1):
            spread = cum[:, head : head + 1] - cum_t[head : head + 1, :] + shut
            mixing.append((jnp.exp(spread) * scores).astype(BF16))
        steps = x_step[:, cols]
        both = jnp.concatenate(
            [jnp.where(lane < HD, steps, 0.0), jnp.where(lane < HD, 0.0, steps)], axis=0
        ).astype(BF16)
        y_ref[:, cols] = y[:, cols] + nn(jnp.concatenate(mixing, axis=1), both)


def scan_backward(
    x_ref, x_halo, bc_ref, dt_ref, dy_ref, state_ref, marks_ref, row_ref, x_taps, head_ref, heads_ref,
    dx_ref, dbc_ref, ddt_ref, wide_ref, thin_ref, ext, held, ahead,
):
    chunk = pl.program_id(1)

    @pl.when(chunk == 0)
    def _():
        held[...] = jnp.zeros_like(held)
        ahead[...] = jnp.zeros_like(ahead)

    @pl.when((chunk == 0) & (pl.program_id(0) == 0))
    def _():
        wide_ref[...] = jnp.zeros_like(wide_ref)
        thin_ref[...] = jnp.zeros_like(thin_ref)

    marks = marks_ref[...]
    total = conv_total(ext, x_ref, x_halo, x_taps, marks, MYC)
    gate = lax.logistic(total)
    x_act = total * gate
    slope = gate * (1.0 + total * (1.0 - gate))
    b, c = bc_ref[:, :NS], bc_ref[:, NS:]
    at_row = lax.broadcasted_iota(jnp.int32, (Q, Q), 0)
    at_col = lax.broadcasted_iota(jnp.int32, (Q, Q), 1)
    lower = (at_row >= at_col).astype(F32)
    shifted, step, rate, log_decay, cum = decays(dt_ref, head_ref, lower)
    cum_t = cum.T
    shut = jnp.where((at_row <= at_col) & (marks[:, 0:1] == row_ref[0]), 0.0, FAR)
    scores = nt(b, c)
    last = cum[Q - 1 : Q, :]
    dy = dy_ref[...].astype(F32)
    step_wide = over_heads(step, heads_ref)
    x_step = x_act * step_wide
    keep = over_heads(jnp.exp(cum) * marks[:, 7:8], heads_ref)
    tail = over_heads(jnp.exp(last - cum) * marks[:, 8:9], heads_ref)
    carry_thin = jnp.broadcast_to(jnp.exp(last) * marks[Q - 1 : Q, 7:8], (8, LANES))
    carry = over_heads(carry_thin, heads_ref)
    state = state_ref[0]
    d_state = held[...]
    d_state_low = d_state.astype(BF16)
    dy_keep = dy * keep
    dy_keep_low = dy_keep.astype(BF16)
    from_state = nn(c, state)
    seen = sum_heads(dy_keep * from_state, heads_ref)
    d_c = nt(dy_keep_low, state)
    to_state = x_step * tail
    d_b = nt(to_state.astype(BF16), d_state_low)
    du_tail = nn(b, d_state_low) * tail
    sent = sum_heads(x_step * du_tail, heads_ref)
    linked = jnp.sum(d_state * state.astype(F32), axis=0, keepdims=True)
    linked = sum_heads(jnp.broadcast_to(linked, (8, MYC)), heads_ref)[0:1, :] * carry_thin[0:1, :]
    held[...] = d_state * carry[0:1, :] + nn(c.T, dy_keep_low)
    lane = lax.broadcasted_iota(jnp.int32, (Q, LANES), 1)
    d_scores = jnp.zeros((Q, Q), F32)
    by_later, by_earlier, du_parts = [], [], []
    for pair in range(MYH // 2):
        cols = slice(pair * LANES, (pair + 1) * LANES)
        steps, dys = x_step[:, cols], dy[:, cols]
        step_both = jnp.concatenate(
            [jnp.where(lane < HD, steps, 0.0), jnp.where(lane < HD, 0.0, steps)], axis=0
        ).astype(BF16)
        dy_both = jnp.concatenate(
            [jnp.where(lane < HD, dys, 0.0), jnp.where(lane < HD, 0.0, dys)], axis=0
        ).astype(BF16)
        met = nt(step_both, dys.astype(BF16))
        mixing = []
        for place, head in enumerate((2 * pair, 2 * pair + 1)):
            decay = jnp.exp(cum_t[head : head + 1, :] - cum[:, head : head + 1] + shut)
            mixing.append((decay * scores).astype(BF16))
            weighed = decay * met[place * Q : (place + 1) * Q, :]
            d_scores = d_scores + weighed
            spent = weighed * scores
            by_later.append(jnp.sum(spent, axis=0, keepdims=True))
            by_earlier.append(jnp.sum(spent, axis=1, keepdims=True))
        du_parts.append(nn(jnp.concatenate(mixing, axis=1), dy_both))
    du = jnp.concatenate(du_parts, axis=1) + du_tail
    d_low = d_scores.astype(BF16)
    d_b = d_b + nn(d_low, c)
    d_c = d_c + nn(d_scores.T.astype(BF16), b)
    dbc_ref[:, :NS] = d_b
    dbc_ref[:, NS:] = d_c
    later = jnp.concatenate(by_later + [jnp.zeros((LANES - MYH, Q), F32)], axis=0).T
    earlier = jnp.zeros((Q, LANES), F32)
    for head in range(MYH):
        earlier = jnp.where(lane == head, by_earlier[head], earlier)
    upper = (at_row <= at_col).astype(F32)
    strict = (at_row > at_col).astype(F32)
    d_log = exact(upper, seen + later - earlier) + exact(strict, sent) + linked
    d_step = sum_heads(x_act * du, heads_ref)
    d_raw = (d_step + rate * d_log) * lax.logistic(shifted)
    live = (lane < MYH).astype(F32)
    d_raw = d_raw * live
    ddt_ref[...] = d_raw.astype(BF16)
    thin_ref[0:1, :] += jnp.sum(d_raw, axis=0, keepdims=True)
    thin_ref[1:2, :] += jnp.sum(d_log * log_decay, axis=0, keepdims=True)
    d_total = (du * step_wide + dy * x_taps[5:6, :]) * slope
    wide_ref[4:5, :] += jnp.sum(d_total, axis=0, keepdims=True)
    wide_ref[5:6, :] += jnp.sum(dy * x_act, axis=0, keepdims=True)
    wide_ref[3:4, :] += jnp.sum(d_total * ext[8 : 8 + Q, :], axis=0, keepdims=True)
    for k in range(KW - 1):
        wide_ref[k : k + 1, :] += jnp.sum(
            d_total * (ext[5 + k : 5 + k + Q, :] * marks[:, 1 + k : 2 + k]), axis=0, keepdims=True
        )
    ext[0:Q, :] = d_total
    ext[Q : Q + 8, :] = ahead[...]
    d_x = d_total * x_taps[3:4, :]
    for k in range(KW - 1):
        d_x = d_x + ext[3 - k : 3 - k + Q, :] * (x_taps[k : k + 1, :] * marks[:, 4 + k : 5 + k])
    ahead[...] = d_total[0:8, :]
    dx_ref[...] = d_x.astype(BF16)


def halo_of(at, blocks):
    return jnp.maximum(at * (Q // 16) - 1, 0)


def run_forward(first, bc_raw, marks, rows, x_taps, bc_taps, head_rows, heads):
    total = first.shape[0]
    blocks = LEN // Q

    def at(s, t):
        return s * blocks + t

    return pl.pallas_call(
        scan_forward,
        grid=(total // LEN, blocks),
        in_specs=[
            pl.BlockSpec((Q, MYC), lambda s, t: (at(s, t), 0)),
            pl.BlockSpec((16, MYC), lambda s, t: (halo_of(at(s, t), blocks), 0)),
            pl.BlockSpec((Q, 2 * NS), lambda s, t: (at(s, t), 0)),
            pl.BlockSpec((16, 2 * NS), lambda s, t: (halo_of(at(s, t), blocks), 0)),
            pl.BlockSpec((Q, LANES), lambda s, t: (at(s, t), MYC // LANES)),
            pl.BlockSpec((Q, 16), lambda s, t: (at(s, t), 0)),
            pl.BlockSpec((1, 1, Q), lambda s, t: (at(s, t), 0, 0)),
            pl.BlockSpec((8, MYC), lambda s, t: (0, 0)),
            pl.BlockSpec((8, 2 * NS), lambda s, t: (0, 0)),
            pl.BlockSpec((8, LANES), lambda s, t: (0, 0)),
            pl.BlockSpec((2 * LANES, MYC), lambda s, t: (0, 0)),
        ],
        out_specs=[
            pl.BlockSpec((Q, MYC), lambda s, t: (at(s, t), 0)),
            pl.BlockSpec((1, NS, MYC), lambda s, t: (at(s, t), 0, 0)),
            pl.BlockSpec((Q, 2 * NS), lambda s, t: (at(s, t), 0)),
        ],
        out_shape=[
            jax.ShapeDtypeStruct((total, MYC), F32),
            jax.ShapeDtypeStruct((total // Q, NS, MYC), BF16),
            jax.ShapeDtypeStruct((total, 2 * NS), BF16),
        ],
        scratch_shapes=[pltpu.VMEM((Q + 8, MYC), F32), pltpu.VMEM((NS, MYC), F32)],
        compiler_params=pltpu.CompilerParams(vmem_limit_bytes=40 * 1024 * 1024),
        cost_estimate=pl.CostEstimate(flops=4 * 10**9, bytes_accessed=20 * 10**6, transcendentals=10**7),
        name="scan_forward",
    )(first, first, bc_raw, bc_raw, first, marks, rows, x_taps, bc_taps, head_rows, heads)


def run_backward(first, bc_act, d_ssm, states, marks, rows, x_taps, head_rows, heads):
    total = first.shape[0]
    blocks = LEN // Q

    def at(s, t):
        return s * blocks + (blocks - 1 - t)

    return pl.pallas_call(
        scan_backward,
        grid=(total // LEN, blocks),
        in_specs=[
            pl.BlockSpec((Q, MYC), lambda s, t: (at(s, t), 0)),
            pl.BlockSpec((16, MYC), lambda s, t: (halo_of(at(s, t), blocks), 0)),
            pl.BlockSpec((Q, 2 * NS), lambda s, t: (at(s, t), 0)),
            pl.BlockSpec((Q, LANES), lambda s, t: (at(s, t), MYC // LANES)),
            pl.BlockSpec((Q, MYC), lambda s, t: (at(s, t), 0)),
            pl.BlockSpec((1, NS, MYC), lambda s, t: (at(s, t), 0, 0)),
            pl.BlockSpec((Q, 16), lambda s, t: (at(s, t), 0)),
            pl.BlockSpec((1, 1, Q), lambda s, t: (at(s, t), 0, 0)),
            pl.BlockSpec((8, MYC), lambda s, t: (0, 0)),
            pl.BlockSpec((8, LANES), lambda s, t: (0, 0)),
            pl.BlockSpec((2 * LANES, MYC), lambda s, t: (0, 0)),
        ],
        out_specs=[
            pl.BlockSpec((Q, MYC), lambda s, t: (at(s, t), 0)),
            pl.BlockSpec((Q, 2 * NS), lambda s, t: (at(s, t), 0)),
            pl.BlockSpec((Q, LANES), lambda s, t: (at(s, t), 0)),
            pl.BlockSpec((8, MYC), lambda s, t: (0, 0)),
            pl.BlockSpec((8, LANES), lambda s, t: (0, 0)),
        ],
        out_shape=[
            jax.ShapeDtypeStruct((total, MYC), BF16),
            jax.ShapeDtypeStruct((total, 2 * NS), F32),
            jax.ShapeDtypeStruct((total, LANES), BF16),
            jax.ShapeDtypeStruct((8, MYC), F32),
            jax.ShapeDtypeStruct((8, LANES), F32),
        ],
        scratch_shapes=[
            pltpu.VMEM((Q + 8, MYC), F32),
            pltpu.VMEM((NS, MYC), F32),
            pltpu.VMEM((8, MYC), F32),
        ],
        compiler_params=pltpu.CompilerParams(vmem_limit_bytes=40 * 1024 * 1024),
        cost_estimate=pl.CostEstimate(flops=10 * 10**9, bytes_accessed=25 * 10**6, transcendentals=10**7),
        name="scan_backward",
    )(first, first, bc_act, first, d_ssm, states, marks, rows, x_taps, head_rows, heads)


def lead(value, by):
    if by == 0:
        return value
    pad = [(0, 0)] * value.ndim
    if by > 0:
        pad[1] = (0, by)
        return jnp.pad(value, pad)[:, by:]
    pad[1] = (-by, 0)
    return jnp.pad(value, pad)[:, :by]


def gather_out(out_weight, split, core, side):
    count = lax.axis_size("zy")
    if split[0] == 1:
        whole = lax.all_gather(out_weight, ("zy", "core", "seq"), axis=0, tiled=True)
        mine = pick(pick(split_heads(whole, 0, split), core), side)
        return mine
    held = lax.ppermute(out_weight, ("core", "seq"), DIAGONAL)
    rows = held.shape[0]
    full = ring_gather(held).reshape(2, count // 2, rows, D)
    mine = in_order(pick(full, core), swap(pick(full, 1 - core), "core"), core)
    return jnp.swapaxes(mine, 0, 1).reshape(MYC, D)


def scatter_out(grad, split, core, side):
    count = lax.axis_size("zy")
    if split[0] == 1:
        own = jnp.zeros((2, 2, MYC, D), BF16)
        own = lax.dynamic_update_slice(own, grad.astype(BF16)[None, None], (core, side, 0, 0))
        whole = join_heads(own, 0, split)
        return lax.psum_scatter(
            whole, ("zy", "core", "seq"), scatter_dimension=0, tiled=True
        ).astype(F32)
    rows = DI // (count * PARTS)
    halves = grad.astype(BF16).reshape(count // 2, 2, rows, D)
    other = swap(pick(halves, 1 - core, 1), "core")
    full = in_order(pick(halves, core, 1), other, core).reshape(count, rows, D)
    held = ring_scatter(full)
    return lax.ppermute(held.astype(BF16), ("core", "seq"), DIAGONAL).astype(F32)


def own_slice(whole, size):
    at = (lax.axis_index("zy") * 2 + lax.axis_index("core")) * 2 + lax.axis_index("seq")
    return lax.dynamic_slice_in_dim(whole, at * size, size, 0)


def body(
    tokens,
    segments,
    norm_gain,
    in_weight,
    conv_weight,
    conv_bias,
    dt_bias,
    a_log,
    d_skip,
    gated_gain,
    out_weight,
    cotangent,
):
    count = lax.axis_size("zy")
    core, side = lax.axis_index("core"), lax.axis_index("seq")
    split = head_split(count)
    rows = tokens.shape[1]
    total = PARTS * rows

    first_cols, gate_cols = split_columns(in_weight, split)
    sent = to_group(jnp.concatenate([first_cols, gate_cols], axis=3), core, side)
    sent = sent.reshape(PARTS * in_weight.shape[0], W1 + MYC)
    w_first = ring_gather(sent[:, :W1]).reshape(D, W1)
    w_gate = ring_gather(sent[:, W1:]).reshape(D, MYC)
    w_out = gather_out(out_weight, split, core, side)

    sizes = (norm_gain.shape[0], conv_weight.size, conv_bias.shape[0], gated_gain.shape[0])
    small = jnp.concatenate([norm_gain, conv_weight.reshape(-1), conv_bias, gated_gain])
    small = small_gather(small[None], core, side).reshape(-1, sum(sizes))
    cuts = np.cumsum(sizes)[:-1]
    gain, taps, bias, gated = (v.reshape(-1).astype(F32) for v in jnp.split(small, cuts, axis=1))
    taps = taps.reshape(CONV, KW)

    def mine(vector, dim=0):
        return pick(pick(split_heads(vector, dim, split), core, dim), side, dim)

    gated_mine = mine(gated)
    x_taps = jnp.concatenate(
        [
            mine(taps[:DI]).T,
            mine(bias[:DI])[None],
            jnp.repeat(mine(d_skip), HD)[None],
            jnp.zeros((2, MYC), F32),
        ],
        axis=0,
    )
    bc_taps = jnp.concatenate(
        [taps[DI:].T, bias[DI:][None], jnp.zeros((3, 2 * NS), F32)], axis=0
    )
    head_rows = jnp.concatenate([mine(dt_bias)[None], mine(a_log)[None]], axis=0)
    head_rows = jnp.pad(head_rows, ((0, 6), (0, LANES - MYH)))
    heads = np.kron(np.eye(LANES, MYH, dtype=np.float32), np.ones((1, HD), np.float32))
    heads = jnp.asarray(np.concatenate([heads, heads], axis=0), BF16)

    segs = group_gather(segments[0], core, side).reshape(2, LEN).astype(F32)
    before = [lead(segs, k - KW + 1) == segs for k in range(KW - 1)]
    place = jnp.arange(LEN)[None, :]
    before = [(m & (place >= KW - 1 - k)).astype(F32) for k, m in enumerate(before)]
    after = [lead(m, KW - 1 - k) for k, m in enumerate(before)]
    ends = segs.reshape(2, LEN // Q, Q)[:, :, -1:]
    starts = jnp.concatenate([jnp.full((2, 1, 1), -1.0, F32), ends[:, :-1]], axis=1)
    keep = (segs.reshape(2, LEN // Q, Q) == starts).astype(F32).reshape(2, LEN)
    tail = (segs.reshape(2, LEN // Q, Q) == ends).astype(F32).reshape(2, LEN)
    marks = jnp.stack([segs] + before + after + [keep, tail] + [jnp.zeros_like(segs)] * 7, axis=-1)
    marks = marks.reshape(total, 16)
    seg_rows = segs.reshape(total // Q, 1, Q)

    def whole_tokens(value):
        near = swap(value, "core")
        far = swap(value, "seq")
        both = swap(far, "core")
        return in_order(in_order(value, far, side), in_order(near, both, side), core)

    token_all = whole_tokens(tokens[0])
    cot_all = whole_tokens(cotangent[0]).reshape(total, D)
    x_all = token_all.reshape(total, D).astype(F32)
    inv_one = lax.rsqrt(jnp.mean(x_all * x_all, axis=-1, keepdims=True) + EPS)
    normed = (x_all * inv_one * gain).astype(BF16)

    first = nn(normed, w_first).astype(BF16)
    bc_mine = first[:, W1 - BCW :]
    bc_core = in_order(bc_mine, swap(bc_mine, "core"), core)
    bc_core = jnp.concatenate([bc_core[0], bc_core[1]], axis=1).reshape(2, total // 2, 2 * BCW)
    bc_half = swap(pick(bc_core, core), "seq")
    bc_other = in_order(bc_half, swap(bc_half, "core"), core).reshape(total, 2 * BCW)
    bc_side = in_order(bc_core.reshape(total, 2 * BCW), bc_other, side)
    bc_raw = jnp.concatenate(
        [bc_side[0, :, :BCW], bc_side[1, :, :BCW], bc_side[0, :, BCW:], bc_side[1, :, BCW:]], axis=1
    )

    y, states, bc_act = run_forward(first, bc_raw, marks, seg_rows, x_taps, bc_taps, head_rows, heads)

    gate = nn(normed, w_gate).astype(BF16).astype(F32)
    sig = lax.logistic(gate)
    silu = gate * sig
    joined = y * silu
    d_two = nt(cot_all, w_out)
    sums = jnp.stack(
        [jnp.sum(joined * joined, axis=-1), jnp.sum(joined * gated_mine * d_two, axis=-1)]
    )
    sums = group_sum(sums)
    inv_two = lax.rsqrt(sums[0] / DI + EPS)[:, None]
    mean_two = (sums[1] / DI)[:, None]
    two = (joined * inv_two * gated_mine).astype(BF16)
    d_joined = inv_two * (gated_mine * d_two) - joined * (inv_two * inv_two * inv_two * mean_two)
    d_ssm = (d_joined * silu).astype(BF16)
    d_gate = (d_joined * y * (sig * (1.0 + gate * (1.0 - sig)))).astype(BF16)
    d_gated = jnp.sum(joined * inv_two * d_two, axis=0)

    def tn(a, b):
        return lax.dot_general(a, b, (((0,), (0,)), ((), ())), preferred_element_type=F32)

    d_out = scatter_out(tn(two, cot_all), split, core, side)
    d_w_gate = ring_scatter(tn(normed, d_gate).reshape(count, D // count, MYC))
    branch = nn(two, w_out).astype(BF16).reshape(2, 2, rows, D)
    branch = group_scatter(branch, core, side)
    block_out = (tokens[0].astype(F32) + branch).astype(BF16)[None]

    d_x, d_bc, d_dt, wide, thin = run_backward(
        first, bc_act, d_ssm, states, marks, seg_rows, x_taps, head_rows, heads
    )
    d_bc = d_bc.reshape(total, 2, 2 * BCW)
    d_core = pick(d_bc, core, 1) + swap(pick(d_bc, 1 - core, 1).astype(BF16), "core").astype(F32)
    d_core = d_core.reshape(total, 2, BCW)
    d_act = pick(d_core, side, 1) + swap(pick(d_core, 1 - side, 1).astype(BF16), "seq").astype(F32)
    d_act = d_act.reshape(2, LEN, BCW)
    raw_mine = bc_mine.astype(F32).reshape(2, LEN, BCW)
    my_taps = lax.dynamic_slice_in_dim(bc_taps, (core * 2 + side) * BCW, BCW, 1)
    reads = [lead(raw_mine, k - KW + 1) * before[k][:, :, None] for k in range(KW - 1)] + [raw_mine]
    bc_total = my_taps[4] + sum(reads[k] * my_taps[k] for k in range(KW))
    bc_sig = lax.logistic(bc_total)
    d_total = d_act * (bc_sig * (1.0 + bc_total * (1.0 - bc_sig)))
    d_bc_raw = d_total * my_taps[3]
    for k in range(KW - 1):
        d_bc_raw = d_bc_raw + lead(d_total, KW - 1 - k) * after[k][:, :, None] * my_taps[k]
    bc_grads = jnp.stack([jnp.sum(d_total * reads[k], axis=(0, 1)) for k in range(KW)] + [jnp.sum(d_total, axis=(0, 1))])
    d_last = jnp.concatenate(
        [d_dt[:, : LANES - BCW], d_bc_raw.reshape(total, BCW).astype(BF16)], axis=1
    )
    d_first = jnp.concatenate([d_x, d_last], axis=1)

    d_w_first = ring_scatter(tn(normed, d_first).reshape(count, D // count, W1))
    d_normed = nt(d_first, w_first) + nt(d_gate, w_gate)
    d_normed = group_scatter(d_normed.astype(BF16).reshape(2, 2, rows, D), core, side)
    x = tokens[0].astype(F32)
    inv = lax.rsqrt(jnp.mean(x * x, axis=-1, keepdims=True) + EPS)
    scaled = gain * d_normed
    input_grad = (
        cotangent[0].astype(F32)
        + inv * scaled
        - x * (inv * inv * inv * jnp.mean(x * scaled, axis=-1, keepdims=True))
    )[None]
    d_gain = jnp.sum(x * inv * d_normed, axis=0)

    d_w = jnp.concatenate([d_w_first, d_w_gate], axis=1).astype(BF16)
    d_w = from_group(d_w.reshape(2, 2, D // (count * PARTS), W1 + MYC), core, side).astype(F32)
    in_sh = join_columns(d_w[..., :W1], d_w[..., W1:], split)

    parts = (
        wide[:KW].reshape(-1),
        wide[KW],
        d_gated,
        bc_grads.reshape(-1),
        thin[0, :MYH],
        thin[1, :MYH],
        jnp.sum(wide[KW + 1].reshape(MYH, HD), axis=1),
        d_gain,
    )
    lengths = [p.shape[0] for p in parts]
    packed = jnp.concatenate(parts)
    packed = jnp.pad(packed, (0, -packed.shape[0] % 1024)).reshape(-1, LANES)
    summed = group_gather(zy_sum(packed), core, side).reshape(2, 2, -1)
    pieces = jnp.split(summed, np.cumsum(lengths), axis=2)
    taps_x, bias_x, gain_two, taps_bc, bias_dt, alog, skip, gain_one = pieces[:8]
    taps_x = jnp.swapaxes(taps_x.reshape(2, 2, KW, MYC), 2, 3)
    taps_bc = taps_bc.reshape(PARTS, KW + 1, BCW)
    conv_w = jnp.concatenate(
        [join_heads(taps_x, 0, split), jnp.swapaxes(taps_bc[:, :KW], 1, 2).reshape(2 * NS, KW)], axis=0
    )
    conv_b = jnp.concatenate([join_heads(bias_x, 0, split), taps_bc[:, KW].reshape(2 * NS)])
    return (
        block_out,
        input_grad,
        own_slice(jnp.sum(gain_one, axis=(0, 1)), norm_gain.shape[0]),
        in_sh,
        own_slice(conv_w, conv_bias.shape[0]),
        own_slice(conv_b, conv_bias.shape[0]),
        join_heads(bias_dt, 0, split),
        join_heads(alog, 0, split),
        join_heads(skip, 0, split),
        own_slice(join_heads(gain_two, 0, split), gated_gain.shape[0]),
        d_out,
    )


def solution(mesh):
    fsdp, seq = mesh.shape["fsdp"], mesh.shape["seq"]
    grid = Mesh(mesh.devices.reshape(fsdp // 2, 2, seq), ("zy", "core", "seq"))
    every = ("zy", "core", "seq")
    rows = P(("zy", "core"), "seq", None)
    in_specs = (
        rows,
        P(("zy", "core"), "seq"),
        P(every),
        P(every, None),
        P(every, None),
        P(every),
        P(),
        P(),
        P(),
        P(every),
        P(every, None),
        rows,
    )
    out_specs = (
        rows,
        rows,
        P(every),
        P(every, None),
        P(every, None),
        P(every),
        P(),
        P(),
        P(),
        P(every),
        P(every, None),
    )
    return jax.shard_map(body, mesh=grid, in_specs=in_specs, out_specs=out_specs, check_vma=False)
```

```python
import functools

import jax
import jax.numpy as jnp
import numpy as np
from jax import lax
from jax.experimental import pallas as pl
from jax.experimental.pallas import tpu as pltpu
from jax.sharding import Mesh
from jax.sharding import PartitionSpec as P

D = 1536
NH = 48
HD = 64
NS = 128
KW = 4
DI = 3072
CONV = 3328
LEN = 1024

EPS = 1e-05
HIGH = lax.Precision.HIGHEST
F32 = jnp.float32
BF16 = jnp.bfloat16

PARTS = 4
MYH = NH // PARTS
MYC = MYH * HD
LANES = 128
BC = 2 * NS
W1 = MYC + BC + LANES
GROUPS = 2
GH = MYH // GROUPS
GC = GH * HD
Q = 128
FAR = -1e30
VMEM_LIMIT = 56 * 1024 * 1024

SWAP = [(0, 1), (1, 0)]


def swap(value, axis):
    return lax.ppermute(value, axis, SWAP)


def pick(value, at, dim=0):
    return lax.dynamic_index_in_dim(value, at, dim, False)


def in_order(mine, other, place):
    buf = jnp.zeros((2,) + mine.shape, mine.dtype)
    buf = lax.dynamic_update_index_in_dim(buf, mine, place, 0)
    return lax.dynamic_update_index_in_dim(buf, other, 1 - place, 0)


GROUP = ("core", "seq")


def to_peer(value, r):
    return (value, GROUP, [(g, g ^ r) for g in range(PARTS)])


def ring_order(count):
    return list(range(0, count, 2)) + list(range(count - 1, 0, -2))


def ring_pairs(count):
    order = ring_order(count)
    right = [(order[i], order[(i + 1) % count]) for i in range(count)]
    return right, [(b, a) for a, b in right]


def ring_place(count):
    zy = lax.axis_index("zy")
    place = jnp.where(zy % 2 == 0, zy // 2, count - 1 - zy // 2)

    def order(at):
        at = at % count
        return jnp.where(at < count // 2, 2 * at, 2 * (count - at) - 1)

    return place, order


class Task:
    def __init__(self, steps):
        self.steps, self.value, self.done = steps, None, False
        self.moves = next(steps)

    def take(self, arrived):
        try:
            self.moves = self.steps.send(arrived)
        except StopIteration as end:
            self.value, self.done = end.value, True


def stage(tasks, work=None, *args):
    tasks = [t for t in tasks if not t.done]
    values = [[m[0] for m in t.moves] for t in tasks]
    values, args = lax.optimization_barrier((values, args))
    arrived = [
        [lax.ppermute(v, m[1], m[2]) for v, m in zip(vs, t.moves)] for vs, t in zip(values, tasks)
    ]
    result = None if work is None else work(*args)
    if work is None:
        arrived = lax.optimization_barrier(arrived)
    else:
        arrived, result = lax.optimization_barrier((arrived, result))
    for t, got in zip(tasks, arrived):
        t.take(got)
    return result


def finish(tasks):
    while not all(t.done for t in tasks):
        stage(tasks)


def gather_steps(block, cuts):
    count = lax.axis_size("zy")
    rows = block.shape[0]
    half = rows // 2
    right, left = ring_pairs(count)
    place, order = ring_place(count)
    ends = list(cuts[1:]) + [block.shape[1]]
    fulls = [jnp.zeros((count, rows, b - a), block.dtype) for a, b in zip(cuts, ends)]

    def put(part, at, off=0):
        for i, (a, b) in enumerate(zip(cuts, ends)):
            fulls[i] = lax.dynamic_update_slice(fulls[i], part[None, :, a:b], (order(at), off, 0))

    put(block, place)
    ahead = back = block
    for step in range(1, count // 2):
        ahead, back = yield [(ahead, "zy", right), (back, "zy", left)]
        put(ahead, place - step + count)
        put(back, place + step)
    ahead, back = yield [(ahead[:half], "zy", right), (back[half:], "zy", left)]
    put(ahead, place + count // 2)
    put(back, place + count // 2, half)
    return fulls


def scatter_steps(full):
    count, rows, cols = full.shape
    half = rows // 2
    right, left = ring_pairs(count)
    place, order = ring_place(count)

    def get(at, off=0, size=rows):
        return lax.dynamic_slice(full, (order(at), off, 0), (1, size, cols))[0].astype(F32)

    far = place + count // 2
    one, two = get(far, 0, half), get(far, half, rows - half)
    for step in range(count // 2 - 1, -1, -1):
        ahead, back = yield [(one.astype(BF16), "zy", right), (two.astype(BF16), "zy", left)]
        if step == 0:
            break
        one, two = get(place + step), get(place + count - step)
        if step == count // 2 - 1:
            one = jnp.concatenate([one[:half] + ahead, one[half:]], axis=0)
            two = jnp.concatenate([two[:half], two[half:] + back], axis=0)
        else:
            one, two = one + ahead, two + back
    return get(place) + ahead.astype(F32) + back.astype(F32)


def small_steps(value, core, side):
    count = lax.axis_size("zy")
    got = yield [to_peer(value, r) for r in range(1, PARTS)]
    held = jnp.stack([value] + list(got))
    held = held.reshape((2, 2) + value.shape)
    held = jnp.where(core == 0, held, held[::-1])
    held = jnp.where(side == 0, held, held[:, ::-1]).reshape((1, PARTS) + value.shape)
    bit = 1
    while bit < count:
        pairs = [(i, i ^ bit) for i in range(count)]
        (got,) = yield [(held, "zy", pairs)]
        upper = (lax.axis_index("zy") // bit) % 2
        held = jnp.concatenate([jnp.where(upper == 0, held, got), jnp.where(upper == 0, got, held)])
        bit *= 2
    return held


def group_steps(value):
    got = yield [to_peer(value, r) for r in range(1, PARTS)]
    return [value] + list(got)


def token_steps(value, pieces):
    rows = value.shape[0]
    cuts = [16 * (rows // 16 * i // pieces) for i in range(pieces + 1)]
    far, both = [], []
    moves = [(value, "core", SWAP)]
    for i in range(pieces):
        got = yield moves + [(value[cuts[i] : cuts[i + 1]], "seq", SWAP)]
        if i == 0:
            near = got[0]
        else:
            both.append(got[0])
        far.append(got[-1])
        moves = [(got[-1], "core", SWAP)]
    (got,) = yield moves
    return near, far, both + [got]


def peer_steps(blocks):
    got = yield [to_peer(blocks[r], r) for r in range(1, PARTS)]
    return [blocks[0]] + list(got)


def sum_steps(value, pieces):
    (got,) = yield [(value[2:], "core", SWAP)]
    sent = (value[1].astype(F32) + got[1].astype(F32)).astype(BF16)
    rows = sent.shape[0] // pieces
    arrived = []
    for i in range(pieces):
        (far,) = yield [(sent[i * rows : (i + 1) * rows], "seq", SWAP)]
        arrived.append(far)
    return value[0].astype(F32) + got[0].astype(F32) + jnp.concatenate(arrived, axis=0).astype(F32)


def far_steps(value, pieces):
    (got,) = yield [(value[1], "core", SWAP)]
    kept = value[0].astype(F32) + got.astype(F32)
    if not pieces:
        return kept
    sent = kept.astype(BF16)
    rows = sent.shape[0] // pieces
    arrived = []
    for i in range(pieces):
        (got,) = yield [(sent[i * rows : (i + 1) * rows], "seq", SWAP)]
        arrived.append(got)
    return jnp.concatenate(arrived, axis=0)


def small_sum_steps(parts, core, side):
    count = lax.axis_size("zy")
    lengths = [p.shape[0] for p in parts]
    packed = jnp.concatenate(parts)
    packed = jnp.pad(packed, (0, -packed.shape[0] % 1024)).reshape(-1, LANES)
    bit = 1
    while bit < count:
        (got,) = yield [(packed, "zy", [(i, i ^ bit) for i in range(count)])]
        packed = packed + got
        bit *= 2
    (got,) = yield [(packed, "core", SWAP)]
    packed = in_order(packed, got, core)
    (got,) = yield [(packed, "seq", SWAP)]
    packed = jnp.swapaxes(in_order(packed, got, side), 0, 1).reshape(2, 2, -1)
    return jnp.split(packed, np.cumsum(lengths), axis=2)[: len(lengths)]


def zy_exchange(value, bit):
    count = lax.axis_size("zy")
    return lax.ppermute(value, "zy", [(i, i ^ bit) for i in range(count)])


def zy_sum(value):
    count = lax.axis_size("zy")
    bit = 1
    while bit < count:
        value = value + zy_exchange(value, bit)
        bit *= 2
    return value


def head_split(count):
    rows = DI // count
    if rows % (2 * HD) == 0 and count % 2 == 0:
        return count // 2, rows // (2 * HD)
    return 1, MYH


def split_heads(value, dim, split):
    q, i = split
    size = value.shape[dim]
    unit = size // NH
    shape = value.shape
    value = value.reshape(shape[:dim] + (2, q, 2, i * unit) + shape[dim + 1 :])
    value = jnp.swapaxes(value, dim + 1, dim + 2)
    return value.reshape(shape[:dim] + (2, 2, size // PARTS) + shape[dim + 1 :])


def join_heads(value, dim, split):
    q, i = split
    shape = value.shape
    mine = shape[dim + 2]
    value = value.reshape(shape[:dim] + (2, 2, q, mine // q) + shape[dim + 3 :])
    value = jnp.swapaxes(value, dim + 1, dim + 2)
    return value.reshape(shape[:dim] + (PARTS * mine,) + shape[dim + 3 :])


HALF = LANES // 2


def half_places(split, core, side):
    q, i = split
    return [((core * q + at) * 2 + side) * i + k for at in range(q) for k in range(i)]


def halves(tile_of, places):
    tiles = []
    for at in range(0, len(places), 2):
        one, two = places[at], places[at + 1]
        if one % 2 == 0 and two == one + 1:
            tiles.append(tile_of(one // 2))
            continue
        left, right = tile_of(one // 2), tile_of(two // 2)
        left = pltpu.roll(left, HALF, 1) if one % 2 else left
        right = right if two % 2 else pltpu.roll(right, HALF, 1)
        lane = lax.broadcasted_iota(jnp.int32, left.shape, 1)
        tiles.append(jnp.where(lane < HALF, left, right))
    return tiles


def head_choice(split):
    choice = np.zeros((PARTS, NH, LANES), np.float32)
    for g in range(PARTS):
        for lane, head in enumerate(half_places(split, g // 2, g % 2)):
            choice[g, head, lane] = 1.0
    return choice


def split_kernel(split, at_ref, w_ref, choice_ref, out_ref):
    me = at_ref[0]

    def tile_of(base):
        return lambda t: w_ref[:, base + t * LANES : base + (t + 1) * LANES].astype(F32)

    bc = w_ref[:, 2 * DI : 2 * DI + BC]
    steps = w_ref[:, DI + CONV :]
    for g in range(PARTS):
        places = half_places(split, g // 2, g % 2)
        at = me ^ g
        tiles = halves(tile_of(DI), places)
        for k, tile in enumerate(tiles):
            out_ref[at, :, k * LANES : (k + 1) * LANES] = tile.astype(BF16)
        out_ref[at, :, MYC : MYC + BC] = bc
        out_ref[at, :, MYC + BC : W1] = nn(steps, choice_ref[g]).astype(BF16)
        for k, tile in enumerate(halves(tile_of(0), places)):
            out_ref[at, :, W1 + k * LANES : W1 + (k + 1) * LANES] = tile.astype(BF16)


def smem(shape=None):
    return pl.BlockSpec(memory_space=pltpu.SMEM)


def split_columns(weight, split, me):
    return pl.pallas_call(
        functools.partial(split_kernel, split),
        out_shape=jax.ShapeDtypeStruct((PARTS, weight.shape[0], W1 + MYC), BF16),
        in_specs=[smem(), pl.BlockSpec(), pl.BlockSpec()],
        name="split_columns",
    )(me, weight, jnp.asarray(head_choice(split), BF16))


def assemble_kernel(at_ref, one, two, three, four, first_ref, gate_ref):
    me = at_ref[0]
    for r, ref in enumerate((one, two, three, four)):
        first_ref[me ^ r] = ref[:, :W1]
        gate_ref[me ^ r] = ref[:, W1:]


def assemble_rows(blocks, me):
    rows = blocks[0].shape[0]
    first, gate = pl.pallas_call(
        assemble_kernel,
        out_shape=[
            jax.ShapeDtypeStruct((PARTS, rows, W1), BF16),
            jax.ShapeDtypeStruct((PARTS, rows, MYC), BF16),
        ],
        in_specs=[smem()] + [pl.BlockSpec()] * PARTS,
        name="assemble_rows",
    )(me, *blocks)
    return first.reshape(PARTS * rows, W1), gate.reshape(PARTS * rows, MYC)


def hand_back_kernel(at_ref, *refs):
    *ins, out_ref = refs
    me = at_ref[0]
    for g in range(PARTS):
        at = 0
        for ref in ins:
            out_ref[me ^ g, :, at : at + ref.shape[2]] = ref[g].astype(BF16)
            at += ref.shape[2]


def hand_back(blocks, me):
    blocks = [b.reshape(PARTS, -1, b.shape[1]) for b in blocks]
    return pl.pallas_call(
        hand_back_kernel,
        out_shape=jax.ShapeDtypeStruct((PARTS, blocks[0].shape[1], W1 + MYC), BF16),
        in_specs=[smem()] + [pl.BlockSpec()] * len(blocks),
        name="hand_back",
    )(me, *blocks)


def join_kernel(split, at_ref, one, two, three, four, choice_ref, out_ref, by):
    me = at_ref[0]
    for r, ref in enumerate((one, two, three, four)):
        by[me ^ r] = ref[...].astype(F32)
    where = {}
    for g in range(PARTS):
        for at, place in enumerate(half_places(split, g // 2, g % 2)):
            where[place] = (g, at)

    def put(base, column):
        for t in range(DI // LANES):
            tiles = []
            for k in range(2):
                g, at = where[2 * t + k]
                start = column + at // 2 * LANES
                tile = by[g, :, start : start + LANES]
                tiles.append(tile if at % 2 == k else pltpu.roll(tile, HALF, 1))
            lane = lax.broadcasted_iota(jnp.int32, tiles[0].shape, 1)
            out_ref[:, base + t * LANES : base + (t + 1) * LANES] = jnp.where(lane < HALF, tiles[0], tiles[1])

    put(0, W1)
    put(DI, 0)
    out_ref[:, 2 * DI : 2 * DI + BC] = sum(by[g, :, MYC : MYC + BC] for g in range(PARTS))
    out_ref[:, DI + CONV :] = sum(
        nt(by[g, :, MYC + BC : W1].astype(BF16), choice_ref[g]) for g in range(PARTS)
    )


def join_columns(blocks, split, me):
    rows = blocks[0].shape[0]
    return pl.pallas_call(
        functools.partial(join_kernel, split),
        out_shape=jax.ShapeDtypeStruct((rows, 2 * DI + BC + NH), F32),
        in_specs=[smem()] + [pl.BlockSpec()] * (PARTS + 1),
        scratch_shapes=[pltpu.VMEM((PARTS, rows, W1 + MYC), F32)],
        name="join_columns",
    )(me, *blocks, jnp.asarray(head_choice(split), BF16))


DIAGONAL = [(0, 0), (1, 2), (2, 1), (3, 3)]


def nt(a, b):
    return lax.dot_general(a, b, (((1,), (1,)), ((), ())), preferred_element_type=F32)


def nn(a, b):
    return lax.dot_general(a, b, (((1,), (0,)), ((), ())), preferred_element_type=F32)


def exact(a, b):
    return lax.dot_general(
        a, b, (((1,), (0,)), ((), ())), preferred_element_type=F32, precision=HIGH
    )


def in_two(value, axis):
    top = value.astype(BF16)
    return jnp.concatenate([top, (value - top.astype(F32)).astype(BF16)], axis=axis)


def over_heads(value, heads_ref):
    return nn(in_two(value, 1), heads_ref[...])


def sum_heads(value, heads_ref):
    top = value.astype(BF16)
    low = (value - top.astype(F32)).astype(BF16)
    heads = heads_ref[:LANES, :]
    return nt(top, heads) + nt(low, heads)


PIECES = 4
PROJECT = 128


def project_kernel(*refs):
    *sources, gain_ref, w_ref, first_ref, normed_ref, turned_ref, held = refs
    step = pl.program_id(0)
    own, near, far, both = sources[0], sources[1], sources[2 : 2 + PIECES], sources[2 + PIECES :]
    order = [own] * PIECES + list(far) + [near] * PIECES + list(both)
    for ref in sources:
        steps = [i for i, r in enumerate(order) if r is ref]

        @pl.when((step >= steps[0]) & (step <= steps[-1]))
        def _():
            held[...] = ref[...]

    x = held[...].astype(F32)
    inv = lax.rsqrt(jnp.mean(x * x, axis=-1, keepdims=True) + EPS)
    normed = x * inv * gain_ref[...]
    low = normed.astype(BF16)
    normed_ref[...] = low
    first_ref[...] = nn(low, w_ref[...]).astype(BF16)
    turned_ref[...] = normed.T.astype(BF16)


def project(own, near, far, both, gain, w_first):
    rows = own.shape[0]
    steps = rows // PROJECT
    total = PARTS * rows

    def at(start):
        return lambda t: (jnp.clip(t - start, 0, steps - 1), 0)

    still = lambda t: (0, 0)
    return pl.pallas_call(
        project_kernel,
        grid=(total // PROJECT,),
        in_specs=[
            pl.BlockSpec((PROJECT, D), at(0)),
            pl.BlockSpec((PROJECT, D), at(2 * steps)),
        ]
        + [pl.BlockSpec((PROJECT, D), still)] * (2 * PIECES)
        + [pl.BlockSpec((1, D), still), pl.BlockSpec((D, W1), still)],
        out_specs=[
            pl.BlockSpec((PROJECT, W1), lambda t: (t, 0)),
            pl.BlockSpec((PROJECT, D), lambda t: (t, 0)),
            pl.BlockSpec((D, PROJECT), lambda t: (0, t)),
        ],
        out_shape=[
            jax.ShapeDtypeStruct((total, W1), BF16),
            jax.ShapeDtypeStruct((total, D), BF16),
            jax.ShapeDtypeStruct((D, total), BF16),
        ],
        scratch_shapes=[pltpu.VMEM((PROJECT, D), BF16)],
        compiler_params=pltpu.CompilerParams(vmem_limit_bytes=VMEM_LIMIT),
        cost_estimate=pl.CostEstimate(flops=12 * 10**9, bytes_accessed=30 * 10**6, transcendentals=10**4),
        name="project",
    )(own, near, *far, *both, gain, w_first)


def softplus(value):
    return jnp.maximum(value, 0.0) + jnp.log1p(jnp.exp(-jnp.abs(value)))


def conv_total(ext, raw_ref, halo_ref, taps_ref, marks):
    ext[0:8, :] = halo_ref[8:16, :].astype(F32)
    ext[8 : 8 + Q, :] = raw_ref[...].astype(F32)
    total = taps_ref[4:5, :] + ext[8 : 8 + Q, :] * taps_ref[3:4, :]
    for k in range(KW - 1):
        total = total + ext[5 + k : 5 + k + Q, :] * taps_ref[k : k + 1, :] * marks[:, 1 + k : 2 + k]
    return total


def conv_back(d_total, ext, ahead, taps_ref, marks, sums_ref):
    sums_ref[4:5, :] += jnp.sum(d_total, axis=0, keepdims=True)
    sums_ref[3:4, :] += jnp.sum(d_total * ext[8 : 8 + Q, :], axis=0, keepdims=True)
    for k in range(KW - 1):
        sums_ref[k : k + 1, :] += jnp.sum(
            d_total * (ext[5 + k : 5 + k + Q, :] * marks[:, 1 + k : 2 + k]), axis=0, keepdims=True
        )
    ext[0:Q, :] = d_total
    ext[Q : Q + 8, :] = ahead[...]
    d_raw = d_total * taps_ref[3:4, :]
    for k in range(KW - 1):
        d_raw = d_raw + ext[3 - k : 3 - k + Q, :] * (taps_ref[k : k + 1, :] * marks[:, 4 + k : 5 + k])
    ahead[...] = d_total[0:8, :]
    return d_raw


def decays(dt_ref, head_ref, lower):
    raw = dt_ref[...].astype(F32)
    lane = lax.broadcasted_iota(jnp.int32, (Q, LANES), 1)
    live = (lane < MYH).astype(F32)
    shifted = raw * live + head_ref[0:1, :]
    step = softplus(shifted) * live
    rate = -jnp.exp(head_ref[1:2, :])
    log_decay = rate * step
    return shifted, step, rate, log_decay, exact(lower, log_decay)


def scan_forward(
    side_ref, x_ref, x_halo, bc_ref, bc_halo, dt_ref, marks_ref, row_ref, x_taps, bc_taps, head_ref, heads_ref,
    y_ref, state_ref, bc_out, ext, bc_ext, held,
):
    chunk = pl.program_id(1)

    @pl.when(chunk == 0)
    def _():
        held[...] = jnp.zeros_like(held)

    marks = marks_ref[...]
    x_act = conv_total(ext, x_ref, x_halo, x_taps, marks)
    x_act = x_act * lax.logistic(x_act)
    bc_act = conv_total(bc_ext, bc_ref, bc_halo, bc_taps, marks)
    bc_act = (bc_act * lax.logistic(bc_act)).astype(BF16)
    bc_out[...] = bc_act
    b, c = bc_act[:, :NS], bc_act[:, NS:]
    at_row = lax.broadcasted_iota(jnp.int32, (Q, Q), 0)
    at_col = lax.broadcasted_iota(jnp.int32, (Q, Q), 1)
    lower = (at_row >= at_col).astype(F32)
    _, step, _, _, cum = decays(dt_ref, head_ref, lower)
    cum_t = cum.T
    shut = jnp.where((at_row >= at_col) & (marks[:, 0:1] == row_ref[0]), 0.0, FAR)
    scores = nt(c, b)
    state = held[...]
    state_low = state.astype(BF16)
    state_ref[0] = state_low
    last = cum[Q - 1 : Q, :]
    x_step = x_act * over_heads(step, heads_ref)
    keep = over_heads(jnp.exp(cum) * marks[:, 7:8], heads_ref)
    y = nn(c, state_low) * keep + x_act * x_taps[5:6, :]
    tail = over_heads(jnp.exp(last - cum) * marks[:, 8:9], heads_ref)
    carry = over_heads(jnp.broadcast_to(jnp.exp(last) * marks[Q - 1 : Q, 7:8], (8, LANES)), heads_ref)
    held[...] = state * carry[0:1, :] + nn(b.T, (x_step * tail).astype(BF16))
    lane = lax.broadcasted_iota(jnp.int32, (Q, LANES), 1)
    for pair in range(MYH // 2):
        cols = slice(pair * LANES, (pair + 1) * LANES)
        mixing = []
        for head in (2 * pair, 2 * pair + 1):
            spread = cum[:, head : head + 1] - cum_t[head : head + 1, :] + shut
            mixing.append((jnp.exp(spread) * scores).astype(BF16))
        steps = x_step[:, cols]
        both = jnp.concatenate(
            [jnp.where(lane < HD, steps, 0.0), jnp.where(lane < HD, 0.0, steps)], axis=0
        ).astype(BF16)
        y_ref[:, cols] = y[:, cols] + nn(jnp.concatenate(mixing, axis=1), both)


def scan_backward(
    group, side_ref, x_ref, x_halo, bc_ref, dt_ref, dy_ref, state_ref, marks_ref, row_ref, x_taps, head_ref, heads_ref,
    *rest,
):
    final = group == GROUPS - 1
    if group > 0:
        dbc_before, *rest = rest
    if final:
        bc_raw_ref, bc_halo, bc_taps, *rest = rest
    dx_ref, dbc_ref, ddt_ref, wide_ref, thin_ref, *rest = rest
    if final:
        bc_sums, *rest = rest
    ext, held, ahead, *rest = rest
    if final:
        bc_ext, bc_ahead = rest
    chunk = pl.program_id(0)

    @pl.when(chunk == 0)
    def _():
        held[...] = jnp.zeros_like(held)
        ahead[...] = jnp.zeros_like(ahead)
        if final:
            bc_ahead[...] = jnp.zeros_like(bc_ahead)

    @pl.when(chunk == 0)
    def _():
        wide_ref[...] = jnp.zeros_like(wide_ref)
        thin_ref[...] = jnp.zeros_like(thin_ref)
        if final:
            bc_sums[...] = jnp.zeros_like(bc_sums)

    marks = marks_ref[...]
    total = conv_total(ext, x_ref, x_halo, x_taps, marks)
    gate = lax.logistic(total)
    x_act = total * gate
    slope = gate * (1.0 + total * (1.0 - gate))
    b, c = bc_ref[:, :NS], bc_ref[:, NS:]
    at_row = lax.broadcasted_iota(jnp.int32, (Q, Q), 0)
    at_col = lax.broadcasted_iota(jnp.int32, (Q, Q), 1)
    lower = (at_row >= at_col).astype(F32)
    shifted, step, rate, log_decay, cum = decays(dt_ref, head_ref, lower)
    cum_t = cum.T
    shut = jnp.where((at_row <= at_col) & (marks[:, 0:1] == row_ref[0]), 0.0, FAR)
    scores = nt(b, c)
    last = cum[Q - 1 : Q, :]
    dy = dy_ref[...].astype(F32)
    step_wide = over_heads(step, heads_ref)
    x_step = x_act * step_wide
    keep = over_heads(jnp.exp(cum) * marks[:, 7:8], heads_ref)
    tail = over_heads(jnp.exp(last - cum) * marks[:, 8:9], heads_ref)
    carry_thin = jnp.broadcast_to(jnp.exp(last) * marks[Q - 1 : Q, 7:8], (8, LANES))
    carry = over_heads(carry_thin, heads_ref)
    state = state_ref[0]
    d_state = held[...]
    d_state_low = d_state.astype(BF16)
    dy_keep = dy * keep
    dy_keep_low = dy_keep.astype(BF16)
    from_state = nn(c, state)
    seen = sum_heads(dy_keep * from_state, heads_ref)
    d_c = nt(dy_keep_low, state)
    to_state = x_step * tail
    d_b = nt(to_state.astype(BF16), d_state_low)
    du_tail = nn(b, d_state_low) * tail
    sent = sum_heads(x_step * du_tail, heads_ref)
    linked = jnp.sum(d_state * state.astype(F32), axis=0, keepdims=True)
    linked = sum_heads(jnp.broadcast_to(linked, (8, GC)), heads_ref)[0:1, :] * carry_thin[0:1, :]
    held[...] = d_state * carry[0:1, :] + nn(c.T, dy_keep_low)
    lane = lax.broadcasted_iota(jnp.int32, (Q, LANES), 1)
    d_scores = jnp.zeros((Q, Q), F32)
    by_later, by_earlier, du_parts = [], [], []
    for pair in range(GH // 2):
        cols = slice(pair * LANES, (pair + 1) * LANES)
        steps, dys = x_step[:, cols], dy[:, cols]
        step_both = jnp.concatenate(
            [jnp.where(lane < HD, steps, 0.0), jnp.where(lane < HD, 0.0, steps)], axis=0
        ).astype(BF16)
        dy_both = jnp.concatenate(
            [jnp.where(lane < HD, dys, 0.0), jnp.where(lane < HD, 0.0, dys)], axis=0
        ).astype(BF16)
        met = nt(step_both, dys.astype(BF16))
        mixing = []
        for place, head in enumerate((group * GH + 2 * pair, group * GH + 2 * pair + 1)):
            decay = jnp.exp(cum_t[head : head + 1, :] - cum[:, head : head + 1] + shut)
            mixing.append((decay * scores).astype(BF16))
            weighed = decay * met[place * Q : (place + 1) * Q, :]
            d_scores = d_scores + weighed
            spent = weighed * scores
            by_later.append(jnp.sum(spent, axis=0, keepdims=True))
            by_earlier.append(jnp.sum(spent, axis=1, keepdims=True))
        du_parts.append(nn(jnp.concatenate(mixing, axis=1), dy_both))
    du = jnp.concatenate(du_parts, axis=1) + du_tail
    d_low = d_scores.astype(BF16)
    d_b = d_b + nn(d_low, c)
    d_c = d_c + nn(d_scores.T.astype(BF16), b)
    d_bc = jnp.concatenate([d_b, d_c], axis=1)
    if group > 0:
        d_bc = d_bc + dbc_before[...]
    if final:
        bc_total = conv_total(bc_ext, bc_raw_ref, bc_halo, bc_taps, marks)
        bc_gate = lax.logistic(bc_total)
        d_bc = d_bc * (bc_gate * (1.0 + bc_total * (1.0 - bc_gate)))
        d_bc = conv_back(d_bc, bc_ext, bc_ahead, bc_taps, marks, bc_sums)
    dbc_ref[...] = d_bc.astype(dbc_ref.dtype)
    low_lanes, high_lanes = group * GH, LANES - (group + 1) * GH
    later = by_later + [jnp.zeros((high_lanes, Q), F32)]
    later = ([jnp.zeros((low_lanes, Q), F32)] if low_lanes else []) + later
    later = jnp.concatenate(later, axis=0).T
    earlier = jnp.zeros((Q, LANES), F32)
    for head in range(GH):
        earlier = jnp.where(lane == low_lanes + head, by_earlier[head], earlier)
    upper = (at_row <= at_col).astype(F32)
    strict = (at_row > at_col).astype(F32)
    d_log = exact(upper, seen + later - earlier) + exact(strict, sent) + linked
    d_step = sum_heads(x_act * du, heads_ref)
    d_raw = (d_step + rate * d_log) * lax.logistic(shifted)
    mine = ((lane >= low_lanes) & (lane < low_lanes + GH)).astype(F32)
    d_raw = d_raw * mine
    ddt_ref[...] = d_raw
    thin_ref[0:1, :] += jnp.sum(d_raw, axis=0, keepdims=True)
    thin_ref[1:2, :] += jnp.sum(d_log * log_decay * mine, axis=0, keepdims=True)
    wide_ref[5:6, :] += jnp.sum(dy * x_act, axis=0, keepdims=True)
    d_total = (du * step_wide + dy * x_taps[5:6, :]) * slope
    dx_ref[...] = conv_back(d_total, ext, ahead, x_taps, marks, wide_ref).astype(BF16)


def block_at(seq, time, side):
    blocks = LEN // Q
    return seq * blocks + (time + side * (blocks // 2)) % blocks


def halo_at(seq, time, side):
    return block_at(seq, jnp.maximum(time - 1, 0), side) * (Q // 16) + Q // 16 - 1


BC_AT = MYC // BC
DT_AT = (MYC + BC) // LANES


def run_forward(side, first, marks, rows, x_taps, bc_taps, head_rows, heads):
    total = first.shape[0]
    blocks = LEN // Q
    here = lambda col: lambda s, t, side: (block_at(s, t, side[0]), col)
    halo = lambda col: lambda s, t, side: (halo_at(s, t, side[0]), col)
    still = lambda s, t, side: (0, 0)
    return pl.pallas_call(
        scan_forward,
        grid_spec=pltpu.PrefetchScalarGridSpec(
            num_scalar_prefetch=1,
            grid=(total // LEN, blocks),
            in_specs=[
                pl.BlockSpec((Q, MYC), here(0)),
                pl.BlockSpec((16, MYC), halo(0)),
                pl.BlockSpec((Q, BC), here(BC_AT)),
                pl.BlockSpec((16, BC), halo(BC_AT)),
                pl.BlockSpec((Q, LANES), here(DT_AT)),
                pl.BlockSpec((Q, 16), lambda s, t, side: (s * blocks + t, 0)),
                pl.BlockSpec((1, 1, Q), lambda s, t, side: (s * blocks + t, 0, 0)),
                pl.BlockSpec((8, MYC), still),
                pl.BlockSpec((8, BC), still),
                pl.BlockSpec((8, LANES), still),
                pl.BlockSpec((2 * LANES, MYC), still),
            ],
            out_specs=[
                pl.BlockSpec((Q, MYC), here(0)),
                pl.BlockSpec((1, NS, MYC), lambda s, t, side: (s * blocks + t, 0, 0)),
                pl.BlockSpec((Q, BC), here(0)),
            ],
            scratch_shapes=[
                pltpu.VMEM((Q + 8, MYC), F32),
                pltpu.VMEM((Q + 8, BC), F32),
                pltpu.VMEM((NS, MYC), F32),
            ],
        ),
        out_shape=[
            jax.ShapeDtypeStruct((total, MYC), F32),
            jax.ShapeDtypeStruct((total // Q, NS, MYC), BF16),
            jax.ShapeDtypeStruct((total, BC), BF16),
        ],
        compiler_params=pltpu.CompilerParams(vmem_limit_bytes=VMEM_LIMIT),
        cost_estimate=pl.CostEstimate(flops=20 * 10**9, bytes_accessed=60 * 10**6, transcendentals=10**7),
        name="scan_forward",
    )(side, first, first, first, first, first, marks, rows, x_taps, bc_taps, head_rows, heads)


def run_backward(group, seq, side, first, bc_act, d_ssm, states, marks, rows, x_taps, bc_taps, head_rows, heads, d_bc):
    blocks = LEN // Q
    final = group == GROUPS - 1
    here = lambda col: lambda t, side: (block_at(seq, blocks - 1 - t, side[0]), col)
    out = lambda t, side: (block_at(0, blocks - 1 - t, side[0]), 0)
    halo = lambda col: lambda t, side: (halo_at(seq, blocks - 1 - t, side[0]), col)
    time = lambda t: seq * blocks + blocks - 1 - t
    still = lambda t, side: (0, 0)
    share = lambda t, side: (0, group)
    in_specs = [
        pl.BlockSpec((Q, GC), here(group)),
        pl.BlockSpec((16, GC), halo(group)),
        pl.BlockSpec((Q, BC), here(0)),
        pl.BlockSpec((Q, LANES), here(DT_AT)),
        pl.BlockSpec((Q, GC), here(group)),
        pl.BlockSpec((1, NS, GC), lambda t, side: (time(t), 0, group)),
        pl.BlockSpec((Q, 16), lambda t, side: (time(t), 0)),
        pl.BlockSpec((1, 1, Q), lambda t, side: (time(t), 0, 0)),
        pl.BlockSpec((8, GC), share),
        pl.BlockSpec((8, LANES), still),
        pl.BlockSpec((2 * LANES, GC), share),
    ]
    inputs = [first, first, bc_act, first, d_ssm, states, marks, rows, x_taps, head_rows, heads]
    out_specs = [
        pl.BlockSpec((Q, GC), out),
        pl.BlockSpec((Q, BC), out),
        pl.BlockSpec((Q, LANES), out),
        pl.BlockSpec((8, GC), still),
        pl.BlockSpec((8, LANES), still),
    ]
    out_shape = [
        jax.ShapeDtypeStruct((LEN, GC), BF16),
        jax.ShapeDtypeStruct((LEN, BC), BF16 if final else F32),
        jax.ShapeDtypeStruct((LEN, LANES), F32),
        jax.ShapeDtypeStruct((8, GC), F32),
        jax.ShapeDtypeStruct((8, LANES), F32),
    ]
    scratch = [pltpu.VMEM((Q + 8, GC), F32), pltpu.VMEM((NS, GC), F32), pltpu.VMEM((8, GC), F32)]
    if group > 0:
        in_specs.append(pl.BlockSpec((Q, BC), out))
        inputs.append(d_bc)
    if final:
        in_specs += [
            pl.BlockSpec((Q, BC), here(BC_AT)),
            pl.BlockSpec((16, BC), halo(BC_AT)),
            pl.BlockSpec((8, BC), still),
        ]
        inputs += [first, first, bc_taps]
        out_specs.append(pl.BlockSpec((8, BC), still))
        out_shape.append(jax.ShapeDtypeStruct((8, BC), F32))
        scratch += [pltpu.VMEM((Q + 8, BC), F32), pltpu.VMEM((8, BC), F32)]
    return pl.pallas_call(
        functools.partial(scan_backward, group),
        grid_spec=pltpu.PrefetchScalarGridSpec(
            num_scalar_prefetch=1, grid=(blocks,), in_specs=in_specs, out_specs=out_specs, scratch_shapes=scratch
        ),
        out_shape=out_shape,
        compiler_params=pltpu.CompilerParams(vmem_limit_bytes=VMEM_LIMIT),
        cost_estimate=pl.CostEstimate(flops=15 * 10**9, bytes_accessed=50 * 10**6, transcendentals=10**7),
        name="scan_backward_%d_%d" % (group, seq),
    )(side, *inputs)


def lead(value, by):
    if by == 0:
        return value
    pad = [(0, 0)] * value.ndim
    if by > 0:
        pad[1] = (0, by)
        return jnp.pad(value, pad)[:, by:]
    pad[1] = (-by, 0)
    return jnp.pad(value, pad)[:, :by]


def fold(block):
    return jnp.concatenate([block[..., : D // 2], block[..., D // 2 :]], axis=-2)


def unfold(block):
    half = block.shape[-2] // 2
    return jnp.concatenate([block[..., :half, :], block[..., half:, :]], axis=-1)


def out_rows(full, core):
    count, rows, cols = full.shape
    full = full.reshape(2, count // 2, rows, cols)
    kept, got = pick(full, core), swap(pick(full, 1 - core), "core")
    first = jnp.where(core == 0, kept, got)
    second = jnp.where(core == 0, got, kept)
    return jnp.stack([unfold(first), unfold(second)], axis=1).reshape(MYC, D)


def out_blocks(grad, count, core):
    rows = DI // (count * PARTS)
    halves = grad.astype(BF16).reshape(count // 2, 2, rows, D)
    kept, got = pick(halves, core, 1), swap(pick(halves, 1 - core, 1), "core")
    first = jnp.where(core == 0, kept, got)
    second = jnp.where(core == 0, got, kept)
    return fold(jnp.concatenate([first, second], axis=0))


def out_whole(out_weight, split, core, side):
    whole = lax.all_gather(out_weight, ("zy", "core", "seq"), axis=0, tiled=True)
    return pick(pick(split_heads(whole, 0, split), core), side)


def out_scattered(grad, split, core, side):
    own = jnp.zeros((2, 2, MYC, D), BF16)
    own = lax.dynamic_update_slice(own, grad.astype(BF16)[None, None], (core, side, 0, 0))
    whole = join_heads(own, 0, split)
    return lax.psum_scatter(whole, ("zy", "core", "seq"), scatter_dimension=0, tiled=True)


def own_slice(whole, size):
    at = (lax.axis_index("zy") * 2 + lax.axis_index("core")) * 2 + lax.axis_index("seq")
    return lax.dynamic_slice_in_dim(whole, at * size, size, 0)


def body(
    tokens,
    segments,
    norm_gain,
    in_weight,
    conv_weight,
    conv_bias,
    dt_bias,
    a_log,
    d_skip,
    gated_gain,
    out_weight,
    cotangent,
):
    count = lax.axis_size("zy")
    core, side = lax.axis_index("core"), lax.axis_index("seq")
    split = head_split(count)
    rows = tokens.shape[1]
    total = PARTS * rows

    blocked = split[0] > 1

    sizes = (norm_gain.shape[0], conv_weight.size, conv_bias.shape[0], gated_gain.shape[0])
    small = jnp.concatenate([norm_gain, conv_weight.reshape(-1), conv_bias, gated_gain])
    me = (core * 2 + side).astype(jnp.int32).reshape(1)
    at_side = side.astype(jnp.int32).reshape(1)
    small = Task(small_steps(small, core, side))
    segs = Task(group_steps(segments[0].reshape(-1, LANES)))

    mix = Task(peer_steps(split_columns(in_weight, split, me)))
    stage([mix, segs, small])
    sent, later = assemble_rows(mix.value, me)
    if blocked:
        held = lax.ppermute(out_weight, GROUP, DIAGONAL)
        later = jnp.concatenate([later, fold(held)], axis=1)
    else:
        w_out = out_whole(out_weight, split, core, side)
    ring = Task(gather_steps(sent, [0]))
    token_all = Task(token_steps(tokens[0], PIECES))
    while not (ring.done and token_all.done and small.done):
        stage([ring, token_all, small])
    w_first = ring.value[0].reshape(D, W1)

    small = small.value.reshape(-1, sum(sizes))
    cuts = np.cumsum(sizes)[:-1]
    gain, taps, bias, gated = (v.reshape(-1).astype(F32) for v in jnp.split(small, cuts, axis=1))
    taps = taps.reshape(CONV, KW)

    def mine(vector, dim=0):
        return pick(pick(split_heads(vector, dim, split), core, dim), side, dim)

    gated_mine = mine(gated)
    x_taps = jnp.concatenate(
        [
            mine(taps[:DI]).T,
            mine(bias[:DI])[None],
            jnp.repeat(mine(d_skip), HD)[None],
            jnp.zeros((2, MYC), F32),
        ],
        axis=0,
    )
    bc_taps = jnp.concatenate(
        [taps[DI:].T, bias[DI:][None], jnp.zeros((3, BC), F32)], axis=0
    )
    head_rows = jnp.concatenate([mine(dt_bias)[None], mine(a_log)[None]], axis=0)
    head_rows = jnp.pad(head_rows, ((0, 6), (0, LANES - MYH)))
    heads = np.kron(np.eye(LANES, MYH, dtype=np.float32), np.ones((1, HD), np.float32))
    heads = jnp.asarray(np.concatenate([heads, heads], axis=0), BF16)

    segs = jnp.stack([v.reshape(-1) for v in segs.value]).reshape(2, 2, rows)
    segs = jnp.where(side == 0, segs, segs[:, ::-1]).reshape(2, LEN).astype(F32)
    before = [lead(segs, k - KW + 1) == segs for k in range(KW - 1)]
    place = jnp.arange(LEN)[None, :]
    before = [(m & (place >= KW - 1 - k)).astype(F32) for k, m in enumerate(before)]
    after = [lead(m, KW - 1 - k) for k, m in enumerate(before)]
    ends = segs.reshape(2, LEN // Q, Q)[:, :, -1:]
    starts = jnp.concatenate([jnp.full((2, 1, 1), -1.0, F32), ends[:, :-1]], axis=1)
    keep = (segs.reshape(2, LEN // Q, Q) == starts).astype(F32).reshape(2, LEN)
    tail = (segs.reshape(2, LEN // Q, Q) == ends).astype(F32).reshape(2, LEN)
    marks = jnp.stack([segs] + before + after + [keep, tail] + [jnp.zeros_like(segs)] * 7, axis=-1)
    marks = marks.reshape(total, 16)
    seg_rows = segs.reshape(total // Q, 1, Q)

    near, far, both = token_all.value
    ring = Task(gather_steps(later, [0, MYC] if blocked else [0]))
    cot_all = Task(token_steps(cotangent[0], 3))
    first, normed, turned = stage(
        [ring, cot_all], project, tokens[0], near, far, both, gain[None], w_first
    )
    scanned = stage(
        [ring, cot_all], run_forward, at_side, first, marks, seg_rows, x_taps, bc_taps, head_rows, heads
    )
    while not (ring.done and cot_all.done):
        stage([ring, cot_all])
    y, states, bc_act = scanned
    near, far, both = cot_all.value
    cot_all = jnp.concatenate([cotangent[0]] + far + [near] + both, axis=0)
    w_gate = ring.value[0].reshape(D, MYC)
    if blocked:
        w_out = out_rows(ring.value[1], core)

    gate = nn(normed, w_gate).astype(BF16).astype(F32)
    sig = lax.logistic(gate)
    silu = gate * sig
    joined = y * silu
    d_two = nt(cot_all, w_out)
    sums = jnp.stack(
        [jnp.sum(joined * joined, axis=-1), jnp.sum(joined * gated_mine * d_two, axis=-1)]
    )
    sums = sums.reshape(2, 2, 2, rows)
    sums = sums + swap(sums, "core")[:, ::-1]
    sums = (sums + swap(sums, "seq")[:, :, ::-1]).reshape(2, total)
    inv_two = lax.rsqrt(sums[0] / DI + EPS)[:, None]
    mean_two = (sums[1] / DI)[:, None]
    two = (joined * inv_two * gated_mine).astype(BF16)
    d_joined = inv_two * (gated_mine * d_two) - joined * (inv_two * inv_two * inv_two * mean_two)
    d_ssm = (d_joined * silu).astype(BF16)
    d_gate = (d_joined * y * (sig * (1.0 + gate * (1.0 - sig)))).astype(BF16)
    d_gated = jnp.sum(joined * inv_two * d_two, axis=0)

    def tn(a, b):
        return lax.dot_general(a, b, (((0,), (0,)), ((), ())), preferred_element_type=F32)

    two, d_ssm, d_gate = lax.optimization_barrier((two, d_ssm, d_gate))
    branch = nn(two, w_out).astype(BF16).reshape(PARTS, rows, D)
    d_out = tn(two, cot_all)
    d_w_gate = nn(turned, d_gate).astype(BF16).reshape(count, D // count, MYC)
    if blocked:
        d_out = out_blocks(d_out, count, core)
        d_w_gate = jnp.concatenate([d_w_gate, d_out], axis=2)
    ring = Task(scatter_steps(d_w_gate))
    branch = Task(sum_steps(branch, 2))

    def back(group, seq, d_bc):
        return (
            functools.partial(run_backward, group, seq),
            at_side, first, bc_act, d_ssm, states, marks, seg_rows, x_taps, bc_taps, head_rows, heads, d_bc,
        )

    def weights(pieces):
        return nn(turned, jnp.concatenate(pieces, axis=0))

    parts = {}
    for seq in range(2):
        parts[0, seq] = stage([ring, branch], *back(0, seq, None))
    early = weights([parts[0, 0][0], parts[0, 1][0]]).reshape(count, D // count, GC)
    early = Task(scatter_steps(early))
    for seq in range(2):
        parts[1, seq] = stage([ring, branch, early], *back(1, seq, parts[0, seq][1]))
    d_dt = [parts[0, seq][2] + parts[1, seq][2] for seq in range(2)]
    d_rest = [jnp.concatenate([parts[1, seq][0], parts[1, seq][1], d_dt[seq].astype(BF16)], axis=1) for seq in range(2)]
    wide = jnp.concatenate([parts[g, 0][3] + parts[g, 1][3] for g in range(GROUPS)], axis=1)
    thin = sum(parts[g, seq][4] for g in range(GROUPS) for seq in range(2))
    bc_sums = parts[1, 0][5] + parts[1, 1][5]
    d_w_rest = stage([ring, branch, early], weights, d_rest).reshape(count, D // count, W1 - GC)
    rest = Task(scatter_steps(d_w_rest))

    d_first = [[parts[0, seq][0], d_rest[seq]] for seq in range(2)]

    def partial_normed(pieces, b, at, w1, w2):
        def rows_of(value, start=0):
            return value[start + at * rows : start + (at + 1) * rows]

        a0 = jnp.concatenate([rows_of(p[0]) for p in pieces], axis=0)
        a1 = jnp.concatenate([rows_of(p[1]) for p in pieces], axis=0)
        b = jnp.concatenate([rows_of(b), rows_of(b, 2 * rows)], axis=0)
        value = nt(a0, w1[:, :GC]) + nt(a1, w1[:, GC:]) + nt(b, w2)
        return value.astype(BF16).reshape(2, rows, D)

    def partial_of(at):
        return (lambda *a: partial_normed(a[0], a[1], at, a[2], a[3])), d_first, d_gate, w_first, w_gate

    far = stage([rest, early, ring, branch], *partial_of(1))
    far = Task(far_steps(far, 2))
    near = stage([rest, early, ring, far], *partial_of(0))
    near = Task(far_steps(near, 0))
    small_grads = Task(small_sum_steps(
        (
            wide[:KW].reshape(-1),
            wide[KW],
            d_gated,
            bc_sums[: KW + 1].reshape(-1),
            thin[0, :MYH],
            thin[1, :MYH],
            jnp.sum(wide[KW + 1].reshape(MYH, HD), axis=1),
        ),
        core, side,
    ))
    stage([rest, early, ring, far, near, small_grads])
    finish([rest, early, ring, far, small_grads])
    d_normed = near.value + far.value.astype(F32)

    d_w = Task(peer_steps(hand_back([early.value, rest.value, ring.value[:, :MYC]], me)))
    if blocked:
        d_out = unfold(ring.value[:, MYC:].astype(BF16))
        d_out = lax.ppermute(d_out, GROUP, DIAGONAL).astype(F32)
    else:
        d_out = out_scattered(d_out, split, core, side).astype(F32)
    finish([d_w])
    in_sh = join_columns(d_w.value, split, me)
    block_out = (tokens[0].astype(F32) + branch.value).astype(BF16)[None]

    x = tokens[0].astype(F32)
    inv = lax.rsqrt(jnp.mean(x * x, axis=-1, keepdims=True) + EPS)
    scaled = gain * d_normed
    input_grad = (
        cotangent[0].astype(F32)
        + inv * scaled
        - x * (inv * inv * inv * jnp.mean(x * scaled, axis=-1, keepdims=True))
    )[None]
    d_gain = jnp.sum(x * inv * d_normed, axis=0)

    taps_x, bias_x, gain_two, taps_bc, bias_dt, alog, skip = small_grads.value
    taps_x = jnp.swapaxes(taps_x.reshape(2, 2, KW, MYC), 2, 3)
    taps_bc = jnp.sum(taps_bc, axis=(0, 1)).reshape(KW + 1, BC)
    conv_w = jnp.concatenate([join_heads(taps_x, 0, split), taps_bc[:KW].T], axis=0)
    conv_b = jnp.concatenate([join_heads(bias_x, 0, split), taps_bc[KW]])
    d_gain = jnp.pad(d_gain, (0, -D % 1024)).reshape(-1, LANES)
    d_gain = zy_sum(d_gain)
    d_gain = d_gain + swap(d_gain, "core")
    d_gain = (d_gain + swap(d_gain, "seq")).reshape(-1)[:D]
    return (
        block_out,
        input_grad,
        own_slice(d_gain, norm_gain.shape[0]),
        in_sh,
        own_slice(conv_w, conv_bias.shape[0]),
        own_slice(conv_b, conv_bias.shape[0]),
        join_heads(bias_dt, 0, split),
        join_heads(alog, 0, split),
        join_heads(skip, 0, split),
        own_slice(join_heads(gain_two, 0, split), gated_gain.shape[0]),
        d_out,
    )


def solution(mesh):
    fsdp, seq = mesh.shape["fsdp"], mesh.shape["seq"]
    grid = Mesh(mesh.devices.reshape(fsdp // 2, 2, seq), ("zy", "core", "seq"))
    every = ("zy", "core", "seq")
    rows = P(("zy", "core"), "seq", None)
    in_specs = (
        rows,
        P(("zy", "core"), "seq"),
        P(every),
        P(every, None),
        P(every, None),
        P(every),
        P(),
        P(),
        P(),
        P(every),
        P(every, None),
        rows,
    )
    out_specs = (
        rows,
        rows,
        P(every),
        P(every, None),
        P(every, None),
        P(every),
        P(),
        P(),
        P(),
        P(every),
        P(every, None),
    )
    return jax.shard_map(body, mesh=grid, in_specs=in_specs, out_specs=out_specs, check_vma=False)
```

```python
import functools

import jax
import jax.numpy as jnp
import numpy as np
from jax import lax
from jax.experimental import pallas as pl
from jax.experimental.pallas import tpu as pltpu
from jax.sharding import Mesh
from jax.sharding import PartitionSpec as P

D = 1536
NH = 48
HD = 64
NS = 128
KW = 4
DI = 3072
CONV = 3328
LEN = 1024

EPS = 1e-05
HIGH = lax.Precision.HIGHEST
F32 = jnp.float32
BF16 = jnp.bfloat16

PARTS = 4
MYH = NH // PARTS
MYC = MYH * HD
LANES = 128
BC = 2 * NS
W1 = MYC + BC + LANES
GROUPS = 2
GH = MYH // GROUPS
GC = GH * HD
Q = 128
FAR = -1e30
MIB = 1024 * 1024

SWAP = [(0, 1), (1, 0)]


def swap(value, axis):
    return lax.ppermute(value, axis, SWAP)


def pick(value, at, dim=0):
    return lax.dynamic_index_in_dim(value, at, dim, False)


def in_order(mine, other, place):
    buf = jnp.zeros((2,) + mine.shape, mine.dtype)
    buf = lax.dynamic_update_index_in_dim(buf, mine, place, 0)
    return lax.dynamic_update_index_in_dim(buf, other, 1 - place, 0)


GROUP = ("core", "seq")


def to_peer(value, r):
    return (value, GROUP, [(g, g ^ r) for g in range(PARTS)])


def ring_order(count):
    return list(range(0, count, 2)) + list(range(count - 1, 0, -2))


def ring_pairs(count):
    order = ring_order(count)
    right = [(order[i], order[(i + 1) % count]) for i in range(count)]
    return right, [(b, a) for a, b in right]


def ring_order_of(at, count):
    at = at % count
    return jnp.where(at < count // 2, 2 * at, 2 * (count - at) - 1)


def ring_place(count):
    zy = lax.axis_index("zy")
    place = jnp.where(zy % 2 == 0, zy // 2, count - 1 - zy // 2)
    return place, lambda at: ring_order_of(at, count)


def half_of(rows):
    return 16 * (rows // 32) if rows >= 32 else rows // 2


def piece_places(count, rows):
    places = [(0, 0)]
    for step in range(1, count // 2):
        places += [(-step, 0), (step, 0)]
    return places + [(count // 2, 0), (count // 2, half_of(rows))]


class Task:
    def __init__(self, steps):
        self.steps, self.value, self.done = steps, None, False
        self.moves = next(steps, None)
        self.done = self.moves is None

    def take(self, arrived):
        try:
            self.moves = self.steps.send(arrived)
        except StopIteration as end:
            self.value, self.done = end.value, True


def stage(tasks, work=None, *args):
    tasks = [t for t in tasks if not t.done]
    values = [[m[0] for m in t.moves] for t in tasks]
    values, args = lax.optimization_barrier((values, args))
    arrived = [
        [lax.ppermute(v, m[1], m[2]) for v, m in zip(vs, t.moves)] for vs, t in zip(values, tasks)
    ]
    result = None if work is None else work(*args)
    if work is None:
        arrived = lax.optimization_barrier(arrived)
    else:
        arrived, result = lax.optimization_barrier((arrived, result))
    for t, got in zip(tasks, arrived):
        t.take(got)
    return result


def finish(tasks):
    while not all(t.done for t in tasks):
        stage(tasks)


def gather_steps(block):
    count = lax.axis_size("zy")
    half = half_of(block.shape[0])
    right, left = ring_pairs(count)
    pieces = [block]
    ahead = back = block
    for _ in range(1, count // 2):
        ahead, back = yield [(ahead, "zy", right), (back, "zy", left)]
        pieces += [ahead, back]
    pieces += yield [(ahead[:half], "zy", right), (back[half:], "zy", left)]
    return pieces


def put_together(pieces, columns, flip):
    count = lax.axis_size("zy")
    place, order = ring_place(count)
    rows = pieces[0].shape[0]
    full = jnp.zeros((count, rows, columns.stop - columns.start), pieces[0].dtype)
    for piece, (step, row) in zip(pieces, piece_places(count, rows)):
        full = lax.dynamic_update_slice(full, piece[None, :, columns], (order(place + step + count) ^ flip, row, 0))
    return full


def scatter_steps(full, split=True):
    count, rows, cols = full.shape
    half = half_of(rows) if split else rows
    right, left = ring_pairs(count)
    place, order = ring_place(count)

    def get(at, off=0, size=rows):
        return lax.dynamic_slice(full, (order(at), off, 0), (1, size, cols))[0].astype(F32)

    far = place + count // 2
    one, two = get(far, 0, half), get(far, half, rows - half) if split else None
    for step in range(count // 2 - 1, -1, -1):
        moves = [(one.astype(BF16), "zy", right)]
        if two is not None:
            moves.append((two.astype(BF16), "zy", left))
        ahead, *back = yield moves
        back = back[0] if back else None
        if step == 0:
            break
        one, two = get(place + step), get(place + count - step)
        if back is None:
            one = one + ahead
        elif step == count // 2 - 1:
            one = jnp.concatenate([one[:half] + ahead, one[half:]], axis=0)
            two = jnp.concatenate([two[:half], two[half:] + back], axis=0)
        else:
            one, two = one + ahead, two + back
    return get(place) + ahead.astype(F32) + back.astype(F32)


def small_steps(value):
    count = lax.axis_size("zy")
    got = yield [to_peer(value, r) for r in range(1, PARTS)]
    held = jnp.stack([value] + list(got))
    bit = 1
    while bit < count:
        (got,) = yield [(held, "zy", [(i, i ^ bit) for i in range(count)])]
        held = jnp.concatenate([held, got])
        bit *= 2
    return held


def single_step(move):
    (got,) = yield [move]
    return got


def group_steps(value):
    got = yield [to_peer(value, r) for r in range(1, PARTS)]
    return [value] + list(got)


def piece_cuts(rows, pieces):
    return [16 * (rows // 16 * i // pieces) for i in range(pieces + 1)]


def token_steps(value, pieces):
    cuts = piece_cuts(value.shape[0], pieces)
    far, both = [], []
    moves = [(value, "core", SWAP)]
    for i in range(pieces):
        got = yield moves + [(value[cuts[i] : cuts[i + 1]], "seq", SWAP)]
        if i == 0:
            near = got[0]
        else:
            both.append(got[0])
        far.append(got[-1])
        moves = [(got[-1], "core", SWAP)]
    (got,) = yield moves
    return near, far, both + [got]


def peer_steps(blocks):
    got = yield [to_peer(blocks[r], r) for r in range(1, PARTS)]
    return [blocks[0]] + list(got)


def sum_steps(own, other, pieces):
    (got,) = yield [(other, "core", SWAP)]
    rows = own.shape[0] // 2
    sent = (own[rows:].astype(F32) + got[rows:].astype(F32)).astype(BF16)
    cuts = piece_cuts(rows, pieces)
    arrived = []
    for a, b in zip(cuts, cuts[1:]):
        (far,) = yield [(sent[a:b], "seq", SWAP)]
        arrived.append(far)
    return own[:rows].astype(F32) + got[:rows].astype(F32) + jnp.concatenate(arrived, axis=0).astype(F32)


def far_steps(own, other, pieces):
    (got,) = yield [(other, "core", SWAP)]
    sent = (own.astype(F32) + got.astype(F32)).astype(BF16)
    cuts = piece_cuts(sent.shape[0], pieces)
    arrived = []
    for a, b in zip(cuts, cuts[1:]):
        (got,) = yield [(sent[a:b], "seq", SWAP)]
        arrived.append(got)
    return arrived


def small_sum_steps(parts, core, side):
    count = lax.axis_size("zy")
    lengths = [p.shape[0] for p in parts]
    packed = jnp.concatenate(parts)
    packed = jnp.pad(packed, (0, -packed.shape[0] % 1024)).reshape(-1, LANES)
    bit = 1
    while bit < count:
        (got,) = yield [(packed, "zy", [(i, i ^ bit) for i in range(count)])]
        packed = packed + got
        bit *= 2
    (got,) = yield [(packed, "core", SWAP)]
    packed = in_order(packed, got, core)
    (got,) = yield [(packed, "seq", SWAP)]
    packed = jnp.swapaxes(in_order(packed, got, side), 0, 1).reshape(2, 2, -1)
    return jnp.split(packed, np.cumsum(lengths), axis=2)[: len(lengths)]


def zy_exchange(value, bit):
    count = lax.axis_size("zy")
    return lax.ppermute(value, "zy", [(i, i ^ bit) for i in range(count)])


def zy_sum(value):
    count = lax.axis_size("zy")
    bit = 1
    while bit < count:
        value = value + zy_exchange(value, bit)
        bit *= 2
    return value


def head_split(count):
    rows = DI // count
    if rows % (2 * HD) == 0 and count % 2 == 0:
        return count // 2, rows // (2 * HD)
    return 1, MYH


def split_heads(value, dim, split):
    q, i = split
    size = value.shape[dim]
    unit = size // NH
    shape = value.shape
    value = value.reshape(shape[:dim] + (2, q, 2, i * unit) + shape[dim + 1 :])
    value = jnp.swapaxes(value, dim + 1, dim + 2)
    return value.reshape(shape[:dim] + (2, 2, size // PARTS) + shape[dim + 1 :])


def join_heads(value, dim, split):
    q, i = split
    shape = value.shape
    mine = shape[dim + 2]
    value = value.reshape(shape[:dim] + (2, 2, q, mine // q) + shape[dim + 3 :])
    value = jnp.swapaxes(value, dim + 1, dim + 2)
    return value.reshape(shape[:dim] + (PARTS * mine,) + shape[dim + 3 :])


HALF = LANES // 2
EXTRA = 16
SEG_AT = 8


def half_places(split, core, side):
    q, i = split
    return [((core * q + at) * 2 + side) * i + k for at in range(q) for k in range(i)]


def halves(tile_of, places):
    tiles = []
    for at in range(0, len(places), 2):
        one, two = places[at], places[at + 1]
        if one % 2 == 0 and two == one + 1:
            tiles.append(tile_of(one // 2))
            continue
        left, right = tile_of(one // 2), tile_of(two // 2)
        left = pltpu.roll(left, HALF, 1) if one % 2 else left
        right = right if two % 2 else pltpu.roll(right, HALF, 1)
        lane = lax.broadcasted_iota(jnp.int32, left.shape, 1)
        tiles.append(jnp.where(lane < HALF, left, right))
    return tiles


def head_choice(split):
    choice = np.zeros((PARTS, LANES, LANES), np.float32)
    for g in range(PARTS):
        for lane, head in enumerate(half_places(split, g // 2, g % 2)):
            choice[g, head, lane] = 1.0
    return choice


def split_kernel(split, at_ref, w_ref, gain_ref, taps_ref, bias_ref, gated_ref, seg_ref, choice_ref, *refs):
    *outs, out_ref, small_ref, turn_ref = refs
    me = at_ref[0]
    small_ref[...] = jnp.zeros_like(small_ref)
    for row, ref in ((0, gain_ref), (1, bias_ref), (6, gated_ref)):
        small_ref[row : row + 1, : ref.shape[1]] = ref[...].astype(F32)
    turn_ref[...] = jnp.zeros_like(turn_ref)
    turn_ref[: taps_ref.shape[0], :KW] = taps_ref[...].astype(F32)
    small_ref[2 : 2 + KW, :] = turn_ref[...].T[:KW, :]
    small_ref[SEG_AT : SEG_AT + seg_ref.shape[0], :] = seg_ref[...].astype(F32)

    def tile_of(base):
        return lambda t: w_ref[:, base + t * LANES : base + (t + 1) * LANES].astype(F32)

    bc = w_ref[:, 2 * DI : 2 * DI + BC]
    steps = w_ref[:, DI + CONV :]
    for g in range(PARTS):
        places = half_places(split, g // 2, g % 2)
        at = me ^ g
        tiles = halves(tile_of(DI), places)
        for k, tile in enumerate(tiles):
            out_ref[at, :, k * LANES : (k + 1) * LANES] = tile.astype(BF16)
        out_ref[at, :, MYC : MYC + BC] = bc
        out_ref[at, :, MYC + BC : W1] = nn(steps, choice_ref[g, :NH, :]).astype(BF16)
        for k, tile in enumerate(halves(tile_of(0), places)):
            out_ref[at, :, W1 + k * LANES : W1 + (k + 1) * LANES] = tile.astype(BF16)
    for r, ref in enumerate(outs):
        ref[:EXTRA, :LANES] = small_ref[...].astype(BF16)
        ref[:EXTRA, LANES:] = jnp.zeros((EXTRA, W1 + MYC - LANES), BF16)
        ref[EXTRA:, :] = out_ref[r]


def smem(shape=None):
    return pl.BlockSpec(memory_space=pltpu.SMEM)


def split_columns(weight, gain, taps, bias, gated, segs, split, me):
    return pl.pallas_call(
        functools.partial(split_kernel, split),
        out_shape=[jax.ShapeDtypeStruct((EXTRA + weight.shape[0], W1 + MYC), BF16)] * PARTS,
        in_specs=[smem()] + [pl.BlockSpec()] * 7,
        scratch_shapes=[
            pltpu.VMEM((PARTS, weight.shape[0], W1 + MYC), BF16),
            pltpu.VMEM((EXTRA, LANES), F32),
            pltpu.VMEM((LANES, LANES), F32),
        ],
        compiler_params=pltpu.CompilerParams(vmem_limit_bytes=12 * MIB),
        name="split_columns",
    )(me, weight, gain[None], taps, bias[None], gated[None], segs, jnp.asarray(head_choice(split), BF16))


def assemble_kernel(at_ref, one, two, three, four, first_ref, gate_ref):
    me = at_ref[0]
    rows = one.shape[0] - EXTRA
    first_ref[:EXTRA, :] = jnp.zeros((EXTRA, W1), BF16)
    for r, ref in enumerate((one, two, three, four)):
        at = me ^ r
        first_ref[pl.ds(pl.multiple_of(EXTRA + at * rows, 16), rows), :] = ref[EXTRA:, :W1]
        gate_ref[pl.ds(pl.multiple_of(at * rows, 16), rows), :] = ref[EXTRA:, W1:]
        for g in range(PARTS):

            @pl.when(at == g)
            def _():
                first_ref[:EXTRA, g * LANES : (g + 1) * LANES] = ref[:EXTRA, :LANES]


def assemble_plain(at_ref, one, two, three, four, extra_ref, first_ref, gate_ref):
    me = at_ref[0]
    extra_ref[...] = jnp.zeros_like(extra_ref)
    for r, ref in enumerate((one, two, three, four)):
        at = me ^ r
        first_ref[at] = ref[EXTRA:, :W1]
        gate_ref[at] = ref[EXTRA:, W1:]
        for g in range(PARTS):

            @pl.when(at == g)
            def _():
                extra_ref[:, g * LANES : (g + 1) * LANES] = ref[:EXTRA, :LANES]


def assemble_rows(blocks, me):
    rows = blocks[0].shape[0] - EXTRA
    if rows % 16 == 0:
        return pl.pallas_call(
            assemble_kernel,
            out_shape=[
                jax.ShapeDtypeStruct((EXTRA + PARTS * rows, W1), BF16),
                jax.ShapeDtypeStruct((PARTS * rows, MYC), BF16),
            ],
            in_specs=[smem()] + [pl.BlockSpec()] * PARTS,
            name="assemble_rows",
        )(me, *blocks)
    extra, first, gate = pl.pallas_call(
        assemble_plain,
        out_shape=[
            jax.ShapeDtypeStruct((EXTRA, W1), BF16),
            jax.ShapeDtypeStruct((PARTS, rows, W1), BF16),
            jax.ShapeDtypeStruct((PARTS, rows, MYC), BF16),
        ],
        in_specs=[smem()] + [pl.BlockSpec()] * PARTS,
        name="assemble_rows",
    )(me, *blocks)
    first = jnp.concatenate([extra, first.reshape(PARTS * rows, W1)], axis=0)
    return first, gate.reshape(PARTS * rows, MYC)


def hand_back_kernel(at_ref, *refs):
    ins, outs, out_ref = refs[: -PARTS - 1], refs[-PARTS - 1 : -1], refs[-1]
    me = at_ref[0]
    for g in range(PARTS):
        at = 0
        for ref in ins:
            out_ref[me ^ g, :, at : at + ref.shape[2]] = ref[g].astype(BF16)
            at += ref.shape[2]
    for r, ref in enumerate(outs):
        ref[...] = out_ref[r]


def hand_back(blocks, me):
    blocks = [b.reshape(PARTS, -1, b.shape[1]) for b in blocks]
    return pl.pallas_call(
        hand_back_kernel,
        out_shape=[jax.ShapeDtypeStruct((blocks[0].shape[1], W1 + MYC), BF16)] * PARTS,
        in_specs=[smem()] + [pl.BlockSpec()] * len(blocks),
        scratch_shapes=[pltpu.VMEM((PARTS, blocks[0].shape[1], W1 + MYC), BF16)],
        name="hand_back",
    )(me, *blocks)


def join_kernel(split, at_ref, one, two, three, four, choice_ref, w_ref, gain_ref, out_ref, grad_ref, by):
    me = at_ref[0]
    for r, ref in enumerate((one, two, three, four)):
        by[me ^ r] = ref[...].astype(F32)
    where = {}
    for g in range(PARTS):
        for at, place in enumerate(half_places(split, g // 2, g % 2)):
            where[place] = (g, at)

    def put(base, column):
        for t in range(DI // LANES):
            tiles = []
            for k in range(2):
                g, at = where[2 * t + k]
                start = column + at // 2 * LANES
                tile = by[g, :, start : start + LANES]
                tiles.append(tile if at % 2 == k else pltpu.roll(tile, HALF, 1))
            lane = lax.broadcasted_iota(jnp.int32, tiles[0].shape, 1)
            out_ref[:, base + t * LANES : base + (t + 1) * LANES] = jnp.where(lane < HALF, tiles[0], tiles[1])

    put(0, W1)
    put(DI, 0)
    out_ref[:, 2 * DI : 2 * DI + BC] = sum(by[g, :, MYC : MYC + BC] for g in range(PARTS))
    out_ref[:, DI + CONV :] = sum(
        nt(by[g, :, MYC + BC : W1].astype(BF16), choice_ref[g, :NH, :]) for g in range(PARTS)
    )
    met = jnp.sum(out_ref[...] * w_ref[...].astype(F32), axis=1, keepdims=True)
    grad_ref[...] = jnp.broadcast_to(met / gain_ref[:, 0:1].astype(F32), grad_ref.shape)


def join_columns(blocks, split, me, weight, gain):
    rows = blocks[0].shape[0]
    return pl.pallas_call(
        functools.partial(join_kernel, split),
        out_shape=[
            jax.ShapeDtypeStruct((rows, 2 * DI + BC + NH), F32),
            jax.ShapeDtypeStruct((rows, LANES), F32),
        ],
        in_specs=[smem()] + [pl.BlockSpec()] * (PARTS + 3),
        scratch_shapes=[pltpu.VMEM((PARTS, rows, W1 + MYC), F32)],
        name="join_columns",
    )(me, *blocks, jnp.asarray(head_choice(split), BF16), weight, gain)


DIAGONAL = [(0, 0), (1, 2), (2, 1), (3, 3)]


def sigmoid(value):
    return 0.5 * jnp.tanh(0.5 * value) + 0.5


def nt(a, b):
    return lax.dot_general(a, b, (((1,), (1,)), ((), ())), preferred_element_type=F32)


def nn(a, b):
    return lax.dot_general(a, b, (((1,), (0,)), ((), ())), preferred_element_type=F32)


def tn(a, b):
    return lax.dot_general(a, b, (((0,), (0,)), ((), ())), preferred_element_type=F32)


def exact(a, b):
    return lax.dot_general(
        a, b, (((1,), (0,)), ((), ())), preferred_element_type=F32, precision=HIGH
    )


def in_two(value, axis):
    top = value.astype(BF16)
    return jnp.concatenate([top, (value - top.astype(F32)).astype(BF16)], axis=axis)


def in_three(value, axis):
    top = value.astype(BF16)
    rest = value - top.astype(F32)
    mid = rest.astype(BF16)
    return jnp.concatenate([top, mid, (rest - mid.astype(F32)).astype(BF16)], axis=axis)


def over_heads(value, heads_ref):
    return nn(in_two(value, 1), heads_ref[...])


def sum_heads(value, heads_ref):
    return nt(value.astype(BF16), heads_ref[:LANES, :])


ROWS = LEN // 2


def row_copies(sources, held, sems):
    half = len(sources) // 2
    copies, at = [], 0
    for q, refs in enumerate((sources[:1], sources[2 : 1 + half], sources[1:2], sources[1 + half :])):
        copies.append([])
        row = 0
        for ref in refs:
            size = ref.shape[0]
            copies[q].append(pltpu.make_async_copy(ref, held.at[q, row : row + size, :], sems.at[at]))
            row += size
            at += 1
    return copies


def wait_rows(step, copies):
    for q, some in enumerate(copies):

        @pl.when(step == q)
        def _():
            for copy in some:
                copy.wait()


def piece_copies(at_ref, refs, full_ref, count, sems, extra=0, small_ref=None):
    block = refs[0].shape[0]
    rows = block - extra
    copies = []
    width = full_ref.shape[1]
    for i, (ref, (step, row)) in enumerate(zip(refs, piece_places(count, block))):
        zy = ring_order_of(at_ref[0] + step + count, count)
        skip = extra if row == 0 else 0
        start = zy * rows + row + skip - extra
        size = ref.shape[0] - skip
        to = full_ref.at[pl.ds(pl.multiple_of(start, 16), size), :]
        copies.append(pltpu.make_async_copy(ref.at[skip : skip + size, :width], to, sems.at[2 * i]))
        if skip:
            to = small_ref.at[pl.ds(pl.multiple_of(zy * extra, 16), extra), :]
            copies.append(pltpu.make_async_copy(ref.at[:skip, : PARTS * LANES], to, sems.at[2 * i + 1]))
    return copies


def anywhere(values):
    return [pl.BlockSpec(memory_space=pltpu.HBM) for _ in values]


def project_kernel(count, parts, split, sizes, at_ref, *refs):
    sources, refs = refs[:parts], refs[parts:]
    per_head_ref, choice_ref, wide_ref, *refs = refs
    pieces, refs = refs[: count + 1], refs[count + 1 :]
    (first_ref, turned_ref, w_ref, x_ref, bc_ref, head_ref, gain_ref,
     held, small_ref, params_ref, row_sems, piece_sems) = refs
    step = pl.program_id(0)
    rows = row_copies(sources, held, row_sems)

    @pl.when(step == 0)
    def _():
        copies = piece_copies(at_ref, pieces, w_ref, count, piece_sems, EXTRA, small_ref)
        for copy in copies + sum(rows, []):
            copy.start()
        for copy in copies:
            copy.wait()
        unpack_small(at_ref, split, sizes, small_ref, per_head_ref, choice_ref, wide_ref, gain_ref, x_ref, bc_ref, head_ref, params_ref)

    wait_rows(step, rows)
    x = held[step].astype(F32)
    inv = lax.rsqrt(jnp.mean(x * x, axis=-1, keepdims=True) + EPS)
    low = (x * inv * gain_ref[0:1, :]).astype(BF16)
    turned_ref[...] = low.T
    first_ref[...] = nn(low, w_ref[...]).astype(BF16)


def project(place, split, sizes, own, near, far, both, per_head, heads, pieces):
    rows = own.shape[0]
    total = PARTS * rows
    count = lax.axis_size("zy")
    still = lambda t, *_: (0, 0)
    choice = jnp.asarray(head_choice(split), BF16)
    return pl.pallas_call(
        functools.partial(project_kernel, count, 2 + len(far) + len(both), split, sizes),
        grid_spec=pltpu.PrefetchScalarGridSpec(
            num_scalar_prefetch=1,
            grid=(total // ROWS,),
            in_specs=anywhere((own, near, *far, *both))
            + [
                pl.BlockSpec((8, LANES), still),
                pl.BlockSpec(choice.shape, lambda t, *_: (0, 0, 0)),
                pl.BlockSpec((2 * LANES, MYC), still),
            ]
            + anywhere(pieces),
            out_specs=[
                pl.BlockSpec((ROWS, W1), lambda t, *_: (t, 0)),
                pl.BlockSpec((D, ROWS), lambda t, *_: (0, t)),
                pl.BlockSpec((D, W1), still),
                pl.BlockSpec((8, MYC), still),
                pl.BlockSpec((8, BC), still),
                pl.BlockSpec((8, LANES), still),
                pl.BlockSpec((8, D), still),
            ],
            scratch_shapes=[
                pltpu.VMEM((PARTS, rows, D), BF16),
                pltpu.VMEM((count * EXTRA, PARTS * LANES), BF16),
                pltpu.VMEM((8, DI), F32),
                pltpu.SemaphoreType.DMA((2 + len(far) + len(both),)),
                pltpu.SemaphoreType.DMA((2 * len(pieces),)),
            ],
        ),
        out_shape=[
            jax.ShapeDtypeStruct((total, W1), BF16),
            jax.ShapeDtypeStruct((D, total), BF16),
            jax.ShapeDtypeStruct((D, W1), BF16),
            jax.ShapeDtypeStruct((8, MYC), F32),
            jax.ShapeDtypeStruct((8, BC), F32),
            jax.ShapeDtypeStruct((8, LANES), F32),
            jax.ShapeDtypeStruct((8, D), F32),
        ],
        compiler_params=pltpu.CompilerParams(vmem_limit_bytes=56 * MIB),
        cost_estimate=pl.CostEstimate(flops=12 * 10**9, bytes_accessed=30 * 10**6, transcendentals=10**4),
        name="project",
    )(place, own, near, *far, *both, per_head, choice, heads, *pieces)


def silu_of(z):
    sig = sigmoid(z)
    return sig, z * sig


def meet_kernel(count, parts, blocked, at_ref, *refs):
    sources, refs = refs[:parts], refs[parts:]
    turned_ref, y_ref, taps_ref, *refs = refs
    blocks, refs = refs[: 1 + blocked], refs[1 + blocked :]
    *pieces, z_ref, d_two_ref, sums_ref, w_ref, w_out_ref, held, row_sems, piece_sems, out_sems = refs
    step = pl.program_id(0)
    half = D // 2
    rows = row_copies(sources, held, row_sems)

    @pl.when(step == 0)
    def _():
        copies = piece_copies(at_ref, pieces, w_ref, count, piece_sems)
        if blocked:
            each, size, _ = blocks[0].shape
            size = size // 2
            for q in range(each):
                for i, (ref, part) in enumerate(zip(blocks, (at_ref[1], 1 - at_ref[1]))):
                    to = pl.ds(pl.multiple_of((2 * q + part) * size, 16), size)
                    for k in range(2):
                        copies.append(
                            pltpu.make_async_copy(
                                ref.at[q, k * size : (k + 1) * size, :],
                                w_out_ref.at[to, k * half : (k + 1) * half],
                                out_sems.at[4 * q + 2 * i + k],
                            )
                        )
        else:
            copies.append(pltpu.make_async_copy(blocks[0], w_out_ref, out_sems.at[0]))
        for copy in copies + sum(rows, []):
            copy.start()
        for copy in copies:
            copy.wait()

    wait_rows(step, rows)
    z = tn(turned_ref[...], w_ref[...]).astype(BF16)
    z_ref[...] = z
    _, silu = silu_of(z.astype(F32))
    joined = y_ref[...].astype(F32) * silu
    d_two = nt(held[step], w_out_ref[...])
    d_two_ref[...] = d_two.astype(BF16)
    row = lax.broadcasted_iota(jnp.int32, (8, MYC), 0)
    squares = nt((row == 0).astype(BF16), (joined * joined).astype(BF16))
    products = nt((row == 1).astype(BF16), (joined * taps_ref[6:7, :] * d_two).astype(BF16))
    sums_ref[...] = squares + products


def meet(place, own, near, far, both, turned, y, x_taps, blocks, pieces):
    rows = own.shape[0]
    total = PARTS * rows
    count = lax.axis_size("zy")
    still = lambda t, *_: (0, 0)
    here = lambda t, *_: (t, 0)
    blocked = len(blocks) > 1
    return pl.pallas_call(
        functools.partial(meet_kernel, count, 2 + len(far) + len(both), blocked),
        grid_spec=pltpu.PrefetchScalarGridSpec(
            num_scalar_prefetch=1,
            grid=(total // ROWS,),
            in_specs=anywhere((own, near, *far, *both))
            + [
                pl.BlockSpec((D, ROWS), lambda t, *_: (0, t)),
                pl.BlockSpec((ROWS, MYC), here),
                pl.BlockSpec((8, MYC), still),
            ]
            + anywhere((*blocks, *pieces)),
            out_specs=[
                pl.BlockSpec((ROWS, MYC), here),
                pl.BlockSpec((ROWS, MYC), here),
                pl.BlockSpec((8, ROWS), lambda t, *_: (0, t)),
                pl.BlockSpec((D, MYC), still),
                pl.BlockSpec((MYC, D), still),
            ],
            scratch_shapes=[
                pltpu.VMEM((PARTS, rows, D), BF16),
                pltpu.SemaphoreType.DMA((2 + len(far) + len(both),)),
                pltpu.SemaphoreType.DMA((2 * len(pieces),)),
                pltpu.SemaphoreType.DMA((4 * blocks[0].shape[0] if blocked else 1,)),
            ],
        ),
        out_shape=[
            jax.ShapeDtypeStruct((total, MYC), BF16),
            jax.ShapeDtypeStruct((total, MYC), BF16),
            jax.ShapeDtypeStruct((8, total), F32),
            jax.ShapeDtypeStruct((D, MYC), BF16),
            jax.ShapeDtypeStruct((MYC, D), BF16),
        ],
        compiler_params=pltpu.CompilerParams(vmem_limit_bytes=56 * MIB),
        cost_estimate=pl.CostEstimate(flops=15 * 10**9, bytes_accessed=40 * 10**6, transcendentals=10**6),
        name="meet",
    )(place, own, near, *far, *both, turned, y, x_taps, *blocks, *pieces)


def out_kernel(parts, *refs):
    sources, refs = refs[:parts], refs[parts:]
    theirs_ref, mine_ref, d_theirs_ref, d_mine_ref, held, sems = refs
    step = pl.program_id(0)
    rows = row_copies(sources, held, sems)

    @pl.when(step == 0)
    def _():
        for copy in sum(rows, []):
            copy.start()
        for copy in sum(rows, []):
            copy.wait()

    for at, a_ref, out_ref in ((0, theirs_ref, d_theirs_ref), (2, mine_ref, d_mine_ref)):

        @pl.when((step >= at) & (step < at + 2))
        def _():
            every = held[...].reshape(PARTS * ROWS, D)
            out_ref[...] = nn(a_ref[...], every).astype(BF16)


def out_product(theirs, mine, own, near, far, both):
    rows, total = theirs.shape
    tile = rows // 2
    one = lambda t: (jnp.minimum(t, 1), 0)
    two = lambda t: (jnp.maximum(t - 2, 0), 0)
    return pl.pallas_call(
        functools.partial(out_kernel, 2 + len(far) + len(both)),
        grid=(4,),
        in_specs=anywhere((own, near, *far, *both))
        + [pl.BlockSpec((tile, total), one), pl.BlockSpec((tile, total), two)],
        out_specs=[pl.BlockSpec((tile, D), one), pl.BlockSpec((tile, D), two)],
        out_shape=[jax.ShapeDtypeStruct((rows, D), BF16)] * 2,
        scratch_shapes=[
            pltpu.VMEM((PARTS, ROWS, D), BF16),
            pltpu.SemaphoreType.DMA((2 + len(far) + len(both),)),
        ],
        compiler_params=pltpu.CompilerParams(vmem_limit_bytes=26 * MIB),
        cost_estimate=pl.CostEstimate(flops=8 * 10**9, bytes_accessed=20 * 10**6, transcendentals=0),
        name="out_product",
    )(own, near, *far, *both, theirs, mine)


def gate_kernel(
    unit, core_ref, sums_0, sums_1, sums_2, sums_3, y_ref, z_ref, d_two_ref, taps_ref, w_out_ref,
    d_ssm_ref, d_gate_ref, mine_ref, theirs_ref, own_ref, other_ref, turned,
):
    step = pl.program_id(0)
    sums = (sums_0[...] + sums_1[...] + sums_2[...] + sums_3[...]).T
    inv = lax.rsqrt(sums[:, 0:1] * (1.0 / DI) + EPS)
    shift = inv * inv * inv * (sums[:, 1:2] * (1.0 / DI))
    z = z_ref[...].astype(F32)
    sig, silu = silu_of(z)
    y = y_ref[...].astype(F32)
    joined = y * silu
    d_two = d_two_ref[...].astype(F32)
    two = (joined * inv * taps_ref[6:7, :]).astype(BF16)
    d_joined = inv * (taps_ref[6:7, :] * d_two) - joined * shift
    d_ssm_ref[...] = (d_joined * silu).astype(BF16)
    d_gate_ref[...] = (d_joined * y * (sig * (1.0 + z * (1.0 - sig)))).astype(BF16)
    branch = nn(two, w_out_ref[...]).astype(BF16)

    @pl.when(step < 2)
    def _():
        own_ref[...] = branch

    @pl.when(step >= 2)
    def _():
        other_ref[...] = branch

    turned[...] = two.T
    core = core_ref[0]
    for at in range(MYC // (2 * unit)):
        to = slice(at * unit, (at + 1) * unit)
        mine_ref[to, :] = turned[pl.ds(pl.multiple_of((2 * at + core) * unit, 16), unit), :]
        theirs_ref[to, :] = turned[pl.ds(pl.multiple_of((2 * at + 1 - core) * unit, 16), unit), :]


def gate_back(core, unit, sums, y, z, d_two, x_taps, w_out):
    total = y.shape[0]
    still = lambda t, *_: (0, 0)
    here = lambda t, *_: (t, 0)
    across = lambda t, *_: (0, t)
    return pl.pallas_call(
        functools.partial(gate_kernel, unit),
        grid_spec=pltpu.PrefetchScalarGridSpec(
            num_scalar_prefetch=1,
            grid=(total // ROWS,),
            in_specs=[pl.BlockSpec((8, ROWS), lambda t, *_, r=r: (0, t ^ r)) for r in range(PARTS)]
            + [
                pl.BlockSpec((ROWS, MYC), here),
                pl.BlockSpec((ROWS, MYC), here),
                pl.BlockSpec((ROWS, MYC), here),
                pl.BlockSpec((8, MYC), still),
                pl.BlockSpec((MYC, D), still),
            ],
            out_specs=[
                pl.BlockSpec((ROWS, MYC), here),
                pl.BlockSpec((ROWS, MYC), here),
                pl.BlockSpec((MYC // 2, ROWS), across),
                pl.BlockSpec((MYC // 2, ROWS), across),
                pl.BlockSpec((ROWS, D), lambda t, *_: (jnp.minimum(t, 1), 0)),
                pl.BlockSpec((ROWS, D), lambda t, *_: (jnp.maximum(t - 2, 0), 0)),
            ],
            scratch_shapes=[pltpu.VMEM((MYC, ROWS), BF16)],
        ),
        out_shape=[
            jax.ShapeDtypeStruct((total, MYC), BF16),
            jax.ShapeDtypeStruct((total, MYC), BF16),
            jax.ShapeDtypeStruct((MYC // 2, total), BF16),
            jax.ShapeDtypeStruct((MYC // 2, total), BF16),
            jax.ShapeDtypeStruct((total // 2, D), BF16),
            jax.ShapeDtypeStruct((total // 2, D), BF16),
        ],
        compiler_params=pltpu.CompilerParams(vmem_limit_bytes=42 * MIB),
        cost_estimate=pl.CostEstimate(flops=8 * 10**9, bytes_accessed=30 * 10**6, transcendentals=10**6),
        name="gate_back",
    )(core, *sums, y, z, d_two, x_taps, w_out)


def normed_kernel(x0_ref, x1_ref, bc_ref, dt_ref, gate_ref, w_first_ref, w_gate_ref, own_ref, other_ref):
    d_first = jnp.concatenate([x0_ref[...], x1_ref[...], bc_ref[...], dt_ref[...]], axis=1)
    value = (nt(d_first, w_first_ref[...]) + nt(gate_ref[...], w_gate_ref[...])).astype(BF16)

    @pl.when(pl.program_id(0) == 0)
    def _():
        own_ref[...] = value

    @pl.when(pl.program_id(0) == 1)
    def _():
        other_ref[...] = value


def normed_part(at, d_x0, d_x1, d_bc, d_dt, d_gate, w_first, w_gate):
    here = lambda t: (2 * t + at, 0)
    still = lambda t: (0, 0)
    rows = [d_x0, d_x1, d_bc, d_dt, d_gate]
    return pl.pallas_call(
        normed_kernel,
        grid=(2,),
        in_specs=[pl.BlockSpec((ROWS, v.shape[1]), here) for v in rows]
        + [pl.BlockSpec((D, W1), still), pl.BlockSpec((D, MYC), still)],
        out_specs=[pl.BlockSpec((ROWS, D), still)] * 2,
        out_shape=[jax.ShapeDtypeStruct((ROWS, D), BF16)] * 2,
        compiler_params=pltpu.CompilerParams(vmem_limit_bytes=36 * MIB),
        cost_estimate=pl.CostEstimate(flops=8 * 10**9, bytes_accessed=20 * 10**6, transcendentals=0),
        name="normed_part_%d" % at,
    )(*rows, w_first, w_gate)


def flat(small, row, count, spread, size):
    every = small[:, row, :]
    rows = jnp.concatenate([every[:, g * LANES : (g + 1) * LANES] for g in range(PARTS)], axis=0)
    value = nn(rows.astype(BF16), spread)
    at = lax.broadcasted_iota(jnp.int32, value.shape, 0)
    device = (at % count) * PARTS + at // count
    lane = lax.broadcasted_iota(jnp.int32, value.shape, 1)
    own = (lane >= device * size) & (lane < (device + 1) * size)
    return jnp.sum(jnp.where(own, value, 0.0), axis=0, keepdims=True)


def spread_of(size, count):
    shape = (LANES, count * PARTS * size)
    lane = lax.broadcasted_iota(jnp.int32, shape, 1).astype(F32)
    part = lane - jnp.floor((lane + 0.5) * (1.0 / size)) * size
    return (part == lax.broadcasted_iota(jnp.int32, shape, 0).astype(F32)).astype(BF16)


def unpack_small(at_ref, split, sizes, small_ref, per_head_ref, choice_ref, wide_ref, gain_ref, x_ref, bc_ref, head_ref, held):
    group = at_ref[2]
    count = small_ref.shape[0] // EXTRA
    small = small_ref[...].astype(F32).reshape(count, EXTRA, PARTS * LANES)
    gain_ref[...] = jnp.broadcast_to(flat(small, 0, count, spread_of(sizes[0], count), sizes[0]), gain_ref.shape)
    spread = spread_of(sizes[1], count)
    conv = [flat(small, r, count, spread, sizes[1]) for r in (2, 3, 4, 5, 1)]
    for k, v in enumerate(conv):
        held[k : k + 1, :] = v[:, :DI]
        bc_ref[k : k + 1, :] = v[:, DI:]
    bc_ref[5:8, :] = jnp.zeros((3, BC), F32)
    held[6:7, :] = flat(small, 6, count, spread_of(sizes[2], count), sizes[2])
    held[5:6, :] = jnp.zeros((1, DI), F32)
    held[7:8, :] = jnp.zeros((1, DI), F32)
    per_head = in_three(per_head_ref[...], 1)
    mine = jnp.zeros((8, LANES), F32)
    for g in range(PARTS):
        chosen = nn(per_head, jnp.concatenate([choice_ref[g]] * 3, axis=0))
        mine = jnp.where(group == g, chosen, mine)

        @pl.when(group == g)
        def _():
            tiles = halves(lambda t: held[:, t * LANES : (t + 1) * LANES], half_places(split, g // 2, g % 2))
            for k, tile in enumerate(tiles):
                x_ref[:, k * LANES : (k + 1) * LANES] = tile

    head_ref[...] = mine
    wide = jnp.concatenate([wide_ref[:LANES, :]] * 3, axis=0)
    x_ref[5:6, :] = nn(in_three(mine, 1), wide)[2:3, :]


def marks_kernel(side_ref, *refs):
    *parts, marks_ref, rows_ref, seg, taken = refs
    side = side_ref[0]
    blocks = LEN // Q
    for s in range(2):
        for j in range(blocks):
            half, row = j // (blocks // 2), j % (blocks // 2)
            near, far = parts[2 * s + half], parts[2 * s + 1 - half]
            at = slice(SEG_AT + row, SEG_AT + row + 1)
            to = s * blocks + j
            seg[to : to + 1, :] = jnp.where(side == 0, near[at, :LANES].astype(F32), far[at, :LANES].astype(F32))
    value = seg[...]
    count = 2 * blocks
    lane = lax.broadcasted_iota(jnp.int32, value.shape, 1)
    row = lax.broadcasted_iota(jnp.int32, value.shape, 0) % blocks
    last = jnp.broadcast_to(value[:, Q - 1 : Q], value.shape)
    taken[...] = jnp.zeros_like(taken)
    taken[0] = value
    for k in range(KW - 1):
        by = KW - 1 - k
        turned = pltpu.roll(value, by, 1)
        early = lane < by
        behind = jnp.where(early, pltpu.roll(turned, 1, 0), turned)
        taken[1 + k] = ((behind == value) & ~(early & (row == 0))).astype(F32)
        turned = pltpu.roll(value, Q - by, 1)
        late = lane >= Q - by
        beyond = jnp.where(late, pltpu.roll(turned, count - 1, 0), turned)
        taken[4 + k] = ((beyond == value) & ~(late & (row == blocks - 1))).astype(F32)
    taken[7] = ((pltpu.roll(last, 1, 0) == value) & (row > 0)).astype(F32)
    taken[8] = (last == value).astype(F32)
    for r in range(count):
        rows_ref[r] = value[r : r + 1, :]
        marks_ref[r] = jnp.concatenate([taken[i, r : r + 1, :] for i in range(16)], axis=0).T


def segment_marks(side, *parts):
    count = 2 * (LEN // Q)
    specs = [pl.BlockSpec((EXTRA, LANES), lambda t: (0, 0))] * PARTS
    marks, rows = pl.pallas_call(
        marks_kernel,
        grid=(1,),
        out_shape=[
            jax.ShapeDtypeStruct((count, Q, 16), F32),
            jax.ShapeDtypeStruct((count, 1, Q), F32),
        ],
        in_specs=[smem()] + specs,
        scratch_shapes=[pltpu.VMEM((count, Q), F32), pltpu.VMEM((16, count, Q), F32)],
        compiler_params=pltpu.CompilerParams(vmem_limit_bytes=8 * MIB),
        name="segment_marks",
    )(side, *parts)
    return marks.reshape(2, LEN, 16), rows.reshape(2, LEN // Q, 1, Q)


def weight_kernel(a_ref, *refs):
    *bs, out_ref = refs
    at = 0
    for b in bs:
        out_ref[:, at : at + b.shape[1]] = nn(a_ref[...], b[...]).astype(BF16)
        at += b.shape[1]


def weight_product(a, *bs, tile=512):
    rows, total = a.shape
    tile = min(tile, rows)
    columns = sum(b.shape[1] for b in bs)
    still = lambda t: (0, 0)
    return pl.pallas_call(
        weight_kernel,
        grid=(rows // tile,),
        in_specs=[pl.BlockSpec((tile, total), lambda t: (t, 0))] + [pl.BlockSpec(b.shape, still) for b in bs],
        out_specs=pl.BlockSpec((tile, columns), lambda t: (t, 0)),
        out_shape=jax.ShapeDtypeStruct((rows, columns), BF16),
        compiler_params=pltpu.CompilerParams(vmem_limit_bytes=56 * MIB),
        cost_estimate=pl.CostEstimate(flops=8 * 10**9, bytes_accessed=20 * 10**6, transcendentals=0),
        name="weight_product",
    )(a, *bs)


def finish_kernel(x_ref, cot_ref, gain_ref, own_ref, got_ref, *refs):
    *far, out_ref, held = refs
    for i, ref in enumerate(far):

        @pl.when(pl.program_id(0) == i)
        def _():
            held[...] = ref[...]

    d_normed = own_ref[...].astype(F32) + got_ref[...].astype(F32) + held[...].astype(F32)
    x = x_ref[...].astype(F32)
    inv = lax.rsqrt(jnp.mean(x * x, axis=-1, keepdims=True) + EPS)
    scaled = gain_ref[0:1, :] * d_normed
    shift = inv * inv * inv * jnp.mean(x * scaled, axis=-1, keepdims=True)
    out_ref[...] = cot_ref[...].astype(F32) + inv * scaled - x * shift


def finish_tokens(x, cot, gain, own, got, *far):
    rows = x.shape[0]
    size = rows // len(far)
    here = pl.BlockSpec((size, D), lambda t: (t, 0))
    still = pl.BlockSpec((size, D), lambda t: (0, 0))
    return pl.pallas_call(
        finish_kernel,
        grid=(len(far),),
        in_specs=[here, here, pl.BlockSpec((8, D), lambda t: (0, 0)), here, here] + [still] * len(far),
        out_specs=here,
        out_shape=jax.ShapeDtypeStruct((rows, D), F32),
        scratch_shapes=[pltpu.VMEM((size, D), BF16)],
        compiler_params=pltpu.CompilerParams(vmem_limit_bytes=32 * MIB),
        cost_estimate=pl.CostEstimate(flops=10**7, bytes_accessed=12 * 10**6, transcendentals=0),
        name="finish_tokens",
    )(x, cot, gain, own, got, *far)


def softplus(value):
    return jnp.maximum(value, 0.0) + jnp.log1p(jnp.exp(-jnp.abs(value)))


def conv_total(ext, shifts, raw, halo, taps_ref, marks):
    ext[0:8, :] = halo[8:16, :].astype(F32)
    ext[8 : 8 + Q, :] = raw.astype(F32)
    total = taps_ref[4:5, :] + ext[8 : 8 + Q, :] * taps_ref[3:4, :]
    for k in range(KW - 1):
        shifted = ext[5 + k : 5 + k + Q, :] * marks[:, 1 + k : 2 + k]
        if shifts is not None:
            shifts[k] = shifted
        total = total + shifted * taps_ref[k : k + 1, :]
    return total


def conv_back(d_total, ext, shifts, ahead, taps_ref, marks, sums_ref):
    sums_ref[4:5, :] += jnp.sum(d_total, axis=0, keepdims=True)
    sums_ref[3:4, :] += jnp.sum(d_total * ext[8 : 8 + Q, :], axis=0, keepdims=True)
    for k in range(KW - 1):
        sums_ref[k : k + 1, :] += jnp.sum(d_total * shifts[k], axis=0, keepdims=True)
    ext[0:Q, :] = d_total
    ext[Q : Q + 8, :] = ahead[...]
    d_raw = d_total * taps_ref[3:4, :]
    for k in range(KW - 1):
        d_raw = d_raw + ext[3 - k : 3 - k + Q, :] * (taps_ref[k : k + 1, :] * marks[:, 4 + k : 5 + k])
    ahead[...] = d_total[0:8, :]
    return d_raw


def scan_forward(
    part, side_ref, x_ref, x_halo, bc_ref, bc_halo, dt_ref, marks_ref, row_ref, x_taps, bc_taps, head_ref, heads_ref,
    *rest,
):
    if part > 0:
        before, rest = rest[6], rest[7:]
    y_ref, state_ref, bc_out, step_out, cum_out, turned_out, helds, exts, bc_exts = rest
    chunk = pl.program_id(0)

    @pl.when(chunk == 0)
    def _():
        helds[...] = before[...] if part > 0 else jnp.zeros_like(helds)

    at_row = lax.broadcasted_iota(jnp.int32, (Q, Q), 0)
    at_col = lax.broadcasted_iota(jnp.int32, (Q, Q), 1)
    lane = lax.broadcasted_iota(jnp.int32, (Q, LANES), 1)
    lower = (at_row >= at_col).astype(BF16)
    lower = jnp.concatenate([lower] * 3, axis=1)
    rate = -jnp.exp(head_ref[1:2, :])
    for s in range(2):
        marks = marks_ref[s]
        held = helds.at[s]
        live = lane < MYH
        step = jnp.where(live, softplus(jnp.where(live, dt_ref[s].astype(F32), 0.0) + head_ref[0:1, :]), 0.0)
        cum = nn(lower, in_three(rate * step, 0))
        cum_t = cum.T
        step_out[s] = step
        cum_out[s] = cum
        turned_out[s, 0] = cum_t[:16, :]
        x_act = conv_total(exts.at[s], None, x_ref[s], x_halo[s], x_taps, marks)
        x_act = x_act * sigmoid(x_act)
        bc_act = conv_total(bc_exts.at[s], None, bc_ref[s], bc_halo[s], bc_taps, marks)
        bc_act = (bc_act * sigmoid(bc_act)).astype(BF16)
        bc_out[s] = bc_act
        b, c = bc_act[:, :NS], bc_act[:, NS:]
        shut = jnp.where((at_row >= at_col) & (marks[:, 0:1] == row_ref[s, 0]), 0.0, FAR)
        scores = nt(c, b)
        state = held[...]
        state_low = state.astype(BF16)
        state_ref[s, 0] = state_low
        last = cum[Q - 1 : Q, :]
        x_step = x_act * over_heads(step, heads_ref)
        keep = over_heads(jnp.exp(cum) * marks[:, 7:8], heads_ref)
        y = nn(c, state_low) * keep + x_act * x_taps[5:6, :]
        tail = over_heads(jnp.exp(last - cum) * marks[:, 8:9], heads_ref)
        carry = over_heads(jnp.broadcast_to(jnp.exp(last) * marks[Q - 1 : Q, 7:8], (8, LANES)), heads_ref)
        held[...] = state * carry[0:1, :] + nn(b.T, (x_step * tail).astype(BF16))
        for pair in range(MYH // 2):
            cols = slice(pair * LANES, (pair + 1) * LANES)
            mixing = []
            for head in (2 * pair, 2 * pair + 1):
                spread = cum[:, head : head + 1] - cum_t[head : head + 1, :] + shut
                mixing.append((jnp.exp(spread) * scores).astype(BF16))
            steps = x_step[:, cols]
            both = jnp.concatenate(
                [jnp.where(lane < HD, steps, 0.0), jnp.where(lane < HD, 0.0, steps)], axis=0
            ).astype(BF16)
            y_ref[s, :, cols] = (y[:, cols] + nn(jnp.concatenate(mixing, axis=1), both)).astype(BF16)


def scan_backward(
    group, part, side_ref, x_ref, x_halo, bc_ref, step_ref, cum_ref, turned_ref, dy_ref, state_ref, marks_ref, row_ref,
    x_taps, head_ref, heads_ref, *rest,
):
    final = group == GROUPS - 1
    if group > 0:
        dbc_before, *rest = rest
    if final:
        bc_raw_ref, bc_halo, bc_taps, *rest = rest
    carried = 6 if final else 4
    if part > 0:
        before, rest = rest[3 : 3 + carried], rest[3 + carried :]
    dx_ref, dbc_ref, ddt_ref, wide_ref, thin_ref, *rest = rest
    if final:
        bc_sums, *rest = rest
    helds, aheads, *rest = rest
    if final:
        bc_aheads, *rest = rest
    exts, shifts, *rest = rest
    if final:
        bc_exts, bc_shifts = rest
    chunk = pl.program_id(0)

    @pl.when(chunk == 0)
    def _():
        running = [wide_ref, thin_ref] + ([bc_sums] if final else []) + [helds, aheads]
        running += [bc_aheads] if final else []
        for i, ref in enumerate(running):
            ref[...] = before[i][...] if part > 0 else jnp.zeros_like(ref)

    at_row = lax.broadcasted_iota(jnp.int32, (Q, Q), 0)
    at_col = lax.broadcasted_iota(jnp.int32, (Q, Q), 1)
    lane = lax.broadcasted_iota(jnp.int32, (Q, LANES), 1)
    low_lanes, high_lanes = group * GH, LANES - (group + 1) * GH
    upper = (at_row <= at_col).astype(BF16)
    strict = (at_row > at_col).astype(BF16)
    spans = jnp.concatenate([upper, upper, strict, strict], axis=1)
    rate = -jnp.exp(head_ref[1:2, :])
    for s in range(2):
        marks = marks_ref[s]
        held = helds.at[s]
        total = conv_total(exts.at[s], shifts.at[s], x_ref[s], x_halo[s], x_taps, marks)
        gate = sigmoid(total)
        x_act = total * gate
        slope = gate * (1.0 + total * (1.0 - gate))
        b, c = bc_ref[s, :, :NS], bc_ref[s, :, NS:]
        step, cum, cum_t = step_ref[s], cum_ref[s], turned_ref[s, 0]
        shut = jnp.where((at_row <= at_col) & (marks[:, 0:1] == row_ref[s, 0]), 0.0, FAR)
        scores = nt(b, c)
        last = cum[Q - 1 : Q, :]
        dy = dy_ref[s].astype(F32)
        step_wide = over_heads(step, heads_ref)
        x_step = x_act * step_wide
        keep = over_heads(jnp.exp(cum) * marks[:, 7:8], heads_ref)
        tail = over_heads(jnp.exp(last - cum) * marks[:, 8:9], heads_ref)
        carry_thin = jnp.broadcast_to(jnp.exp(last) * marks[Q - 1 : Q, 7:8], (8, LANES))
        carry = over_heads(carry_thin, heads_ref)
        state = state_ref[s, 0]
        d_state = held[...]
        d_state_low = d_state.astype(BF16)
        dy_keep = dy * keep
        dy_keep_low = dy_keep.astype(BF16)
        from_state = nn(c, state)
        seen = sum_heads(dy_keep * from_state, heads_ref)
        d_c = nt(dy_keep_low, state)
        to_state = x_step * tail
        d_b = nt(to_state.astype(BF16), d_state_low)
        du_tail = nn(b, d_state_low) * tail
        sent = sum_heads(x_step * du_tail, heads_ref)
        linked = jnp.sum(d_state * state.astype(F32), axis=0, keepdims=True)
        linked = sum_heads(jnp.broadcast_to(linked, (8, GC)), heads_ref)[0:1, :] * carry_thin[0:1, :]
        held[...] = d_state * carry[0:1, :] + nn(c.T, dy_keep_low)
        d_scores = jnp.zeros((Q, Q), F32)
        by_later, by_earlier, du_parts = [], [], []
        for pair in range(GH // 2):
            cols = slice(pair * LANES, (pair + 1) * LANES)
            steps, dys = x_step[:, cols], dy[:, cols]
            step_both = jnp.concatenate(
                [jnp.where(lane < HD, steps, 0.0), jnp.where(lane < HD, 0.0, steps)], axis=0
            ).astype(BF16)
            dy_both = jnp.concatenate(
                [jnp.where(lane < HD, dys, 0.0), jnp.where(lane < HD, 0.0, dys)], axis=0
            ).astype(BF16)
            met = nt(step_both, dys.astype(BF16))
            mixing = []
            for place in range(2):
                head = low_lanes + 2 * pair + place
                decay = jnp.exp(cum_t[head : head + 1, :] - cum[:, head : head + 1] + shut)
                mixing.append((decay * scores).astype(BF16))
                weighed = decay * met[place * Q : (place + 1) * Q, :]
                d_scores = d_scores + weighed
                spent = weighed * scores
                by_later.append(jnp.sum(spent, axis=0, keepdims=True))
                by_earlier.append(jnp.sum(spent, axis=1, keepdims=True))
            du_parts.append(nn(jnp.concatenate(mixing, axis=1), dy_both))
        du = jnp.concatenate(du_parts, axis=1) + du_tail
        d_low = d_scores.astype(BF16)
        d_b = d_b + nn(d_low, c)
        d_c = d_c + nn(d_scores.T.astype(BF16), b)
        d_bc = jnp.concatenate([d_b, d_c], axis=1)
        if group > 0:
            d_bc = d_bc + dbc_before[s]
        if final:
            bc_total = conv_total(bc_exts.at[s], bc_shifts.at[s], bc_raw_ref[s], bc_halo[s], bc_taps, marks)
            bc_gate = sigmoid(bc_total)
            d_bc = d_bc * (bc_gate * (1.0 + bc_total * (1.0 - bc_gate)))
            d_bc = conv_back(d_bc, bc_exts.at[s], bc_shifts.at[s], bc_aheads.at[s], bc_taps, marks, bc_sums)
        dbc_ref[s] = d_bc.astype(dbc_ref.dtype)
        later = by_later + [jnp.zeros((high_lanes, Q), F32)]
        later = ([jnp.zeros((low_lanes, Q), F32)] if low_lanes else []) + later
        later = jnp.concatenate(later, axis=0).T
        earlier = jnp.zeros((Q, LANES), F32)
        for head in range(GH):
            earlier = jnp.where(lane == low_lanes + head, by_earlier[head], earlier)
        mine = (lane >= low_lanes) & (lane < low_lanes + GH)
        crossed = jnp.concatenate([in_two(seen + later - earlier, 0), in_two(sent, 0)], axis=0)
        d_log = jnp.where(mine, nn(spans, crossed) + linked, 0.0)
        d_step = sum_heads(x_act * du, heads_ref)
        ddt_ref[s] = d_step + rate * d_log
        thin_ref[1:2, :] += jnp.sum(d_log * (rate * step), axis=0, keepdims=True)
        wide_ref[5:6, :] += jnp.sum(dy * x_act, axis=0, keepdims=True)
        d_total = (du * step_wide + dy * x_taps[5:6, :]) * slope
        d_raw = conv_back(d_total, exts.at[s], shifts.at[s], aheads.at[s], x_taps, marks, wide_ref)
        dx_ref[s] = d_raw.astype(BF16)


def block_at(time, side):
    blocks = LEN // Q
    return (time + side * (blocks // 2)) % blocks


def halo_at(time, side):
    return block_at(jnp.maximum(time - 1, 0), side) * (Q // 16) + Q // 16 - 1


BC_AT = MYC // BC
DT_AT = (MYC + BC) // LANES


def run_forward(part, side, first, marks, rows, x_taps, bc_taps, head_rows, heads, before):
    blocks = LEN // Q
    steps = blocks // 2
    now = lambda t: part * steps + t
    here = lambda col: lambda t, side: (0, block_at(now(t), side[0]), col)
    halo = lambda col: lambda t, side: (0, halo_at(now(t), side[0]), col)
    time = lambda t, side: (0, now(t), 0)
    time_four = lambda t, side: (0, now(t), 0, 0)
    still = lambda t, side: (0, 0)
    inputs = [first, first, first, first, first, marks, rows, x_taps, bc_taps, head_rows, heads]
    in_specs = [
        pl.BlockSpec((2, Q, MYC), here(0)),
        pl.BlockSpec((2, 16, MYC), halo(0)),
        pl.BlockSpec((2, Q, BC), here(BC_AT)),
        pl.BlockSpec((2, 16, BC), halo(BC_AT)),
        pl.BlockSpec((2, Q, LANES), here(DT_AT)),
        pl.BlockSpec((2, Q, 16), time),
        pl.BlockSpec((2, 1, 1, Q), time_four),
        pl.BlockSpec((8, MYC), still),
        pl.BlockSpec((8, BC), still),
        pl.BlockSpec((8, LANES), still),
        pl.BlockSpec((2 * LANES, MYC), still),
    ]
    running = pl.BlockSpec((2, NS, MYC), lambda t, side: (0, 0, 0))
    aliases = {}
    if part > 0:
        aliases = {1 + len(inputs) + i: i for i in range(6)}
        inputs += before
        in_specs += [pl.BlockSpec(memory_space=pl.ANY)] * 6 + [running]
    return pl.pallas_call(
        functools.partial(scan_forward, part),
        grid_spec=pltpu.PrefetchScalarGridSpec(
            num_scalar_prefetch=1,
            grid=(steps,),
            in_specs=in_specs,
            out_specs=[
                pl.BlockSpec((2, Q, MYC), here(0)),
                pl.BlockSpec((2, 1, NS, MYC), time_four),
                pl.BlockSpec((2, Q, BC), here(0)),
                pl.BlockSpec((2, Q, LANES), time),
                pl.BlockSpec((2, Q, LANES), time),
                pl.BlockSpec((2, 1, 16, Q), time_four),
                running,
            ],
            scratch_shapes=[pltpu.VMEM((2, Q + 8, MYC), F32), pltpu.VMEM((2, Q + 8, BC), F32)],
        ),
        out_shape=[
            jax.ShapeDtypeStruct((2, LEN, MYC), BF16),
            jax.ShapeDtypeStruct((2, blocks, NS, MYC), BF16),
            jax.ShapeDtypeStruct((2, LEN, BC), BF16),
            jax.ShapeDtypeStruct((2, LEN, LANES), F32),
            jax.ShapeDtypeStruct((2, LEN, LANES), F32),
            jax.ShapeDtypeStruct((2, blocks, 16, Q), F32),
            jax.ShapeDtypeStruct((2, NS, MYC), F32),
        ],
        input_output_aliases=aliases,
        compiler_params=pltpu.CompilerParams(vmem_limit_bytes=18 * MIB),
        cost_estimate=pl.CostEstimate(flops=9 * 10**9, bytes_accessed=30 * 10**6, transcendentals=10**7),
        name="scan_forward_%d" % part,
    )(side, *inputs)


def run_backward(group, part, side, first, scanned, d_ssm, marks, rows, x_taps, bc_taps, head_rows, heads, d_bc, before):
    _, states, bc_act, step, cum, turned, _ = scanned
    blocks = LEN // Q
    steps = blocks // 2
    final = group == GROUPS - 1
    now = lambda t: blocks - 1 - part * steps - t
    here = lambda col: lambda t, side: (0, block_at(now(t), side[0]), col)
    halo = lambda col: lambda t, side: (0, halo_at(now(t), side[0]), col)
    time = lambda t, side: (0, now(t), 0)
    time_four = lambda col: lambda t, side: (0, now(t), 0, col)
    still = lambda t, side: (0, 0)
    still_three = lambda t, side: (0, 0, 0)
    share = lambda t, side: (0, group)
    in_specs = [
        pl.BlockSpec((2, Q, GC), here(group)),
        pl.BlockSpec((2, 16, GC), halo(group)),
        pl.BlockSpec((2, Q, BC), here(0)),
        pl.BlockSpec((2, Q, LANES), time),
        pl.BlockSpec((2, Q, LANES), time),
        pl.BlockSpec((2, 1, 16, Q), time_four(0)),
        pl.BlockSpec((2, Q, GC), here(group)),
        pl.BlockSpec((2, 1, NS, GC), time_four(group)),
        pl.BlockSpec((2, Q, 16), time),
        pl.BlockSpec((2, 1, 1, Q), time_four(0)),
        pl.BlockSpec((8, GC), share),
        pl.BlockSpec((8, LANES), still),
        pl.BlockSpec((2 * LANES, GC), share),
    ]
    inputs = [first, first, bc_act, step, cum, turned, d_ssm, states, marks, rows, x_taps, head_rows, heads]
    if group > 0:
        in_specs.append(pl.BlockSpec((2, Q, BC), here(0)))
        inputs.append(d_bc)
    if final:
        in_specs += [
            pl.BlockSpec((2, Q, BC), here(BC_AT)),
            pl.BlockSpec((2, 16, BC), halo(BC_AT)),
            pl.BlockSpec((8, BC), still),
        ]
        inputs += [first, first, bc_taps]
    running = [(8, GC), (8, LANES)] + ([(8, BC)] if final else []) + [(2, NS, GC), (2, 8, GC)]
    running += [(2, 8, BC)] if final else []
    running_specs = [pl.BlockSpec(v, still if len(v) == 2 else still_three) for v in running]
    out_specs = [
        pl.BlockSpec((2, Q, GC), here(0)),
        pl.BlockSpec((2, Q, BC), here(0)),
        pl.BlockSpec((2, Q, LANES), here(0)),
    ] + running_specs
    out_shape = [
        jax.ShapeDtypeStruct((2, LEN, GC), BF16),
        jax.ShapeDtypeStruct((2, LEN, BC), BF16 if final else F32),
        jax.ShapeDtypeStruct((2, LEN, LANES), F32),
    ] + [jax.ShapeDtypeStruct(v, F32) for v in running]
    aliases = {}
    if part > 0:
        aliases = {1 + len(inputs) + i: i for i in range(3)}
        in_specs += [pl.BlockSpec(memory_space=pl.ANY)] * 3 + running_specs
        inputs += before
    scratch = [pltpu.VMEM((2, Q + 8, GC), F32), pltpu.VMEM((2, KW - 1, Q, GC), F32)]
    if final:
        scratch += [pltpu.VMEM((2, Q + 8, BC), F32), pltpu.VMEM((2, KW - 1, Q, BC), F32)]
    return pl.pallas_call(
        functools.partial(scan_backward, group, part),
        grid_spec=pltpu.PrefetchScalarGridSpec(
            num_scalar_prefetch=1, grid=(steps,), in_specs=in_specs, out_specs=out_specs, scratch_shapes=scratch
        ),
        out_shape=out_shape,
        input_output_aliases=aliases,
        compiler_params=pltpu.CompilerParams(vmem_limit_bytes=18 * MIB),
        cost_estimate=pl.CostEstimate(flops=14 * 10**9, bytes_accessed=40 * 10**6, transcendentals=10**7),
        name="scan_backward_%d_%d" % (group, part),
    )(side, *inputs)


def lead(value, by):
    if by == 0:
        return value
    pad = [(0, 0)] * value.ndim
    if by > 0:
        pad[1] = (0, by)
        return jnp.pad(value, pad)[:, by:]
    pad[1] = (-by, 0)
    return jnp.pad(value, pad)[:, :by]


def fold(block):
    return jnp.concatenate([block[..., : D // 2], block[..., D // 2 :]], axis=-2)


def unfold(block):
    half = block.shape[-2] // 2
    return jnp.concatenate([block[..., :half, :], block[..., half:, :]], axis=-1)


def out_whole(out_weight, split, core, side):
    whole = lax.all_gather(out_weight, ("zy", "core", "seq"), axis=0, tiled=True)
    return pick(pick(split_heads(whole, 0, split), core), side)


def out_scattered(grad, split, core, side):
    own = jnp.zeros((2, 2, MYC, D), BF16)
    own = lax.dynamic_update_slice(own, grad.astype(BF16)[None, None], (core, side, 0, 0))
    whole = join_heads(own, 0, split)
    return lax.psum_scatter(whole, ("zy", "core", "seq"), scatter_dimension=0, tiled=True)


def own_slice(whole, size):
    at = (lax.axis_index("zy") * 2 + lax.axis_index("core")) * 2 + lax.axis_index("seq")
    return lax.dynamic_slice_in_dim(whole, at * size, size, 0)


def body(
    tokens,
    segments,
    norm_gain,
    in_weight,
    conv_weight,
    conv_bias,
    dt_bias,
    a_log,
    d_skip,
    gated_gain,
    out_weight,
    cotangent,
):
    count = lax.axis_size("zy")
    core, side = lax.axis_index("core"), lax.axis_index("seq")
    split = head_split(count)
    rows = tokens.shape[1]
    total = PARTS * rows

    blocked = split[0] > 1

    me = (core * 2 + side).astype(jnp.int32).reshape(1)
    at_side = side.astype(jnp.int32).reshape(1)
    at_core = core.astype(jnp.int32).reshape(1)
    at_ring = jnp.stack([ring_place(count)[0], core, core * 2 + side]).astype(jnp.int32)

    heads = np.kron(np.eye(LANES, MYH, dtype=np.float32), np.ones((1, HD), np.float32))
    heads = jnp.asarray(np.concatenate([heads, heads], axis=0), BF16)
    per_head = jnp.stack([dt_bias, a_log, d_skip])
    per_head = jnp.pad(per_head, ((0, 5), (0, LANES - NH)))

    sizes = (norm_gain.shape[0], conv_bias.shape[0], gated_gain.shape[0])
    seg_own = segments[0].reshape(-1, LANES)
    mix = split_columns(in_weight, norm_gain, conv_weight, conv_bias, gated_gain, seg_own, split, me)
    mix = Task(peer_steps(mix))
    stage([mix])
    sent, later = assemble_rows(mix.value, me)
    ring = Task(gather_steps(sent))
    token_all = Task(token_steps(tokens[0], 3))
    marks, seg_rows = stage([ring, token_all], functools.partial(segment_marks, at_side), *mix.value)
    if blocked:
        held = Task(single_step((out_weight, GROUP, DIAGONAL)))
        for _ in range(count // 2 - 2):
            stage([ring, token_all])
        stage([ring, token_all, held])
        later = jnp.concatenate([later, fold(held.value)], axis=1)
    else:
        w_out = out_whole(out_weight, split, core, side)
    while not (ring.done and token_all.done):
        stage([ring, token_all])

    near, far, both = token_all.value
    w_pieces = ring.value
    ring = Task(gather_steps(later))
    cot_all = Task(token_steps(cotangent[0], 3))
    first, turned, w_first, x_taps, bc_taps, head_rows, gain = stage(
        [ring, cot_all], functools.partial(project, at_ring, split, sizes), tokens[0], near, far, both, per_head, heads, w_pieces
    )
    first_by_seq = first.reshape(2, LEN, W1)

    def forward(part, first, before):
        return run_forward(part, at_side, first, marks, seg_rows, x_taps, bc_taps, head_rows, heads, before)

    scanned = stage([ring, cot_all], functools.partial(forward, 0), first_by_seq, None)
    scanned = stage([ring, cot_all], functools.partial(forward, 1), first_by_seq, scanned)
    while not (ring.done and cot_all.done):
        stage([ring, cot_all])
    y = scanned[0].reshape(total, MYC)
    if blocked:
        w_out = put_together(ring.value, slice(MYC, 2 * MYC), core * (count // 2))
        blocks = [w_out[: count // 2], swap(w_out[count // 2 :], "core")]
    else:
        blocks = [w_out]
    cot_rows = (cotangent[0], *cot_all.value)
    z, d_two, sums, w_gate, w_out = meet(at_ring, *cot_rows, turned, y, x_taps, blocks, ring.value)
    sums = Task(group_steps(sums))
    stage([sums])
    unit = DI // (count * PARTS) if blocked else MYC // 2
    d_ssm, d_gate, mine, theirs, own, other = gate_back(
        at_core, unit, sums.value, y, z, d_two, x_taps, w_out
    )

    branch = Task(sum_steps(own, other, 3))
    d_theirs, d_mine = out_product(theirs, mine, *cot_rows)
    d_theirs = Task(single_step((d_theirs, "core", SWAP)))
    d_ssm = d_ssm.reshape(2, LEN, MYC)

    def back(group, part, d_bc, before):
        def run(first, d_ssm, scanned, d_bc, before):
            return run_backward(
                group, part, at_side, first, scanned, d_ssm, marks, seg_rows, x_taps, bc_taps, head_rows, heads, d_bc, before
            )

        return run, first_by_seq, d_ssm, scanned, d_bc, before

    zero = stage([d_theirs, branch], *back(0, 0, None, None))
    d_w_gate = weight_product(turned, d_gate).reshape(count, D // count, MYC)
    if blocked:
        d_first_half = jnp.where(core == 0, d_mine, d_theirs.value).reshape(count // 2, -1, D)
        d_second_half = jnp.where(core == 0, d_theirs.value, d_mine).reshape(count // 2, -1, D)
        d_w_gate = jnp.concatenate(
            [d_w_gate, jnp.concatenate([fold(d_first_half), fold(d_second_half)], axis=0)], axis=2
        )
    gate_ring = Task(scatter_steps(d_w_gate, split=True))

    zero = stage([gate_ring, branch], *back(0, 1, None, zero))
    one = stage([gate_ring, branch], *back(1, 0, zero[1], None))
    one = stage([gate_ring, branch], *back(1, 1, zero[1], one))
    d_x0, _, d_dt0, wide0, thin0 = zero[:5]
    d_x1, d_bc, d_dt1, wide1, thin1, bc_sums = one[:6]
    wide = jnp.concatenate([wide0, wide1], axis=1)
    thin = thin0 + thin1
    d_dt = (d_dt0 + d_dt1).reshape(total, LANES)
    d_dt = d_dt * lax.logistic(first[:, MYC + BC :].astype(F32) + head_rows[:1])
    d_rows = [d_x0.reshape(total, GC), d_x1.reshape(total, GC), d_bc.reshape(total, BC), d_dt.astype(BF16)]
    far = stage([gate_ring, branch], functools.partial(normed_part, 1), *d_rows, d_gate, w_first, w_gate)
    far = Task(far_steps(*far, 4))
    while not (branch.done and gate_ring.done):
        stage([gate_ring, branch])
    d_w_first = stage([far], weight_product, turned, *d_rows)
    rest = Task(scatter_steps(d_w_first.reshape(count, D // count, W1)))
    near = stage([rest, far], functools.partial(normed_part, 0), *d_rows, d_gate, w_first, w_gate)
    near = Task(single_step((near[1], "core", SWAP))), near[0]
    small_grads = Task(small_sum_steps(
        (
            wide[:KW].reshape(-1),
            wide[KW],
            bc_sums[: KW + 1].reshape(-1),
            jnp.sum(d_dt, axis=0)[:MYH],
            thin[1, :MYH],
            jnp.sum(wide[KW + 1].reshape(MYH, HD), axis=1),
        ),
        core, side,
    ))
    tasks = [rest, far, near[0], small_grads]
    if blocked:
        d_out = Task(single_step((unfold(gate_ring.value[:, MYC:].astype(BF16)), GROUP, DIAGONAL)))
        tasks.append(d_out)
    stage(tasks)
    if blocked:
        d_out = d_out.value.astype(F32)
    else:
        d_mine, d_theirs = jnp.where(core == 0, d_mine, d_theirs.value), jnp.where(core == 0, d_theirs.value, d_mine)
        d_out = out_scattered(jnp.concatenate([d_mine, d_theirs], axis=0), split, core, side).astype(F32)

    def ends(x, branch, out_weight, gated_gain, d_out):
        gain_two = jnp.sum(out_weight.astype(F32) * d_out, axis=1) / gated_gain.astype(F32)
        return (x.astype(F32) + branch).astype(BF16), gain_two

    block_out, gain_two = stage(
        [rest, far, small_grads], ends, tokens[0], branch.value, out_weight, gated_gain, d_out
    )
    while not (rest.done and far.done):
        stage([rest, far, small_grads])

    d_w = Task(peer_steps(hand_back([rest.value, gate_ring.value[:, :MYC]], me)))
    input_grad = stage(
        [d_w, small_grads], finish_tokens, tokens[0], cotangent[0], gain, near[1], near[0].value, *far.value
    )
    finish([d_w, small_grads])
    in_sh, gain_one = join_columns(d_w.value, split, me, in_weight, jnp.broadcast_to(norm_gain[:, None], (norm_gain.shape[0], LANES)))

    taps_x, bias_x, taps_bc, bias_dt, alog, skip = small_grads.value
    taps_x = jnp.swapaxes(taps_x.reshape(2, 2, KW, MYC), 2, 3)
    taps_bc = jnp.sum(taps_bc, axis=(0, 1)).reshape(KW + 1, BC)
    conv_w = jnp.concatenate([join_heads(taps_x, 0, split), taps_bc[:KW].T], axis=0)
    conv_b = jnp.concatenate([join_heads(bias_x, 0, split), taps_bc[KW]])
    return (
        block_out[None],
        input_grad[None],
        gain_one[:, 0],
        in_sh,
        own_slice(conv_w, conv_bias.shape[0]),
        own_slice(conv_b, conv_bias.shape[0]),
        join_heads(bias_dt, 0, split),
        join_heads(alog, 0, split),
        join_heads(skip, 0, split),
        gain_two,
        d_out,
    )


def solution(mesh):
    fsdp, seq = mesh.shape["fsdp"], mesh.shape["seq"]
    grid = Mesh(mesh.devices.reshape(fsdp // 2, 2, seq), ("zy", "core", "seq"))
    every = ("zy", "core", "seq")
    rows = P(("zy", "core"), "seq", None)
    in_specs = (
        rows,
        P(("zy", "core"), "seq"),
        P(every),
        P(every, None),
        P(every, None),
        P(every),
        P(),
        P(),
        P(),
        P(every),
        P(every, None),
        rows,
    )
    out_specs = (
        rows,
        rows,
        P(every),
        P(every, None),
        P(every, None),
        P(every),
        P(),
        P(),
        P(),
        P(every),
        P(every, None),
    )
    return jax.shard_map(body, mesh=grid, in_specs=in_specs, out_specs=out_specs, check_vma=False)
```

```python
import functools

import jax
import jax.numpy as jnp
import numpy as np
from jax import lax
from jax.experimental import pallas as pl
from jax.experimental.pallas import tpu as pltpu
from jax.sharding import Mesh
from jax.sharding import PartitionSpec as P

D = 1536
NH = 48
HD = 64
NS = 128
KW = 4
DI = 3072
CONV = 3328
LEN = 1024

EPS = 1e-05
HIGH = lax.Precision.HIGHEST
F32 = jnp.float32
BF16 = jnp.bfloat16

PARTS = 4
MYH = NH // PARTS
MYC = MYH * HD
LANES = 128
BC = 2 * NS
W1 = MYC + BC + LANES
GROUPS = 2
GH = MYH // GROUPS
GC = GH * HD
Q = 128
FAR = -1e30
MIB = 1024 * 1024

SWAP = [(0, 1), (1, 0)]


def swap(value, axis):
    return lax.ppermute(value, axis, SWAP)


def pick(value, at, dim=0):
    return lax.dynamic_index_in_dim(value, at, dim, False)


def in_order(mine, other, place):
    buf = jnp.zeros((2,) + mine.shape, mine.dtype)
    buf = lax.dynamic_update_index_in_dim(buf, mine, place, 0)
    return lax.dynamic_update_index_in_dim(buf, other, 1 - place, 0)


GROUP = ("core", "seq")


def to_peer(value, r):
    return (value, GROUP, [(g, g ^ r) for g in range(PARTS)])


def ring_order(count):
    return list(range(0, count, 2)) + list(range(count - 1, 0, -2))


def ring_pairs(count):
    order = ring_order(count)
    right = [(order[i], order[(i + 1) % count]) for i in range(count)]
    return right, [(b, a) for a, b in right]


def ring_order_of(at, count):
    at = at % count
    return jnp.where(at < count // 2, 2 * at, 2 * (count - at) - 1)


def ring_place(count):
    zy = lax.axis_index("zy")
    place = jnp.where(zy % 2 == 0, zy // 2, count - 1 - zy // 2)
    return place, lambda at: ring_order_of(at, count)


def half_of(rows):
    return 16 * (rows // 32) if rows >= 32 else rows // 2


def piece_places(count, rows):
    places = [(0, 0)]
    for step in range(1, count // 2):
        places += [(-step, 0), (step, 0)]
    return places + [(count // 2, 0), (count // 2, half_of(rows))]


class Task:
    def __init__(self, steps):
        self.steps, self.value, self.done = steps, None, False
        self.moves = next(steps, None)
        self.done = self.moves is None

    def take(self, arrived):
        try:
            self.moves = self.steps.send(arrived)
        except StopIteration as end:
            self.value, self.done = end.value, True


def stage(tasks, work=None, *args):
    tasks = [t for t in tasks if not t.done]
    values = [[m[0] for m in t.moves] for t in tasks]
    values, args = lax.optimization_barrier((values, args))
    arrived = [
        [lax.ppermute(v, m[1], m[2]) for v, m in zip(vs, t.moves)] for vs, t in zip(values, tasks)
    ]
    result = None if work is None else work(*args)
    if work is None:
        arrived = lax.optimization_barrier(arrived)
    else:
        arrived, result = lax.optimization_barrier((arrived, result))
    for t, got in zip(tasks, arrived):
        t.take(got)
    return result


def finish(tasks):
    while not all(t.done for t in tasks):
        stage(tasks)


def gather_steps(block):
    count = lax.axis_size("zy")
    half = half_of(block.shape[0])
    right, left = ring_pairs(count)
    pieces = [block]
    ahead = back = block
    for _ in range(1, count // 2):
        ahead, back = yield [(ahead, "zy", right), (back, "zy", left)]
        pieces += [ahead, back]
    pieces += yield [(ahead[:half], "zy", right), (back[half:], "zy", left)]
    return pieces


def put_together(pieces, columns, flip):
    count = lax.axis_size("zy")
    place, order = ring_place(count)
    rows = pieces[0].shape[0]
    full = jnp.zeros((count, rows, columns.stop - columns.start), pieces[0].dtype)
    for piece, (step, row) in zip(pieces, piece_places(count, rows)):
        full = lax.dynamic_update_slice(full, piece[None, :, columns], (order(place + step + count) ^ flip, row, 0))
    return full


def add_kernel(at_ref, one_ref, two_ref, ahead_ref, back_ref, first_ref, second_ref):
    def add(out_ref, full, got, start):
        end = start + got.shape[0]
        out_ref[start:end, :] = (full[start:end, :].astype(F32) + got[...].astype(F32)).astype(BF16)
        if start > 0:
            out_ref[:start, :] = full[:start, :]
        if end < out_ref.shape[0]:
            out_ref[end:, :] = full[end:, :]

    rows = first_ref.shape[0]
    add(first_ref, one_ref[0], ahead_ref, 0)
    add(second_ref, two_ref[0], back_ref, rows - back_ref.shape[0])


def ring_add(full, one, two, ahead, back):
    _, rows, cols = full.shape
    tile = cols // 3
    at = jnp.stack([one, two]).astype(jnp.int32)
    return pl.pallas_call(
        add_kernel,
        grid_spec=pltpu.PrefetchScalarGridSpec(
            num_scalar_prefetch=1,
            grid=(3,),
            in_specs=[
                pl.BlockSpec((1, rows, tile), lambda t, at: (at[0], 0, t)),
                pl.BlockSpec((1, rows, tile), lambda t, at: (at[1], 0, t)),
                pl.BlockSpec((ahead.shape[0], tile), lambda t, at: (0, t)),
                pl.BlockSpec((back.shape[0], tile), lambda t, at: (0, t)),
            ],
            out_specs=[pl.BlockSpec((rows, tile), lambda t, at: (0, t))] * 2,
        ),
        out_shape=[jax.ShapeDtypeStruct((rows, cols), BF16)] * 2,
        compiler_params=pltpu.CompilerParams(vmem_limit_bytes=16 * MIB),
        name="ring_add",
    )(at, full, full, ahead, back)


def scatter_steps(full):
    count, rows, cols = full.shape
    half = half_of(rows)
    right, left = ring_pairs(count)
    place, order = ring_place(count)
    far = lax.dynamic_index_in_dim(full, order(place + count // 2), 0, False)
    one, two = far[:half], far[half:]
    for step in range(count // 2 - 1, -1, -1):
        ahead, back = yield [(one, "zy", right), (two, "zy", left)]
        if step > 0:
            one, two = ring_add(full, order(place + step), order(place + count - step), ahead, back)
    return lax.dynamic_index_in_dim(full, order(place), 0, False), ahead, back


def single_step(move):
    (got,) = yield [move]
    return got


def group_steps(value):
    got = yield [to_peer(value, r) for r in range(1, PARTS)]
    return [value] + list(got)


def piece_cuts(rows, pieces):
    return [16 * (rows // 16 * i // pieces) for i in range(pieces + 1)]


def token_steps(value, pieces):
    cuts = piece_cuts(value.shape[0], pieces)
    far, both = [], []
    moves = [(value, "core", SWAP)]
    for i in range(pieces):
        got = yield moves + [(value[cuts[i] : cuts[i + 1]], "seq", SWAP)]
        if i == 0:
            near = got[0]
        else:
            both.append(got[0])
        far.append(got[-1])
        moves = [(got[-1], "core", SWAP)]
    (got,) = yield moves
    return near, far, both + [got]


def peer_steps(blocks):
    got = yield [to_peer(blocks[r], r) for r in range(1, PARTS)]
    return [blocks[0]] + list(got)


def sum_steps(own, other, pieces):
    (got,) = yield [(other, "core", SWAP)]
    rows = own.shape[0] // 2
    sent = (own[rows:].astype(F32) + got[rows:].astype(F32)).astype(BF16)
    cuts = piece_cuts(rows, pieces)
    arrived = []
    for a, b in zip(cuts, cuts[1:]):
        (far,) = yield [(sent[a:b], "seq", SWAP)]
        arrived.append(far)
    return own[:rows].astype(F32) + got[:rows].astype(F32) + jnp.concatenate(arrived, axis=0).astype(F32)


def far_steps(own, other, pieces):
    (got,) = yield [(other, "core", SWAP)]
    sent = (own.astype(F32) + got.astype(F32)).astype(BF16)
    cuts = piece_cuts(sent.shape[0], pieces)
    arrived = []
    for a, b in zip(cuts, cuts[1:]):
        (got,) = yield [(sent[a:b], "seq", SWAP)]
        arrived.append(got)
    return arrived


def small_sum_steps(parts, core, side):
    count = lax.axis_size("zy")
    lengths = [p.shape[0] for p in parts]
    packed = jnp.concatenate(parts)
    packed = jnp.pad(packed, (0, -packed.shape[0] % 1024)).reshape(-1, LANES)
    bit = 1
    while bit < count:
        (got,) = yield [(packed, "zy", [(i, i ^ bit) for i in range(count)])]
        packed = packed + got
        bit *= 2
    (got,) = yield [(packed, "core", SWAP)]
    packed = in_order(packed, got, core)
    (got,) = yield [(packed, "seq", SWAP)]
    packed = jnp.swapaxes(in_order(packed, got, side), 0, 1).reshape(2, 2, -1)
    return jnp.split(packed, np.cumsum(lengths), axis=2)[: len(lengths)]


def zy_exchange(value, bit):
    count = lax.axis_size("zy")
    return lax.ppermute(value, "zy", [(i, i ^ bit) for i in range(count)])


def zy_sum(value):
    count = lax.axis_size("zy")
    bit = 1
    while bit < count:
        value = value + zy_exchange(value, bit)
        bit *= 2
    return value


def head_split(count):
    rows = DI // count
    if rows % (2 * HD) == 0 and count % 2 == 0:
        return count // 2, rows // (2 * HD)
    return 1, MYH


def split_heads(value, dim, split):
    q, i = split
    size = value.shape[dim]
    unit = size // NH
    shape = value.shape
    value = value.reshape(shape[:dim] + (2, q, 2, i * unit) + shape[dim + 1 :])
    value = jnp.swapaxes(value, dim + 1, dim + 2)
    return value.reshape(shape[:dim] + (2, 2, size // PARTS) + shape[dim + 1 :])


def join_heads(value, dim, split):
    q, i = split
    shape = value.shape
    mine = shape[dim + 2]
    value = value.reshape(shape[:dim] + (2, 2, q, mine // q) + shape[dim + 3 :])
    value = jnp.swapaxes(value, dim + 1, dim + 2)
    return value.reshape(shape[:dim] + (PARTS * mine,) + shape[dim + 3 :])


HALF = LANES // 2
EXTRA = 16
SEG_AT = 8


def half_places(split, core, side):
    q, i = split
    return [((core * q + at) * 2 + side) * i + k for at in range(q) for k in range(i)]


def halves(tile_of, places):
    tiles = []
    for at in range(0, len(places), 2):
        one, two = places[at], places[at + 1]
        if one % 2 == 0 and two == one + 1:
            tiles.append(tile_of(one // 2))
            continue
        left, right = tile_of(one // 2), tile_of(two // 2)
        left = pltpu.roll(left, HALF, 1) if one % 2 else left
        right = right if two % 2 else pltpu.roll(right, HALF, 1)
        lane = lax.broadcasted_iota(jnp.int32, left.shape, 1)
        tiles.append(jnp.where(lane < HALF, left, right))
    return tiles


def head_choice(split):
    choice = np.zeros((PARTS, LANES, LANES), np.float32)
    for g in range(PARTS):
        for lane, head in enumerate(half_places(split, g // 2, g % 2)):
            choice[g, head, lane] = 1.0
    return choice


def split_kernel(split, at_ref, w_ref, gain_ref, taps_ref, bias_ref, gated_ref, seg_ref, choice_ref, *refs):
    *outs, out_ref, small_ref, turn_ref = refs
    me = at_ref[0]
    small_ref[...] = jnp.zeros_like(small_ref)
    for row, ref in ((0, gain_ref), (1, bias_ref), (6, gated_ref)):
        small_ref[row : row + 1, : ref.shape[1]] = ref[...].astype(F32)
    turn_ref[...] = jnp.zeros_like(turn_ref)
    turn_ref[: taps_ref.shape[0], :KW] = taps_ref[...].astype(F32)
    small_ref[2 : 2 + KW, :] = turn_ref[...].T[:KW, :]
    small_ref[SEG_AT : SEG_AT + seg_ref.shape[0], :] = seg_ref[...].astype(F32)

    def tile_of(base):
        return lambda t: w_ref[:, base + t * LANES : base + (t + 1) * LANES].astype(F32)

    bc = w_ref[:, 2 * DI : 2 * DI + BC]
    steps = w_ref[:, DI + CONV :]
    for g in range(PARTS):
        places = half_places(split, g // 2, g % 2)
        at = me ^ g
        tiles = halves(tile_of(DI), places)
        for k, tile in enumerate(tiles):
            out_ref[at, :, k * LANES : (k + 1) * LANES] = tile.astype(BF16)
        out_ref[at, :, MYC : MYC + BC] = bc
        out_ref[at, :, MYC + BC : W1] = nn(steps, choice_ref[g, :NH, :]).astype(BF16)
        for k, tile in enumerate(halves(tile_of(0), places)):
            out_ref[at, :, W1 + k * LANES : W1 + (k + 1) * LANES] = tile.astype(BF16)
    for r, ref in enumerate(outs):
        ref[:EXTRA, :LANES] = small_ref[...].astype(BF16)
        ref[:EXTRA, LANES:] = jnp.zeros((EXTRA, W1 + MYC - LANES), BF16)
        ref[EXTRA:, :] = out_ref[r]


def smem(shape=None):
    return pl.BlockSpec(memory_space=pltpu.SMEM)


def split_columns(weight, gain, taps, bias, gated, segs, split, me):
    return pl.pallas_call(
        functools.partial(split_kernel, split),
        out_shape=[jax.ShapeDtypeStruct((EXTRA + weight.shape[0], W1 + MYC), BF16)] * PARTS,
        in_specs=[smem()] + [pl.BlockSpec()] * 7,
        scratch_shapes=[
            pltpu.VMEM((PARTS, weight.shape[0], W1 + MYC), BF16),
            pltpu.VMEM((EXTRA, LANES), F32),
            pltpu.VMEM((LANES, LANES), F32),
        ],
        compiler_params=pltpu.CompilerParams(vmem_limit_bytes=56 * MIB),
        name="split_columns",
    )(me, weight, gain[None], taps, bias[None], gated[None], segs, jnp.asarray(head_choice(split), BF16))


def assemble_kernel(at_ref, one, two, three, four, first_ref, gate_ref):
    me = at_ref[0]
    rows = one.shape[0] - EXTRA
    first_ref[:EXTRA, :] = jnp.zeros((EXTRA, W1), BF16)
    for r, ref in enumerate((one, two, three, four)):
        at = me ^ r
        first_ref[pl.ds(pl.multiple_of(EXTRA + at * rows, 16), rows), :] = ref[EXTRA:, :W1]
        gate_ref[pl.ds(pl.multiple_of(at * rows, 16), rows), :] = ref[EXTRA:, W1:]
        for g in range(PARTS):

            @pl.when(at == g)
            def _():
                first_ref[:EXTRA, g * LANES : (g + 1) * LANES] = ref[:EXTRA, :LANES]


def assemble_plain(at_ref, one, two, three, four, extra_ref, first_ref, gate_ref):
    me = at_ref[0]
    extra_ref[...] = jnp.zeros_like(extra_ref)
    for r, ref in enumerate((one, two, three, four)):
        at = me ^ r
        first_ref[at] = ref[EXTRA:, :W1]
        gate_ref[at] = ref[EXTRA:, W1:]
        for g in range(PARTS):

            @pl.when(at == g)
            def _():
                extra_ref[:, g * LANES : (g + 1) * LANES] = ref[:EXTRA, :LANES]


def assemble_rows(blocks, me):
    rows = blocks[0].shape[0] - EXTRA
    if rows % 16 == 0:
        return pl.pallas_call(
            assemble_kernel,
            out_shape=[
                jax.ShapeDtypeStruct((EXTRA + PARTS * rows, W1), BF16),
                jax.ShapeDtypeStruct((PARTS * rows, MYC), BF16),
            ],
            in_specs=[smem()] + [pl.BlockSpec()] * PARTS,
            compiler_params=pltpu.CompilerParams(vmem_limit_bytes=56 * MIB),
            name="assemble_rows",
        )(me, *blocks)
    extra, first, gate = pl.pallas_call(
        assemble_plain,
        out_shape=[
            jax.ShapeDtypeStruct((EXTRA, W1), BF16),
            jax.ShapeDtypeStruct((PARTS, rows, W1), BF16),
            jax.ShapeDtypeStruct((PARTS, rows, MYC), BF16),
        ],
        in_specs=[smem()] + [pl.BlockSpec()] * PARTS,
        name="assemble_rows",
    )(me, *blocks)
    first = jnp.concatenate([extra, first.reshape(PARTS * rows, W1)], axis=0)
    return first, gate.reshape(PARTS * rows, MYC)


def hand_back_kernel(at_ref, own, ahead, back, gate, *refs):
    outs, out_ref = refs[:-1], refs[-1]
    me = at_ref[0]
    for g in range(PARTS):
        first = own[g].astype(F32) + ahead[g].astype(F32) + back[g].astype(F32)
        out_ref[me ^ g, :, :W1] = first.astype(BF16)
        out_ref[me ^ g, :, W1:] = gate[g].astype(BF16)
    for r, ref in enumerate(outs):
        ref[...] = out_ref[r]


def hand_back(own, ahead, back, gate, me):
    blocks = [b.reshape(PARTS, -1, b.shape[1]) for b in (own, ahead, back, gate)]
    return pl.pallas_call(
        hand_back_kernel,
        out_shape=[jax.ShapeDtypeStruct((blocks[0].shape[1], W1 + MYC), BF16)] * PARTS,
        in_specs=[smem()] + [pl.BlockSpec()] * len(blocks),
        scratch_shapes=[pltpu.VMEM((PARTS, blocks[0].shape[1], W1 + MYC), BF16)],
        compiler_params=pltpu.CompilerParams(vmem_limit_bytes=32 * MIB),
        name="hand_back",
    )(me, *blocks)


def join_kernel(split, at_ref, one, two, three, four, choice_ref, w_ref, gain_ref, out_ref, grad_ref, by):
    me = at_ref[0]
    for r, ref in enumerate((one, two, three, four)):
        by[me ^ r] = ref[...].astype(F32)
    where = {}
    for g in range(PARTS):
        for at, place in enumerate(half_places(split, g // 2, g % 2)):
            where[place] = (g, at)

    def put(base, column):
        for t in range(DI // LANES):
            tiles = []
            for k in range(2):
                g, at = where[2 * t + k]
                start = column + at // 2 * LANES
                tile = by[g, :, start : start + LANES]
                tiles.append(tile if at % 2 == k else pltpu.roll(tile, HALF, 1))
            lane = lax.broadcasted_iota(jnp.int32, tiles[0].shape, 1)
            out_ref[:, base + t * LANES : base + (t + 1) * LANES] = jnp.where(lane < HALF, tiles[0], tiles[1])

    put(0, W1)
    put(DI, 0)
    out_ref[:, 2 * DI : 2 * DI + BC] = sum(by[g, :, MYC : MYC + BC] for g in range(PARTS))
    out_ref[:, DI + CONV :] = sum(
        nt(by[g, :, MYC + BC : W1].astype(BF16), choice_ref[g, :NH, :]) for g in range(PARTS)
    )
    met = jnp.sum(out_ref[...] * w_ref[...].astype(F32), axis=1, keepdims=True)
    grad_ref[...] = jnp.broadcast_to(met / gain_ref[:, 0:1].astype(F32), grad_ref.shape)


def join_columns(blocks, split, me, weight, gain):
    rows = blocks[0].shape[0]
    return pl.pallas_call(
        functools.partial(join_kernel, split),
        out_shape=[
            jax.ShapeDtypeStruct((rows, 2 * DI + BC + NH), F32),
            jax.ShapeDtypeStruct((rows, LANES), F32),
        ],
        in_specs=[smem()] + [pl.BlockSpec()] * (PARTS + 3),
        scratch_shapes=[pltpu.VMEM((PARTS, rows, W1 + MYC), F32)],
        name="join_columns",
    )(me, *blocks, jnp.asarray(head_choice(split), BF16), weight, gain)


DIAGONAL = [(0, 0), (1, 2), (2, 1), (3, 3)]


def sigmoid(value):
    return 0.5 * jnp.tanh(0.5 * value) + 0.5


def nt(a, b):
    return lax.dot_general(a, b, (((1,), (1,)), ((), ())), preferred_element_type=F32)


def nn(a, b):
    return lax.dot_general(a, b, (((1,), (0,)), ((), ())), preferred_element_type=F32)


def tn(a, b):
    return lax.dot_general(a, b, (((0,), (0,)), ((), ())), preferred_element_type=F32)


def exact(a, b):
    return lax.dot_general(
        a, b, (((1,), (0,)), ((), ())), preferred_element_type=F32, precision=HIGH
    )


def in_two(value, axis):
    top = value.astype(BF16)
    return jnp.concatenate([top, (value - top.astype(F32)).astype(BF16)], axis=axis)


def in_three(value, axis):
    top = value.astype(BF16)
    rest = value - top.astype(F32)
    mid = rest.astype(BF16)
    return jnp.concatenate([top, mid, (rest - mid.astype(F32)).astype(BF16)], axis=axis)


def over_heads(value, heads_ref):
    return nn(in_two(value, 1), heads_ref[...])


def over_heads_all(values, heads_ref):
    wide = over_heads(jnp.concatenate(values, axis=0), heads_ref)
    cuts = np.cumsum([0] + [v.shape[0] for v in values])
    return [wide[a:b, :] for a, b in zip(cuts, cuts[1:])]


def sum_heads_all(values, heads_ref):
    thin = sum_heads(jnp.concatenate(values, axis=0), heads_ref)
    cuts = np.cumsum([0] + [v.shape[0] for v in values])
    return [thin[a:b, :] for a, b in zip(cuts, cuts[1:])]


def spreads(cum, marks):
    last = cum[Q - 1 : Q, :]
    return (
        jnp.exp(cum) * marks[:, 7:8],
        jnp.exp(last - cum) * marks[:, 8:9],
        jnp.broadcast_to(jnp.exp(last) * marks[Q - 1 : Q, 7:8], (8, LANES)),
    )


def sum_heads(value, heads_ref):
    return nt(value.astype(BF16), heads_ref[:LANES, :])


ROWS = LEN // 2


def row_copies(sources, held, sems):
    half = len(sources) // 2
    copies, at = [], 0
    for q, refs in enumerate((sources[:1], sources[2 : 1 + half], sources[1:2], sources[1 + half :])):
        copies.append([])
        row = 0
        for ref in refs:
            size = ref.shape[0]
            copies[q].append(pltpu.make_async_copy(ref, held.at[q, row : row + size, :], sems.at[at]))
            row += size
            at += 1
    return copies


def wait_rows(step, copies):
    for q, some in enumerate(copies):

        @pl.when(step == q)
        def _():
            for copy in some:
                copy.wait()


def piece_copies(at_ref, refs, full_ref, count, sems, extra=0, small_ref=None, columns=None):
    block = refs[0].shape[0]
    rows = block - extra
    copies, smalls = [], []
    start_col, width = (0, full_ref.shape[1]) if columns is None else columns
    for i, (ref, (step, row)) in enumerate(zip(refs, piece_places(count, block))):
        zy = ring_order_of(at_ref[0] + step + count, count)
        skip = extra if row == 0 else 0
        start = zy * rows + row + skip - extra
        size = ref.shape[0] - skip
        to = full_ref.at[pl.ds(pl.multiple_of(start, 16), size), start_col : start_col + width]
        copies.append(pltpu.make_async_copy(ref.at[skip : skip + size, :width], to, sems.at[2 * i]))
        if skip and small_ref is not None:
            to = small_ref.at[pl.ds(pl.multiple_of(zy * extra, 16), extra), :]
            smalls.append(pltpu.make_async_copy(ref.at[:skip, : PARTS * LANES], to, sems.at[2 * i + 1]))
    return copies, smalls


def anywhere(values):
    return [pl.BlockSpec(memory_space=pltpu.HBM) for _ in values]


def project_kernel(count, parts, split, sizes, at_ref, *refs):
    sources, refs = refs[:parts], refs[parts:]
    per_head_ref, choice_ref, wide_ref, *refs = refs
    pieces, refs = refs[: count + 1], refs[count + 1 :]
    (first_ref, turned_ref, x_ref, bc_ref, head_ref, gain_ref,
     w_ref, held, small_ref, params_ref, row_sems, piece_sems) = refs
    step = pl.program_id(0)
    rows = row_copies(sources, held, row_sems)

    @pl.when(step == 0)
    def _():
        weights, smalls = piece_copies(at_ref, pieces, w_ref, count, piece_sems, EXTRA, small_ref)
        for copy in smalls + weights + sum(rows, []):
            copy.start()
        for copy in smalls:
            copy.wait()
        unpack_small(at_ref, split, sizes, small_ref, per_head_ref, choice_ref, wide_ref, gain_ref, x_ref, bc_ref, head_ref, params_ref)
        for copy in weights:
            copy.wait()

    wait_rows(step, rows)
    x = held[step].astype(F32)
    inv = lax.rsqrt(jnp.mean(x * x, axis=-1, keepdims=True) + EPS)
    low = (x * inv * gain_ref[0:1, :]).astype(BF16)
    turned_ref[...] = low.T
    first_ref[...] = nn(low, w_ref[...]).astype(BF16)


def project(place, split, sizes, own, near, far, both, per_head, heads, pieces):
    rows = own.shape[0]
    total = PARTS * rows
    count = lax.axis_size("zy")
    still = lambda t, *_: (0, 0)
    choice = jnp.asarray(head_choice(split), BF16)
    return pl.pallas_call(
        functools.partial(project_kernel, count, 2 + len(far) + len(both), split, sizes),
        grid_spec=pltpu.PrefetchScalarGridSpec(
            num_scalar_prefetch=1,
            grid=(total // ROWS,),
            in_specs=anywhere((own, near, *far, *both))
            + [
                pl.BlockSpec((8, LANES), still),
                pl.BlockSpec(choice.shape, lambda t, *_: (0, 0, 0)),
                pl.BlockSpec((2 * LANES, MYC), still),
            ]
            + anywhere(pieces),
            out_specs=[
                pl.BlockSpec((ROWS, W1), lambda t, *_: (t, 0)),
                pl.BlockSpec((D, ROWS), lambda t, *_: (0, t)),
                pl.BlockSpec((8, MYC), still),
                pl.BlockSpec((8, BC), still),
                pl.BlockSpec((8, LANES), still),
                pl.BlockSpec((8, D), still),
            ],
            scratch_shapes=[
                pltpu.VMEM((D, W1), BF16),
                pltpu.VMEM((PARTS, rows, D), BF16),
                pltpu.VMEM((count * EXTRA, PARTS * LANES), BF16),
                pltpu.VMEM((8, DI), F32),
                pltpu.SemaphoreType.DMA((2 + len(far) + len(both),)),
                pltpu.SemaphoreType.DMA((2 * len(pieces),)),
            ],
        ),
        out_shape=[
            jax.ShapeDtypeStruct((total, W1), BF16),
            jax.ShapeDtypeStruct((D, total), BF16),
            jax.ShapeDtypeStruct((8, MYC), F32),
            jax.ShapeDtypeStruct((8, BC), F32),
            jax.ShapeDtypeStruct((8, LANES), F32),
            jax.ShapeDtypeStruct((8, D), F32),
        ],
        compiler_params=pltpu.CompilerParams(vmem_limit_bytes=56 * MIB),
        cost_estimate=pl.CostEstimate(flops=12 * 10**9, bytes_accessed=30 * 10**6, transcendentals=10**4),
        name="project",
    )(place, own, near, *far, *both, per_head, choice, heads, *pieces)


def silu_of(z):
    sig = sigmoid(z)
    return sig, z * sig


def meet_kernel(count, parts, blocked, at_ref, *refs):
    sources, refs = refs[:parts], refs[parts:]
    turned_ref, y_ref, taps_ref, *refs = refs
    blocks, refs = refs[: 1 + blocked], refs[1 + blocked :]
    *pieces, z_ref, d_two_ref, sums_ref, w_out_ref, w_ref, held, row_sems, piece_sems, out_sems = refs
    step = pl.program_id(0)
    half = D // 2
    rows = row_copies(sources, held, row_sems)

    @pl.when(step == 0)
    def _():
        copies, _ = piece_copies(at_ref, pieces, w_ref, count, piece_sems)
        if blocked:
            each, size, _ = blocks[0].shape
            size = size // 2
            for q in range(each):
                for i, (ref, part) in enumerate(zip(blocks, (at_ref[1], 1 - at_ref[1]))):
                    to = pl.ds(pl.multiple_of((2 * q + part) * size, 16), size)
                    for k in range(2):
                        copies.append(
                            pltpu.make_async_copy(
                                ref.at[q, k * size : (k + 1) * size, :],
                                w_out_ref.at[to, k * half : (k + 1) * half],
                                out_sems.at[4 * q + 2 * i + k],
                            )
                        )
        else:
            copies.append(pltpu.make_async_copy(blocks[0], w_out_ref, out_sems.at[0]))
        for copy in copies + sum(rows, []):
            copy.start()
        for copy in copies:
            copy.wait()

    wait_rows(step, rows)
    z = tn(turned_ref[...], w_ref[...]).astype(BF16)
    z_ref[...] = z
    _, silu = silu_of(z.astype(F32))
    joined = y_ref[...].astype(F32) * silu
    d_two = nt(held[step], w_out_ref[...])
    d_two_ref[...] = d_two.astype(BF16)
    row = lax.broadcasted_iota(jnp.int32, (8, MYC), 0)
    squares = nt((row == 0).astype(BF16), (joined * joined).astype(BF16))
    products = nt((row == 1).astype(BF16), (joined * taps_ref[6:7, :] * d_two).astype(BF16))
    sums_ref[...] = squares + products


def meet(place, own, near, far, both, turned, y, x_taps, blocks, pieces):
    rows = own.shape[0]
    total = PARTS * rows
    count = lax.axis_size("zy")
    still = lambda t, *_: (0, 0)
    here = lambda t, *_: (t, 0)
    blocked = len(blocks) > 1
    return pl.pallas_call(
        functools.partial(meet_kernel, count, 2 + len(far) + len(both), blocked),
        grid_spec=pltpu.PrefetchScalarGridSpec(
            num_scalar_prefetch=1,
            grid=(total // ROWS,),
            in_specs=anywhere((own, near, *far, *both))
            + [
                pl.BlockSpec((D, ROWS), lambda t, *_: (0, t)),
                pl.BlockSpec((ROWS, MYC), here),
                pl.BlockSpec((8, MYC), still),
            ]
            + anywhere((*blocks, *pieces)),
            out_specs=[
                pl.BlockSpec((ROWS, MYC), here),
                pl.BlockSpec((ROWS, MYC), here),
                pl.BlockSpec((8, ROWS), lambda t, *_: (0, t)),
                pl.BlockSpec((MYC, D), still),
            ],
            scratch_shapes=[
                pltpu.VMEM((D, MYC), BF16),
                pltpu.VMEM((PARTS, rows, D), BF16),
                pltpu.SemaphoreType.DMA((2 + len(far) + len(both),)),
                pltpu.SemaphoreType.DMA((2 * len(pieces),)),
                pltpu.SemaphoreType.DMA((4 * blocks[0].shape[0] if blocked else 1,)),
            ],
        ),
        out_shape=[
            jax.ShapeDtypeStruct((total, MYC), BF16),
            jax.ShapeDtypeStruct((total, MYC), BF16),
            jax.ShapeDtypeStruct((8, total), F32),
            jax.ShapeDtypeStruct((MYC, D), BF16),
        ],
        compiler_params=pltpu.CompilerParams(vmem_limit_bytes=56 * MIB),
        cost_estimate=pl.CostEstimate(flops=15 * 10**9, bytes_accessed=40 * 10**6, transcendentals=10**6),
        name="meet",
    )(place, own, near, *far, *both, turned, y, x_taps, *blocks, *pieces)


def out_kernel(parts, *refs):
    sources, refs = refs[:parts], refs[parts:]
    theirs_ref, mine_ref, d_theirs_ref, d_mine_ref, held, sems = refs
    step = pl.program_id(0)
    rows = row_copies(sources, held, sems)

    @pl.when(step == 0)
    def _():
        for copy in sum(rows, []):
            copy.start()
        for copy in sum(rows, []):
            copy.wait()

    for at, a_ref, out_ref in ((0, theirs_ref, d_theirs_ref), (2, mine_ref, d_mine_ref)):

        @pl.when((step >= at) & (step < at + 2))
        def _():
            every = held[...].reshape(PARTS * ROWS, D)
            out_ref[...] = nn(a_ref[...], every).astype(BF16)


def out_product(theirs, mine, own, near, far, both):
    rows, total = theirs.shape
    tile = rows // 2
    one = lambda t: (jnp.minimum(t, 1), 0)
    two = lambda t: (jnp.maximum(t - 2, 0), 0)
    return pl.pallas_call(
        functools.partial(out_kernel, 2 + len(far) + len(both)),
        grid=(4,),
        in_specs=anywhere((own, near, *far, *both))
        + [pl.BlockSpec((tile, total), one), pl.BlockSpec((tile, total), two)],
        out_specs=[pl.BlockSpec((tile, D), one), pl.BlockSpec((tile, D), two)],
        out_shape=[jax.ShapeDtypeStruct((rows, D), BF16)] * 2,
        scratch_shapes=[
            pltpu.VMEM((PARTS, ROWS, D), BF16),
            pltpu.SemaphoreType.DMA((2 + len(far) + len(both),)),
        ],
        compiler_params=pltpu.CompilerParams(vmem_limit_bytes=26 * MIB),
        cost_estimate=pl.CostEstimate(flops=8 * 10**9, bytes_accessed=20 * 10**6, transcendentals=0),
        name="out_product",
    )(own, near, *far, *both, theirs, mine)


def gate_kernel(
    unit, core_ref, sums_0, sums_1, sums_2, sums_3, y_ref, z_ref, d_two_ref, taps_ref, w_out_ref,
    d_ssm_ref, d_gate_ref, mine_ref, theirs_ref, own_ref, other_ref, turned,
):
    step = pl.program_id(0)
    sums = (sums_0[...] + sums_1[...] + sums_2[...] + sums_3[...]).T
    inv = lax.rsqrt(sums[:, 0:1] * (1.0 / DI) + EPS)
    shift = inv * inv * inv * (sums[:, 1:2] * (1.0 / DI))
    z = z_ref[...].astype(F32)
    sig, silu = silu_of(z)
    y = y_ref[...].astype(F32)
    joined = y * silu
    d_two = d_two_ref[...].astype(F32)
    two = (joined * inv * taps_ref[6:7, :]).astype(BF16)
    d_joined = inv * (taps_ref[6:7, :] * d_two) - joined * shift
    d_ssm_ref[...] = (d_joined * silu).astype(BF16)
    d_gate_ref[...] = (d_joined * y * (sig * (1.0 + z * (1.0 - sig)))).astype(BF16)
    branch = nn(two, w_out_ref[...]).astype(BF16)

    @pl.when(step < 2)
    def _():
        own_ref[...] = branch

    @pl.when(step >= 2)
    def _():
        other_ref[...] = branch

    turned[...] = two.T
    core = core_ref[0]
    for at in range(MYC // (2 * unit)):
        to = slice(at * unit, (at + 1) * unit)
        mine_ref[to, :] = turned[pl.ds(pl.multiple_of((2 * at + core) * unit, 16), unit), :]
        theirs_ref[to, :] = turned[pl.ds(pl.multiple_of((2 * at + 1 - core) * unit, 16), unit), :]


def gate_back(core, unit, sums, y, z, d_two, x_taps, w_out):
    total = y.shape[0]
    still = lambda t, *_: (0, 0)
    here = lambda t, *_: (t, 0)
    across = lambda t, *_: (0, t)
    return pl.pallas_call(
        functools.partial(gate_kernel, unit),
        grid_spec=pltpu.PrefetchScalarGridSpec(
            num_scalar_prefetch=1,
            grid=(total // ROWS,),
            in_specs=[pl.BlockSpec((8, ROWS), lambda t, *_, r=r: (0, t ^ r)) for r in range(PARTS)]
            + [
                pl.BlockSpec((ROWS, MYC), here),
                pl.BlockSpec((ROWS, MYC), here),
                pl.BlockSpec((ROWS, MYC), here),
                pl.BlockSpec((8, MYC), still),
                pl.BlockSpec((MYC, D), still),
            ],
            out_specs=[
                pl.BlockSpec((ROWS, MYC), here),
                pl.BlockSpec((ROWS, MYC), here),
                pl.BlockSpec((MYC // 2, ROWS), across),
                pl.BlockSpec((MYC // 2, ROWS), across),
                pl.BlockSpec((ROWS, D), lambda t, *_: (jnp.minimum(t, 1), 0)),
                pl.BlockSpec((ROWS, D), lambda t, *_: (jnp.maximum(t - 2, 0), 0)),
            ],
            scratch_shapes=[pltpu.VMEM((MYC, ROWS), BF16)],
        ),
        out_shape=[
            jax.ShapeDtypeStruct((total, MYC), BF16),
            jax.ShapeDtypeStruct((total, MYC), BF16),
            jax.ShapeDtypeStruct((MYC // 2, total), BF16),
            jax.ShapeDtypeStruct((MYC // 2, total), BF16),
            jax.ShapeDtypeStruct((total // 2, D), BF16),
            jax.ShapeDtypeStruct((total // 2, D), BF16),
        ],
        compiler_params=pltpu.CompilerParams(vmem_limit_bytes=42 * MIB),
        cost_estimate=pl.CostEstimate(flops=8 * 10**9, bytes_accessed=30 * 10**6, transcendentals=10**6),
        name="gate_back",
    )(core, *sums, y, z, d_two, x_taps, w_out)


def normed_kernel(count, at, parts, at_ref, *refs):
    values, refs = refs[:parts], refs[parts:]
    firsts, gates, refs = refs[: count + 1], refs[count + 1 : 2 * count + 2], refs[2 * count + 2 :]
    other_ref, own_ref, weight, rows, first_sems, gate_sems, row_sems = refs
    step = pl.program_id(0)
    copies, _ = piece_copies(at_ref, firsts, weight, count, first_sems, EXTRA, columns=(0, W1))
    copies += piece_copies(at_ref, gates, weight, count, gate_sems, columns=(W1, MYC))[0]
    row_copies_of = []
    for i in range(2):
        start, col = (2 * (1 - i) + at) * ROWS, 0
        row_copies_of.append([])
        for k, ref in enumerate(values):
            width = ref.shape[1]
            row_copies_of[i].append(
                pltpu.make_async_copy(
                    ref.at[start : start + ROWS, :], rows.at[i, :, col : col + width], row_sems.at[i, k]
                )
            )
            col += width

    @pl.when(step == 0)
    def _():
        for copy in row_copies_of[0] + copies + row_copies_of[1]:
            copy.start()
        for copy in copies:
            copy.wait()

    for i, ref in enumerate((other_ref, own_ref)):

        @pl.when(step == i)
        def _():
            for copy in row_copies_of[i]:
                copy.wait()
            ref[...] = nt(rows[i], weight[...]).astype(BF16)


def normed_part(at, place, d_x0, d_x1, d_bc, d_dt, d_gate, firsts, gates):
    still = lambda t, *_: (0, 0)
    values = [d_x0, d_x1, d_bc, d_dt, d_gate]
    count = len(firsts) - 1
    return pl.pallas_call(
        functools.partial(normed_kernel, count, at, len(values)),
        grid_spec=pltpu.PrefetchScalarGridSpec(
            num_scalar_prefetch=1,
            grid=(2,),
            in_specs=anywhere((*values, *firsts, *gates)),
            out_specs=[pl.BlockSpec((ROWS, D), still)] * 2,
            scratch_shapes=[
                pltpu.VMEM((D, W1 + MYC), BF16),
                pltpu.VMEM((2, ROWS, W1 + MYC), BF16),
                pltpu.SemaphoreType.DMA((2 * len(firsts),)),
                pltpu.SemaphoreType.DMA((2 * len(gates),)),
                pltpu.SemaphoreType.DMA((2, len(values))),
            ],
        ),
        out_shape=[jax.ShapeDtypeStruct((ROWS, D), BF16)] * 2,
        compiler_params=pltpu.CompilerParams(vmem_limit_bytes=56 * MIB),
        cost_estimate=pl.CostEstimate(flops=8 * 10**9, bytes_accessed=20 * 10**6, transcendentals=0),
        name="normed_part_%d" % at,
    )(place, *values, *firsts, *gates)


def flat(small, row, count, spread, size):
    every = small[:, row, :]
    rows = jnp.concatenate([every[:, g * LANES : (g + 1) * LANES] for g in range(PARTS)], axis=0)
    value = nn(rows.astype(BF16), spread)
    at = lax.broadcasted_iota(jnp.int32, value.shape, 0)
    device = (at % count) * PARTS + at // count
    lane = lax.broadcasted_iota(jnp.int32, value.shape, 1)
    own = (lane >= device * size) & (lane < (device + 1) * size)
    return jnp.sum(jnp.where(own, value, 0.0), axis=0, keepdims=True)


def spread_of(size, count):
    shape = (LANES, count * PARTS * size)
    lane = lax.broadcasted_iota(jnp.int32, shape, 1).astype(F32)
    part = lane - jnp.floor((lane + 0.5) * (1.0 / size)) * size
    return (part == lax.broadcasted_iota(jnp.int32, shape, 0).astype(F32)).astype(BF16)


def unpack_small(at_ref, split, sizes, small_ref, per_head_ref, choice_ref, wide_ref, gain_ref, x_ref, bc_ref, head_ref, held):
    group = at_ref[2]
    count = small_ref.shape[0] // EXTRA
    small = small_ref[...].astype(F32).reshape(count, EXTRA, PARTS * LANES)
    gain_ref[...] = jnp.broadcast_to(flat(small, 0, count, spread_of(sizes[0], count), sizes[0]), gain_ref.shape)
    spread = spread_of(sizes[1], count)
    conv = [flat(small, r, count, spread, sizes[1]) for r in (2, 3, 4, 5, 1)]
    for k, v in enumerate(conv):
        held[k : k + 1, :] = v[:, :DI]
        bc_ref[k : k + 1, :] = v[:, DI:]
    bc_ref[5:8, :] = jnp.zeros((3, BC), F32)
    held[6:7, :] = flat(small, 6, count, spread_of(sizes[2], count), sizes[2])
    held[5:6, :] = jnp.zeros((1, DI), F32)
    held[7:8, :] = jnp.zeros((1, DI), F32)
    per_head = in_three(per_head_ref[...], 1)
    mine = jnp.zeros((8, LANES), F32)
    for g in range(PARTS):
        chosen = nn(per_head, jnp.concatenate([choice_ref[g]] * 3, axis=0))
        mine = jnp.where(group == g, chosen, mine)

        @pl.when(group == g)
        def _():
            tiles = halves(lambda t: held[:, t * LANES : (t + 1) * LANES], half_places(split, g // 2, g % 2))
            for k, tile in enumerate(tiles):
                x_ref[:, k * LANES : (k + 1) * LANES] = tile

    head_ref[...] = mine
    wide = jnp.concatenate([wide_ref[:LANES, :]] * 3, axis=0)
    x_ref[5:6, :] = nn(in_three(mine, 1), wide)[2:3, :]


def marks_kernel(side_ref, *refs):
    *parts, marks_ref, rows_ref, seg, taken = refs
    side = side_ref[0]
    blocks = LEN // Q
    for s in range(2):
        for j in range(blocks):
            half, row = j // (blocks // 2), j % (blocks // 2)
            near, far = parts[2 * s + half], parts[2 * s + 1 - half]
            at = slice(SEG_AT + row, SEG_AT + row + 1)
            to = s * blocks + j
            seg[to : to + 1, :] = jnp.where(side == 0, near[at, :LANES].astype(F32), far[at, :LANES].astype(F32))
    value = seg[...]
    count = 2 * blocks
    lane = lax.broadcasted_iota(jnp.int32, value.shape, 1)
    row = lax.broadcasted_iota(jnp.int32, value.shape, 0) % blocks
    last = jnp.broadcast_to(value[:, Q - 1 : Q], value.shape)
    taken[...] = jnp.zeros_like(taken)
    taken[0] = value
    for k in range(KW - 1):
        by = KW - 1 - k
        turned = pltpu.roll(value, by, 1)
        early = lane < by
        behind = jnp.where(early, pltpu.roll(turned, 1, 0), turned)
        taken[1 + k] = ((behind == value) & ~(early & (row == 0))).astype(F32)
        turned = pltpu.roll(value, Q - by, 1)
        late = lane >= Q - by
        beyond = jnp.where(late, pltpu.roll(turned, count - 1, 0), turned)
        taken[4 + k] = ((beyond == value) & ~(late & (row == blocks - 1))).astype(F32)
    taken[7] = ((pltpu.roll(last, 1, 0) == value) & (row > 0)).astype(F32)
    taken[8] = (last == value).astype(F32)
    for r in range(count):
        rows_ref[r] = value[r : r + 1, :]
        marks_ref[r] = jnp.concatenate([taken[i, r : r + 1, :] for i in range(16)], axis=0).T


def segment_marks(side, *parts):
    count = 2 * (LEN // Q)
    specs = [pl.BlockSpec((EXTRA, LANES), lambda t: (0, 0))] * PARTS
    marks, rows = pl.pallas_call(
        marks_kernel,
        grid=(1,),
        out_shape=[
            jax.ShapeDtypeStruct((count, Q, 16), F32),
            jax.ShapeDtypeStruct((count, 1, Q), F32),
        ],
        in_specs=[smem()] + specs,
        scratch_shapes=[pltpu.VMEM((count, Q), F32), pltpu.VMEM((16, count, Q), F32)],
        compiler_params=pltpu.CompilerParams(vmem_limit_bytes=56 * MIB),
        name="segment_marks",
    )(side, *parts)
    return marks.reshape(2, LEN, 16), rows.reshape(2, LEN // Q, 1, Q)


def weight_kernel(a_ref, *refs):
    *bs, out_ref, held, sems = refs
    copies, at = [], 0
    for i, b in enumerate(bs):
        copies.append(pltpu.make_async_copy(b, held.at[:, at : at + b.shape[1]], sems.at[i]))
        at += b.shape[1]

    @pl.when(pl.program_id(0) == 0)
    def _():
        for copy in copies:
            copy.start()
        for copy in copies:
            copy.wait()

    out_ref[...] = nn(a_ref[...], held[...]).astype(BF16)


def both_kernel(a_ref, b_ref, core_ref, mine_ref, theirs_ref, out_ref):
    each, rows, cols = out_ref.shape
    out_ref[:, :, : b_ref.shape[1]] = nn(a_ref[...], b_ref[...]).astype(BF16).reshape(each, rows, b_ref.shape[1])
    size = rows // 2
    blocks = mine_ref.shape[0] // size
    for k in range(each):
        zy = pl.program_id(0) * each + k
        at = pl.ds(pl.multiple_of(zy % blocks * size, 16), size)
        for own, ref in ((True, mine_ref), (False, theirs_ref)):

            @pl.when((zy // blocks == core_ref[0]) == own)
            def _():
                out_ref[k, :size, b_ref.shape[1] :] = ref[at, : D // 2]
                out_ref[k, size:, b_ref.shape[1] :] = ref[at, D // 2 :]


def both_products(count, core, a, b, mine, theirs):
    rows, total = a.shape
    each = 2
    tile = rows // count * each
    still = lambda t: (0, 0)
    return pl.pallas_call(
        both_kernel,
        grid=(count // each,),
        in_specs=[
            pl.BlockSpec((tile, total), lambda t: (t, 0)),
            pl.BlockSpec(b.shape, still),
            smem(),
            pl.BlockSpec(mine.shape, still),
            pl.BlockSpec(theirs.shape, still),
        ],
        out_specs=pl.BlockSpec((each, rows // count, b.shape[1] + D // 2), lambda t: (t, 0, 0)),
        out_shape=jax.ShapeDtypeStruct((count, rows // count, b.shape[1] + D // 2), BF16),
        compiler_params=pltpu.CompilerParams(vmem_limit_bytes=56 * MIB),
        cost_estimate=pl.CostEstimate(flops=8 * 10**9, bytes_accessed=20 * 10**6, transcendentals=0),
        name="both_products",
    )(a, b, core, mine, theirs)


def weight_product(a, *bs, tile=512):
    rows, total = a.shape
    tile = min(tile, rows)
    columns = sum(b.shape[1] for b in bs)
    return pl.pallas_call(
        weight_kernel,
        grid=(rows // tile,),
        in_specs=[pl.BlockSpec((tile, total), lambda t: (t, 0))] + anywhere(bs),
        out_specs=pl.BlockSpec((tile, columns), lambda t: (t, 0)),
        out_shape=jax.ShapeDtypeStruct((rows, columns), BF16),
        scratch_shapes=[pltpu.VMEM((total, columns), BF16), pltpu.SemaphoreType.DMA((len(bs),))],
        compiler_params=pltpu.CompilerParams(vmem_limit_bytes=56 * MIB),
        cost_estimate=pl.CostEstimate(flops=8 * 10**9, bytes_accessed=20 * 10**6, transcendentals=0),
        name="weight_product",
    )(a, *bs)


def finish_kernel(x_ref, cot_ref, gain_ref, own_ref, got_ref, *refs):
    *far, out_ref, held = refs
    for i, ref in enumerate(far):

        @pl.when(pl.program_id(0) == i)
        def _():
            held[...] = ref[...]

    d_normed = own_ref[...].astype(F32) + got_ref[...].astype(F32) + held[...].astype(F32)
    x = x_ref[...].astype(F32)
    inv = lax.rsqrt(jnp.mean(x * x, axis=-1, keepdims=True) + EPS)
    scaled = gain_ref[0:1, :] * d_normed
    shift = inv * inv * inv * jnp.mean(x * scaled, axis=-1, keepdims=True)
    out_ref[...] = cot_ref[...].astype(F32) + inv * scaled - x * shift


def finish_tokens(x, cot, gain, own, got, *far):
    rows = x.shape[0]
    size = rows // len(far)
    here = pl.BlockSpec((size, D), lambda t: (t, 0))
    still = pl.BlockSpec((size, D), lambda t: (0, 0))
    return pl.pallas_call(
        finish_kernel,
        grid=(len(far),),
        in_specs=[here, here, pl.BlockSpec((8, D), lambda t: (0, 0)), here, here] + [still] * len(far),
        out_specs=here,
        out_shape=jax.ShapeDtypeStruct((rows, D), F32),
        scratch_shapes=[pltpu.VMEM((size, D), BF16)],
        compiler_params=pltpu.CompilerParams(vmem_limit_bytes=56 * MIB),
        cost_estimate=pl.CostEstimate(flops=10**7, bytes_accessed=12 * 10**6, transcendentals=0),
        name="finish_tokens",
    )(x, cot, gain, own, got, *far)


def softplus(value):
    return jnp.maximum(value, 0.0) + jnp.log1p(jnp.exp(-jnp.abs(value)))


def conv_total(ext, shifts, raw, halo, taps_ref, marks):
    ext[0:8, :] = halo[8:16, :].astype(F32)
    ext[8 : 8 + Q, :] = raw.astype(F32)
    total = taps_ref[4:5, :] + ext[8 : 8 + Q, :] * taps_ref[3:4, :]
    for k in range(KW - 1):
        shifted = ext[5 + k : 5 + k + Q, :] * marks[:, 1 + k : 2 + k]
        if shifts is not None:
            shifts[k] = shifted
        total = total + shifted * taps_ref[k : k + 1, :]
    return total


def conv_back(d_total, ext, shifts, ahead, taps_ref, marks, sums_ref):
    sums_ref[4:5, :] += jnp.sum(d_total, axis=0, keepdims=True)
    sums_ref[3:4, :] += jnp.sum(d_total * ext[8 : 8 + Q, :], axis=0, keepdims=True)
    for k in range(KW - 1):
        sums_ref[k : k + 1, :] += jnp.sum(d_total * shifts[k], axis=0, keepdims=True)
    ext[0:Q, :] = d_total
    ext[Q : Q + 8, :] = ahead[...]
    d_raw = d_total * taps_ref[3:4, :]
    for k in range(KW - 1):
        d_raw = d_raw + ext[3 - k : 3 - k + Q, :] * (taps_ref[k : k + 1, :] * marks[:, 4 + k : 5 + k])
    ahead[...] = d_total[0:8, :]
    return d_raw


def scan_forward(
    part, side_ref, x_ref, x_halo, bc_ref, bc_halo, dt_ref, marks_ref, row_ref, x_taps, bc_taps, head_ref, heads_ref,
    *rest,
):
    if part > 0:
        before, rest = rest[6], rest[7:]
    y_ref, state_ref, bc_out, step_out, cum_out, turned_out, helds, exts, bc_exts = rest
    chunk = pl.program_id(0)

    @pl.when(chunk == 0)
    def _():
        helds[...] = before[...] if part > 0 else jnp.zeros_like(helds)

    at_row = lax.broadcasted_iota(jnp.int32, (Q, Q), 0)
    at_col = lax.broadcasted_iota(jnp.int32, (Q, Q), 1)
    lane = lax.broadcasted_iota(jnp.int32, (Q, LANES), 1)
    lower = (at_row >= at_col).astype(BF16)
    lower = jnp.concatenate([lower] * 3, axis=1)
    rate = -jnp.exp(head_ref[1:2, :])
    thin = []
    for s in range(2):
        marks = marks_ref[s]
        live = lane < MYH
        step = jnp.where(live, softplus(jnp.where(live, dt_ref[s].astype(F32), 0.0) + head_ref[0:1, :]), 0.0)
        cum = nn(lower, in_three(rate * step, 0))
        cum_t = cum.T
        step_out[s] = step
        cum_out[s] = cum
        turned_out[s, 0] = cum_t[:16, :]
        thin.append((step, cum, cum_t) + spreads(cum, marks))
    wide = over_heads_all([v for some in thin for v in (some[0],) + some[3:]], heads_ref)
    for s in range(2):
        marks = marks_ref[s]
        held = helds.at[s]
        _, cum, cum_t = thin[s][:3]
        step_wide, keep, tail, carry = wide[4 * s : 4 * s + 4]
        x_act = conv_total(exts.at[s], None, x_ref[s], x_halo[s], x_taps, marks)
        x_act = x_act * sigmoid(x_act)
        bc_act = conv_total(bc_exts.at[s], None, bc_ref[s], bc_halo[s], bc_taps, marks)
        bc_act = (bc_act * sigmoid(bc_act)).astype(BF16)
        bc_out[s] = bc_act
        b, c = bc_act[:, :NS], bc_act[:, NS:]
        shut = jnp.where((at_row >= at_col) & (marks[:, 0:1] == row_ref[s, 0]), 0.0, FAR)
        scores = nt(c, b)
        state = held[...]
        state_low = state.astype(BF16)
        state_ref[s, 0] = state_low
        x_step = x_act * step_wide
        y = nn(c, state_low) * keep + x_act * x_taps[5:6, :]
        held[...] = state * carry[0:1, :] + nn(b.T, (x_step * tail).astype(BF16))
        for pair in range(MYH // 2):
            cols = slice(pair * LANES, (pair + 1) * LANES)
            mixing = []
            for head in (2 * pair, 2 * pair + 1):
                spread = cum[:, head : head + 1] - cum_t[head : head + 1, :] + shut
                mixing.append((jnp.exp(spread) * scores).astype(BF16))
            steps = x_step[:, cols]
            both = jnp.concatenate(
                [jnp.where(lane < HD, steps, 0.0), jnp.where(lane < HD, 0.0, steps)], axis=0
            ).astype(BF16)
            y_ref[s, :, cols] = (y[:, cols] + nn(jnp.concatenate(mixing, axis=1), both)).astype(BF16)


def scan_backward(
    group, part, side_ref, x_ref, x_halo, bc_ref, step_ref, cum_ref, turned_ref, dy_ref, state_ref, marks_ref, row_ref,
    x_taps, head_ref, heads_ref, *rest,
):
    final = group == GROUPS - 1
    if group > 0:
        dbc_before, *rest = rest
    if final:
        bc_raw_ref, bc_halo, bc_taps, *rest = rest
    carried = 6 if final else 4
    if part > 0:
        before, rest = rest[3 : 3 + carried], rest[3 + carried :]
    dx_ref, dbc_ref, ddt_ref, wide_ref, thin_ref, *rest = rest
    if final:
        bc_sums, *rest = rest
    helds, aheads, *rest = rest
    if final:
        bc_aheads, *rest = rest
    exts, shifts, *rest = rest
    if final:
        bc_exts, bc_shifts = rest
    chunk = pl.program_id(0)

    @pl.when(chunk == 0)
    def _():
        running = [wide_ref, thin_ref] + ([bc_sums] if final else []) + [helds, aheads]
        running += [bc_aheads] if final else []
        for i, ref in enumerate(running):
            ref[...] = before[i][...] if part > 0 else jnp.zeros_like(ref)

    at_row = lax.broadcasted_iota(jnp.int32, (Q, Q), 0)
    at_col = lax.broadcasted_iota(jnp.int32, (Q, Q), 1)
    lane = lax.broadcasted_iota(jnp.int32, (Q, LANES), 1)
    low_lanes, high_lanes = group * GH, LANES - (group + 1) * GH
    upper = (at_row <= at_col).astype(BF16)
    strict = (at_row > at_col).astype(BF16)
    spans = jnp.concatenate([upper, upper, strict, strict], axis=1)
    rate = -jnp.exp(head_ref[1:2, :])
    thin = [(step_ref[s],) + spreads(cum_ref[s], marks_ref[s]) for s in range(2)]
    wide = over_heads_all([v for some in thin for v in some], heads_ref)
    made = []
    for s in range(2):
        marks = marks_ref[s]
        held = helds.at[s]
        step_wide, keep, tail, carry = wide[4 * s : 4 * s + 4]
        total = conv_total(exts.at[s], shifts.at[s], x_ref[s], x_halo[s], x_taps, marks)
        gate = sigmoid(total)
        x_act = total * gate
        slope = gate * (1.0 + total * (1.0 - gate))
        b, c = bc_ref[s, :, :NS], bc_ref[s, :, NS:]
        dy = dy_ref[s].astype(F32)
        x_step = x_act * step_wide
        state = state_ref[s, 0]
        d_state = held[...]
        d_state_low = d_state.astype(BF16)
        dy_keep = dy * keep
        dy_keep_low = dy_keep.astype(BF16)
        from_state = nn(c, state)
        d_c = nt(dy_keep_low, state)
        d_b = nt((x_step * tail).astype(BF16), d_state_low)
        du_tail = nn(b, d_state_low) * tail
        linked = jnp.sum(d_state * state.astype(F32), axis=0, keepdims=True)
        linked = jnp.broadcast_to(linked, (8, GC))
        held[...] = d_state * carry[0:1, :] + nn(c.T, dy_keep_low)
        made.append((dy, x_act, slope, x_step, b, c, d_b, d_c, du_tail, dy_keep * from_state, x_step * du_tail, linked))
    sums = sum_heads_all([v for some in made for v in some[9:]], heads_ref)
    d_us = []
    for s in range(2):
        marks = marks_ref[s]
        dy, x_act, slope, x_step, b, c, d_b, d_c, du_tail = made[s][:9]
        cum, cum_t = cum_ref[s], turned_ref[s, 0]
        shut = jnp.where((at_row <= at_col) & (marks[:, 0:1] == row_ref[s, 0]), 0.0, FAR)
        scores = nt(b, c)
        d_scores = jnp.zeros((Q, Q), F32)
        by_later, by_earlier, du_parts = [], [], []
        for pair in range(GH // 2):
            cols = slice(pair * LANES, (pair + 1) * LANES)
            steps, dys = x_step[:, cols], dy[:, cols]
            step_both = jnp.concatenate(
                [jnp.where(lane < HD, steps, 0.0), jnp.where(lane < HD, 0.0, steps)], axis=0
            ).astype(BF16)
            dy_both = jnp.concatenate(
                [jnp.where(lane < HD, dys, 0.0), jnp.where(lane < HD, 0.0, dys)], axis=0
            ).astype(BF16)
            met = nt(step_both, dys.astype(BF16))
            mixing = []
            for place in range(2):
                head = low_lanes + 2 * pair + place
                decay = jnp.exp(cum_t[head : head + 1, :] - cum[:, head : head + 1] + shut)
                mixing.append((decay * scores).astype(BF16))
                weighed = decay * met[place * Q : (place + 1) * Q, :]
                d_scores = d_scores + weighed
                spent = weighed * scores
                by_later.append(jnp.sum(spent, axis=0, keepdims=True))
                by_earlier.append(jnp.sum(spent, axis=1, keepdims=True))
            du_parts.append(nn(jnp.concatenate(mixing, axis=1), dy_both))
        du = jnp.concatenate(du_parts, axis=1) + du_tail
        d_low = d_scores.astype(BF16)
        d_b = d_b + nn(d_low, c)
        d_c = d_c + nn(d_scores.T.astype(BF16), b)
        d_bc = jnp.concatenate([d_b, d_c], axis=1)
        if group > 0:
            d_bc = d_bc + dbc_before[s]
        if final:
            bc_total = conv_total(bc_exts.at[s], bc_shifts.at[s], bc_raw_ref[s], bc_halo[s], bc_taps, marks)
            bc_gate = sigmoid(bc_total)
            d_bc = d_bc * (bc_gate * (1.0 + bc_total * (1.0 - bc_gate)))
            d_bc = conv_back(d_bc, bc_exts.at[s], bc_shifts.at[s], bc_aheads.at[s], bc_taps, marks, bc_sums)
        dbc_ref[s] = d_bc.astype(dbc_ref.dtype)
        later = by_later + [jnp.zeros((high_lanes, Q), F32)]
        later = ([jnp.zeros((low_lanes, Q), F32)] if low_lanes else []) + later
        later = jnp.concatenate(later, axis=0).T
        earlier = jnp.zeros((Q, LANES), F32)
        for head in range(GH):
            earlier = jnp.where(lane == low_lanes + head, by_earlier[head], earlier)
        d_us.append((du, later - earlier))
    d_steps = sum_heads_all([made[s][1] * d_us[s][0] for s in range(2)], heads_ref)
    for s in range(2):
        marks = marks_ref[s]
        dy, x_act, slope = made[s][:3]
        du, within = d_us[s]
        seen, sent, linked = sums[3 * s : 3 * s + 3]
        step = step_ref[s]
        linked = linked[0:1, :] * thin[s][3][0:1, :]
        mine = (lane >= low_lanes) & (lane < low_lanes + GH)
        crossed = jnp.concatenate([in_two(seen + within, 0), in_two(sent, 0)], axis=0)
        d_log = jnp.where(mine, nn(spans, crossed) + linked, 0.0)
        ddt_ref[s] = d_steps[s] + rate * d_log
        thin_ref[1:2, :] += jnp.sum(d_log * (rate * step), axis=0, keepdims=True)
        wide_ref[5:6, :] += jnp.sum(dy * x_act, axis=0, keepdims=True)
        d_total = (du * wide[4 * s] + dy * x_taps[5:6, :]) * slope
        d_raw = conv_back(d_total, exts.at[s], shifts.at[s], aheads.at[s], x_taps, marks, wide_ref)
        dx_ref[s] = d_raw.astype(BF16)


def block_at(time, side):
    blocks = LEN // Q
    return (time + side * (blocks // 2)) % blocks


def halo_at(time, side):
    return block_at(jnp.maximum(time - 1, 0), side) * (Q // 16) + Q // 16 - 1


BC_AT = MYC // BC
DT_AT = (MYC + BC) // LANES


def run_forward(part, side, first, marks, rows, x_taps, bc_taps, head_rows, heads, before):
    blocks = LEN // Q
    steps = blocks // 2
    now = lambda t: part * steps + t
    here = lambda col: lambda t, side: (0, block_at(now(t), side[0]), col)
    halo = lambda col: lambda t, side: (0, halo_at(now(t), side[0]), col)
    time = lambda t, side: (0, now(t), 0)
    time_four = lambda t, side: (0, now(t), 0, 0)
    still = lambda t, side: (0, 0)
    inputs = [first, first, first, first, first, marks, rows, x_taps, bc_taps, head_rows, heads]
    in_specs = [
        pl.BlockSpec((2, Q, MYC), here(0)),
        pl.BlockSpec((2, 16, MYC), halo(0)),
        pl.BlockSpec((2, Q, BC), here(BC_AT)),
        pl.BlockSpec((2, 16, BC), halo(BC_AT)),
        pl.BlockSpec((2, Q, LANES), here(DT_AT)),
        pl.BlockSpec((2, Q, 16), time),
        pl.BlockSpec((2, 1, 1, Q), time_four),
        pl.BlockSpec((8, MYC), still),
        pl.BlockSpec((8, BC), still),
        pl.BlockSpec((8, LANES), still),
        pl.BlockSpec((2 * LANES, MYC), still),
    ]
    running = pl.BlockSpec((2, NS, MYC), lambda t, side: (0, 0, 0))
    aliases = {}
    if part > 0:
        aliases = {1 + len(inputs) + i: i for i in range(6)}
        inputs += before
        in_specs += [pl.BlockSpec(memory_space=pl.ANY)] * 6 + [running]
    return pl.pallas_call(
        functools.partial(scan_forward, part),
        grid_spec=pltpu.PrefetchScalarGridSpec(
            num_scalar_prefetch=1,
            grid=(steps,),
            in_specs=in_specs,
            out_specs=[
                pl.BlockSpec((2, Q, MYC), here(0)),
                pl.BlockSpec((2, 1, NS, MYC), time_four),
                pl.BlockSpec((2, Q, BC), here(0)),
                pl.BlockSpec((2, Q, LANES), time),
                pl.BlockSpec((2, Q, LANES), time),
                pl.BlockSpec((2, 1, 16, Q), time_four),
                running,
            ],
            scratch_shapes=[pltpu.VMEM((2, Q + 8, MYC), F32), pltpu.VMEM((2, Q + 8, BC), F32)],
        ),
        out_shape=[
            jax.ShapeDtypeStruct((2, LEN, MYC), BF16),
            jax.ShapeDtypeStruct((2, blocks, NS, MYC), BF16),
            jax.ShapeDtypeStruct((2, LEN, BC), BF16),
            jax.ShapeDtypeStruct((2, LEN, LANES), F32),
            jax.ShapeDtypeStruct((2, LEN, LANES), F32),
            jax.ShapeDtypeStruct((2, blocks, 16, Q), F32),
            jax.ShapeDtypeStruct((2, NS, MYC), F32),
        ],
        input_output_aliases=aliases,
        compiler_params=pltpu.CompilerParams(vmem_limit_bytes=18 * MIB),
        cost_estimate=pl.CostEstimate(flops=9 * 10**9, bytes_accessed=30 * 10**6, transcendentals=10**7),
        name="scan_forward_%d" % part,
    )(side, *inputs)


def run_backward(group, part, side, first, scanned, d_ssm, marks, rows, x_taps, bc_taps, head_rows, heads, d_bc, before):
    _, states, bc_act, step, cum, turned, _ = scanned
    blocks = LEN // Q
    steps = blocks // 2
    final = group == GROUPS - 1
    now = lambda t: blocks - 1 - part * steps - t
    here = lambda col: lambda t, side: (0, block_at(now(t), side[0]), col)
    halo = lambda col: lambda t, side: (0, halo_at(now(t), side[0]), col)
    time = lambda t, side: (0, now(t), 0)
    time_four = lambda col: lambda t, side: (0, now(t), 0, col)
    still = lambda t, side: (0, 0)
    still_three = lambda t, side: (0, 0, 0)
    share = lambda t, side: (0, group)
    in_specs = [
        pl.BlockSpec((2, Q, GC), here(group)),
        pl.BlockSpec((2, 16, GC), halo(group)),
        pl.BlockSpec((2, Q, BC), here(0)),
        pl.BlockSpec((2, Q, LANES), time),
        pl.BlockSpec((2, Q, LANES), time),
        pl.BlockSpec((2, 1, 16, Q), time_four(0)),
        pl.BlockSpec((2, Q, GC), here(group)),
        pl.BlockSpec((2, 1, NS, GC), time_four(group)),
        pl.BlockSpec((2, Q, 16), time),
        pl.BlockSpec((2, 1, 1, Q), time_four(0)),
        pl.BlockSpec((8, GC), share),
        pl.BlockSpec((8, LANES), still),
        pl.BlockSpec((2 * LANES, GC), share),
    ]
    inputs = [first, first, bc_act, step, cum, turned, d_ssm, states, marks, rows, x_taps, head_rows, heads]
    if group > 0:
        in_specs.append(pl.BlockSpec((2, Q, BC), here(0)))
        inputs.append(d_bc)
    if final:
        in_specs += [
            pl.BlockSpec((2, Q, BC), here(BC_AT)),
            pl.BlockSpec((2, 16, BC), halo(BC_AT)),
            pl.BlockSpec((8, BC), still),
        ]
        inputs += [first, first, bc_taps]
    running = [(8, GC), (8, LANES)] + ([(8, BC)] if final else []) + [(2, NS, GC), (2, 8, GC)]
    running += [(2, 8, BC)] if final else []
    running_specs = [pl.BlockSpec(v, still if len(v) == 2 else still_three) for v in running]
    out_specs = [
        pl.BlockSpec((2, Q, GC), here(0)),
        pl.BlockSpec((2, Q, BC), here(0)),
        pl.BlockSpec((2, Q, LANES), here(0)),
    ] + running_specs
    out_shape = [
        jax.ShapeDtypeStruct((2, LEN, GC), BF16),
        jax.ShapeDtypeStruct((2, LEN, BC), BF16 if final else F32),
        jax.ShapeDtypeStruct((2, LEN, LANES), F32),
    ] + [jax.ShapeDtypeStruct(v, F32) for v in running]
    aliases = {}
    if part > 0:
        aliases = {1 + len(inputs) + i: i for i in range(3)}
        in_specs += [pl.BlockSpec(memory_space=pl.ANY)] * 3 + running_specs
        inputs += before
    scratch = [pltpu.VMEM((2, Q + 8, GC), F32), pltpu.VMEM((2, KW - 1, Q, GC), F32)]
    if final:
        scratch += [pltpu.VMEM((2, Q + 8, BC), F32), pltpu.VMEM((2, KW - 1, Q, BC), F32)]
    return pl.pallas_call(
        functools.partial(scan_backward, group, part),
        grid_spec=pltpu.PrefetchScalarGridSpec(
            num_scalar_prefetch=1, grid=(steps,), in_specs=in_specs, out_specs=out_specs, scratch_shapes=scratch
        ),
        out_shape=out_shape,
        input_output_aliases=aliases,
        compiler_params=pltpu.CompilerParams(vmem_limit_bytes=56 * MIB),
        cost_estimate=pl.CostEstimate(flops=14 * 10**9, bytes_accessed=40 * 10**6, transcendentals=10**7),
        name="scan_backward_%d_%d" % (group, part),
    )(side, *inputs)


def lead(value, by):
    if by == 0:
        return value
    pad = [(0, 0)] * value.ndim
    if by > 0:
        pad[1] = (0, by)
        return jnp.pad(value, pad)[:, by:]
    pad[1] = (-by, 0)
    return jnp.pad(value, pad)[:, :by]


def fold(block):
    return jnp.concatenate([block[..., : D // 2], block[..., D // 2 :]], axis=-2)


def unfold(block):
    half = block.shape[-2] // 2
    return jnp.concatenate([block[..., :half, :], block[..., half:, :]], axis=-1)


def out_whole(out_weight, split, core, side):
    whole = lax.all_gather(out_weight, ("zy", "core", "seq"), axis=0, tiled=True)
    return pick(pick(split_heads(whole, 0, split), core), side)


def out_scattered(grad, split, core, side):
    own = jnp.zeros((2, 2, MYC, D), BF16)
    own = lax.dynamic_update_slice(own, grad.astype(BF16)[None, None], (core, side, 0, 0))
    whole = join_heads(own, 0, split)
    return lax.psum_scatter(whole, ("zy", "core", "seq"), scatter_dimension=0, tiled=True)


def own_slice(whole, size):
    at = (lax.axis_index("zy") * 2 + lax.axis_index("core")) * 2 + lax.axis_index("seq")
    return lax.dynamic_slice_in_dim(whole, at * size, size, 0)


def body(
    tokens,
    segments,
    norm_gain,
    in_weight,
    conv_weight,
    conv_bias,
    dt_bias,
    a_log,
    d_skip,
    gated_gain,
    out_weight,
    cotangent,
):
    count = lax.axis_size("zy")
    core, side = lax.axis_index("core"), lax.axis_index("seq")
    split = head_split(count)
    rows = tokens.shape[1]
    total = PARTS * rows

    blocked = split[0] > 1

    me = (core * 2 + side).astype(jnp.int32).reshape(1)
    at_side = side.astype(jnp.int32).reshape(1)
    at_core = core.astype(jnp.int32).reshape(1)
    at_ring = jnp.stack([ring_place(count)[0], core, core * 2 + side]).astype(jnp.int32)

    heads = np.kron(np.eye(LANES, MYH, dtype=np.float32), np.ones((1, HD), np.float32))
    heads = jnp.asarray(np.concatenate([heads, heads], axis=0), BF16)
    per_head = jnp.stack([dt_bias, a_log, d_skip])
    per_head = jnp.pad(per_head, ((0, 5), (0, LANES - NH)))

    sizes = (norm_gain.shape[0], conv_bias.shape[0], gated_gain.shape[0])
    seg_own = segments[0].reshape(-1, LANES)
    mix = split_columns(in_weight, norm_gain, conv_weight, conv_bias, gated_gain, seg_own, split, me)
    mix = Task(peer_steps(mix))
    stage([mix])
    sent, later = assemble_rows(mix.value, me)
    ring = Task(gather_steps(sent))
    token_all = Task(token_steps(tokens[0], 3))
    marks, seg_rows = stage([ring, token_all], functools.partial(segment_marks, at_side), *mix.value)
    if blocked:
        held = Task(single_step((out_weight, GROUP, DIAGONAL)))
        for _ in range(count // 2 - 2):
            stage([ring, token_all])
        stage([ring, token_all, held])
        later = jnp.concatenate([later, fold(held.value)], axis=1)
    else:
        w_out = out_whole(out_weight, split, core, side)
    while not (ring.done and token_all.done):
        stage([ring, token_all])

    near, far, both = token_all.value
    w_pieces = ring.value
    ring = Task(gather_steps(later))
    cot_all = Task(token_steps(cotangent[0], 3))
    first, turned, x_taps, bc_taps, head_rows, gain = stage(
        [ring, cot_all], functools.partial(project, at_ring, split, sizes), tokens[0], near, far, both, per_head, heads, w_pieces
    )
    first_by_seq = first.reshape(2, LEN, W1)

    def forward(part, first, before):
        return run_forward(part, at_side, first, marks, seg_rows, x_taps, bc_taps, head_rows, heads, before)

    scanned = stage([ring, cot_all], functools.partial(forward, 0), first_by_seq, None)
    scanned = stage([ring, cot_all], functools.partial(forward, 1), first_by_seq, scanned)
    while not (ring.done and cot_all.done):
        stage([ring, cot_all])
    y = scanned[0].reshape(total, MYC)
    if blocked:
        w_out = put_together(ring.value, slice(MYC, 2 * MYC), core * (count // 2))
        blocks = [w_out[: count // 2], swap(w_out[count // 2 :], "core")]
    else:
        blocks = [w_out]
    gate_pieces = ring.value
    cot_rows = (cotangent[0], *cot_all.value)
    z, d_two, sums, w_out = meet(at_ring, *cot_rows, turned, y, x_taps, blocks, ring.value)
    sums = Task(group_steps(sums))
    stage([sums])
    unit = DI // (count * PARTS) if blocked else MYC // 2
    d_ssm, d_gate, mine, theirs, own, other = gate_back(
        at_core, unit, sums.value, y, z, d_two, x_taps, w_out
    )

    branch = Task(sum_steps(own, other, 3))
    d_theirs, d_mine = out_product(theirs, mine, *cot_rows)
    d_theirs = Task(single_step((d_theirs, "core", SWAP)))
    d_ssm = d_ssm.reshape(2, LEN, MYC)

    def back(group, part, d_bc, before):
        def run(first, d_ssm, scanned, d_bc, before):
            return run_backward(
                group, part, at_side, first, scanned, d_ssm, marks, seg_rows, x_taps, bc_taps, head_rows, heads, d_bc, before
            )

        return run, first_by_seq, d_ssm, scanned, d_bc, before

    zero = stage([d_theirs, branch], *back(0, 0, None, None))
    if blocked:
        d_w_gate = both_products(count, at_core, turned, d_gate, d_mine, d_theirs.value)
    else:
        d_w_gate = weight_product(turned, d_gate).reshape(count, D // count, MYC)
    gate_ring = Task(scatter_steps(d_w_gate))

    zero = stage([gate_ring, branch], *back(0, 1, None, zero))
    one = stage([gate_ring, branch], *back(1, 0, zero[1], None))
    one = stage([gate_ring, branch], *back(1, 1, zero[1], one))
    d_x0, _, d_dt0, wide0, thin0 = zero[:5]
    d_x1, d_bc, d_dt1, wide1, thin1, bc_sums = one[:6]
    wide = jnp.concatenate([wide0, wide1], axis=1)
    thin = thin0 + thin1
    d_dt = (d_dt0 + d_dt1).reshape(total, LANES)
    d_dt = d_dt * lax.logistic(first[:, MYC + BC :].astype(F32) + head_rows[:1])
    d_rows = [d_x0.reshape(total, GC), d_x1.reshape(total, GC), d_bc.reshape(total, BC), d_dt.astype(BF16)]
    far_other, far = stage([gate_ring, branch], functools.partial(normed_part, 1), at_ring, *d_rows, d_gate, w_pieces, gate_pieces)
    while not (branch.done and gate_ring.done):
        stage([gate_ring, branch])
    far = Task(far_steps(far, far_other, 4))
    d_w_first = stage([far], weight_product, turned, *d_rows)
    rest = Task(scatter_steps(d_w_first.reshape(count, D // count, W1)))
    near_other, near = stage([rest, far], functools.partial(normed_part, 0), at_ring, *d_rows, d_gate, w_pieces, gate_pieces)
    near = Task(single_step((near_other, "core", SWAP))), near
    small_grads = Task(small_sum_steps(
        (
            wide[:KW].reshape(-1),
            wide[KW],
            bc_sums[: KW + 1].reshape(-1),
            jnp.sum(d_dt, axis=0)[:MYH],
            thin[1, :MYH],
            jnp.sum(wide[KW + 1].reshape(MYH, HD), axis=1),
        ),
        core, side,
    ))
    gate_sum = sum(v.astype(F32) for v in gate_ring.value).astype(BF16)
    tasks = [rest, far, near[0], small_grads]
    if blocked:
        d_out = Task(single_step((unfold(gate_sum[:, MYC:]), GROUP, DIAGONAL)))
        tasks.append(d_out)
    stage(tasks)
    if blocked:
        d_out = d_out.value.astype(F32)
    else:
        d_mine, d_theirs = jnp.where(core == 0, d_mine, d_theirs.value), jnp.where(core == 0, d_theirs.value, d_mine)
        d_out = out_scattered(jnp.concatenate([d_mine, d_theirs], axis=0), split, core, side).astype(F32)

    def ends(x, branch, out_weight, gated_gain, d_out):
        gain_two = jnp.sum(out_weight.astype(F32) * d_out, axis=1) / gated_gain.astype(F32)
        return (x.astype(F32) + branch).astype(BF16), gain_two

    block_out, gain_two = stage(
        [rest, far, small_grads], ends, tokens[0], branch.value, out_weight, gated_gain, d_out
    )
    while not (rest.done and far.done):
        stage([rest, far, small_grads])

    d_w = Task(peer_steps(hand_back(*rest.value, gate_sum[:, :MYC], me)))
    input_grad = stage(
        [d_w, small_grads], finish_tokens, tokens[0], cotangent[0], gain, near[1], near[0].value, *far.value
    )
    finish([d_w, small_grads])
    in_sh, gain_one = join_columns(d_w.value, split, me, in_weight, jnp.broadcast_to(norm_gain[:, None], (norm_gain.shape[0], LANES)))

    taps_x, bias_x, taps_bc, bias_dt, alog, skip = small_grads.value
    taps_x = jnp.swapaxes(taps_x.reshape(2, 2, KW, MYC), 2, 3)
    taps_bc = jnp.sum(taps_bc, axis=(0, 1)).reshape(KW + 1, BC)
    conv_w = jnp.concatenate([join_heads(taps_x, 0, split), taps_bc[:KW].T], axis=0)
    conv_b = jnp.concatenate([join_heads(bias_x, 0, split), taps_bc[KW]])
    return (
        block_out[None],
        input_grad[None],
        gain_one[:, 0],
        in_sh,
        own_slice(conv_w, conv_bias.shape[0]),
        own_slice(conv_b, conv_bias.shape[0]),
        join_heads(bias_dt, 0, split),
        join_heads(alog, 0, split),
        join_heads(skip, 0, split),
        gain_two,
        d_out,
    )


def solution(mesh):
    fsdp, seq = mesh.shape["fsdp"], mesh.shape["seq"]
    grid = Mesh(mesh.devices.reshape(fsdp // 2, 2, seq), ("zy", "core", "seq"))
    every = ("zy", "core", "seq")
    rows = P(("zy", "core"), "seq", None)
    in_specs = (
        rows,
        P(("zy", "core"), "seq"),
        P(every),
        P(every, None),
        P(every, None),
        P(every),
        P(),
        P(),
        P(),
        P(every),
        P(every, None),
        rows,
    )
    out_specs = (
        rows,
        rows,
        P(every),
        P(every, None),
        P(every, None),
        P(every),
        P(),
        P(),
        P(),
        P(every),
        P(every, None),
    )
    return jax.shard_map(body, mesh=grid, in_specs=in_specs, out_specs=out_specs, check_vma=False)
```

```python
import functools

import jax
import jax.numpy as jnp
import numpy as np
from jax import lax
from jax.experimental import pallas as pl
from jax.experimental.pallas import tpu as pltpu
from jax.sharding import Mesh
from jax.sharding import PartitionSpec as P

D = 1536
NH = 48
HD = 64
NS = 128
KW = 4
DI = 3072
CONV = 3328
LEN = 1024

EPS = 1e-05
HIGH = lax.Precision.HIGHEST
F32 = jnp.float32
BF16 = jnp.bfloat16

PARTS = 4
MYH = NH // PARTS
MYC = MYH * HD
LANES = 128
BC = 2 * NS
W1 = MYC + BC + LANES
GROUPS = 2
GH = MYH // GROUPS
GC = GH * HD
Q = 128
FAR = -1e30
MIB = 1024 * 1024

SWAP = [(0, 1), (1, 0)]


def swap(value, axis):
    return lax.ppermute(value, axis, SWAP)


def pick(value, at, dim=0):
    return lax.dynamic_index_in_dim(value, at, dim, False)


def in_order(mine, other, place):
    buf = jnp.zeros((2,) + mine.shape, mine.dtype)
    buf = lax.dynamic_update_index_in_dim(buf, mine, place, 0)
    return lax.dynamic_update_index_in_dim(buf, other, 1 - place, 0)


GROUP = ("core", "seq")


def to_peer(value, r):
    return (value, GROUP, [(g, g ^ r) for g in range(PARTS)])


def ring_order(count):
    return list(range(0, count, 2)) + list(range(count - 1, 0, -2))


def ring_pairs(count):
    order = ring_order(count)
    right = [(order[i], order[(i + 1) % count]) for i in range(count)]
    return right, [(b, a) for a, b in right]


def ring_order_of(at, count):
    at = at % count
    return jnp.where(at < count // 2, 2 * at, 2 * (count - at) - 1)


def ring_place(count):
    zy = lax.axis_index("zy")
    place = jnp.where(zy % 2 == 0, zy // 2, count - 1 - zy // 2)
    return place, lambda at: ring_order_of(at, count)


def half_of(rows):
    return 16 * (rows // 32) if rows >= 32 else rows // 2


def piece_places(count, rows):
    places = [(0, 0)]
    for step in range(1, count // 2):
        places += [(-step, 0), (step, 0)]
    return places + [(count // 2, 0), (count // 2, half_of(rows))]


class Task:
    def __init__(self, steps):
        self.steps, self.value, self.done = steps, None, False
        self.moves = next(steps, None)
        self.done = self.moves is None

    def take(self, arrived):
        try:
            self.moves = self.steps.send(arrived)
        except StopIteration as end:
            self.value, self.done = end.value, True


def stage(tasks, work=None, *args):
    tasks = [t for t in tasks if not t.done]
    values = [[m[0] for m in t.moves] for t in tasks]
    values, args = lax.optimization_barrier((values, args))
    arrived = [
        [lax.ppermute(v, m[1], m[2]) for v, m in zip(vs, t.moves)] for vs, t in zip(values, tasks)
    ]
    result = None if work is None else work(*args)
    if work is None:
        arrived = lax.optimization_barrier(arrived)
    else:
        arrived, result = lax.optimization_barrier((arrived, result))
    for t, got in zip(tasks, arrived):
        t.take(got)
    return result


def finish(tasks):
    while not all(t.done for t in tasks):
        stage(tasks)


def gather_steps(block):
    count = lax.axis_size("zy")
    half = half_of(block.shape[0])
    right, left = ring_pairs(count)
    pieces = [block]
    ahead = back = block
    for _ in range(1, count // 2):
        ahead, back = yield [(ahead, "zy", right), (back, "zy", left)]
        pieces += [ahead, back]
    pieces += yield [(ahead[:half], "zy", right), (back[half:], "zy", left)]
    return pieces


def put_together(pieces, columns, flip):
    count = lax.axis_size("zy")
    place, order = ring_place(count)
    rows = pieces[0].shape[0]
    full = jnp.zeros((count, rows, columns.stop - columns.start), pieces[0].dtype)
    for piece, (step, row) in zip(pieces, piece_places(count, rows)):
        full = lax.dynamic_update_slice(full, piece[None, :, columns], (order(place + step + count) ^ flip, row, 0))
    return full


def add_kernel(at_ref, one_ref, two_ref, ahead_ref, back_ref, first_ref, second_ref):
    def add(out_ref, full, got, start):
        end = start + got.shape[0]
        out_ref[start:end, :] = (full[start:end, :].astype(F32) + got[...].astype(F32)).astype(BF16)
        if start > 0:
            out_ref[:start, :] = full[:start, :]
        if end < out_ref.shape[0]:
            out_ref[end:, :] = full[end:, :]

    rows = first_ref.shape[0]
    add(first_ref, one_ref[0], ahead_ref, 0)
    add(second_ref, two_ref[0], back_ref, rows - back_ref.shape[0])


def ring_add(full, one, two, ahead, back):
    _, rows, cols = full.shape
    tile = cols // 3
    at = jnp.stack([one, two]).astype(jnp.int32)
    return pl.pallas_call(
        add_kernel,
        grid_spec=pltpu.PrefetchScalarGridSpec(
            num_scalar_prefetch=1,
            grid=(3,),
            in_specs=[
                pl.BlockSpec((1, rows, tile), lambda t, at: (at[0], 0, t)),
                pl.BlockSpec((1, rows, tile), lambda t, at: (at[1], 0, t)),
                pl.BlockSpec((ahead.shape[0], tile), lambda t, at: (0, t)),
                pl.BlockSpec((back.shape[0], tile), lambda t, at: (0, t)),
            ],
            out_specs=[pl.BlockSpec((rows, tile), lambda t, at: (0, t))] * 2,
        ),
        out_shape=[jax.ShapeDtypeStruct((rows, cols), BF16)] * 2,
        compiler_params=pltpu.CompilerParams(vmem_limit_bytes=16 * MIB),
        name="ring_add",
    )(at, full, full, ahead, back)


def scatter_steps(full):
    count, rows, cols = full.shape
    half = half_of(rows)
    right, left = ring_pairs(count)
    place, order = ring_place(count)
    far = lax.dynamic_index_in_dim(full, order(place + count // 2), 0, False)
    one, two = far[:half], far[half:]
    for step in range(count // 2 - 1, -1, -1):
        ahead, back = yield [(one, "zy", right), (two, "zy", left)]
        if step > 0:
            one, two = ring_add(full, order(place + step), order(place + count - step), ahead, back)
    return lax.dynamic_index_in_dim(full, order(place), 0, False), ahead, back


def single_step(move):
    (got,) = yield [move]
    return got


def group_steps(value):
    got = yield [to_peer(value, r) for r in range(1, PARTS)]
    return [value] + list(got)


def piece_cuts(rows, pieces):
    return [16 * (rows // 16 * i // pieces) for i in range(pieces + 1)]


def token_steps(value, pieces):
    cuts = piece_cuts(value.shape[0], pieces)
    far, both = [], []
    moves = [(value, "core", SWAP)]
    for i in range(pieces):
        got = yield moves + [(value[cuts[i] : cuts[i + 1]], "seq", SWAP)]
        if i == 0:
            near = got[0]
        else:
            both.append(got[0])
        far.append(got[-1])
        moves = [(got[-1], "core", SWAP)]
    (got,) = yield moves
    return near, far, both + [got]


def peer_steps(blocks):
    got = yield [to_peer(blocks[r], r) for r in range(1, PARTS)]
    return [blocks[0]] + list(got)


def sum_steps(own, other, pieces):
    (got,) = yield [(other, "core", SWAP)]
    rows = own.shape[0] // 2
    sent = (own[rows:].astype(F32) + got[rows:].astype(F32)).astype(BF16)
    cuts = piece_cuts(rows, pieces)
    arrived = []
    for a, b in zip(cuts, cuts[1:]):
        (far,) = yield [(sent[a:b], "seq", SWAP)]
        arrived.append(far)
    return own[:rows].astype(F32) + got[:rows].astype(F32) + jnp.concatenate(arrived, axis=0).astype(F32)


def far_steps(own, other, parts):
    (got,) = yield [(other, "core", SWAP)]
    sent = (own.astype(F32) + got.astype(F32)).astype(BF16)
    cuts = [0] + [int(v) * sent.shape[0] // 16 for v in np.cumsum(parts)]
    arrived = []
    for a, b in zip(cuts, cuts[1:]):
        (got,) = yield [(sent[a:b], "seq", SWAP)]
        arrived.append(got)
    return arrived


def small_sum_steps(parts, core, side):
    count = lax.axis_size("zy")
    lengths = [p.shape[0] for p in parts]
    packed = jnp.concatenate(parts)
    packed = jnp.pad(packed, (0, -packed.shape[0] % 1024)).reshape(-1, LANES)
    bit = 1
    while bit < count:
        (got,) = yield [(packed, "zy", [(i, i ^ bit) for i in range(count)])]
        packed = packed + got
        bit *= 2
    (got,) = yield [(packed, "core", SWAP)]
    packed = in_order(packed, got, core)
    (got,) = yield [(packed, "seq", SWAP)]
    packed = jnp.swapaxes(in_order(packed, got, side), 0, 1).reshape(2, 2, -1)
    return jnp.split(packed, np.cumsum(lengths), axis=2)[: len(lengths)]


def zy_exchange(value, bit):
    count = lax.axis_size("zy")
    return lax.ppermute(value, "zy", [(i, i ^ bit) for i in range(count)])


def zy_sum(value):
    count = lax.axis_size("zy")
    bit = 1
    while bit < count:
        value = value + zy_exchange(value, bit)
        bit *= 2
    return value


def head_split(count):
    rows = DI // count
    if rows % (2 * HD) == 0 and count % 2 == 0:
        return count // 2, rows // (2 * HD)
    return 1, MYH


def split_heads(value, dim, split):
    q, i = split
    size = value.shape[dim]
    unit = size // NH
    shape = value.shape
    value = value.reshape(shape[:dim] + (2, q, 2, i * unit) + shape[dim + 1 :])
    value = jnp.swapaxes(value, dim + 1, dim + 2)
    return value.reshape(shape[:dim] + (2, 2, size // PARTS) + shape[dim + 1 :])


def join_heads(value, dim, split):
    q, i = split
    shape = value.shape
    mine = shape[dim + 2]
    value = value.reshape(shape[:dim] + (2, 2, q, mine // q) + shape[dim + 3 :])
    value = jnp.swapaxes(value, dim + 1, dim + 2)
    return value.reshape(shape[:dim] + (PARTS * mine,) + shape[dim + 3 :])


HALF = LANES // 2
EXTRA = 16
SEG_AT = 8


def half_places(split, core, side):
    q, i = split
    return [((core * q + at) * 2 + side) * i + k for at in range(q) for k in range(i)]


def halves(tile_of, places):
    tiles = []
    for at in range(0, len(places), 2):
        one, two = places[at], places[at + 1]
        if one % 2 == 0 and two == one + 1:
            tiles.append(tile_of(one // 2))
            continue
        left, right = tile_of(one // 2), tile_of(two // 2)
        left = pltpu.roll(left, HALF, 1) if one % 2 else left
        right = right if two % 2 else pltpu.roll(right, HALF, 1)
        lane = lax.broadcasted_iota(jnp.int32, left.shape, 1)
        tiles.append(jnp.where(lane < HALF, left, right))
    return tiles


def head_choice(split):
    choice = np.zeros((PARTS, LANES, LANES), np.float32)
    for g in range(PARTS):
        for lane, head in enumerate(half_places(split, g // 2, g % 2)):
            choice[g, head, lane] = 1.0
    return choice


def split_kernel(split, at_ref, w_ref, gain_ref, taps_ref, bias_ref, gated_ref, seg_ref, choice_ref, *refs):
    *outs, out_ref, small_ref = refs
    me = at_ref[0]
    small_ref[...] = jnp.zeros_like(small_ref)
    for row, ref in ((0, gain_ref), (1, bias_ref), (6, gated_ref)):
        small_ref[row : row + 1, : ref.shape[1]] = ref[...].astype(F32)
    small_ref[2 : 2 + KW, : taps_ref.shape[1]] = taps_ref[...].astype(F32)
    small_ref[SEG_AT : SEG_AT + seg_ref.shape[0], :] = seg_ref[...].astype(F32)

    def tile_of(base):
        return lambda t: w_ref[:, base + t * LANES : base + (t + 1) * LANES].astype(F32)

    bc = w_ref[:, 2 * DI : 2 * DI + BC]
    steps = w_ref[:, DI + CONV :]
    for g in range(PARTS):
        places = half_places(split, g // 2, g % 2)
        at = me ^ g
        tiles = halves(tile_of(DI), places)
        for k, tile in enumerate(tiles):
            out_ref[at, :, k * LANES : (k + 1) * LANES] = tile.astype(BF16)
        out_ref[at, :, MYC : MYC + BC] = bc
        out_ref[at, :, MYC + BC : W1] = nn(steps, choice_ref[g, :NH, :]).astype(BF16)
        for k, tile in enumerate(halves(tile_of(0), places)):
            out_ref[at, :, W1 + k * LANES : W1 + (k + 1) * LANES] = tile.astype(BF16)
    for r, ref in enumerate(outs):
        ref[:EXTRA, :LANES] = small_ref[...].astype(BF16)
        ref[:EXTRA, LANES:] = jnp.zeros((EXTRA, W1 + MYC - LANES), BF16)
        ref[EXTRA:, :] = out_ref[r]


def smem(shape=None):
    return pl.BlockSpec(memory_space=pltpu.SMEM)


def split_columns(weight, gain, taps, bias, gated, segs, split, me):
    return pl.pallas_call(
        functools.partial(split_kernel, split),
        out_shape=[jax.ShapeDtypeStruct((EXTRA + weight.shape[0], W1 + MYC), BF16)] * PARTS,
        in_specs=[smem()] + [pl.BlockSpec()] * 7,
        scratch_shapes=[
            pltpu.VMEM((PARTS, weight.shape[0], W1 + MYC), BF16),
            pltpu.VMEM((EXTRA, LANES), F32),
        ],
        compiler_params=pltpu.CompilerParams(vmem_limit_bytes=56 * MIB),
        name="split_columns",
    )(me, weight, gain[None], taps.T, bias[None], gated[None], segs, jnp.asarray(head_choice(split), BF16))


def assemble_kernel(at_ref, one, two, three, four, first_ref, gate_ref):
    me = at_ref[0]
    rows = one.shape[0] - EXTRA
    first_ref[:EXTRA, :] = jnp.zeros((EXTRA, W1), BF16)
    for r, ref in enumerate((one, two, three, four)):
        at = me ^ r
        first_ref[pl.ds(pl.multiple_of(EXTRA + at * rows, 16), rows), :] = ref[EXTRA:, :W1]
        gate_ref[pl.ds(pl.multiple_of(at * rows, 16), rows), :] = ref[EXTRA:, W1:]
        for g in range(PARTS):

            @pl.when(at == g)
            def _():
                first_ref[:EXTRA, g * LANES : (g + 1) * LANES] = ref[:EXTRA, :LANES]


def assemble_plain(at_ref, one, two, three, four, extra_ref, first_ref, gate_ref):
    me = at_ref[0]
    extra_ref[...] = jnp.zeros_like(extra_ref)
    for r, ref in enumerate((one, two, three, four)):
        at = me ^ r
        first_ref[at] = ref[EXTRA:, :W1]
        gate_ref[at] = ref[EXTRA:, W1:]
        for g in range(PARTS):

            @pl.when(at == g)
            def _():
                extra_ref[:, g * LANES : (g + 1) * LANES] = ref[:EXTRA, :LANES]


def assemble_rows(blocks, me):
    rows = blocks[0].shape[0] - EXTRA
    if rows % 16 == 0:
        return pl.pallas_call(
            assemble_kernel,
            out_shape=[
                jax.ShapeDtypeStruct((EXTRA + PARTS * rows, W1), BF16),
                jax.ShapeDtypeStruct((PARTS * rows, MYC), BF16),
            ],
            in_specs=[smem()] + [pl.BlockSpec()] * PARTS,
            compiler_params=pltpu.CompilerParams(vmem_limit_bytes=56 * MIB),
            name="assemble_rows",
        )(me, *blocks)
    extra, first, gate = pl.pallas_call(
        assemble_plain,
        out_shape=[
            jax.ShapeDtypeStruct((EXTRA, W1), BF16),
            jax.ShapeDtypeStruct((PARTS, rows, W1), BF16),
            jax.ShapeDtypeStruct((PARTS, rows, MYC), BF16),
        ],
        in_specs=[smem()] + [pl.BlockSpec()] * PARTS,
        name="assemble_rows",
    )(me, *blocks)
    first = jnp.concatenate([extra, first.reshape(PARTS * rows, W1)], axis=0)
    return first, gate.reshape(PARTS * rows, MYC)


def hand_back_kernel(at_ref, own, ahead, back, gate, *refs):
    outs, out_ref = refs[:-1], refs[-1]
    me = at_ref[0]
    for g in range(PARTS):
        first = own[g].astype(F32) + ahead[g].astype(F32) + back[g].astype(F32)
        out_ref[me ^ g, :, :W1] = first.astype(BF16)
        out_ref[me ^ g, :, W1:] = gate[g].astype(BF16)
    for r, ref in enumerate(outs):
        ref[...] = out_ref[r]


def hand_back(own, ahead, back, gate, me):
    blocks = [b.reshape(PARTS, -1, b.shape[1]) for b in (own, ahead, back, gate)]
    return pl.pallas_call(
        hand_back_kernel,
        out_shape=[jax.ShapeDtypeStruct((blocks[0].shape[1], W1 + MYC), BF16)] * PARTS,
        in_specs=[smem()] + [pl.BlockSpec()] * len(blocks),
        scratch_shapes=[pltpu.VMEM((PARTS, blocks[0].shape[1], W1 + MYC), BF16)],
        compiler_params=pltpu.CompilerParams(vmem_limit_bytes=32 * MIB),
        name="hand_back",
    )(me, *blocks)


def join_kernel(split, at_ref, one, two, three, four, choice_ref, w_ref, gain_ref, out_ref, grad_ref, by):
    me = at_ref[0]
    for r, ref in enumerate((one, two, three, four)):
        by[me ^ r] = ref[...].astype(F32)
    where = {}
    for g in range(PARTS):
        for at, place in enumerate(half_places(split, g // 2, g % 2)):
            where[place] = (g, at)

    def put(base, column):
        for t in range(DI // LANES):
            tiles = []
            for k in range(2):
                g, at = where[2 * t + k]
                start = column + at // 2 * LANES
                tile = by[g, :, start : start + LANES]
                tiles.append(tile if at % 2 == k else pltpu.roll(tile, HALF, 1))
            lane = lax.broadcasted_iota(jnp.int32, tiles[0].shape, 1)
            out_ref[:, base + t * LANES : base + (t + 1) * LANES] = jnp.where(lane < HALF, tiles[0], tiles[1])

    put(0, W1)
    put(DI, 0)
    out_ref[:, 2 * DI : 2 * DI + BC] = sum(by[g, :, MYC : MYC + BC] for g in range(PARTS))
    out_ref[:, DI + CONV :] = sum(
        nt(by[g, :, MYC + BC : W1].astype(BF16), choice_ref[g, :NH, :]) for g in range(PARTS)
    )
    met = jnp.sum(out_ref[...] * w_ref[...].astype(F32), axis=1, keepdims=True)
    grad_ref[...] = jnp.broadcast_to(met / gain_ref[:, 0:1].astype(F32), grad_ref.shape)


def join_columns(blocks, split, me, weight, gain):
    rows = blocks[0].shape[0]
    return pl.pallas_call(
        functools.partial(join_kernel, split),
        out_shape=[
            jax.ShapeDtypeStruct((rows, 2 * DI + BC + NH), F32),
            jax.ShapeDtypeStruct((rows, LANES), F32),
        ],
        in_specs=[smem()] + [pl.BlockSpec()] * (PARTS + 3),
        scratch_shapes=[pltpu.VMEM((PARTS, rows, W1 + MYC), F32)],
        name="join_columns",
    )(me, *blocks, jnp.asarray(head_choice(split), BF16), weight, gain)


DIAGONAL = [(0, 0), (1, 2), (2, 1), (3, 3)]


def sigmoid(value):
    return 0.5 * jnp.tanh(0.5 * value) + 0.5


def nt(a, b):
    return lax.dot_general(a, b, (((1,), (1,)), ((), ())), preferred_element_type=F32)


def nn(a, b):
    return lax.dot_general(a, b, (((1,), (0,)), ((), ())), preferred_element_type=F32)


def tn(a, b):
    return lax.dot_general(a, b, (((0,), (0,)), ((), ())), preferred_element_type=F32)


def exact(a, b):
    return lax.dot_general(
        a, b, (((1,), (0,)), ((), ())), preferred_element_type=F32, precision=HIGH
    )


def in_two(value, axis):
    top = value.astype(BF16)
    return jnp.concatenate([top, (value - top.astype(F32)).astype(BF16)], axis=axis)


def in_three(value, axis):
    top = value.astype(BF16)
    rest = value - top.astype(F32)
    mid = rest.astype(BF16)
    return jnp.concatenate([top, mid, (rest - mid.astype(F32)).astype(BF16)], axis=axis)


def over_heads(value, heads_ref):
    return nn(in_two(value, 1), heads_ref[...])


def over_heads_all(values, heads_ref):
    wide = over_heads(jnp.concatenate(values, axis=0), heads_ref)
    cuts = np.cumsum([0] + [v.shape[0] for v in values])
    return [wide[a:b, :] for a, b in zip(cuts, cuts[1:])]


def sum_heads_all(values, heads_ref):
    thin = sum_heads(jnp.concatenate(values, axis=0), heads_ref)
    cuts = np.cumsum([0] + [v.shape[0] for v in values])
    return [thin[a:b, :] for a, b in zip(cuts, cuts[1:])]


def spreads(cum, marks):
    last = cum[Q - 1 : Q, :]
    return (
        jnp.exp(cum) * marks[:, 7:8],
        jnp.exp(last - cum) * marks[:, 8:9],
        jnp.broadcast_to(jnp.exp(last) * marks[Q - 1 : Q, 7:8], (8, LANES)),
    )


def sum_heads(value, heads_ref):
    return nt(value.astype(BF16), heads_ref[:LANES, :])


ROWS = LEN // 2


def row_copies(sources, held, sems):
    half = len(sources) // 2
    copies, at = [], 0
    for q, refs in enumerate((sources[:1], sources[2 : 1 + half], sources[1:2], sources[1 + half :])):
        copies.append([])
        row = 0
        for ref in refs:
            size = ref.shape[0]
            copies[q].append(pltpu.make_async_copy(ref, held.at[q, row : row + size, :], sems.at[at]))
            row += size
            at += 1
    return copies


def wait_rows(step, copies):
    for q, some in enumerate(copies):

        @pl.when(step == q)
        def _():
            for copy in some:
                copy.wait()


def piece_copies(at_ref, refs, full_ref, count, sems, extra=0, small_ref=None, columns=None):
    block = refs[0].shape[0]
    rows = block - extra
    copies, smalls = [], []
    start_col, width = (0, full_ref.shape[1]) if columns is None else columns
    for i, (ref, (step, row)) in enumerate(zip(refs, piece_places(count, block))):
        zy = ring_order_of(at_ref[0] + step + count, count)
        skip = extra if row == 0 else 0
        start = zy * rows + row + skip - extra
        size = ref.shape[0] - skip
        to = full_ref.at[pl.ds(pl.multiple_of(start, 16), size), start_col : start_col + width]
        copies.append(pltpu.make_async_copy(ref.at[skip : skip + size, :width], to, sems.at[2 * i]))
        if skip and small_ref is not None:
            to = small_ref.at[pl.ds(pl.multiple_of(zy * extra, 16), extra), :]
            smalls.append(pltpu.make_async_copy(ref.at[:skip, : PARTS * LANES], to, sems.at[2 * i + 1]))
    return copies, smalls


def anywhere(values):
    return [pl.BlockSpec(memory_space=pltpu.HBM) for _ in values]


def project_kernel(count, parts, split, sizes, at_ref, *refs):
    sources, refs = refs[:parts], refs[parts:]
    per_head_ref, choice_ref, wide_ref, *refs = refs
    pieces, refs = refs[: count + 1], refs[count + 1 :]
    (first_ref, turned_ref, x_ref, bc_ref, head_ref, gain_ref,
     w_ref, held, small_ref, params_ref, row_sems, piece_sems) = refs
    step = pl.program_id(0)
    rows = row_copies(sources, held, row_sems)

    @pl.when(step == 0)
    def _():
        weights, smalls = piece_copies(at_ref, pieces, w_ref, count, piece_sems, EXTRA, small_ref)
        for copy in smalls + weights + sum(rows, []):
            copy.start()
        for copy in smalls:
            copy.wait()
        unpack_small(at_ref, split, sizes, small_ref, per_head_ref, choice_ref, wide_ref, gain_ref, x_ref, bc_ref, head_ref, params_ref)
        for copy in weights:
            copy.wait()

    wait_rows(step, rows)
    x = held[step].astype(F32)
    inv = lax.rsqrt(jnp.mean(x * x, axis=-1, keepdims=True) + EPS)
    low = (x * inv * gain_ref[0:1, :]).astype(BF16)
    turned_ref[...] = low.T
    first_ref[...] = nn(low, w_ref[...]).astype(BF16)


def project(place, split, sizes, own, near, far, both, per_head, heads, pieces):
    rows = own.shape[0]
    total = PARTS * rows
    count = lax.axis_size("zy")
    still = lambda t, *_: (0, 0)
    choice = jnp.asarray(head_choice(split), BF16)
    return pl.pallas_call(
        functools.partial(project_kernel, count, 2 + len(far) + len(both), split, sizes),
        grid_spec=pltpu.PrefetchScalarGridSpec(
            num_scalar_prefetch=1,
            grid=(total // ROWS,),
            in_specs=anywhere((own, near, *far, *both))
            + [
                pl.BlockSpec((8, LANES), still),
                pl.BlockSpec(choice.shape, lambda t, *_: (0, 0, 0)),
                pl.BlockSpec((2 * LANES, MYC), still),
            ]
            + anywhere(pieces),
            out_specs=[
                pl.BlockSpec((ROWS, W1), lambda t, *_: (t, 0)),
                pl.BlockSpec((D, ROWS), lambda t, *_: (0, t)),
                pl.BlockSpec((8, MYC), still),
                pl.BlockSpec((8, BC), still),
                pl.BlockSpec((8, LANES), still),
                pl.BlockSpec((8, D), still),
            ],
            scratch_shapes=[
                pltpu.VMEM((D, W1), BF16),
                pltpu.VMEM((PARTS, rows, D), BF16),
                pltpu.VMEM((count * EXTRA, PARTS * LANES), BF16),
                pltpu.VMEM((8, DI), F32),
                pltpu.SemaphoreType.DMA((2 + len(far) + len(both),)),
                pltpu.SemaphoreType.DMA((2 * len(pieces),)),
            ],
        ),
        out_shape=[
            jax.ShapeDtypeStruct((total, W1), BF16),
            jax.ShapeDtypeStruct((D, total), BF16),
            jax.ShapeDtypeStruct((8, MYC), F32),
            jax.ShapeDtypeStruct((8, BC), F32),
            jax.ShapeDtypeStruct((8, LANES), F32),
            jax.ShapeDtypeStruct((8, D), F32),
        ],
        compiler_params=pltpu.CompilerParams(vmem_limit_bytes=56 * MIB),
        cost_estimate=pl.CostEstimate(flops=12 * 10**9, bytes_accessed=30 * 10**6, transcendentals=10**4),
        name="project",
    )(place, own, near, *far, *both, per_head, choice, heads, *pieces)


def silu_of(z):
    sig = sigmoid(z)
    return sig, z * sig


def meet_kernel(count, parts, blocked, at_ref, *refs):
    sources, refs = refs[:parts], refs[parts:]
    turned_ref, y_ref, taps_ref, *refs = refs
    blocks, refs = refs[: 1 + blocked], refs[1 + blocked :]
    *pieces, z_ref, d_two_ref, sums_ref, w_out_ref, w_ref, held, row_sems, piece_sems, out_sems = refs
    step = pl.program_id(0)
    half = D // 2
    rows = row_copies(sources, held, row_sems)

    @pl.when(step == 0)
    def _():
        copies, _ = piece_copies(at_ref, pieces, w_ref, count, piece_sems)
        if blocked:
            each, size, _ = blocks[0].shape
            size = size // 2
            for q in range(each):
                for i, (ref, part) in enumerate(zip(blocks, (at_ref[1], 1 - at_ref[1]))):
                    to = pl.ds(pl.multiple_of((2 * q + part) * size, 16), size)
                    for k in range(2):
                        copies.append(
                            pltpu.make_async_copy(
                                ref.at[q, k * size : (k + 1) * size, :],
                                w_out_ref.at[to, k * half : (k + 1) * half],
                                out_sems.at[4 * q + 2 * i + k],
                            )
                        )
        else:
            copies.append(pltpu.make_async_copy(blocks[0], w_out_ref, out_sems.at[0]))
        for copy in copies + sum(rows, []):
            copy.start()
        for copy in copies:
            copy.wait()

    wait_rows(step, rows)
    z = tn(turned_ref[...], w_ref[...]).astype(BF16)
    z_ref[...] = z
    _, silu = silu_of(z.astype(F32))
    joined = y_ref[...].astype(F32) * silu
    d_two = nt(held[step], w_out_ref[...])
    d_two_ref[...] = d_two.astype(BF16)
    row = lax.broadcasted_iota(jnp.int32, (8, MYC), 0)
    squares = nt((row == 0).astype(BF16), (joined * joined).astype(BF16))
    products = nt((row == 1).astype(BF16), (joined * taps_ref[6:7, :] * d_two).astype(BF16))
    sums_ref[...] = squares + products


def meet(place, own, near, far, both, turned, y, x_taps, blocks, pieces):
    rows = own.shape[0]
    total = PARTS * rows
    count = lax.axis_size("zy")
    still = lambda t, *_: (0, 0)
    here = lambda t, *_: (t, 0)
    blocked = len(blocks) > 1
    return pl.pallas_call(
        functools.partial(meet_kernel, count, 2 + len(far) + len(both), blocked),
        grid_spec=pltpu.PrefetchScalarGridSpec(
            num_scalar_prefetch=1,
            grid=(total // ROWS,),
            in_specs=anywhere((own, near, *far, *both))
            + [
                pl.BlockSpec((D, ROWS), lambda t, *_: (0, t)),
                pl.BlockSpec((ROWS, MYC), here),
                pl.BlockSpec((8, MYC), still),
            ]
            + anywhere((*blocks, *pieces)),
            out_specs=[
                pl.BlockSpec((ROWS, MYC), here),
                pl.BlockSpec((ROWS, MYC), here),
                pl.BlockSpec((8, ROWS), lambda t, *_: (0, t)),
                pl.BlockSpec((MYC, D), still),
            ],
            scratch_shapes=[
                pltpu.VMEM((D, MYC), BF16),
                pltpu.VMEM((PARTS, rows, D), BF16),
                pltpu.SemaphoreType.DMA((2 + len(far) + len(both),)),
                pltpu.SemaphoreType.DMA((2 * len(pieces),)),
                pltpu.SemaphoreType.DMA((4 * blocks[0].shape[0] if blocked else 1,)),
            ],
        ),
        out_shape=[
            jax.ShapeDtypeStruct((total, MYC), BF16),
            jax.ShapeDtypeStruct((total, MYC), BF16),
            jax.ShapeDtypeStruct((8, total), F32),
            jax.ShapeDtypeStruct((MYC, D), BF16),
        ],
        compiler_params=pltpu.CompilerParams(vmem_limit_bytes=56 * MIB),
        cost_estimate=pl.CostEstimate(flops=15 * 10**9, bytes_accessed=40 * 10**6, transcendentals=10**6),
        name="meet",
    )(place, own, near, *far, *both, turned, y, x_taps, *blocks, *pieces)


def out_kernel(parts, *refs):
    sources, refs = refs[:parts], refs[parts:]
    theirs_ref, mine_ref, d_theirs_ref, d_mine_ref, held, sems = refs
    step = pl.program_id(0)
    rows = row_copies(sources, held, sems)

    @pl.when(step == 0)
    def _():
        for copy in sum(rows, []):
            copy.start()
        for copy in sum(rows, []):
            copy.wait()

    for at, a_ref, out_ref in ((0, theirs_ref, d_theirs_ref), (2, mine_ref, d_mine_ref)):

        @pl.when((step >= at) & (step < at + 2))
        def _():
            every = held[...].reshape(PARTS * ROWS, D)
            out_ref[...] = nn(a_ref[...], every).astype(BF16)


def out_product(theirs, mine, own, near, far, both):
    rows, total = theirs.shape
    tile = rows // 2
    one = lambda t: (jnp.minimum(t, 1), 0)
    two = lambda t: (jnp.maximum(t - 2, 0), 0)
    return pl.pallas_call(
        functools.partial(out_kernel, 2 + len(far) + len(both)),
        grid=(4,),
        in_specs=anywhere((own, near, *far, *both))
        + [pl.BlockSpec((tile, total), one), pl.BlockSpec((tile, total), two)],
        out_specs=[pl.BlockSpec((tile, D), one), pl.BlockSpec((tile, D), two)],
        out_shape=[jax.ShapeDtypeStruct((rows, D), BF16)] * 2,
        scratch_shapes=[
            pltpu.VMEM((PARTS, ROWS, D), BF16),
            pltpu.SemaphoreType.DMA((2 + len(far) + len(both),)),
        ],
        compiler_params=pltpu.CompilerParams(vmem_limit_bytes=56 * MIB),
        cost_estimate=pl.CostEstimate(flops=8 * 10**9, bytes_accessed=20 * 10**6, transcendentals=0),
        name="out_product",
    )(own, near, *far, *both, theirs, mine)


def gate_kernel(
    unit, core_ref, sums_0, sums_1, sums_2, sums_3, y_ref, z_ref, d_two_ref, taps_ref, w_out_ref,
    d_ssm_ref, d_gate_ref, mine_ref, theirs_ref, own_ref, other_ref, turned,
):
    step = pl.program_id(0)
    sums = (sums_0[...] + sums_1[...] + sums_2[...] + sums_3[...]).T
    inv = lax.rsqrt(sums[:, 0:1] * (1.0 / DI) + EPS)
    shift = inv * inv * inv * (sums[:, 1:2] * (1.0 / DI))
    z = z_ref[...].astype(F32)
    sig, silu = silu_of(z)
    y = y_ref[...].astype(F32)
    joined = y * silu
    d_two = d_two_ref[...].astype(F32)
    two = (joined * inv * taps_ref[6:7, :]).astype(BF16)
    d_joined = inv * (taps_ref[6:7, :] * d_two) - joined * shift
    d_ssm_ref[...] = (d_joined * silu).astype(BF16)
    d_gate_ref[...] = (d_joined * y * (sig * (1.0 + z * (1.0 - sig)))).astype(BF16)
    branch = nn(two, w_out_ref[...]).astype(BF16)

    @pl.when(step < 4)
    def _():
        own_ref[...] = branch

    @pl.when(step >= 4)
    def _():
        other_ref[...] = branch

    turned[...] = two.T
    core = core_ref[0]
    for at in range(MYC // (2 * unit)):
        to = slice(at * unit, (at + 1) * unit)
        mine_ref[to, :] = turned[pl.ds(pl.multiple_of((2 * at + core) * unit, 16), unit), :]
        theirs_ref[to, :] = turned[pl.ds(pl.multiple_of((2 * at + 1 - core) * unit, 16), unit), :]


def gate_back(core, unit, sums, y, z, d_two, x_taps, w_out):
    total = y.shape[0]
    size = ROWS // 2
    still = lambda t, *_: (0, 0)
    here = lambda t, *_: (t, 0)
    across = lambda t, *_: (0, t)
    return pl.pallas_call(
        functools.partial(gate_kernel, unit),
        grid_spec=pltpu.PrefetchScalarGridSpec(
            num_scalar_prefetch=1,
            grid=(total // size,),
            in_specs=[pl.BlockSpec((8, size), lambda t, *_, r=r: (0, t ^ (2 * r))) for r in range(PARTS)]
            + [
                pl.BlockSpec((size, MYC), here),
                pl.BlockSpec((size, MYC), here),
                pl.BlockSpec((size, MYC), here),
                pl.BlockSpec((8, MYC), still),
                pl.BlockSpec((MYC, D), still),
            ],
            out_specs=[
                pl.BlockSpec((size, MYC), here),
                pl.BlockSpec((size, MYC), here),
                pl.BlockSpec((MYC // 2, size), across),
                pl.BlockSpec((MYC // 2, size), across),
                pl.BlockSpec((size, D), lambda t, *_: (jnp.minimum(t, 3), 0)),
                pl.BlockSpec((size, D), lambda t, *_: (jnp.maximum(t - 4, 0), 0)),
            ],
            scratch_shapes=[pltpu.VMEM((MYC, size), BF16)],
        ),
        out_shape=[
            jax.ShapeDtypeStruct((total, MYC), BF16),
            jax.ShapeDtypeStruct((total, MYC), BF16),
            jax.ShapeDtypeStruct((MYC // 2, total), BF16),
            jax.ShapeDtypeStruct((MYC // 2, total), BF16),
            jax.ShapeDtypeStruct((total // 2, D), BF16),
            jax.ShapeDtypeStruct((total // 2, D), BF16),
        ],
        compiler_params=pltpu.CompilerParams(vmem_limit_bytes=56 * MIB),
        cost_estimate=pl.CostEstimate(flops=8 * 10**9, bytes_accessed=30 * 10**6, transcendentals=10**6),
        name="gate_back",
    )(core, *sums, y, z, d_two, x_taps, w_out)


def normed_kernel(count, at, parts, at_ref, *refs):
    values, refs = refs[:parts], refs[parts:]
    firsts, gates, refs = refs[: count + 1], refs[count + 1 : 2 * count + 2], refs[2 * count + 2 :]
    other_ref, own_ref, weight, rows, first_sems, gate_sems, row_sems = refs
    step = pl.program_id(0)
    copies, _ = piece_copies(at_ref, firsts, weight, count, first_sems, EXTRA, columns=(0, W1))
    copies += piece_copies(at_ref, gates, weight, count, gate_sems, columns=(W1, MYC))[0]
    row_copies_of = []
    for i in range(2):
        start, col = (2 * (1 - i) + at) * ROWS, 0
        row_copies_of.append([])
        for k, ref in enumerate(values):
            width = ref.shape[1]
            row_copies_of[i].append(
                pltpu.make_async_copy(
                    ref.at[start : start + ROWS, :], rows.at[i, :, col : col + width], row_sems.at[i, k]
                )
            )
            col += width

    @pl.when(step == 0)
    def _():
        for copy in row_copies_of[0] + copies + row_copies_of[1]:
            copy.start()
        for copy in copies:
            copy.wait()

    for i, ref in enumerate((other_ref, own_ref)):

        @pl.when(step == i)
        def _():
            for copy in row_copies_of[i]:
                copy.wait()
            ref[...] = nt(rows[i], weight[...]).astype(BF16)


def normed_part(at, place, d_x0, d_x1, d_bc, d_dt, d_gate, firsts, gates):
    still = lambda t, *_: (0, 0)
    values = [d_x0, d_x1, d_bc, d_dt, d_gate]
    count = len(firsts) - 1
    return pl.pallas_call(
        functools.partial(normed_kernel, count, at, len(values)),
        grid_spec=pltpu.PrefetchScalarGridSpec(
            num_scalar_prefetch=1,
            grid=(2,),
            in_specs=anywhere((*values, *firsts, *gates)),
            out_specs=[pl.BlockSpec((ROWS, D), still)] * 2,
            scratch_shapes=[
                pltpu.VMEM((D, W1 + MYC), BF16),
                pltpu.VMEM((2, ROWS, W1 + MYC), BF16),
                pltpu.SemaphoreType.DMA((2 * len(firsts),)),
                pltpu.SemaphoreType.DMA((2 * len(gates),)),
                pltpu.SemaphoreType.DMA((2, len(values))),
            ],
        ),
        out_shape=[jax.ShapeDtypeStruct((ROWS, D), BF16)] * 2,
        compiler_params=pltpu.CompilerParams(vmem_limit_bytes=56 * MIB),
        cost_estimate=pl.CostEstimate(flops=8 * 10**9, bytes_accessed=20 * 10**6, transcendentals=0),
        name="normed_part_%d" % at,
    )(place, *values, *firsts, *gates)


def flat(small, row, count, spread, size):
    every = small[:, row, :]
    rows = jnp.concatenate([every[:, g * LANES : (g + 1) * LANES] for g in range(PARTS)], axis=0)
    value = nn(rows.astype(BF16), spread)
    at = lax.broadcasted_iota(jnp.int32, value.shape, 0)
    device = (at % count) * PARTS + at // count
    lane = lax.broadcasted_iota(jnp.int32, value.shape, 1)
    own = (lane >= device * size) & (lane < (device + 1) * size)
    return jnp.sum(jnp.where(own, value, 0.0), axis=0, keepdims=True)


def spread_of(size, count):
    shape = (LANES, count * PARTS * size)
    lane = lax.broadcasted_iota(jnp.int32, shape, 1).astype(F32)
    part = lane - jnp.floor((lane + 0.5) * (1.0 / size)) * size
    return (part == lax.broadcasted_iota(jnp.int32, shape, 0).astype(F32)).astype(BF16)


def unpack_small(at_ref, split, sizes, small_ref, per_head_ref, choice_ref, wide_ref, gain_ref, x_ref, bc_ref, head_ref, held):
    group = at_ref[2]
    count = small_ref.shape[0] // EXTRA
    small = small_ref[...].astype(F32).reshape(count, EXTRA, PARTS * LANES)
    gain_ref[...] = jnp.broadcast_to(flat(small, 0, count, spread_of(sizes[0], count), sizes[0]), gain_ref.shape)
    spread = spread_of(sizes[1], count)
    conv = [flat(small, r, count, spread, sizes[1]) for r in (2, 3, 4, 5, 1)]
    for k, v in enumerate(conv):
        held[k : k + 1, :] = v[:, :DI]
        bc_ref[k : k + 1, :] = v[:, DI:]
    bc_ref[5:8, :] = jnp.zeros((3, BC), F32)
    held[6:7, :] = flat(small, 6, count, spread_of(sizes[2], count), sizes[2])
    held[5:6, :] = jnp.zeros((1, DI), F32)
    held[7:8, :] = jnp.zeros((1, DI), F32)
    per_head = in_three(per_head_ref[...], 1)
    mine = jnp.zeros((8, LANES), F32)
    for g in range(PARTS):
        chosen = nn(per_head, jnp.concatenate([choice_ref[g]] * 3, axis=0))
        mine = jnp.where(group == g, chosen, mine)

        @pl.when(group == g)
        def _():
            tiles = halves(lambda t: held[:, t * LANES : (t + 1) * LANES], half_places(split, g // 2, g % 2))
            for k, tile in enumerate(tiles):
                x_ref[:, k * LANES : (k + 1) * LANES] = tile

    head_ref[...] = mine
    wide = jnp.concatenate([wide_ref[:LANES, :]] * 3, axis=0)
    x_ref[5:6, :] = nn(in_three(mine, 1), wide)[2:3, :]


def marks_kernel(side_ref, *refs):
    *parts, marks_ref, rows_ref, seg, taken = refs
    side = side_ref[0]
    blocks = LEN // Q
    for s in range(2):
        for j in range(blocks):
            half, row = j // (blocks // 2), j % (blocks // 2)
            near, far = parts[2 * s + half], parts[2 * s + 1 - half]
            at = slice(SEG_AT + row, SEG_AT + row + 1)
            to = s * blocks + j
            seg[to : to + 1, :] = jnp.where(side == 0, near[at, :LANES].astype(F32), far[at, :LANES].astype(F32))
    value = seg[...]
    count = 2 * blocks
    lane = lax.broadcasted_iota(jnp.int32, value.shape, 1)
    row = lax.broadcasted_iota(jnp.int32, value.shape, 0) % blocks
    last = jnp.broadcast_to(value[:, Q - 1 : Q], value.shape)
    taken[...] = jnp.zeros_like(taken)
    taken[0] = value
    for k in range(KW - 1):
        by = KW - 1 - k
        turned = pltpu.roll(value, by, 1)
        early = lane < by
        behind = jnp.where(early, pltpu.roll(turned, 1, 0), turned)
        taken[1 + k] = ((behind == value) & ~(early & (row == 0))).astype(F32)
        turned = pltpu.roll(value, Q - by, 1)
        late = lane >= Q - by
        beyond = jnp.where(late, pltpu.roll(turned, count - 1, 0), turned)
        taken[4 + k] = ((beyond == value) & ~(late & (row == blocks - 1))).astype(F32)
    taken[7] = ((pltpu.roll(last, 1, 0) == value) & (row > 0)).astype(F32)
    taken[8] = (last == value).astype(F32)
    for r in range(count):
        rows_ref[r] = value[r : r + 1, :]
        marks_ref[r] = jnp.concatenate([taken[i, r : r + 1, :] for i in range(16)], axis=0).T


def segment_marks(side, *parts):
    count = 2 * (LEN // Q)
    specs = [pl.BlockSpec((EXTRA, LANES), lambda t: (0, 0))] * PARTS
    marks, rows = pl.pallas_call(
        marks_kernel,
        grid=(1,),
        out_shape=[
            jax.ShapeDtypeStruct((count, Q, 16), F32),
            jax.ShapeDtypeStruct((count, 1, Q), F32),
        ],
        in_specs=[smem()] + specs,
        scratch_shapes=[pltpu.VMEM((count, Q), F32), pltpu.VMEM((16, count, Q), F32)],
        compiler_params=pltpu.CompilerParams(vmem_limit_bytes=56 * MIB),
        name="segment_marks",
    )(side, *parts)
    return marks.reshape(2, LEN, 16), rows.reshape(2, LEN // Q, 1, Q)


def weight_kernel(a_ref, *refs):
    *bs, out_ref, held, sems = refs
    copies, at = [], 0
    for i, b in enumerate(bs):
        copies.append(pltpu.make_async_copy(b, held.at[:, at : at + b.shape[1]], sems.at[i]))
        at += b.shape[1]

    @pl.when(pl.program_id(0) == 0)
    def _():
        for copy in copies:
            copy.start()
        for copy in copies:
            copy.wait()

    out_ref[...] = nn(a_ref[...], held[...]).astype(BF16)


def both_kernel(a_ref, b_ref, core_ref, mine_ref, theirs_ref, out_ref):
    each, rows, cols = out_ref.shape
    out_ref[:, :, : b_ref.shape[1]] = nn(a_ref[...], b_ref[...]).astype(BF16).reshape(each, rows, b_ref.shape[1])
    size = rows // 2
    blocks = mine_ref.shape[0] // size
    for k in range(each):
        zy = pl.program_id(0) * each + k
        at = pl.ds(pl.multiple_of(zy % blocks * size, 16), size)
        for own, ref in ((True, mine_ref), (False, theirs_ref)):

            @pl.when((zy // blocks == core_ref[0]) == own)
            def _():
                out_ref[k, :size, b_ref.shape[1] :] = ref[at, : D // 2]
                out_ref[k, size:, b_ref.shape[1] :] = ref[at, D // 2 :]


def both_products(count, core, a, b, mine, theirs):
    rows, total = a.shape
    each = 2
    tile = rows // count * each
    still = lambda t: (0, 0)
    return pl.pallas_call(
        both_kernel,
        grid=(count // each,),
        in_specs=[
            pl.BlockSpec((tile, total), lambda t: (t, 0)),
            pl.BlockSpec(b.shape, still),
            smem(),
            pl.BlockSpec(mine.shape, still),
            pl.BlockSpec(theirs.shape, still),
        ],
        out_specs=pl.BlockSpec((each, rows // count, b.shape[1] + D // 2), lambda t: (t, 0, 0)),
        out_shape=jax.ShapeDtypeStruct((count, rows // count, b.shape[1] + D // 2), BF16),
        compiler_params=pltpu.CompilerParams(vmem_limit_bytes=56 * MIB),
        cost_estimate=pl.CostEstimate(flops=8 * 10**9, bytes_accessed=20 * 10**6, transcendentals=0),
        name="both_products",
    )(a, b, core, mine, theirs)


def weight_product(a, *bs, tile=512):
    rows, total = a.shape
    tile = min(tile, rows)
    columns = sum(b.shape[1] for b in bs)
    return pl.pallas_call(
        weight_kernel,
        grid=(rows // tile,),
        in_specs=[pl.BlockSpec((tile, total), lambda t: (t, 0))] + anywhere(bs),
        out_specs=pl.BlockSpec((tile, columns), lambda t: (t, 0)),
        out_shape=jax.ShapeDtypeStruct((rows, columns), BF16),
        scratch_shapes=[pltpu.VMEM((total, columns), BF16), pltpu.SemaphoreType.DMA((len(bs),))],
        compiler_params=pltpu.CompilerParams(vmem_limit_bytes=56 * MIB),
        cost_estimate=pl.CostEstimate(flops=8 * 10**9, bytes_accessed=20 * 10**6, transcendentals=0),
        name="weight_product",
    )(a, *bs)


def finish_kernel(x_ref, cot_ref, gain_ref, own_ref, got_ref, *refs):
    *far, out_ref, held, sems = refs
    step = pl.program_id(0)
    copies, row = [], 0
    for i, ref in enumerate(far):
        copies.append(pltpu.make_async_copy(ref, held.at[row : row + ref.shape[0], :], sems.at[i]))
        row += ref.shape[0]

    @pl.when(step == 0)
    def _():
        for copy in copies:
            copy.start()
        for copy in copies:
            copy.wait()

    d_normed = own_ref[...].astype(F32) + got_ref[...].astype(F32)
    d_normed = d_normed + held[pl.ds(pl.multiple_of(step * Q, Q), Q), :].astype(F32)
    x = x_ref[...].astype(F32)
    inv = lax.rsqrt(jnp.mean(x * x, axis=-1, keepdims=True) + EPS)
    scaled = gain_ref[0:1, :] * d_normed
    shift = inv * inv * inv * jnp.mean(x * scaled, axis=-1, keepdims=True)
    out_ref[...] = cot_ref[...].astype(F32) + inv * scaled - x * shift


def finish_tokens(x, cot, gain, own, got, *far):
    rows = x.shape[0]
    here = pl.BlockSpec((Q, D), lambda t: (t, 0))
    return pl.pallas_call(
        finish_kernel,
        grid=(rows // Q,),
        in_specs=[here, here, pl.BlockSpec((8, D), lambda t: (0, 0)), here, here] + anywhere(far),
        out_specs=here,
        out_shape=jax.ShapeDtypeStruct((rows, D), F32),
        scratch_shapes=[pltpu.VMEM((rows, D), BF16), pltpu.SemaphoreType.DMA((len(far),))],
        compiler_params=pltpu.CompilerParams(vmem_limit_bytes=56 * MIB),
        cost_estimate=pl.CostEstimate(flops=8 * 10**9, bytes_accessed=50 * 10**6, transcendentals=0),
        name="finish_tokens",
    )(x, cot, gain, own, got, *far)


def softplus(value):
    return jnp.maximum(value, 0.0) + jnp.log1p(jnp.exp(-jnp.abs(value)))


def conv_total(ext, shifts, raw, halo, taps_ref, marks):
    ext[0:8, :] = halo[8:16, :].astype(F32)
    ext[8 : 8 + Q, :] = raw.astype(F32)
    total = taps_ref[4:5, :] + ext[8 : 8 + Q, :] * taps_ref[3:4, :]
    for k in range(KW - 1):
        shifted = ext[5 + k : 5 + k + Q, :] * marks[:, 1 + k : 2 + k]
        if shifts is not None:
            shifts[k] = shifted
        total = total + shifted * taps_ref[k : k + 1, :]
    return total


def conv_back(d_total, ext, shifts, ahead, taps_ref, marks, sums_ref):
    sums_ref[4:5, :] += jnp.sum(d_total, axis=0, keepdims=True)
    sums_ref[3:4, :] += jnp.sum(d_total * ext[8 : 8 + Q, :], axis=0, keepdims=True)
    for k in range(KW - 1):
        sums_ref[k : k + 1, :] += jnp.sum(d_total * shifts[k], axis=0, keepdims=True)
    ext[0:Q, :] = d_total
    ext[Q : Q + 8, :] = ahead[...]
    d_raw = d_total * taps_ref[3:4, :]
    for k in range(KW - 1):
        d_raw = d_raw + ext[3 - k : 3 - k + Q, :] * (taps_ref[k : k + 1, :] * marks[:, 4 + k : 5 + k])
    ahead[...] = d_total[0:8, :]
    return d_raw


def scan_forward(
    part, side_ref, x_ref, x_halo, bc_ref, bc_halo, dt_ref, marks_ref, row_ref, x_taps, bc_taps, head_ref, heads_ref,
    *rest,
):
    if part > 0:
        before, rest = rest[6], rest[7:]
    y_ref, state_ref, bc_out, step_out, cum_out, turned_out, helds, exts, bc_exts = rest
    chunk = pl.program_id(0)

    @pl.when(chunk == 0)
    def _():
        helds[...] = before[...] if part > 0 else jnp.zeros_like(helds)

    at_row = lax.broadcasted_iota(jnp.int32, (Q, Q), 0)
    at_col = lax.broadcasted_iota(jnp.int32, (Q, Q), 1)
    lane = lax.broadcasted_iota(jnp.int32, (Q, LANES), 1)
    lower = (at_row >= at_col).astype(BF16)
    lower = jnp.concatenate([lower] * 3, axis=1)
    rate = -jnp.exp(head_ref[1:2, :])

    def one(s, _):
        marks = marks_ref[s]
        held = helds.at[s]
        live = lane < MYH
        step = jnp.where(live, softplus(jnp.where(live, dt_ref[s].astype(F32), 0.0) + head_ref[0:1, :]), 0.0)
        cum = nn(lower, in_three(rate * step, 0))
        cum_t = cum.T
        step_out[s] = step
        cum_out[s] = cum
        turned_out[s, 0] = cum_t[:16, :]
        step_wide, keep, tail, carry = over_heads_all((step,) + spreads(cum, marks), heads_ref)
        x_act = conv_total(exts.at[s], None, x_ref[s], x_halo[s], x_taps, marks)
        x_act = x_act * sigmoid(x_act)
        bc_act = conv_total(bc_exts.at[s], None, bc_ref[s], bc_halo[s], bc_taps, marks)
        bc_act = (bc_act * sigmoid(bc_act)).astype(BF16)
        bc_out[s] = bc_act
        b, c = bc_act[:, :NS], bc_act[:, NS:]
        shut = jnp.where((at_row >= at_col) & (marks[:, 0:1] == row_ref[s, 0]), 0.0, FAR)
        scores = nt(c, b)
        state = held[...]
        state_low = state.astype(BF16)
        state_ref[s, 0] = state_low
        x_step = x_act * step_wide
        y = nn(c, state_low) * keep + x_act * x_taps[5:6, :]
        held[...] = state * carry[0:1, :] + nn(b.T, (x_step * tail).astype(BF16))
        for pair in range(MYH // 2):
            cols = slice(pair * LANES, (pair + 1) * LANES)
            mixing = []
            for head in (2 * pair, 2 * pair + 1):
                spread = cum[:, head : head + 1] - cum_t[head : head + 1, :] + shut
                mixing.append((jnp.exp(spread) * scores).astype(BF16))
            steps = x_step[:, cols]
            both = jnp.concatenate(
                [jnp.where(lane < HD, steps, 0.0), jnp.where(lane < HD, 0.0, steps)], axis=0
            ).astype(BF16)
            y_ref[s, :, cols] = (y[:, cols] + nn(jnp.concatenate(mixing, axis=1), both)).astype(BF16)
        return 0

    lax.fori_loop(0, 2, one, 0)


def scan_backward(
    group, part, side_ref, x_ref, x_halo, bc_ref, step_ref, cum_ref, turned_ref, dy_ref, state_ref, marks_ref, row_ref,
    x_taps, head_ref, heads_ref, *rest,
):
    final = group == GROUPS - 1
    if group > 0:
        dbc_before, ddt_before, *rest = rest
    if final:
        bc_raw_ref, bc_halo, dt_ref, bc_taps, *rest = rest
    carried = 6 if final else 4
    if part > 0:
        before, rest = rest[3 : 3 + carried], rest[3 + carried :]
    dx_ref, dbc_ref, ddt_ref, wide_ref, thin_ref, *rest = rest
    if final:
        bc_sums, *rest = rest
    helds, aheads, *rest = rest
    if final:
        bc_aheads, *rest = rest
    exts, shifts, *rest = rest
    if final:
        bc_exts, bc_shifts = rest
    chunk = pl.program_id(0)

    @pl.when(chunk == 0)
    def _():
        running = [wide_ref, thin_ref] + ([bc_sums] if final else []) + [helds, aheads]
        running += [bc_aheads] if final else []
        for i, ref in enumerate(running):
            ref[...] = before[i][...] if part > 0 else jnp.zeros_like(ref)

    at_row = lax.broadcasted_iota(jnp.int32, (Q, Q), 0)
    at_col = lax.broadcasted_iota(jnp.int32, (Q, Q), 1)
    lane = lax.broadcasted_iota(jnp.int32, (Q, LANES), 1)
    low_lanes, high_lanes = group * GH, LANES - (group + 1) * GH
    upper = (at_row <= at_col).astype(BF16)
    strict = (at_row > at_col).astype(BF16)
    spans = jnp.concatenate([upper, upper, strict, strict], axis=1)
    rate = -jnp.exp(head_ref[1:2, :])
    thin = [(step_ref[s],) + spreads(cum_ref[s], marks_ref[s]) for s in range(2)]
    wide = over_heads_all([v for some in thin for v in some], heads_ref)
    made = []
    for s in range(2):
        marks = marks_ref[s]
        held = helds.at[s]
        step_wide, keep, tail, carry = wide[4 * s : 4 * s + 4]
        total = conv_total(exts.at[s], shifts.at[s], x_ref[s], x_halo[s], x_taps, marks)
        gate = sigmoid(total)
        x_act = total * gate
        slope = gate * (1.0 + total * (1.0 - gate))
        b, c = bc_ref[s, :, :NS], bc_ref[s, :, NS:]
        dy = dy_ref[s].astype(F32)
        x_step = x_act * step_wide
        state = state_ref[s, 0]
        d_state = held[...]
        d_state_low = d_state.astype(BF16)
        dy_keep = dy * keep
        dy_keep_low = dy_keep.astype(BF16)
        from_state = nn(c, state)
        d_c = nt(dy_keep_low, state)
        d_b = nt((x_step * tail).astype(BF16), d_state_low)
        du_tail = nn(b, d_state_low) * tail
        linked = jnp.sum(d_state * state.astype(F32), axis=0, keepdims=True)
        linked = jnp.broadcast_to(linked, (8, GC))
        held[...] = d_state * carry[0:1, :] + nn(c.T, dy_keep_low)
        made.append((dy, x_act, slope, x_step, b, c, d_b, d_c, du_tail, dy_keep * from_state, x_step * du_tail, linked))
    sums = sum_heads_all([v for some in made for v in some[9:]], heads_ref)
    d_us = []
    for s in range(2):
        marks = marks_ref[s]
        dy, x_act, slope, x_step, b, c, d_b, d_c, du_tail = made[s][:9]
        cum, cum_t = cum_ref[s], turned_ref[s, 0]
        shut = jnp.where((at_row <= at_col) & (marks[:, 0:1] == row_ref[s, 0]), 0.0, FAR)
        scores = nt(b, c)
        d_scores = jnp.zeros((Q, Q), F32)
        by_later, by_earlier, du_parts = [], [], []
        for pair in range(GH // 2):
            cols = slice(pair * LANES, (pair + 1) * LANES)
            steps, dys = x_step[:, cols], dy[:, cols]
            step_both = jnp.concatenate(
                [jnp.where(lane < HD, steps, 0.0), jnp.where(lane < HD, 0.0, steps)], axis=0
            ).astype(BF16)
            dy_both = jnp.concatenate(
                [jnp.where(lane < HD, dys, 0.0), jnp.where(lane < HD, 0.0, dys)], axis=0
            ).astype(BF16)
            met = nt(step_both, dys.astype(BF16))
            mixing = []
            for place in range(2):
                head = low_lanes + 2 * pair + place
                decay = jnp.exp(cum_t[head : head + 1, :] - cum[:, head : head + 1] + shut)
                mixing.append((decay * scores).astype(BF16))
                weighed = decay * met[place * Q : (place + 1) * Q, :]
                d_scores = d_scores + weighed
                spent = weighed * scores
                by_later.append(jnp.sum(spent, axis=0, keepdims=True))
                by_earlier.append(jnp.sum(spent, axis=1, keepdims=True))
            du_parts.append(nn(jnp.concatenate(mixing, axis=1), dy_both))
        du = jnp.concatenate(du_parts, axis=1) + du_tail
        d_low = d_scores.astype(BF16)
        d_b = d_b + nn(d_low, c)
        d_c = d_c + nn(d_scores.T.astype(BF16), b)
        d_bc = jnp.concatenate([d_b, d_c], axis=1)
        if group > 0:
            d_bc = d_bc + dbc_before[s]
        if final:
            bc_total = conv_total(bc_exts.at[s], bc_shifts.at[s], bc_raw_ref[s], bc_halo[s], bc_taps, marks)
            bc_gate = sigmoid(bc_total)
            d_bc = d_bc * (bc_gate * (1.0 + bc_total * (1.0 - bc_gate)))
            d_bc = conv_back(d_bc, bc_exts.at[s], bc_shifts.at[s], bc_aheads.at[s], bc_taps, marks, bc_sums)
        dbc_ref[s] = d_bc.astype(dbc_ref.dtype)
        later = by_later + [jnp.zeros((high_lanes, Q), F32)]
        later = ([jnp.zeros((low_lanes, Q), F32)] if low_lanes else []) + later
        later = jnp.concatenate(later, axis=0).T
        earlier = jnp.zeros((Q, LANES), F32)
        for head in range(GH):
            earlier = jnp.where(lane == low_lanes + head, by_earlier[head], earlier)
        d_us.append((du, later - earlier))
    d_steps = sum_heads_all([made[s][1] * d_us[s][0] for s in range(2)], heads_ref)
    for s in range(2):
        marks = marks_ref[s]
        dy, x_act, slope = made[s][:3]
        du, within = d_us[s]
        seen, sent, linked = sums[3 * s : 3 * s + 3]
        step = step_ref[s]
        linked = linked[0:1, :] * thin[s][3][0:1, :]
        mine = (lane >= low_lanes) & (lane < low_lanes + GH)
        crossed = jnp.concatenate([in_two(seen + within, 0), in_two(sent, 0)], axis=0)
        d_log = jnp.where(mine, nn(spans, crossed) + linked, 0.0)
        d_raw = d_steps[s] + rate * d_log
        if group > 0:
            d_raw = d_raw + ddt_before[s]
        if final:
            live = lane < MYH
            d_raw = jnp.where(live, d_raw * sigmoid(jnp.where(live, dt_ref[s].astype(F32), 0.0) + head_ref[0:1, :]), 0.0)
            thin_ref[0:1, :] += jnp.sum(d_raw, axis=0, keepdims=True)
        ddt_ref[s] = d_raw.astype(ddt_ref.dtype)
        thin_ref[1:2, :] += jnp.sum(d_log * (rate * step), axis=0, keepdims=True)
        wide_ref[5:6, :] += jnp.sum(dy * x_act, axis=0, keepdims=True)
        d_total = (du * wide[4 * s] + dy * x_taps[5:6, :]) * slope
        d_raw = conv_back(d_total, exts.at[s], shifts.at[s], aheads.at[s], x_taps, marks, wide_ref)
        dx_ref[s] = d_raw.astype(BF16)


def block_at(time, side):
    blocks = LEN // Q
    return (time + side * (blocks // 2)) % blocks


def halo_at(time, side):
    return block_at(jnp.maximum(time - 1, 0), side) * (Q // 16) + Q // 16 - 1


BC_AT = MYC // BC
DT_AT = (MYC + BC) // LANES


def run_forward(part, side, first, marks, rows, x_taps, bc_taps, head_rows, heads, before):
    blocks = LEN // Q
    steps = blocks // 2
    now = lambda t: part * steps + t
    here = lambda col: lambda t, side: (0, block_at(now(t), side[0]), col)
    halo = lambda col: lambda t, side: (0, halo_at(now(t), side[0]), col)
    time = lambda t, side: (0, now(t), 0)
    time_four = lambda t, side: (0, now(t), 0, 0)
    still = lambda t, side: (0, 0)
    inputs = [first, first, first, first, first, marks, rows, x_taps, bc_taps, head_rows, heads]
    in_specs = [
        pl.BlockSpec((2, Q, MYC), here(0)),
        pl.BlockSpec((2, 16, MYC), halo(0)),
        pl.BlockSpec((2, Q, BC), here(BC_AT)),
        pl.BlockSpec((2, 16, BC), halo(BC_AT)),
        pl.BlockSpec((2, Q, LANES), here(DT_AT)),
        pl.BlockSpec((2, Q, 16), time),
        pl.BlockSpec((2, 1, 1, Q), time_four),
        pl.BlockSpec((8, MYC), still),
        pl.BlockSpec((8, BC), still),
        pl.BlockSpec((8, LANES), still),
        pl.BlockSpec((2 * LANES, MYC), still),
    ]
    running = pl.BlockSpec((2, NS, MYC), lambda t, side: (0, 0, 0))
    aliases = {}
    if part > 0:
        aliases = {1 + len(inputs) + i: i for i in range(6)}
        inputs += before
        in_specs += [pl.BlockSpec(memory_space=pl.ANY)] * 6 + [running]
    return pl.pallas_call(
        functools.partial(scan_forward, part),
        grid_spec=pltpu.PrefetchScalarGridSpec(
            num_scalar_prefetch=1,
            grid=(steps,),
            in_specs=in_specs,
            out_specs=[
                pl.BlockSpec((2, Q, MYC), here(0)),
                pl.BlockSpec((2, 1, NS, MYC), time_four),
                pl.BlockSpec((2, Q, BC), here(0)),
                pl.BlockSpec((2, Q, LANES), time),
                pl.BlockSpec((2, Q, LANES), time),
                pl.BlockSpec((2, 1, 16, Q), time_four),
                running,
            ],
            scratch_shapes=[pltpu.VMEM((2, Q + 8, MYC), F32), pltpu.VMEM((2, Q + 8, BC), F32)],
        ),
        out_shape=[
            jax.ShapeDtypeStruct((2, LEN, MYC), BF16),
            jax.ShapeDtypeStruct((2, blocks, NS, MYC), BF16),
            jax.ShapeDtypeStruct((2, LEN, BC), BF16),
            jax.ShapeDtypeStruct((2, LEN, LANES), F32),
            jax.ShapeDtypeStruct((2, LEN, LANES), F32),
            jax.ShapeDtypeStruct((2, blocks, 16, Q), F32),
            jax.ShapeDtypeStruct((2, NS, MYC), F32),
        ],
        input_output_aliases=aliases,
        compiler_params=pltpu.CompilerParams(vmem_limit_bytes=18 * MIB),
        cost_estimate=pl.CostEstimate(flops=9 * 10**9, bytes_accessed=30 * 10**6, transcendentals=10**7),
        name="scan_forward_%d" % part,
    )(side, *inputs)


def run_backward(group, part, side, first, scanned, d_ssm, marks, rows, x_taps, bc_taps, head_rows, heads, d_bc, before):
    _, states, bc_act, step, cum, turned, _ = scanned
    blocks = LEN // Q
    steps = blocks // 2
    final = group == GROUPS - 1
    now = lambda t: blocks - 1 - part * steps - t
    here = lambda col: lambda t, side: (0, block_at(now(t), side[0]), col)
    halo = lambda col: lambda t, side: (0, halo_at(now(t), side[0]), col)
    time = lambda t, side: (0, now(t), 0)
    time_four = lambda col: lambda t, side: (0, now(t), 0, col)
    still = lambda t, side: (0, 0)
    still_three = lambda t, side: (0, 0, 0)
    share = lambda t, side: (0, group)
    in_specs = [
        pl.BlockSpec((2, Q, GC), here(group)),
        pl.BlockSpec((2, 16, GC), halo(group)),
        pl.BlockSpec((2, Q, BC), here(0)),
        pl.BlockSpec((2, Q, LANES), time),
        pl.BlockSpec((2, Q, LANES), time),
        pl.BlockSpec((2, 1, 16, Q), time_four(0)),
        pl.BlockSpec((2, Q, GC), here(group)),
        pl.BlockSpec((2, 1, NS, GC), time_four(group)),
        pl.BlockSpec((2, Q, 16), time),
        pl.BlockSpec((2, 1, 1, Q), time_four(0)),
        pl.BlockSpec((8, GC), share),
        pl.BlockSpec((8, LANES), still),
        pl.BlockSpec((2 * LANES, GC), share),
    ]
    inputs = [first, first, bc_act, step, cum, turned, d_ssm, states, marks, rows, x_taps, head_rows, heads]
    if group > 0:
        in_specs += [pl.BlockSpec((2, Q, BC), here(0)), pl.BlockSpec((2, Q, LANES), here(0))]
        inputs += d_bc
    if final:
        in_specs += [
            pl.BlockSpec((2, Q, BC), here(BC_AT)),
            pl.BlockSpec((2, 16, BC), halo(BC_AT)),
            pl.BlockSpec((2, Q, LANES), here(DT_AT)),
            pl.BlockSpec((8, BC), still),
        ]
        inputs += [first, first, first, bc_taps]
    running = [(8, GC), (8, LANES)] + ([(8, BC)] if final else []) + [(2, NS, GC), (2, 8, GC)]
    running += [(2, 8, BC)] if final else []
    running_specs = [pl.BlockSpec(v, still if len(v) == 2 else still_three) for v in running]
    out_specs = [
        pl.BlockSpec((2, Q, GC), here(0)),
        pl.BlockSpec((2, Q, BC), here(0)),
        pl.BlockSpec((2, Q, LANES), here(0)),
    ] + running_specs
    out_shape = [
        jax.ShapeDtypeStruct((2, LEN, GC), BF16),
        jax.ShapeDtypeStruct((2, LEN, BC), BF16 if final else F32),
        jax.ShapeDtypeStruct((2, LEN, LANES), BF16 if final else F32),
    ] + [jax.ShapeDtypeStruct(v, F32) for v in running]
    aliases = {}
    if part > 0:
        aliases = {1 + len(inputs) + i: i for i in range(3)}
        in_specs += [pl.BlockSpec(memory_space=pl.ANY)] * 3 + running_specs
        inputs += before
    scratch = [pltpu.VMEM((2, Q + 8, GC), F32), pltpu.VMEM((2, KW - 1, Q, GC), F32)]
    if final:
        scratch += [pltpu.VMEM((2, Q + 8, BC), F32), pltpu.VMEM((2, KW - 1, Q, BC), F32)]
    return pl.pallas_call(
        functools.partial(scan_backward, group, part),
        grid_spec=pltpu.PrefetchScalarGridSpec(
            num_scalar_prefetch=1, grid=(steps,), in_specs=in_specs, out_specs=out_specs, scratch_shapes=scratch
        ),
        out_shape=out_shape,
        input_output_aliases=aliases,
        compiler_params=pltpu.CompilerParams(vmem_limit_bytes=56 * MIB),
        cost_estimate=pl.CostEstimate(flops=14 * 10**9, bytes_accessed=40 * 10**6, transcendentals=10**7),
        name="scan_backward_%d_%d" % (group, part),
    )(side, *inputs)


def lead(value, by):
    if by == 0:
        return value
    pad = [(0, 0)] * value.ndim
    if by > 0:
        pad[1] = (0, by)
        return jnp.pad(value, pad)[:, by:]
    pad[1] = (-by, 0)
    return jnp.pad(value, pad)[:, :by]


def fold(block):
    return jnp.concatenate([block[..., : D // 2], block[..., D // 2 :]], axis=-2)


def unfold(block):
    half = block.shape[-2] // 2
    return jnp.concatenate([block[..., :half, :], block[..., half:, :]], axis=-1)


def out_whole(out_weight, split, core, side):
    whole = lax.all_gather(out_weight, ("zy", "core", "seq"), axis=0, tiled=True)
    return pick(pick(split_heads(whole, 0, split), core), side)


def out_scattered(grad, split, core, side):
    own = jnp.zeros((2, 2, MYC, D), BF16)
    own = lax.dynamic_update_slice(own, grad.astype(BF16)[None, None], (core, side, 0, 0))
    whole = join_heads(own, 0, split)
    return lax.psum_scatter(whole, ("zy", "core", "seq"), scatter_dimension=0, tiled=True)


def own_slice(whole, size):
    at = (lax.axis_index("zy") * 2 + lax.axis_index("core")) * 2 + lax.axis_index("seq")
    return lax.dynamic_slice_in_dim(whole, at * size, size, 0)


def body(
    tokens,
    segments,
    norm_gain,
    in_weight,
    conv_weight,
    conv_bias,
    dt_bias,
    a_log,
    d_skip,
    gated_gain,
    out_weight,
    cotangent,
):
    count = lax.axis_size("zy")
    core, side = lax.axis_index("core"), lax.axis_index("seq")
    split = head_split(count)
    rows = tokens.shape[1]
    total = PARTS * rows

    blocked = split[0] > 1

    me = (core * 2 + side).astype(jnp.int32).reshape(1)
    at_side = side.astype(jnp.int32).reshape(1)
    at_core = core.astype(jnp.int32).reshape(1)
    at_ring = jnp.stack([ring_place(count)[0], core, core * 2 + side]).astype(jnp.int32)

    heads = np.kron(np.eye(LANES, MYH, dtype=np.float32), np.ones((1, HD), np.float32))
    heads = jnp.asarray(np.concatenate([heads, heads], axis=0), BF16)
    per_head = jnp.stack([dt_bias, a_log, d_skip])
    per_head = jnp.pad(per_head, ((0, 5), (0, LANES - NH)))

    sizes = (norm_gain.shape[0], conv_bias.shape[0], gated_gain.shape[0])
    seg_own = segments[0].reshape(-1, LANES)
    mix = split_columns(in_weight, norm_gain, conv_weight, conv_bias, gated_gain, seg_own, split, me)
    mix = Task(peer_steps(mix))
    stage([mix])
    sent, later = assemble_rows(mix.value, me)
    ring = Task(gather_steps(sent))
    token_all = Task(token_steps(tokens[0], 3))
    marks, seg_rows = stage([ring, token_all], functools.partial(segment_marks, at_side), *mix.value)
    if blocked:
        held = Task(single_step((out_weight, GROUP, DIAGONAL)))
        for _ in range(count // 2 - 2):
            stage([ring, token_all])
        stage([ring, token_all, held])
        later = jnp.concatenate([later, fold(held.value)], axis=1)
    else:
        w_out = out_whole(out_weight, split, core, side)
    while not (ring.done and token_all.done):
        stage([ring, token_all])

    near, far, both = token_all.value
    w_pieces = ring.value
    ring = Task(gather_steps(later))
    cot_all = Task(token_steps(cotangent[0], 3))
    first, turned, x_taps, bc_taps, head_rows, gain = stage(
        [ring, cot_all], functools.partial(project, at_ring, split, sizes), tokens[0], near, far, both, per_head, heads, w_pieces
    )
    first_by_seq = first.reshape(2, LEN, W1)

    def forward(part, first, before):
        return run_forward(part, at_side, first, marks, seg_rows, x_taps, bc_taps, head_rows, heads, before)

    scanned = stage([ring, cot_all], functools.partial(forward, 0), first_by_seq, None)
    scanned = stage([ring, cot_all], functools.partial(forward, 1), first_by_seq, scanned)
    while not (ring.done and cot_all.done):
        stage([ring, cot_all])
    y = scanned[0].reshape(total, MYC)
    if blocked:
        w_out = put_together(ring.value, slice(MYC, 2 * MYC), core * (count // 2))
        blocks = [w_out[: count // 2], swap(w_out[count // 2 :], "core")]
    else:
        blocks = [w_out]
    gate_pieces = ring.value
    cot_rows = (cotangent[0], *cot_all.value)
    z, d_two, sums, w_out = meet(at_ring, *cot_rows, turned, y, x_taps, blocks, ring.value)
    sums = Task(group_steps(sums))
    stage([sums])
    unit = DI // (count * PARTS) if blocked else MYC // 2
    d_ssm, d_gate, mine, theirs, own, other = gate_back(
        at_core, unit, sums.value, y, z, d_two, x_taps, w_out
    )

    branch = Task(sum_steps(own, other, 3))
    d_theirs, d_mine = out_product(theirs, mine, *cot_rows)
    d_theirs = Task(single_step((d_theirs, "core", SWAP)))
    d_ssm = d_ssm.reshape(2, LEN, MYC)

    def back(group, part, d_bc, before):
        def run(first, d_ssm, scanned, d_bc, before):
            return run_backward(
                group, part, at_side, first, scanned, d_ssm, marks, seg_rows, x_taps, bc_taps, head_rows, heads, d_bc, before
            )

        return run, first_by_seq, d_ssm, scanned, d_bc, before

    zero = stage([d_theirs, branch], *back(0, 0, None, None))
    if blocked:
        d_w_gate = both_products(count, at_core, turned, d_gate, d_mine, d_theirs.value)
    else:
        d_w_gate = weight_product(turned, d_gate).reshape(count, D // count, MYC)
    gate_ring = Task(scatter_steps(d_w_gate))

    zero = stage([gate_ring, branch], *back(0, 1, None, zero))
    one = stage([gate_ring, branch], *back(1, 0, zero[1:3], None))
    one = stage([gate_ring, branch], *back(1, 1, zero[1:3], one))
    d_x0, _, _, wide0, thin0 = zero[:5]
    d_x1, d_bc, d_dt, wide1, thin1, bc_sums = one[:6]
    wide = jnp.concatenate([wide0, wide1], axis=1)
    thin = thin0 + thin1
    d_rows = [d_x0.reshape(total, GC), d_x1.reshape(total, GC), d_bc.reshape(total, BC), d_dt.reshape(total, LANES)]
    far_other, far = stage([gate_ring, branch], functools.partial(normed_part, 1), at_ring, *d_rows, d_gate, w_pieces, gate_pieces)
    while not (branch.done and gate_ring.done):
        stage([gate_ring, branch])
    far = Task(far_steps(far, far_other, (6, 3, 3, 4)))
    gate_sum = sum(v.astype(F32) for v in gate_ring.value).astype(BF16)
    tasks = [far]
    if blocked:
        d_out = Task(single_step((unfold(gate_sum[:, MYC:]), GROUP, DIAGONAL)))
        tasks.append(d_out)
    d_w_first = stage(tasks, weight_product, turned, *d_rows)
    rest = Task(scatter_steps(d_w_first.reshape(count, D // count, W1)))
    near_other, near = stage([rest, far], functools.partial(normed_part, 0), at_ring, *d_rows, d_gate, w_pieces, gate_pieces)
    near = Task(single_step((near_other, "core", SWAP))), near
    small_grads = Task(small_sum_steps(
        (
            wide[:KW].reshape(-1),
            wide[KW],
            bc_sums[: KW + 1].reshape(-1),
            thin[0, :MYH],
            thin[1, :MYH],
            jnp.sum(wide[KW + 1].reshape(MYH, HD), axis=1),
        ),
        core, side,
    ))
    stage([rest, far, near[0], small_grads])
    if blocked:
        d_out = d_out.value.astype(F32)
    else:
        d_mine, d_theirs = jnp.where(core == 0, d_mine, d_theirs.value), jnp.where(core == 0, d_theirs.value, d_mine)
        d_out = out_scattered(jnp.concatenate([d_mine, d_theirs], axis=0), split, core, side).astype(F32)

    def ends(x, branch, out_weight, gated_gain, d_out):
        gain_two = jnp.sum(out_weight.astype(F32) * d_out, axis=1) / gated_gain.astype(F32)
        return (x.astype(F32) + branch).astype(BF16), gain_two

    block_out, gain_two = stage(
        [rest, far, small_grads], ends, tokens[0], branch.value, out_weight, gated_gain, d_out
    )
    while not (rest.done and far.done):
        stage([rest, far, small_grads])

    d_w = Task(peer_steps(hand_back(*rest.value, gate_sum[:, :MYC], me)))
    input_grad = stage(
        [d_w, small_grads], finish_tokens, tokens[0], cotangent[0], gain, near[1], near[0].value, *far.value
    )
    finish([d_w, small_grads])
    in_sh, gain_one = join_columns(d_w.value, split, me, in_weight, jnp.broadcast_to(norm_gain[:, None], (norm_gain.shape[0], LANES)))

    taps_x, bias_x, taps_bc, bias_dt, alog, skip = small_grads.value
    taps_x = jnp.swapaxes(taps_x.reshape(2, 2, KW, MYC), 2, 3)
    taps_bc = jnp.sum(taps_bc, axis=(0, 1)).reshape(KW + 1, BC)
    conv_w = jnp.concatenate([join_heads(taps_x, 0, split), taps_bc[:KW].T], axis=0)
    conv_b = jnp.concatenate([join_heads(bias_x, 0, split), taps_bc[KW]])
    return (
        block_out[None],
        input_grad[None],
        gain_one[:, 0],
        in_sh,
        own_slice(conv_w, conv_bias.shape[0]),
        own_slice(conv_b, conv_bias.shape[0]),
        join_heads(bias_dt, 0, split),
        join_heads(alog, 0, split),
        join_heads(skip, 0, split),
        gain_two,
        d_out,
    )


def solution(mesh):
    fsdp, seq = mesh.shape["fsdp"], mesh.shape["seq"]
    grid = Mesh(mesh.devices.reshape(fsdp // 2, 2, seq), ("zy", "core", "seq"))
    every = ("zy", "core", "seq")
    rows = P(("zy", "core"), "seq", None)
    in_specs = (
        rows,
        P(("zy", "core"), "seq"),
        P(every),
        P(every, None),
        P(every, None),
        P(every),
        P(),
        P(),
        P(),
        P(every),
        P(every, None),
        rows,
    )
    out_specs = (
        rows,
        rows,
        P(every),
        P(every, None),
        P(every, None),
        P(every),
        P(),
        P(),
        P(),
        P(every),
        P(every, None),
    )
    return jax.shard_map(body, mesh=grid, in_specs=in_specs, out_specs=out_specs, check_vma=False)
```

```python
import functools

import jax
import jax.numpy as jnp
import numpy as np
from jax import lax
from jax.experimental import pallas as pl
from jax.experimental.pallas import tpu as pltpu
from jax.sharding import Mesh
from jax.sharding import PartitionSpec as P

D = 1536
NH = 48
HD = 64
NS = 128
KW = 4
DI = 3072
CONV = 3328
LEN = 1024

EPS = 1e-05
HIGH = lax.Precision.HIGHEST
F32 = jnp.float32
BF16 = jnp.bfloat16

PARTS = 4
MYH = NH // PARTS
MYC = MYH * HD
LANES = 128
BC = 2 * NS
W1 = MYC + BC + LANES
GROUPS = 2
GH = MYH // GROUPS
GC = GH * HD
Q = 128
FAR = -1e30
MIB = 1024 * 1024

SWAP = [(0, 1), (1, 0)]


def swap(value, axis):
    return lax.ppermute(value, axis, SWAP)


def pick(value, at, dim=0):
    return lax.dynamic_index_in_dim(value, at, dim, False)


def in_order(mine, other, place):
    buf = jnp.zeros((2,) + mine.shape, mine.dtype)
    buf = lax.dynamic_update_index_in_dim(buf, mine, place, 0)
    return lax.dynamic_update_index_in_dim(buf, other, 1 - place, 0)


GROUP = ("core", "seq")


def to_peer(value, r):
    return (value, GROUP, [(g, g ^ r) for g in range(PARTS)])


def ring_order(count):
    return list(range(0, count, 2)) + list(range(count - 1, 0, -2))


def ring_pairs(count):
    order = ring_order(count)
    right = [(order[i], order[(i + 1) % count]) for i in range(count)]
    return right, [(b, a) for a, b in right]


def ring_order_of(at, count):
    at = at % count
    return jnp.where(at < count // 2, 2 * at, 2 * (count - at) - 1)


def ring_place(count):
    zy = lax.axis_index("zy")
    place = jnp.where(zy % 2 == 0, zy // 2, count - 1 - zy // 2)
    return place, lambda at: ring_order_of(at, count)


def half_of(rows):
    return 16 * (rows // 32) if rows >= 32 else rows // 2


def piece_places(count, rows):
    places = [(0, 0)]
    for step in range(1, count // 2):
        places += [(-step, 0), (step, 0)]
    return places + [(count // 2, 0), (count // 2, half_of(rows))]


class Task:
    def __init__(self, steps):
        self.steps, self.value, self.done = steps, None, False
        self.moves = next(steps, None)
        self.done = self.moves is None

    def take(self, arrived):
        try:
            self.moves = self.steps.send(arrived)
        except StopIteration as end:
            self.value, self.done = end.value, True


def stage(tasks, work=None, *args):
    tasks = [t for t in tasks if not t.done]
    values = [[m[0] for m in t.moves] for t in tasks]
    values, args = lax.optimization_barrier((values, args))
    arrived = [
        [lax.ppermute(v, m[1], m[2]) for v, m in zip(vs, t.moves)] for vs, t in zip(values, tasks)
    ]
    result = None if work is None else work(*args)
    if work is None:
        arrived = lax.optimization_barrier(arrived)
    else:
        arrived, result = lax.optimization_barrier((arrived, result))
    for t, got in zip(tasks, arrived):
        t.take(got)
    return result


def finish(tasks):
    while not all(t.done for t in tasks):
        stage(tasks)


def gather_steps(block):
    count = lax.axis_size("zy")
    half = half_of(block.shape[0])
    right, left = ring_pairs(count)
    pieces = [block]
    ahead = back = block
    for _ in range(1, count // 2):
        ahead, back = yield [(ahead, "zy", right), (back, "zy", left)]
        pieces += [ahead, back]
    pieces += yield [(ahead[:half], "zy", right), (back[half:], "zy", left)]
    return pieces


def put_together(pieces, columns, flip):
    count = lax.axis_size("zy")
    place, order = ring_place(count)
    rows = pieces[0].shape[0]
    full = jnp.zeros((count, rows, columns.stop - columns.start), pieces[0].dtype)
    for piece, (step, row) in zip(pieces, piece_places(count, rows)):
        full = lax.dynamic_update_slice(full, piece[None, :, columns], (order(place + step + count) ^ flip, row, 0))
    return full


def add_kernel(at_ref, one_ref, two_ref, ahead_ref, back_ref, first_ref, second_ref):
    def add(out_ref, full, got, start):
        end = start + got.shape[0]
        out_ref[start:end, :] = (full[start:end, :].astype(F32) + got[...].astype(F32)).astype(BF16)
        if start > 0:
            out_ref[:start, :] = full[:start, :]
        if end < out_ref.shape[0]:
            out_ref[end:, :] = full[end:, :]

    rows = first_ref.shape[0]
    add(first_ref, one_ref[0], ahead_ref, 0)
    add(second_ref, two_ref[0], back_ref, rows - back_ref.shape[0])


def ring_add(full, one, two, ahead, back):
    _, rows, cols = full.shape
    tile = cols // 3
    at = jnp.stack([one, two]).astype(jnp.int32)
    return pl.pallas_call(
        add_kernel,
        grid_spec=pltpu.PrefetchScalarGridSpec(
            num_scalar_prefetch=1,
            grid=(3,),
            in_specs=[
                pl.BlockSpec((1, rows, tile), lambda t, at: (at[0], 0, t)),
                pl.BlockSpec((1, rows, tile), lambda t, at: (at[1], 0, t)),
                pl.BlockSpec((ahead.shape[0], tile), lambda t, at: (0, t)),
                pl.BlockSpec((back.shape[0], tile), lambda t, at: (0, t)),
            ],
            out_specs=[pl.BlockSpec((rows, tile), lambda t, at: (0, t))] * 2,
        ),
        out_shape=[jax.ShapeDtypeStruct((rows, cols), BF16)] * 2,
        compiler_params=pltpu.CompilerParams(vmem_limit_bytes=16 * MIB),
        name="ring_add",
    )(at, full, full, ahead, back)


def scatter_steps(full):
    count, rows, cols = full.shape
    half = half_of(rows)
    right, left = ring_pairs(count)
    place, order = ring_place(count)
    far = lax.dynamic_index_in_dim(full, order(place + count // 2), 0, False)
    one, two = far[:half], far[half:]
    for step in range(count // 2 - 1, -1, -1):
        ahead, back = yield [(one, "zy", right), (two, "zy", left)]
        if step > 0:
            one, two = ring_add(full, order(place + step), order(place + count - step), ahead, back)
    return lax.dynamic_index_in_dim(full, order(place), 0, False), ahead, back


def single_step(move):
    (got,) = yield [move]
    return got


def group_steps(value):
    got = yield [to_peer(value, r) for r in range(1, PARTS)]
    return [value] + list(got)


def piece_cuts(rows, pieces):
    return [16 * (rows // 16 * i // pieces) for i in range(pieces + 1)]


def token_steps(value, pieces):
    cuts = piece_cuts(value.shape[0], pieces)
    far, both = [], []
    moves = [(value, "core", SWAP)]
    for i in range(pieces):
        got = yield moves + [(value[cuts[i] : cuts[i + 1]], "seq", SWAP)]
        if i == 0:
            near = got[0]
        else:
            both.append(got[0])
        far.append(got[-1])
        moves = [(got[-1], "core", SWAP)]
    (got,) = yield moves
    return near, far, both + [got]


def peer_steps(blocks):
    got = yield [to_peer(blocks[r], r) for r in range(1, PARTS)]
    return [blocks[0]] + list(got)


def sum_steps(own, other, pieces):
    (got,) = yield [(other, "core", SWAP)]
    rows = own.shape[0] // 2
    sent = (own[rows:].astype(F32) + got[rows:].astype(F32)).astype(BF16)
    cuts = piece_cuts(rows, pieces)
    arrived = []
    for a, b in zip(cuts, cuts[1:]):
        (far,) = yield [(sent[a:b], "seq", SWAP)]
        arrived.append(far)
    return own[:rows].astype(F32) + got[:rows].astype(F32) + jnp.concatenate(arrived, axis=0).astype(F32)


def far_steps(own, other, parts):
    (got,) = yield [(other, "core", SWAP)]
    sent = (own.astype(F32) + got.astype(F32)).astype(BF16)
    cuts = [0] + [int(v) * sent.shape[0] // 16 for v in np.cumsum(parts)]
    arrived = []
    for a, b in zip(cuts, cuts[1:]):
        (got,) = yield [(sent[a:b], "seq", SWAP)]
        arrived.append(got)
    return arrived


def small_sum_steps(parts, core, side):
    count = lax.axis_size("zy")
    lengths = [p.shape[0] for p in parts]
    packed = jnp.concatenate(parts)
    packed = jnp.pad(packed, (0, -packed.shape[0] % 1024)).reshape(-1, LANES)
    bit = 1
    while bit < count:
        (got,) = yield [(packed, "zy", [(i, i ^ bit) for i in range(count)])]
        packed = packed + got
        bit *= 2
    (got,) = yield [(packed, "core", SWAP)]
    packed = in_order(packed, got, core)
    (got,) = yield [(packed, "seq", SWAP)]
    packed = jnp.swapaxes(in_order(packed, got, side), 0, 1).reshape(2, 2, -1)
    return jnp.split(packed, np.cumsum(lengths), axis=2)[: len(lengths)]


def zy_exchange(value, bit):
    count = lax.axis_size("zy")
    return lax.ppermute(value, "zy", [(i, i ^ bit) for i in range(count)])


def zy_sum(value):
    count = lax.axis_size("zy")
    bit = 1
    while bit < count:
        value = value + zy_exchange(value, bit)
        bit *= 2
    return value


def head_split(count):
    rows = DI // count
    if rows % (2 * HD) == 0 and count % 2 == 0:
        return count // 2, rows // (2 * HD)
    return 1, MYH


def split_heads(value, dim, split):
    q, i = split
    size = value.shape[dim]
    unit = size // NH
    shape = value.shape
    value = value.reshape(shape[:dim] + (2, q, 2, i * unit) + shape[dim + 1 :])
    value = jnp.swapaxes(value, dim + 1, dim + 2)
    return value.reshape(shape[:dim] + (2, 2, size // PARTS) + shape[dim + 1 :])


def join_heads(value, dim, split):
    q, i = split
    shape = value.shape
    mine = shape[dim + 2]
    value = value.reshape(shape[:dim] + (2, 2, q, mine // q) + shape[dim + 3 :])
    value = jnp.swapaxes(value, dim + 1, dim + 2)
    return value.reshape(shape[:dim] + (PARTS * mine,) + shape[dim + 3 :])


HALF = LANES // 2
EXTRA = 16
SEG_AT = 8
FREE = 24


def half_places(split, core, side):
    q, i = split
    return [((core * q + at) * 2 + side) * i + k for at in range(q) for k in range(i)]


def halves(tile_of, places):
    tiles = []
    for at in range(0, len(places), 2):
        one, two = places[at], places[at + 1]
        if one % 2 == 0 and two == one + 1:
            tiles.append(tile_of(one // 2))
            continue
        left, right = tile_of(one // 2), tile_of(two // 2)
        left = pltpu.roll(left, HALF, 1) if one % 2 else left
        right = right if two % 2 else pltpu.roll(right, HALF, 1)
        lane = lax.broadcasted_iota(jnp.int32, left.shape, 1)
        tiles.append(jnp.where(lane < HALF, left, right))
    return tiles


def head_choice(split):
    choice = np.zeros((PARTS, LANES, LANES), np.float32)
    for g in range(PARTS):
        for lane, head in enumerate(half_places(split, g // 2, g % 2)):
            choice[g, head, lane] = 1.0
    return choice


def split_kernel(split, at_ref, w_ref, gain_ref, taps_ref, bias_ref, gated_ref, seg_ref, choice_ref, *refs):
    *outs, out_ref, small_ref = refs
    me = at_ref[0]
    small_ref[...] = jnp.zeros_like(small_ref)
    for row, ref in ((0, gain_ref), (1, bias_ref), (6, gated_ref)):
        small_ref[row : row + 1, : ref.shape[1]] = ref[...].astype(F32)
    small_ref[2 : 2 + KW, : taps_ref.shape[1]] = taps_ref[...].astype(F32)
    small_ref[SEG_AT : SEG_AT + seg_ref.shape[0], :] = seg_ref[...].astype(F32)

    def tile_of(base):
        return lambda t: w_ref[:, base + t * LANES : base + (t + 1) * LANES].astype(F32)

    bc = w_ref[:, 2 * DI : 2 * DI + BC]
    steps = w_ref[:, DI + CONV :]
    for g in range(PARTS):
        places = half_places(split, g // 2, g % 2)
        at = me ^ g
        tiles = halves(tile_of(DI), places)
        for k, tile in enumerate(tiles):
            out_ref[at, :, k * LANES : (k + 1) * LANES] = tile.astype(BF16)
        out_ref[at, :, MYC : MYC + BC] = bc
        out_ref[at, :, MYC + BC : W1] = nn(steps, choice_ref[g, :NH, :]).astype(BF16)
        for k, tile in enumerate(halves(tile_of(0), places)):
            out_ref[at, :, W1 + k * LANES : W1 + (k + 1) * LANES] = tile.astype(BF16)
    for r, ref in enumerate(outs):
        ref[:EXTRA, :LANES] = small_ref[...].astype(BF16)
        ref[:EXTRA, LANES:] = jnp.zeros((EXTRA, W1 + MYC - LANES), BF16)
        ref[EXTRA:, :] = out_ref[r]


def smem(shape=None):
    return pl.BlockSpec(memory_space=pltpu.SMEM)


def split_columns(weight, gain, taps, bias, gated, segs, split, me):
    return pl.pallas_call(
        functools.partial(split_kernel, split),
        out_shape=[jax.ShapeDtypeStruct((EXTRA + weight.shape[0], W1 + MYC), BF16)] * PARTS,
        in_specs=[smem()] + [pl.BlockSpec()] * 7,
        scratch_shapes=[
            pltpu.VMEM((PARTS, weight.shape[0], W1 + MYC), BF16),
            pltpu.VMEM((EXTRA, LANES), F32),
        ],
        compiler_params=pltpu.CompilerParams(vmem_limit_bytes=56 * MIB),
        name="split_columns",
    )(me, weight, gain[None], taps.T, bias[None], gated[None], segs, jnp.asarray(head_choice(split), BF16))


def assemble_kernel(at_ref, one, two, three, four, first_ref, gate_ref):
    me = at_ref[0]
    for r, ref in enumerate((one, two, three, four)):
        at = me ^ r
        first_ref[at, :, : MYC + BC] = ref[EXTRA:, : MYC + BC]
        small = pltpu.roll(ref[:EXTRA, :LANES].astype(F32)[:SEG_AT], FREE, 1)
        lane = lax.broadcasted_iota(jnp.int32, small.shape, 1)
        steps = ref[EXTRA:, MYC + BC : W1].astype(F32)
        steps = jnp.concatenate([jnp.where(lane < FREE, steps[:SEG_AT], small), steps[SEG_AT:]], axis=0)
        first_ref[at, :, MYC + BC :] = steps.astype(BF16)
        gate_ref[at] = ref[EXTRA:, W1:]


def assemble_rows(blocks, me):
    rows = blocks[0].shape[0] - EXTRA
    first, gate = pl.pallas_call(
        assemble_kernel,
        out_shape=[
            jax.ShapeDtypeStruct((PARTS, rows, W1), BF16),
            jax.ShapeDtypeStruct((PARTS, rows, MYC), BF16),
        ],
        in_specs=[smem()] + [pl.BlockSpec()] * PARTS,
        compiler_params=pltpu.CompilerParams(vmem_limit_bytes=56 * MIB),
        name="assemble_rows",
    )(me, *blocks)
    return first.reshape(PARTS * rows, W1), gate.reshape(PARTS * rows, MYC)


def hand_back_kernel(at_ref, own, ahead, back, gate, *refs):
    outs, out_ref = refs[:-1], refs[-1]
    me = at_ref[0]
    for g in range(PARTS):
        first = own[g].astype(F32) + ahead[g].astype(F32) + back[g].astype(F32)
        out_ref[me ^ g, :, :W1] = first.astype(BF16)
        out_ref[me ^ g, :, W1:] = gate[g].astype(BF16)
    for r, ref in enumerate(outs):
        ref[...] = out_ref[r]


def hand_back(own, ahead, back, gate, me):
    blocks = [b.reshape(PARTS, -1, b.shape[1]) for b in (own, ahead, back, gate)]
    return pl.pallas_call(
        hand_back_kernel,
        out_shape=[jax.ShapeDtypeStruct((blocks[0].shape[1], W1 + MYC), BF16)] * PARTS,
        in_specs=[smem()] + [pl.BlockSpec()] * len(blocks),
        scratch_shapes=[pltpu.VMEM((PARTS, blocks[0].shape[1], W1 + MYC), BF16)],
        compiler_params=pltpu.CompilerParams(vmem_limit_bytes=32 * MIB),
        name="hand_back",
    )(me, *blocks)


def join_kernel(split, at_ref, one, two, three, four, choice_ref, w_ref, gain_ref, out_ref, grad_ref, by):
    me = at_ref[0]
    for r, ref in enumerate((one, two, three, four)):
        by[me ^ r] = ref[...].astype(F32)
    where = {}
    for g in range(PARTS):
        for at, place in enumerate(half_places(split, g // 2, g % 2)):
            where[place] = (g, at)

    def put(base, column):
        for t in range(DI // LANES):
            tiles = []
            for k in range(2):
                g, at = where[2 * t + k]
                start = column + at // 2 * LANES
                tile = by[g, :, start : start + LANES]
                tiles.append(tile if at % 2 == k else pltpu.roll(tile, HALF, 1))
            lane = lax.broadcasted_iota(jnp.int32, tiles[0].shape, 1)
            out_ref[:, base + t * LANES : base + (t + 1) * LANES] = jnp.where(lane < HALF, tiles[0], tiles[1])

    put(0, W1)
    put(DI, 0)
    out_ref[:, 2 * DI : 2 * DI + BC] = sum(by[g, :, MYC : MYC + BC] for g in range(PARTS))
    out_ref[:, DI + CONV :] = sum(
        nt(by[g, :, MYC + BC : W1].astype(BF16), choice_ref[g, :NH, :]) for g in range(PARTS)
    )
    met = jnp.sum(out_ref[...] * w_ref[...].astype(F32), axis=1, keepdims=True)
    grad_ref[...] = jnp.broadcast_to(met / gain_ref[:, 0:1].astype(F32), grad_ref.shape)


def join_columns(blocks, split, me, weight, gain):
    rows = blocks[0].shape[0]
    return pl.pallas_call(
        functools.partial(join_kernel, split),
        out_shape=[
            jax.ShapeDtypeStruct((rows, 2 * DI + BC + NH), F32),
            jax.ShapeDtypeStruct((rows, LANES), F32),
        ],
        in_specs=[smem()] + [pl.BlockSpec()] * (PARTS + 3),
        scratch_shapes=[pltpu.VMEM((PARTS, rows, W1 + MYC), F32)],
        name="join_columns",
    )(me, *blocks, jnp.asarray(head_choice(split), BF16), weight, gain)


DIAGONAL = [(0, 0), (1, 2), (2, 1), (3, 3)]


def sigmoid(value):
    return 0.5 * jnp.tanh(0.5 * value) + 0.5


def nt(a, b):
    return lax.dot_general(a, b, (((1,), (1,)), ((), ())), preferred_element_type=F32)


def nn(a, b):
    return lax.dot_general(a, b, (((1,), (0,)), ((), ())), preferred_element_type=F32)


def tn(a, b):
    return lax.dot_general(a, b, (((0,), (0,)), ((), ())), preferred_element_type=F32)


def exact(a, b):
    return lax.dot_general(
        a, b, (((1,), (0,)), ((), ())), preferred_element_type=F32, precision=HIGH
    )


def in_two(value, axis):
    top = value.astype(BF16)
    return jnp.concatenate([top, (value - top.astype(F32)).astype(BF16)], axis=axis)


def in_three(value, axis):
    top = value.astype(BF16)
    rest = value - top.astype(F32)
    mid = rest.astype(BF16)
    return jnp.concatenate([top, mid, (rest - mid.astype(F32)).astype(BF16)], axis=axis)


def over_heads(value, heads_ref):
    return nn(in_two(value, 1), heads_ref[...])


def over_heads_all(values, heads_ref):
    wide = over_heads(jnp.concatenate(values, axis=0), heads_ref)
    cuts = np.cumsum([0] + [v.shape[0] for v in values])
    return [wide[a:b, :] for a, b in zip(cuts, cuts[1:])]


def sum_heads_all(values, heads_ref):
    thin = sum_heads(jnp.concatenate(values, axis=0), heads_ref)
    cuts = np.cumsum([0] + [v.shape[0] for v in values])
    return [thin[a:b, :] for a, b in zip(cuts, cuts[1:])]


def spreads(cum, marks):
    last = cum[Q - 1 : Q, :]
    return (
        jnp.exp(cum) * marks[:, 7:8],
        jnp.exp(last - cum) * marks[:, 8:9],
        jnp.broadcast_to(jnp.exp(last) * marks[Q - 1 : Q, 7:8], (8, LANES)),
    )


def sum_heads(value, heads_ref):
    return nt(value.astype(BF16), heads_ref[:LANES, :])


ROWS = LEN // 2


def row_copies(sources, held, sems):
    half = len(sources) // 2
    copies, at = [], 0
    for q, refs in enumerate((sources[:1], sources[2 : 1 + half], sources[1:2], sources[1 + half :])):
        copies.append([])
        row = 0
        for ref in refs:
            size = ref.shape[0]
            copies[q].append(pltpu.make_async_copy(ref, held.at[q, row : row + size, :], sems.at[at]))
            row += size
            at += 1
    return copies


def wait_rows(step, copies):
    for q, some in enumerate(copies):

        @pl.when(step == q)
        def _():
            for copy in some:
                copy.wait()


def piece_copies(at_ref, refs, full_ref, count, sems, extra=0, small_ref=None, columns=None, source=0):
    block = refs[0].shape[0]
    rows = block - extra
    copies, smalls = [], []
    start_col, width = (0, full_ref.shape[1]) if columns is None else columns
    for i, (ref, (step, row)) in enumerate(zip(refs, piece_places(count, block))):
        zy = ring_order_of(at_ref[0] + step + count, count)
        skip = extra if row == 0 else 0
        start = zy * rows + row + skip - extra
        size = ref.shape[0] - skip
        to = full_ref.at[pl.ds(pl.multiple_of(start, 16), size), start_col : start_col + width]
        copies.append(pltpu.make_async_copy(ref.at[skip : skip + size, source : source + width], to, sems.at[2 * i]))
        if skip and small_ref is not None:
            to = small_ref.at[pl.ds(pl.multiple_of(zy * extra, 16), extra), :]
            smalls.append(pltpu.make_async_copy(ref.at[:skip, : PARTS * LANES], to, sems.at[2 * i + 1]))
    return copies, smalls


def anywhere(values):
    return [pl.BlockSpec(memory_space=pltpu.HBM) for _ in values]


def project_kernel(count, parts, split, sizes, at_ref, *refs):
    sources, refs = refs[:parts], refs[parts:]
    per_head_ref, choice_ref, wide_ref, *refs = refs
    pieces, refs = refs[: count + 1], refs[count + 1 :]
    (first_ref, turned_ref, x_ref, bc_ref, head_ref, gain_ref,
     w_ref, held, params_ref, row_sems, piece_sems, tile_sems) = refs
    step = pl.program_id(0)
    rows = row_copies(sources, held, row_sems)

    @pl.when(step == 0)
    def _():
        at = MYC + BC
        tiles, _ = piece_copies(at_ref, pieces, w_ref, count, tile_sems, columns=(at, LANES), source=at)
        weights, _ = piece_copies(at_ref, pieces, w_ref, count, piece_sems, columns=(0, at))
        for copy in tiles + weights + sum(rows, []):
            copy.start()
        for copy in tiles:
            copy.wait()
        unpack_small(at_ref, split, sizes, w_ref, per_head_ref, choice_ref, wide_ref, gain_ref, x_ref, bc_ref, head_ref, params_ref)
        for copy in weights:
            copy.wait()

    wait_rows(step, rows)
    x = held[step].astype(F32)
    inv = lax.rsqrt(jnp.mean(x * x, axis=-1, keepdims=True) + EPS)
    low = (x * inv * gain_ref[0:1, :]).astype(BF16)
    turned_ref[...] = low.T
    first_ref[...] = nn(low, w_ref[...]).astype(BF16)


def project(place, split, sizes, own, near, far, both, per_head, heads, pieces):
    rows = own.shape[0]
    total = PARTS * rows
    count = lax.axis_size("zy")
    still = lambda t, *_: (0, 0)
    choice = jnp.asarray(head_choice(split), BF16)
    return pl.pallas_call(
        functools.partial(project_kernel, count, 2 + len(far) + len(both), split, sizes),
        grid_spec=pltpu.PrefetchScalarGridSpec(
            num_scalar_prefetch=1,
            grid=(total // ROWS,),
            in_specs=anywhere((own, near, *far, *both))
            + [
                pl.BlockSpec((8, LANES), still),
                pl.BlockSpec(choice.shape, lambda t, *_: (0, 0, 0)),
                pl.BlockSpec((2 * LANES, MYC), still),
            ]
            + anywhere(pieces),
            out_specs=[
                pl.BlockSpec((ROWS, W1), lambda t, *_: (t, 0)),
                pl.BlockSpec((D, ROWS), lambda t, *_: (0, t)),
                pl.BlockSpec((8, MYC), still),
                pl.BlockSpec((8, BC), still),
                pl.BlockSpec((8, LANES), still),
                pl.BlockSpec((8, D), still),
            ],
            scratch_shapes=[
                pltpu.VMEM((D, W1), BF16),
                pltpu.VMEM((PARTS, rows, D), BF16),
                pltpu.VMEM((8, DI), F32),
                pltpu.SemaphoreType.DMA((2 + len(far) + len(both),)),
                pltpu.SemaphoreType.DMA((2 * len(pieces),)),
                pltpu.SemaphoreType.DMA((2 * len(pieces),)),
            ],
        ),
        out_shape=[
            jax.ShapeDtypeStruct((total, W1), BF16),
            jax.ShapeDtypeStruct((D, total), BF16),
            jax.ShapeDtypeStruct((8, MYC), F32),
            jax.ShapeDtypeStruct((8, BC), F32),
            jax.ShapeDtypeStruct((8, LANES), F32),
            jax.ShapeDtypeStruct((8, D), F32),
        ],
        compiler_params=pltpu.CompilerParams(vmem_limit_bytes=56 * MIB),
        cost_estimate=pl.CostEstimate(flops=12 * 10**9, bytes_accessed=30 * 10**6, transcendentals=10**4),
        name="project",
    )(place, own, near, *far, *both, per_head, choice, heads, *pieces)


def silu_of(z):
    sig = sigmoid(z)
    return sig, z * sig


def meet_kernel(count, parts, blocked, at_ref, *refs):
    sources, refs = refs[:parts], refs[parts:]
    turned_ref, y_ref, taps_ref, *refs = refs
    blocks, refs = refs[: 1 + blocked], refs[1 + blocked :]
    *pieces, z_ref, d_two_ref, sums_ref, w_out_ref, w_ref, held, row_sems, piece_sems, out_sems = refs
    step = pl.program_id(0)
    half = D // 2
    rows = row_copies(sources, held, row_sems)

    @pl.when(step == 0)
    def _():
        copies, _ = piece_copies(at_ref, pieces, w_ref, count, piece_sems)
        if blocked:
            each, size, _ = blocks[0].shape
            size = size // 2
            for q in range(each):
                for i, (ref, part) in enumerate(zip(blocks, (at_ref[1], 1 - at_ref[1]))):
                    to = pl.ds(pl.multiple_of((2 * q + part) * size, 16), size)
                    for k in range(2):
                        copies.append(
                            pltpu.make_async_copy(
                                ref.at[q, k * size : (k + 1) * size, :],
                                w_out_ref.at[to, k * half : (k + 1) * half],
                                out_sems.at[4 * q + 2 * i + k],
                            )
                        )
        else:
            copies.append(pltpu.make_async_copy(blocks[0], w_out_ref, out_sems.at[0]))
        for copy in copies + sum(rows, []):
            copy.start()
        for copy in copies:
            copy.wait()

    wait_rows(step, rows)
    z = tn(turned_ref[...], w_ref[...]).astype(BF16)
    z_ref[...] = z
    _, silu = silu_of(z.astype(F32))
    joined = y_ref[...].astype(F32) * silu
    d_two = nt(held[step], w_out_ref[...])
    d_two_ref[...] = d_two.astype(BF16)
    row = lax.broadcasted_iota(jnp.int32, (8, MYC), 0)
    squares = nt((row == 0).astype(BF16), (joined * joined).astype(BF16))
    products = nt((row == 1).astype(BF16), (joined * taps_ref[6:7, :] * d_two).astype(BF16))
    sums_ref[...] = squares + products


def meet(place, own, near, far, both, turned, y, x_taps, blocks, pieces):
    rows = own.shape[0]
    total = PARTS * rows
    count = lax.axis_size("zy")
    still = lambda t, *_: (0, 0)
    here = lambda t, *_: (t, 0)
    blocked = len(blocks) > 1
    return pl.pallas_call(
        functools.partial(meet_kernel, count, 2 + len(far) + len(both), blocked),
        grid_spec=pltpu.PrefetchScalarGridSpec(
            num_scalar_prefetch=1,
            grid=(total // ROWS,),
            in_specs=anywhere((own, near, *far, *both))
            + [
                pl.BlockSpec((D, ROWS), lambda t, *_: (0, t)),
                pl.BlockSpec((ROWS, MYC), here),
                pl.BlockSpec((8, MYC), still),
            ]
            + anywhere((*blocks, *pieces)),
            out_specs=[
                pl.BlockSpec((ROWS, MYC), here),
                pl.BlockSpec((ROWS, MYC), here),
                pl.BlockSpec((8, ROWS), lambda t, *_: (0, t)),
                pl.BlockSpec((MYC, D), still),
            ],
            scratch_shapes=[
                pltpu.VMEM((D, MYC), BF16),
                pltpu.VMEM((PARTS, rows, D), BF16),
                pltpu.SemaphoreType.DMA((2 + len(far) + len(both),)),
                pltpu.SemaphoreType.DMA((2 * len(pieces),)),
                pltpu.SemaphoreType.DMA((4 * blocks[0].shape[0] if blocked else 1,)),
            ],
        ),
        out_shape=[
            jax.ShapeDtypeStruct((total, MYC), BF16),
            jax.ShapeDtypeStruct((total, MYC), BF16),
            jax.ShapeDtypeStruct((8, total), F32),
            jax.ShapeDtypeStruct((MYC, D), BF16),
        ],
        compiler_params=pltpu.CompilerParams(vmem_limit_bytes=56 * MIB),
        cost_estimate=pl.CostEstimate(flops=15 * 10**9, bytes_accessed=40 * 10**6, transcendentals=10**6),
        name="meet",
    )(place, own, near, *far, *both, turned, y, x_taps, *blocks, *pieces)


def out_kernel(parts, *refs):
    sources, refs = refs[:parts], refs[parts:]
    theirs_ref, mine_ref, d_theirs_ref, d_mine_ref, held, sems = refs
    step = pl.program_id(0)
    rows = row_copies(sources, held, sems)

    @pl.when(step == 0)
    def _():
        for copy in sum(rows, []):
            copy.start()
        for copy in sum(rows, []):
            copy.wait()

    for at, a_ref, out_ref in ((0, theirs_ref, d_theirs_ref), (2, mine_ref, d_mine_ref)):

        @pl.when((step >= at) & (step < at + 2))
        def _():
            every = held[...].reshape(PARTS * ROWS, D)
            out_ref[...] = nn(a_ref[...], every).astype(BF16)


def out_product(theirs, mine, own, near, far, both):
    rows, total = theirs.shape
    tile = rows // 2
    one = lambda t: (jnp.minimum(t, 1), 0)
    two = lambda t: (jnp.maximum(t - 2, 0), 0)
    return pl.pallas_call(
        functools.partial(out_kernel, 2 + len(far) + len(both)),
        grid=(4,),
        in_specs=anywhere((own, near, *far, *both))
        + [pl.BlockSpec((tile, total), one), pl.BlockSpec((tile, total), two)],
        out_specs=[pl.BlockSpec((tile, D), one), pl.BlockSpec((tile, D), two)],
        out_shape=[jax.ShapeDtypeStruct((rows, D), BF16)] * 2,
        scratch_shapes=[
            pltpu.VMEM((PARTS, ROWS, D), BF16),
            pltpu.SemaphoreType.DMA((2 + len(far) + len(both),)),
        ],
        compiler_params=pltpu.CompilerParams(vmem_limit_bytes=56 * MIB),
        cost_estimate=pl.CostEstimate(flops=8 * 10**9, bytes_accessed=20 * 10**6, transcendentals=0),
        name="out_product",
    )(own, near, *far, *both, theirs, mine)


def gate_kernel(
    unit, core_ref, sums_0, sums_1, sums_2, sums_3, y_ref, z_ref, d_two_ref, taps_ref, w_out_ref,
    d_ssm_ref, d_gate_ref, mine_ref, theirs_ref, own_ref, other_ref, turned,
):
    step = pl.program_id(0)
    sums = (sums_0[...] + sums_1[...] + sums_2[...] + sums_3[...]).T
    inv = lax.rsqrt(sums[:, 0:1] * (1.0 / DI) + EPS)
    shift = inv * inv * inv * (sums[:, 1:2] * (1.0 / DI))
    z = z_ref[...].astype(F32)
    sig, silu = silu_of(z)
    y = y_ref[...].astype(F32)
    joined = y * silu
    d_two = d_two_ref[...].astype(F32)
    two = (joined * inv * taps_ref[6:7, :]).astype(BF16)
    d_joined = inv * (taps_ref[6:7, :] * d_two) - joined * shift
    d_ssm_ref[...] = (d_joined * silu).astype(BF16)
    d_gate_ref[...] = (d_joined * y * (sig * (1.0 + z * (1.0 - sig)))).astype(BF16)
    branch = nn(two, w_out_ref[...]).astype(BF16)

    @pl.when(step < 4)
    def _():
        own_ref[...] = branch

    @pl.when(step >= 4)
    def _():
        other_ref[...] = branch

    turned[...] = two.T
    core = core_ref[0]
    for at in range(MYC // (2 * unit)):
        to = slice(at * unit, (at + 1) * unit)
        mine_ref[to, :] = turned[pl.ds(pl.multiple_of((2 * at + core) * unit, 16), unit), :]
        theirs_ref[to, :] = turned[pl.ds(pl.multiple_of((2 * at + 1 - core) * unit, 16), unit), :]


def gate_back(core, unit, sums, y, z, d_two, x_taps, w_out):
    total = y.shape[0]
    size = ROWS // 2
    still = lambda t, *_: (0, 0)
    here = lambda t, *_: (t, 0)
    across = lambda t, *_: (0, t)
    return pl.pallas_call(
        functools.partial(gate_kernel, unit),
        grid_spec=pltpu.PrefetchScalarGridSpec(
            num_scalar_prefetch=1,
            grid=(total // size,),
            in_specs=[pl.BlockSpec((8, size), lambda t, *_, r=r: (0, t ^ (2 * r))) for r in range(PARTS)]
            + [
                pl.BlockSpec((size, MYC), here),
                pl.BlockSpec((size, MYC), here),
                pl.BlockSpec((size, MYC), here),
                pl.BlockSpec((8, MYC), still),
                pl.BlockSpec((MYC, D), still),
            ],
            out_specs=[
                pl.BlockSpec((size, MYC), here),
                pl.BlockSpec((size, MYC), here),
                pl.BlockSpec((MYC // 2, size), across),
                pl.BlockSpec((MYC // 2, size), across),
                pl.BlockSpec((size, D), lambda t, *_: (jnp.minimum(t, 3), 0)),
                pl.BlockSpec((size, D), lambda t, *_: (jnp.maximum(t - 4, 0), 0)),
            ],
            scratch_shapes=[pltpu.VMEM((MYC, size), BF16)],
        ),
        out_shape=[
            jax.ShapeDtypeStruct((total, MYC), BF16),
            jax.ShapeDtypeStruct((total, MYC), BF16),
            jax.ShapeDtypeStruct((MYC // 2, total), BF16),
            jax.ShapeDtypeStruct((MYC // 2, total), BF16),
            jax.ShapeDtypeStruct((total // 2, D), BF16),
            jax.ShapeDtypeStruct((total // 2, D), BF16),
        ],
        compiler_params=pltpu.CompilerParams(vmem_limit_bytes=56 * MIB),
        cost_estimate=pl.CostEstimate(flops=8 * 10**9, bytes_accessed=30 * 10**6, transcendentals=10**6),
        name="gate_back",
    )(core, *sums, y, z, d_two, x_taps, w_out)


def normed_kernel(count, at, parts, at_ref, *refs):
    values, refs = refs[:parts], refs[parts:]
    firsts, gates, refs = refs[: count + 1], refs[count + 1 : 2 * count + 2], refs[2 * count + 2 :]
    other_ref, own_ref, weight, rows, first_sems, gate_sems, row_sems = refs
    step = pl.program_id(0)
    copies, _ = piece_copies(at_ref, firsts, weight, count, first_sems, columns=(0, W1))
    copies += piece_copies(at_ref, gates, weight, count, gate_sems, columns=(W1, MYC))[0]
    row_copies_of = []
    for i in range(2):
        start, col = (2 * (1 - i) + at) * ROWS, 0
        row_copies_of.append([])
        for k, ref in enumerate(values):
            width = ref.shape[1]
            row_copies_of[i].append(
                pltpu.make_async_copy(
                    ref.at[start : start + ROWS, :], rows.at[i, :, col : col + width], row_sems.at[i, k]
                )
            )
            col += width

    @pl.when(step == 0)
    def _():
        for copy in row_copies_of[0] + copies + row_copies_of[1]:
            copy.start()
        for copy in copies:
            copy.wait()

    for i, ref in enumerate((other_ref, own_ref)):

        @pl.when(step == i)
        def _():
            for copy in row_copies_of[i]:
                copy.wait()
            ref[...] = nt(rows[i], weight[...]).astype(BF16)


def normed_part(at, place, d_x0, d_x1, d_bc, d_dt, d_gate, firsts, gates):
    still = lambda t, *_: (0, 0)
    values = [d_x0, d_x1, d_bc, d_dt, d_gate]
    count = len(firsts) - 1
    return pl.pallas_call(
        functools.partial(normed_kernel, count, at, len(values)),
        grid_spec=pltpu.PrefetchScalarGridSpec(
            num_scalar_prefetch=1,
            grid=(2,),
            in_specs=anywhere((*values, *firsts, *gates)),
            out_specs=[pl.BlockSpec((ROWS, D), still)] * 2,
            scratch_shapes=[
                pltpu.VMEM((D, W1 + MYC), BF16),
                pltpu.VMEM((2, ROWS, W1 + MYC), BF16),
                pltpu.SemaphoreType.DMA((2 * len(firsts),)),
                pltpu.SemaphoreType.DMA((2 * len(gates),)),
                pltpu.SemaphoreType.DMA((2, len(values))),
            ],
        ),
        out_shape=[jax.ShapeDtypeStruct((ROWS, D), BF16)] * 2,
        compiler_params=pltpu.CompilerParams(vmem_limit_bytes=56 * MIB),
        cost_estimate=pl.CostEstimate(flops=8 * 10**9, bytes_accessed=20 * 10**6, transcendentals=0),
        name="normed_part_%d" % at,
    )(place, *values, *firsts, *gates)


def flat(rows, spread, size):
    value = nn(rows.astype(BF16), spread)
    device = lax.broadcasted_iota(jnp.int32, value.shape, 0)
    lane = lax.broadcasted_iota(jnp.int32, value.shape, 1)
    own = (lane >= device * size) & (lane < (device + 1) * size)
    return jnp.sum(jnp.where(own, value, 0.0), axis=0, keepdims=True)


def spread_of(size, count):
    shape = (LANES, count * PARTS * size)
    lane = lax.broadcasted_iota(jnp.int32, shape, 1).astype(F32)
    part = lane - jnp.floor((lane + 0.5) * (1.0 / size)) * size
    return (part == lax.broadcasted_iota(jnp.int32, shape, 0).astype(F32)).astype(BF16)


def unpack_small(at_ref, split, sizes, w_ref, per_head_ref, choice_ref, wide_ref, gain_ref, x_ref, bc_ref, head_ref, held):
    group = at_ref[2]
    every = D // sizes[0]
    count = every // PARTS
    at = lax.broadcasted_iota(jnp.int32, (SEG_AT * every, D), 0)
    chosen = lax.broadcasted_iota(jnp.int32, at.shape, 1) == (at % every) * sizes[0] + at // every
    small = pltpu.roll(nn(chosen.astype(BF16), w_ref[:, MYC + BC :]), LANES - FREE, 1)
    small = [small[r * every : (r + 1) * every] for r in range(SEG_AT)]
    gain_ref[...] = jnp.broadcast_to(flat(small[0], spread_of(sizes[0], count), sizes[0]), gain_ref.shape)
    spread = spread_of(sizes[1], count)
    conv = [flat(small[r], spread, sizes[1]) for r in (2, 3, 4, 5, 1)]
    for k, v in enumerate(conv):
        held[k : k + 1, :] = v[:, :DI]
        bc_ref[k : k + 1, :] = v[:, DI:]
    bc_ref[5:8, :] = jnp.zeros((3, BC), F32)
    held[6:7, :] = flat(small[6], spread_of(sizes[2], count), sizes[2])
    held[5:6, :] = jnp.zeros((1, DI), F32)
    held[7:8, :] = jnp.zeros((1, DI), F32)
    per_head = in_three(per_head_ref[...], 1)
    mine = jnp.zeros((8, LANES), F32)
    for g in range(PARTS):
        chosen = nn(per_head, jnp.concatenate([choice_ref[g]] * 3, axis=0))
        mine = jnp.where(group == g, chosen, mine)

        @pl.when(group == g)
        def _():
            tiles = halves(lambda t: held[:, t * LANES : (t + 1) * LANES], half_places(split, g // 2, g % 2))
            for k, tile in enumerate(tiles):
                x_ref[:, k * LANES : (k + 1) * LANES] = tile

    head_ref[...] = mine
    wide = jnp.concatenate([wide_ref[:LANES, :]] * 3, axis=0)
    x_ref[5:6, :] = nn(in_three(mine, 1), wide)[2:3, :]


def marks_kernel(side_ref, *refs):
    *parts, marks_ref, rows_ref, seg, taken = refs
    side = side_ref[0]
    blocks = LEN // Q
    for s in range(2):
        for j in range(blocks):
            half, row = j // (blocks // 2), j % (blocks // 2)
            near, far = parts[2 * s + half], parts[2 * s + 1 - half]
            at = slice(SEG_AT + row, SEG_AT + row + 1)
            to = s * blocks + j
            seg[to : to + 1, :] = jnp.where(side == 0, near[at, :LANES].astype(F32), far[at, :LANES].astype(F32))
    value = seg[...]
    count = 2 * blocks
    lane = lax.broadcasted_iota(jnp.int32, value.shape, 1)
    row = lax.broadcasted_iota(jnp.int32, value.shape, 0) % blocks
    last = jnp.broadcast_to(value[:, Q - 1 : Q], value.shape)
    taken[...] = jnp.zeros_like(taken)
    taken[0] = value
    for k in range(KW - 1):
        by = KW - 1 - k
        turned = pltpu.roll(value, by, 1)
        early = lane < by
        behind = jnp.where(early, pltpu.roll(turned, 1, 0), turned)
        taken[1 + k] = ((behind == value) & ~(early & (row == 0))).astype(F32)
        turned = pltpu.roll(value, Q - by, 1)
        late = lane >= Q - by
        beyond = jnp.where(late, pltpu.roll(turned, count - 1, 0), turned)
        taken[4 + k] = ((beyond == value) & ~(late & (row == blocks - 1))).astype(F32)
    taken[7] = ((pltpu.roll(last, 1, 0) == value) & (row > 0)).astype(F32)
    taken[8] = (last == value).astype(F32)
    for r in range(count):
        rows_ref[r] = value[r : r + 1, :]
        marks_ref[r] = jnp.concatenate([taken[i, r : r + 1, :] for i in range(16)], axis=0).T


def segment_marks(side, *parts):
    count = 2 * (LEN // Q)
    specs = [pl.BlockSpec((EXTRA, LANES), lambda t: (0, 0))] * PARTS
    marks, rows = pl.pallas_call(
        marks_kernel,
        grid=(1,),
        out_shape=[
            jax.ShapeDtypeStruct((count, Q, 16), F32),
            jax.ShapeDtypeStruct((count, 1, Q), F32),
        ],
        in_specs=[smem()] + specs,
        scratch_shapes=[pltpu.VMEM((count, Q), F32), pltpu.VMEM((16, count, Q), F32)],
        compiler_params=pltpu.CompilerParams(vmem_limit_bytes=56 * MIB),
        name="segment_marks",
    )(side, *parts)
    return marks.reshape(2, LEN, 16), rows.reshape(2, LEN // Q, 1, Q)


def weight_kernel(a_ref, *refs):
    *bs, out_ref, held, sems = refs
    copies, at = [], 0
    for i, b in enumerate(bs):
        copies.append(pltpu.make_async_copy(b, held.at[:, at : at + b.shape[1]], sems.at[i]))
        at += b.shape[1]

    @pl.when(pl.program_id(0) == 0)
    def _():
        for copy in copies:
            copy.start()
        for copy in copies:
            copy.wait()

    out_ref[...] = nn(a_ref[...], held[...]).astype(BF16)


def both_kernel(a_ref, b_ref, core_ref, mine_ref, theirs_ref, out_ref):
    each, rows, cols = out_ref.shape
    out_ref[:, :, : b_ref.shape[1]] = nn(a_ref[...], b_ref[...]).astype(BF16).reshape(each, rows, b_ref.shape[1])
    size = rows // 2
    blocks = mine_ref.shape[0] // size
    for k in range(each):
        zy = pl.program_id(0) * each + k
        at = pl.ds(pl.multiple_of(zy % blocks * size, 16), size)
        for own, ref in ((True, mine_ref), (False, theirs_ref)):

            @pl.when((zy // blocks == core_ref[0]) == own)
            def _():
                out_ref[k, :size, b_ref.shape[1] :] = ref[at, : D // 2]
                out_ref[k, size:, b_ref.shape[1] :] = ref[at, D // 2 :]


def both_products(count, core, a, b, mine, theirs):
    rows, total = a.shape
    each = 2
    tile = rows // count * each
    still = lambda t: (0, 0)
    return pl.pallas_call(
        both_kernel,
        grid=(count // each,),
        in_specs=[
            pl.BlockSpec((tile, total), lambda t: (t, 0)),
            pl.BlockSpec(b.shape, still),
            smem(),
            pl.BlockSpec(mine.shape, still),
            pl.BlockSpec(theirs.shape, still),
        ],
        out_specs=pl.BlockSpec((each, rows // count, b.shape[1] + D // 2), lambda t: (t, 0, 0)),
        out_shape=jax.ShapeDtypeStruct((count, rows // count, b.shape[1] + D // 2), BF16),
        compiler_params=pltpu.CompilerParams(vmem_limit_bytes=56 * MIB),
        cost_estimate=pl.CostEstimate(flops=8 * 10**9, bytes_accessed=20 * 10**6, transcendentals=0),
        name="both_products",
    )(a, b, core, mine, theirs)


def weight_product(a, *bs, tile=512):
    rows, total = a.shape
    tile = min(tile, rows)
    columns = sum(b.shape[1] for b in bs)
    return pl.pallas_call(
        weight_kernel,
        grid=(rows // tile,),
        in_specs=[pl.BlockSpec((tile, total), lambda t: (t, 0))] + anywhere(bs),
        out_specs=pl.BlockSpec((tile, columns), lambda t: (t, 0)),
        out_shape=jax.ShapeDtypeStruct((rows, columns), BF16),
        scratch_shapes=[pltpu.VMEM((total, columns), BF16), pltpu.SemaphoreType.DMA((len(bs),))],
        compiler_params=pltpu.CompilerParams(vmem_limit_bytes=56 * MIB),
        cost_estimate=pl.CostEstimate(flops=8 * 10**9, bytes_accessed=20 * 10**6, transcendentals=0),
        name="weight_product",
    )(a, *bs)


def finish_kernel(x_ref, cot_ref, gain_ref, own_ref, got_ref, *refs):
    *far, out_ref, held, sems = refs
    step = pl.program_id(0)
    copies, row = [], 0
    for i, ref in enumerate(far):
        copies.append(pltpu.make_async_copy(ref, held.at[row : row + ref.shape[0], :], sems.at[i]))
        row += ref.shape[0]

    @pl.when(step == 0)
    def _():
        for copy in copies:
            copy.start()
        for copy in copies:
            copy.wait()

    d_normed = own_ref[...].astype(F32) + got_ref[...].astype(F32)
    d_normed = d_normed + held[pl.ds(pl.multiple_of(step * Q, Q), Q), :].astype(F32)
    x = x_ref[...].astype(F32)
    inv = lax.rsqrt(jnp.mean(x * x, axis=-1, keepdims=True) + EPS)
    scaled = gain_ref[0:1, :] * d_normed
    shift = inv * inv * inv * jnp.mean(x * scaled, axis=-1, keepdims=True)
    out_ref[...] = cot_ref[...].astype(F32) + inv * scaled - x * shift


def finish_tokens(x, cot, gain, own, got, *far):
    rows = x.shape[0]
    here = pl.BlockSpec((Q, D), lambda t: (t, 0))
    return pl.pallas_call(
        finish_kernel,
        grid=(rows // Q,),
        in_specs=[here, here, pl.BlockSpec((8, D), lambda t: (0, 0)), here, here] + anywhere(far),
        out_specs=here,
        out_shape=jax.ShapeDtypeStruct((rows, D), F32),
        scratch_shapes=[pltpu.VMEM((rows, D), BF16), pltpu.SemaphoreType.DMA((len(far),))],
        compiler_params=pltpu.CompilerParams(vmem_limit_bytes=56 * MIB),
        cost_estimate=pl.CostEstimate(flops=8 * 10**9, bytes_accessed=50 * 10**6, transcendentals=0),
        name="finish_tokens",
    )(x, cot, gain, own, got, *far)


def softplus(value):
    return jnp.maximum(value, 0.0) + jnp.log1p(jnp.exp(-jnp.abs(value)))


def conv_total(ext, shifts, raw, halo, taps_ref, marks):
    ext[0:8, :] = halo[8:16, :].astype(F32)
    ext[8 : 8 + Q, :] = raw.astype(F32)
    total = taps_ref[4:5, :] + ext[8 : 8 + Q, :] * taps_ref[3:4, :]
    for k in range(KW - 1):
        shifted = ext[5 + k : 5 + k + Q, :] * marks[:, 1 + k : 2 + k]
        if shifts is not None:
            shifts[k] = shifted
        total = total + shifted * taps_ref[k : k + 1, :]
    return total


def conv_back(d_total, ext, shifts, ahead, taps_ref, marks, sums_ref):
    sums_ref[4:5, :] += jnp.sum(d_total, axis=0, keepdims=True)
    sums_ref[3:4, :] += jnp.sum(d_total * ext[8 : 8 + Q, :], axis=0, keepdims=True)
    for k in range(KW - 1):
        sums_ref[k : k + 1, :] += jnp.sum(d_total * shifts[k], axis=0, keepdims=True)
    ext[0:Q, :] = d_total
    ext[Q : Q + 8, :] = ahead[...]
    d_raw = d_total * taps_ref[3:4, :]
    for k in range(KW - 1):
        d_raw = d_raw + ext[3 - k : 3 - k + Q, :] * (taps_ref[k : k + 1, :] * marks[:, 4 + k : 5 + k])
    ahead[...] = d_total[0:8, :]
    return d_raw


def scan_forward(
    part, side_ref, x_ref, x_halo, bc_ref, bc_halo, dt_ref, marks_ref, row_ref, x_taps, bc_taps, head_ref, heads_ref,
    *rest,
):
    if part > 0:
        before, rest = rest[6], rest[7:]
    y_ref, state_ref, bc_out, step_out, cum_out, turned_out, helds, exts, bc_exts = rest
    chunk = pl.program_id(0)

    @pl.when(chunk == 0)
    def _():
        helds[...] = before[...] if part > 0 else jnp.zeros_like(helds)

    at_row = lax.broadcasted_iota(jnp.int32, (Q, Q), 0)
    at_col = lax.broadcasted_iota(jnp.int32, (Q, Q), 1)
    lane = lax.broadcasted_iota(jnp.int32, (Q, LANES), 1)
    lower = (at_row >= at_col).astype(BF16)
    lower = jnp.concatenate([lower] * 3, axis=1)
    rate = -jnp.exp(head_ref[1:2, :])

    def one(s, _):
        marks = marks_ref[s]
        held = helds.at[s]
        live = lane < MYH
        step = jnp.where(live, softplus(jnp.where(live, dt_ref[s].astype(F32), 0.0) + head_ref[0:1, :]), 0.0)
        cum = nn(lower, in_three(rate * step, 0))
        cum_t = cum.T
        step_out[s] = step
        cum_out[s] = cum
        turned_out[s, 0] = cum_t[:16, :]
        step_wide, keep, tail, carry = over_heads_all((step,) + spreads(cum, marks), heads_ref)
        x_act = conv_total(exts.at[s], None, x_ref[s], x_halo[s], x_taps, marks)
        x_act = x_act * sigmoid(x_act)
        bc_act = conv_total(bc_exts.at[s], None, bc_ref[s], bc_halo[s], bc_taps, marks)
        bc_act = (bc_act * sigmoid(bc_act)).astype(BF16)
        bc_out[s] = bc_act
        b, c = bc_act[:, :NS], bc_act[:, NS:]
        shut = jnp.where((at_row >= at_col) & (marks[:, 0:1] == row_ref[s, 0]), 0.0, FAR)
        scores = nt(c, b)
        state = held[...]
        state_low = state.astype(BF16)
        state_ref[s, 0] = state_low
        x_step = x_act * step_wide
        y = nn(c, state_low) * keep + x_act * x_taps[5:6, :]
        held[...] = state * carry[0:1, :] + nn(b.T, (x_step * tail).astype(BF16))
        for pair in range(MYH // 2):
            cols = slice(pair * LANES, (pair + 1) * LANES)
            mixing = []
            for head in (2 * pair, 2 * pair + 1):
                spread = cum[:, head : head + 1] - cum_t[head : head + 1, :] + shut
                mixing.append((jnp.exp(spread) * scores).astype(BF16))
            steps = x_step[:, cols]
            both = jnp.concatenate(
                [jnp.where(lane < HD, steps, 0.0), jnp.where(lane < HD, 0.0, steps)], axis=0
            ).astype(BF16)
            y_ref[s, :, cols] = (y[:, cols] + nn(jnp.concatenate(mixing, axis=1), both)).astype(BF16)
        return 0

    lax.fori_loop(0, 2, one, 0)


def scan_backward(
    group, part, side_ref, x_ref, x_halo, bc_ref, step_ref, cum_ref, turned_ref, dy_ref, state_ref, marks_ref, row_ref,
    x_taps, head_ref, heads_ref, *rest,
):
    final = group == GROUPS - 1
    if group > 0:
        dbc_before, ddt_before, *rest = rest
    if final:
        bc_raw_ref, bc_halo, dt_ref, bc_taps, *rest = rest
    carried = 6 if final else 4
    if part > 0:
        before, rest = rest[3 : 3 + carried], rest[3 + carried :]
    dx_ref, dbc_ref, ddt_ref, wide_ref, thin_ref, *rest = rest
    if final:
        bc_sums, *rest = rest
    helds, aheads, *rest = rest
    if final:
        bc_aheads, *rest = rest
    exts, shifts, *rest = rest
    if final:
        bc_exts, bc_shifts = rest
    chunk = pl.program_id(0)

    @pl.when(chunk == 0)
    def _():
        running = [wide_ref, thin_ref] + ([bc_sums] if final else []) + [helds, aheads]
        running += [bc_aheads] if final else []
        for i, ref in enumerate(running):
            ref[...] = before[i][...] if part > 0 else jnp.zeros_like(ref)

    at_row = lax.broadcasted_iota(jnp.int32, (Q, Q), 0)
    at_col = lax.broadcasted_iota(jnp.int32, (Q, Q), 1)
    lane = lax.broadcasted_iota(jnp.int32, (Q, LANES), 1)
    low_lanes, high_lanes = group * GH, LANES - (group + 1) * GH
    upper = (at_row <= at_col).astype(BF16)
    strict = (at_row > at_col).astype(BF16)
    spans = jnp.concatenate([upper, upper, strict, strict], axis=1)
    rate = -jnp.exp(head_ref[1:2, :])
    thin = [(step_ref[s],) + spreads(cum_ref[s], marks_ref[s]) for s in range(2)]
    wide = over_heads_all([v for some in thin for v in some], heads_ref)
    made = []
    for s in range(2):
        marks = marks_ref[s]
        held = helds.at[s]
        step_wide, keep, tail, carry = wide[4 * s : 4 * s + 4]
        total = conv_total(exts.at[s], shifts.at[s], x_ref[s], x_halo[s], x_taps, marks)
        gate = sigmoid(total)
        x_act = total * gate
        slope = gate * (1.0 + total * (1.0 - gate))
        b, c = bc_ref[s, :, :NS], bc_ref[s, :, NS:]
        dy = dy_ref[s].astype(F32)
        x_step = x_act * step_wide
        state = state_ref[s, 0]
        d_state = held[...]
        d_state_low = d_state.astype(BF16)
        dy_keep = dy * keep
        dy_keep_low = dy_keep.astype(BF16)
        from_state = nn(c, state)
        d_c = nt(dy_keep_low, state)
        d_b = nt((x_step * tail).astype(BF16), d_state_low)
        du_tail = nn(b, d_state_low) * tail
        linked = jnp.sum(d_state * state.astype(F32), axis=0, keepdims=True)
        linked = jnp.broadcast_to(linked, (8, GC))
        held[...] = d_state * carry[0:1, :] + nn(c.T, dy_keep_low)
        made.append((dy, x_act, slope, x_step, b, c, d_b, d_c, du_tail, dy_keep * from_state, x_step * du_tail, linked))
    sums = sum_heads_all([v for some in made for v in some[9:]], heads_ref)
    d_us = []
    for s in range(2):
        marks = marks_ref[s]
        dy, x_act, slope, x_step, b, c, d_b, d_c, du_tail = made[s][:9]
        cum, cum_t = cum_ref[s], turned_ref[s, 0]
        shut = jnp.where((at_row <= at_col) & (marks[:, 0:1] == row_ref[s, 0]), 0.0, FAR)
        scores = nt(b, c)
        d_scores = jnp.zeros((Q, Q), F32)
        by_later, by_earlier, du_parts = [], [], []
        for pair in range(GH // 2):
            cols = slice(pair * LANES, (pair + 1) * LANES)
            steps, dys = x_step[:, cols], dy[:, cols]
            step_both = jnp.concatenate(
                [jnp.where(lane < HD, steps, 0.0), jnp.where(lane < HD, 0.0, steps)], axis=0
            ).astype(BF16)
            dy_both = jnp.concatenate(
                [jnp.where(lane < HD, dys, 0.0), jnp.where(lane < HD, 0.0, dys)], axis=0
            ).astype(BF16)
            met = nt(step_both, dys.astype(BF16))
            mixing = []
            for place in range(2):
                head = low_lanes + 2 * pair + place
                decay = jnp.exp(cum_t[head : head + 1, :] - cum[:, head : head + 1] + shut)
                mixing.append((decay * scores).astype(BF16))
                weighed = decay * met[place * Q : (place + 1) * Q, :]
                d_scores = d_scores + weighed
                spent = weighed * scores
                by_later.append(jnp.sum(spent, axis=0, keepdims=True))
                by_earlier.append(jnp.sum(spent, axis=1, keepdims=True))
            du_parts.append(nn(jnp.concatenate(mixing, axis=1), dy_both))
        du = jnp.concatenate(du_parts, axis=1) + du_tail
        d_low = d_scores.astype(BF16)
        d_b = d_b + nn(d_low, c)
        d_c = d_c + nn(d_scores.T.astype(BF16), b)
        d_bc = jnp.concatenate([d_b, d_c], axis=1)
        if group > 0:
            d_bc = d_bc + dbc_before[s]
        if final:
            bc_total = conv_total(bc_exts.at[s], bc_shifts.at[s], bc_raw_ref[s], bc_halo[s], bc_taps, marks)
            bc_gate = sigmoid(bc_total)
            d_bc = d_bc * (bc_gate * (1.0 + bc_total * (1.0 - bc_gate)))
            d_bc = conv_back(d_bc, bc_exts.at[s], bc_shifts.at[s], bc_aheads.at[s], bc_taps, marks, bc_sums)
        dbc_ref[s] = d_bc.astype(dbc_ref.dtype)
        later = by_later + [jnp.zeros((high_lanes, Q), F32)]
        later = ([jnp.zeros((low_lanes, Q), F32)] if low_lanes else []) + later
        later = jnp.concatenate(later, axis=0).T
        earlier = jnp.zeros((Q, LANES), F32)
        for head in range(GH):
            earlier = jnp.where(lane == low_lanes + head, by_earlier[head], earlier)
        d_us.append((du, later - earlier))
    d_steps = sum_heads_all([made[s][1] * d_us[s][0] for s in range(2)], heads_ref)
    for s in range(2):
        marks = marks_ref[s]
        dy, x_act, slope = made[s][:3]
        du, within = d_us[s]
        seen, sent, linked = sums[3 * s : 3 * s + 3]
        step = step_ref[s]
        linked = linked[0:1, :] * thin[s][3][0:1, :]
        mine = (lane >= low_lanes) & (lane < low_lanes + GH)
        crossed = jnp.concatenate([in_two(seen + within, 0), in_two(sent, 0)], axis=0)
        d_log = jnp.where(mine, nn(spans, crossed) + linked, 0.0)
        d_raw = d_steps[s] + rate * d_log
        if group > 0:
            d_raw = d_raw + ddt_before[s]
        if final:
            live = lane < MYH
            d_raw = jnp.where(live, d_raw * sigmoid(jnp.where(live, dt_ref[s].astype(F32), 0.0) + head_ref[0:1, :]), 0.0)
            thin_ref[0:1, :] += jnp.sum(d_raw, axis=0, keepdims=True)
        ddt_ref[s] = d_raw.astype(ddt_ref.dtype)
        thin_ref[1:2, :] += jnp.sum(d_log * (rate * step), axis=0, keepdims=True)
        wide_ref[5:6, :] += jnp.sum(dy * x_act, axis=0, keepdims=True)
        d_total = (du * wide[4 * s] + dy * x_taps[5:6, :]) * slope
        d_raw = conv_back(d_total, exts.at[s], shifts.at[s], aheads.at[s], x_taps, marks, wide_ref)
        dx_ref[s] = d_raw.astype(BF16)


def block_at(time, side):
    blocks = LEN // Q
    return (time + side * (blocks // 2)) % blocks


def halo_at(time, side):
    return block_at(jnp.maximum(time - 1, 0), side) * (Q // 16) + Q // 16 - 1


BC_AT = MYC // BC
DT_AT = (MYC + BC) // LANES


def run_forward(part, side, first, marks, rows, x_taps, bc_taps, head_rows, heads, before):
    blocks = LEN // Q
    steps = blocks // 2
    now = lambda t: part * steps + t
    here = lambda col: lambda t, side: (0, block_at(now(t), side[0]), col)
    halo = lambda col: lambda t, side: (0, halo_at(now(t), side[0]), col)
    time = lambda t, side: (0, now(t), 0)
    time_four = lambda t, side: (0, now(t), 0, 0)
    still = lambda t, side: (0, 0)
    inputs = [first, first, first, first, first, marks, rows, x_taps, bc_taps, head_rows, heads]
    in_specs = [
        pl.BlockSpec((2, Q, MYC), here(0)),
        pl.BlockSpec((2, 16, MYC), halo(0)),
        pl.BlockSpec((2, Q, BC), here(BC_AT)),
        pl.BlockSpec((2, 16, BC), halo(BC_AT)),
        pl.BlockSpec((2, Q, LANES), here(DT_AT)),
        pl.BlockSpec((2, Q, 16), time),
        pl.BlockSpec((2, 1, 1, Q), time_four),
        pl.BlockSpec((8, MYC), still),
        pl.BlockSpec((8, BC), still),
        pl.BlockSpec((8, LANES), still),
        pl.BlockSpec((2 * LANES, MYC), still),
    ]
    running = pl.BlockSpec((2, NS, MYC), lambda t, side: (0, 0, 0))
    aliases = {}
    if part > 0:
        aliases = {1 + len(inputs) + i: i for i in range(6)}
        inputs += before
        in_specs += [pl.BlockSpec(memory_space=pl.ANY)] * 6 + [running]
    return pl.pallas_call(
        functools.partial(scan_forward, part),
        grid_spec=pltpu.PrefetchScalarGridSpec(
            num_scalar_prefetch=1,
            grid=(steps,),
            in_specs=in_specs,
            out_specs=[
                pl.BlockSpec((2, Q, MYC), here(0)),
                pl.BlockSpec((2, 1, NS, MYC), time_four),
                pl.BlockSpec((2, Q, BC), here(0)),
                pl.BlockSpec((2, Q, LANES), time),
                pl.BlockSpec((2, Q, LANES), time),
                pl.BlockSpec((2, 1, 16, Q), time_four),
                running,
            ],
            scratch_shapes=[pltpu.VMEM((2, Q + 8, MYC), F32), pltpu.VMEM((2, Q + 8, BC), F32)],
        ),
        out_shape=[
            jax.ShapeDtypeStruct((2, LEN, MYC), BF16),
            jax.ShapeDtypeStruct((2, blocks, NS, MYC), BF16),
            jax.ShapeDtypeStruct((2, LEN, BC), BF16),
            jax.ShapeDtypeStruct((2, LEN, LANES), F32),
            jax.ShapeDtypeStruct((2, LEN, LANES), F32),
            jax.ShapeDtypeStruct((2, blocks, 16, Q), F32),
            jax.ShapeDtypeStruct((2, NS, MYC), F32),
        ],
        input_output_aliases=aliases,
        compiler_params=pltpu.CompilerParams(vmem_limit_bytes=18 * MIB),
        cost_estimate=pl.CostEstimate(flops=9 * 10**9, bytes_accessed=30 * 10**6, transcendentals=10**7),
        name="scan_forward_%d" % part,
    )(side, *inputs)


def run_backward(group, part, side, first, scanned, d_ssm, marks, rows, x_taps, bc_taps, head_rows, heads, d_bc, before):
    _, states, bc_act, step, cum, turned, _ = scanned
    blocks = LEN // Q
    steps = blocks // 2
    final = group == GROUPS - 1
    now = lambda t: blocks - 1 - part * steps - t
    here = lambda col: lambda t, side: (0, block_at(now(t), side[0]), col)
    halo = lambda col: lambda t, side: (0, halo_at(now(t), side[0]), col)
    time = lambda t, side: (0, now(t), 0)
    time_four = lambda col: lambda t, side: (0, now(t), 0, col)
    still = lambda t, side: (0, 0)
    still_three = lambda t, side: (0, 0, 0)
    share = lambda t, side: (0, group)
    in_specs = [
        pl.BlockSpec((2, Q, GC), here(group)),
        pl.BlockSpec((2, 16, GC), halo(group)),
        pl.BlockSpec((2, Q, BC), here(0)),
        pl.BlockSpec((2, Q, LANES), time),
        pl.BlockSpec((2, Q, LANES), time),
        pl.BlockSpec((2, 1, 16, Q), time_four(0)),
        pl.BlockSpec((2, Q, GC), here(group)),
        pl.BlockSpec((2, 1, NS, GC), time_four(group)),
        pl.BlockSpec((2, Q, 16), time),
        pl.BlockSpec((2, 1, 1, Q), time_four(0)),
        pl.BlockSpec((8, GC), share),
        pl.BlockSpec((8, LANES), still),
        pl.BlockSpec((2 * LANES, GC), share),
    ]
    inputs = [first, first, bc_act, step, cum, turned, d_ssm, states, marks, rows, x_taps, head_rows, heads]
    if group > 0:
        in_specs += [pl.BlockSpec((2, Q, BC), here(0)), pl.BlockSpec((2, Q, LANES), here(0))]
        inputs += d_bc
    if final:
        in_specs += [
            pl.BlockSpec((2, Q, BC), here(BC_AT)),
            pl.BlockSpec((2, 16, BC), halo(BC_AT)),
            pl.BlockSpec((2, Q, LANES), here(DT_AT)),
            pl.BlockSpec((8, BC), still),
        ]
        inputs += [first, first, first, bc_taps]
    running = [(8, GC), (8, LANES)] + ([(8, BC)] if final else []) + [(2, NS, GC), (2, 8, GC)]
    running += [(2, 8, BC)] if final else []
    running_specs = [pl.BlockSpec(v, still if len(v) == 2 else still_three) for v in running]
    out_specs = [
        pl.BlockSpec((2, Q, GC), here(0)),
        pl.BlockSpec((2, Q, BC), here(0)),
        pl.BlockSpec((2, Q, LANES), here(0)),
    ] + running_specs
    out_shape = [
        jax.ShapeDtypeStruct((2, LEN, GC), BF16),
        jax.ShapeDtypeStruct((2, LEN, BC), BF16 if final else F32),
        jax.ShapeDtypeStruct((2, LEN, LANES), BF16 if final else F32),
    ] + [jax.ShapeDtypeStruct(v, F32) for v in running]
    aliases = {}
    if part > 0:
        aliases = {1 + len(inputs) + i: i for i in range(3)}
        in_specs += [pl.BlockSpec(memory_space=pl.ANY)] * 3 + running_specs
        inputs += before
    scratch = [pltpu.VMEM((2, Q + 8, GC), F32), pltpu.VMEM((2, KW - 1, Q, GC), F32)]
    if final:
        scratch += [pltpu.VMEM((2, Q + 8, BC), F32), pltpu.VMEM((2, KW - 1, Q, BC), F32)]
    return pl.pallas_call(
        functools.partial(scan_backward, group, part),
        grid_spec=pltpu.PrefetchScalarGridSpec(
            num_scalar_prefetch=1, grid=(steps,), in_specs=in_specs, out_specs=out_specs, scratch_shapes=scratch
        ),
        out_shape=out_shape,
        input_output_aliases=aliases,
        compiler_params=pltpu.CompilerParams(vmem_limit_bytes=56 * MIB),
        cost_estimate=pl.CostEstimate(flops=14 * 10**9, bytes_accessed=40 * 10**6, transcendentals=10**7),
        name="scan_backward_%d_%d" % (group, part),
    )(side, *inputs)


def lead(value, by):
    if by == 0:
        return value
    pad = [(0, 0)] * value.ndim
    if by > 0:
        pad[1] = (0, by)
        return jnp.pad(value, pad)[:, by:]
    pad[1] = (-by, 0)
    return jnp.pad(value, pad)[:, :by]


def fold(block):
    return jnp.concatenate([block[..., : D // 2], block[..., D // 2 :]], axis=-2)


def unfold(block):
    half = block.shape[-2] // 2
    return jnp.concatenate([block[..., :half, :], block[..., half:, :]], axis=-1)


def out_whole(out_weight, split, core, side):
    whole = lax.all_gather(out_weight, ("zy", "core", "seq"), axis=0, tiled=True)
    return pick(pick(split_heads(whole, 0, split), core), side)


def out_scattered(grad, split, core, side):
    own = jnp.zeros((2, 2, MYC, D), BF16)
    own = lax.dynamic_update_slice(own, grad.astype(BF16)[None, None], (core, side, 0, 0))
    whole = join_heads(own, 0, split)
    return lax.psum_scatter(whole, ("zy", "core", "seq"), scatter_dimension=0, tiled=True)


def own_slice(whole, size):
    at = (lax.axis_index("zy") * 2 + lax.axis_index("core")) * 2 + lax.axis_index("seq")
    return lax.dynamic_slice_in_dim(whole, at * size, size, 0)


def body(
    tokens,
    segments,
    norm_gain,
    in_weight,
    conv_weight,
    conv_bias,
    dt_bias,
    a_log,
    d_skip,
    gated_gain,
    out_weight,
    cotangent,
):
    count = lax.axis_size("zy")
    core, side = lax.axis_index("core"), lax.axis_index("seq")
    split = head_split(count)
    rows = tokens.shape[1]
    total = PARTS * rows

    blocked = split[0] > 1

    me = (core * 2 + side).astype(jnp.int32).reshape(1)
    at_side = side.astype(jnp.int32).reshape(1)
    at_core = core.astype(jnp.int32).reshape(1)
    at_ring = jnp.stack([ring_place(count)[0], core, core * 2 + side]).astype(jnp.int32)

    heads = np.kron(np.eye(LANES, MYH, dtype=np.float32), np.ones((1, HD), np.float32))
    heads = jnp.asarray(np.concatenate([heads, heads], axis=0), BF16)
    per_head = jnp.stack([dt_bias, a_log, d_skip])
    per_head = jnp.pad(per_head, ((0, 5), (0, LANES - NH)))

    sizes = (norm_gain.shape[0], conv_bias.shape[0], gated_gain.shape[0])
    seg_own = segments[0].reshape(-1, LANES)
    mix = split_columns(in_weight, norm_gain, conv_weight, conv_bias, gated_gain, seg_own, split, me)
    mix = Task(peer_steps(mix))
    stage([mix])
    sent, later = assemble_rows(mix.value, me)
    ring = Task(gather_steps(sent))
    token_all = Task(token_steps(tokens[0], 3))
    marks, seg_rows = stage([ring, token_all], functools.partial(segment_marks, at_side), *mix.value)
    if blocked:
        held = Task(single_step((out_weight, GROUP, DIAGONAL)))
        for _ in range(count // 2 - 2):
            stage([ring, token_all])
        stage([ring, token_all, held])
        later = jnp.concatenate([later, fold(held.value)], axis=1)
    else:
        w_out = out_whole(out_weight, split, core, side)
    while not (ring.done and token_all.done):
        stage([ring, token_all])

    near, far, both = token_all.value
    w_pieces = ring.value
    ring = Task(gather_steps(later))
    cot_all = Task(token_steps(cotangent[0], 3))
    first, turned, x_taps, bc_taps, head_rows, gain = stage(
        [ring, cot_all], functools.partial(project, at_ring, split, sizes), tokens[0], near, far, both, per_head, heads, w_pieces
    )
    first_by_seq = first.reshape(2, LEN, W1)

    def forward(part, first, before):
        return run_forward(part, at_side, first, marks, seg_rows, x_taps, bc_taps, head_rows, heads, before)

    scanned = stage([ring, cot_all], functools.partial(forward, 0), first_by_seq, None)
    scanned = stage([ring, cot_all], functools.partial(forward, 1), first_by_seq, scanned)
    while not (ring.done and cot_all.done):
        stage([ring, cot_all])
    y = scanned[0].reshape(total, MYC)
    if blocked:
        w_out = put_together(ring.value, slice(MYC, 2 * MYC), core * (count // 2))
        blocks = [w_out[: count // 2], swap(w_out[count // 2 :], "core")]
    else:
        blocks = [w_out]
    gate_pieces = ring.value
    cot_rows = (cotangent[0], *cot_all.value)
    z, d_two, sums, w_out = meet(at_ring, *cot_rows, turned, y, x_taps, blocks, ring.value)
    sums = Task(group_steps(sums))
    stage([sums])
    unit = DI // (count * PARTS) if blocked else MYC // 2
    d_ssm, d_gate, mine, theirs, own, other = gate_back(
        at_core, unit, sums.value, y, z, d_two, x_taps, w_out
    )

    branch = Task(sum_steps(own, other, 3))
    d_theirs, d_mine = out_product(theirs, mine, *cot_rows)
    d_theirs = Task(single_step((d_theirs, "core", SWAP)))
    d_ssm = d_ssm.reshape(2, LEN, MYC)

    def back(group, part, d_bc, before):
        def run(first, d_ssm, scanned, d_bc, before):
            return run_backward(
                group, part, at_side, first, scanned, d_ssm, marks, seg_rows, x_taps, bc_taps, head_rows, heads, d_bc, before
            )

        return run, first_by_seq, d_ssm, scanned, d_bc, before

    zero = stage([d_theirs, branch], *back(0, 0, None, None))
    if blocked:
        d_w_gate = both_products(count, at_core, turned, d_gate, d_mine, d_theirs.value)
    else:
        d_w_gate = weight_product(turned, d_gate).reshape(count, D // count, MYC)
    gate_ring = Task(scatter_steps(d_w_gate))

    zero = stage([gate_ring, branch], *back(0, 1, None, zero))
    one = stage([gate_ring, branch], *back(1, 0, zero[1:3], None))
    one = stage([gate_ring, branch], *back(1, 1, zero[1:3], one))
    d_x0, _, _, wide0, thin0 = zero[:5]
    d_x1, d_bc, d_dt, wide1, thin1, bc_sums = one[:6]
    wide = jnp.concatenate([wide0, wide1], axis=1)
    thin = thin0 + thin1
    d_rows = [d_x0.reshape(total, GC), d_x1.reshape(total, GC), d_bc.reshape(total, BC), d_dt.reshape(total, LANES)]
    far_other, far = stage([gate_ring, branch], functools.partial(normed_part, 1), at_ring, *d_rows, d_gate, w_pieces, gate_pieces)
    while not (branch.done and gate_ring.done):
        stage([gate_ring, branch])
    far = Task(far_steps(far, far_other, (6, 3, 3, 4)))
    gate_sum = sum(v.astype(F32) for v in gate_ring.value).astype(BF16)
    tasks = [far]
    if blocked:
        d_out = Task(single_step((unfold(gate_sum[:, MYC:]), GROUP, DIAGONAL)))
        tasks.append(d_out)
    d_w_first = stage(tasks, weight_product, turned, *d_rows)
    rest = Task(scatter_steps(d_w_first.reshape(count, D // count, W1)))
    near_other, near = stage([rest, far], functools.partial(normed_part, 0), at_ring, *d_rows, d_gate, w_pieces, gate_pieces)
    near = Task(single_step((near_other, "core", SWAP))), near
    small_grads = Task(small_sum_steps(
        (
            wide[:KW].reshape(-1),
            wide[KW],
            bc_sums[: KW + 1].reshape(-1),
            thin[0, :MYH],
            thin[1, :MYH],
            jnp.sum(wide[KW + 1].reshape(MYH, HD), axis=1),
        ),
        core, side,
    ))
    stage([rest, far, near[0], small_grads])
    if blocked:
        d_out = d_out.value.astype(F32)
    else:
        d_mine, d_theirs = jnp.where(core == 0, d_mine, d_theirs.value), jnp.where(core == 0, d_theirs.value, d_mine)
        d_out = out_scattered(jnp.concatenate([d_mine, d_theirs], axis=0), split, core, side).astype(F32)

    def ends(x, branch, out_weight, gated_gain, d_out):
        gain_two = jnp.sum(out_weight.astype(F32) * d_out, axis=1) / gated_gain.astype(F32)
        return (x.astype(F32) + branch).astype(BF16), gain_two

    block_out, gain_two = stage(
        [rest, far, small_grads], ends, tokens[0], branch.value, out_weight, gated_gain, d_out
    )
    while not (rest.done and far.done):
        stage([rest, far, small_grads])

    d_w = Task(peer_steps(hand_back(*rest.value, gate_sum[:, :MYC], me)))
    input_grad = stage(
        [d_w, small_grads], finish_tokens, tokens[0], cotangent[0], gain, near[1], near[0].value, *far.value
    )
    finish([d_w, small_grads])
    in_sh, gain_one = join_columns(d_w.value, split, me, in_weight, jnp.broadcast_to(norm_gain[:, None], (norm_gain.shape[0], LANES)))

    taps_x, bias_x, taps_bc, bias_dt, alog, skip = small_grads.value
    taps_x = jnp.swapaxes(taps_x.reshape(2, 2, KW, MYC), 2, 3)
    taps_bc = jnp.sum(taps_bc, axis=(0, 1)).reshape(KW + 1, BC)
    conv_w = jnp.concatenate([join_heads(taps_x, 0, split), taps_bc[:KW].T], axis=0)
    conv_b = jnp.concatenate([join_heads(bias_x, 0, split), taps_bc[KW]])
    return (
        block_out[None],
        input_grad[None],
        gain_one[:, 0],
        in_sh,
        own_slice(conv_w, conv_bias.shape[0]),
        own_slice(conv_b, conv_bias.shape[0]),
        join_heads(bias_dt, 0, split),
        join_heads(alog, 0, split),
        join_heads(skip, 0, split),
        gain_two,
        d_out,
    )


def solution(mesh):
    fsdp, seq = mesh.shape["fsdp"], mesh.shape["seq"]
    grid = Mesh(mesh.devices.reshape(fsdp // 2, 2, seq), ("zy", "core", "seq"))
    every = ("zy", "core", "seq")
    rows = P(("zy", "core"), "seq", None)
    in_specs = (
        rows,
        P(("zy", "core"), "seq"),
        P(every),
        P(every, None),
        P(every, None),
        P(every),
        P(),
        P(),
        P(),
        P(every),
        P(every, None),
        rows,
    )
    out_specs = (
        rows,
        rows,
        P(every),
        P(every, None),
        P(every, None),
        P(every),
        P(),
        P(),
        P(),
        P(every),
        P(every, None),
    )
    return jax.shard_map(body, mesh=grid, in_specs=in_specs, out_specs=out_specs, check_vma=False)
```
